32 devices in a mesh: frame: 16 (over z, x, core), quad: 2 (over y).
Axes of the slice: x: 2, y: 2, z: 4, core: 2. Of those that a mesh axis runs over, the one named last changes fastest.
Arguments:
- activations: bfloat16 [64, 32, 1280], P('frame', 'quad'), may hold values from -48 to 48
- cotangent: bfloat16 [64, 32, 1280], P('frame', 'quad'), may hold values from -6 to 6
- spatial_weights: bfloat16 [4, 1280, 640], replicated, may hold values from -2 to 2
- spatial_gain: float32 [1280], replicated, may hold values from 0.1 to 1.9
- motion_weights: bfloat16 [4, 1280, 640], P(None, 'quad'), may hold values from -2 to 2
- motion_gain: float32 [1280], replicated, may hold values from 0.1 to 1.9
Outputs:
- block_output: bfloat16 [64, 32, 1280], P('frame', 'quad')
- input_grad: bfloat16 [64, 32, 1280], P('frame', 'quad')
- weight_grad: float32 [4, 1280, 640], P(None, ('frame', 'quad'))
- gain_grad: float32 [1280], P(('frame', 'quad'))
The draws below stay inside these ranges and needn't reach their ends.
All inputs are finite; a program needn't handle non-finite values.
Results may differ from the reference program's by a relative error of at most 0.03.
Values may be sent and summed in bfloat16 or wider, within the bound.
No kernel may reach another device: no remote copies, remote signals or barrier semaphores. Data moves between devices by JAX's collectives and lax.ppermute only.
A program may use at most 128 MiB of HBM per device.

```python
import math
import jax
import jax.numpy as jnp
from jax import lax

C = 1280
HEADS = 4
HEAD_DIM = 160
FRAMES = 64
POS = 32


def projection_draw(key, strength_low, strength_high, amplitude):
    pieces = jnp.clip(jax.random.normal(key, (4, C, HEADS * HEAD_DIM), jnp.float32), -4.0, 4.0)
    head_key = jax.random.fold_in(key, 5)
    strength = jnp.exp(jax.random.uniform(head_key, (HEADS,), jnp.float32, math.log(strength_low), math.log(strength_high)))
    strength = jnp.repeat(strength, HEAD_DIM)
    query_part = pieces[0] * C ** (-0.5) * strength
    key_part = pieces[1] * C ** (-0.5) * strength
    value_part = pieces[2] * C ** (-0.5) * amplitude
    output_part = pieces[3] * (HEADS * HEAD_DIM) ** (-0.5) * amplitude
    stacked = jnp.stack([query_part, key_part, value_part, output_part])
    return jnp.clip(stacked, -2.0, 2.0).astype(jnp.bfloat16)


def draw_activations(key, part):
    key = jax.random.fold_in(key, 11)
    base = jnp.clip(jax.random.normal(key, (FRAMES, POS, C), jnp.float32), -4.0, 4.0)
    return base.astype(jnp.bfloat16)


def draw_spatial_weights(key, part):
    key = jax.random.fold_in(key, 21)
    return projection_draw(key, 1.0, 1.0, 2.0)


def draw_motion_weights(key, part):
    key = jax.random.fold_in(key, 31)
    return projection_draw(key, 1.0, 1.0, 1.0)


def strengthened(values, stream_key, source, target, shards_of, factor):
    def block_of(position):
        return (jnp.arange(values.shape[position]) // (values.shape[position] // shards_of)).reshape((-1,) + (1,) * (values.ndim - 1 - position))

    near = jax.random.permutation(stream_key, shards_of)[block_of(target)]
    far = (block_of(target) + shards_of // 2) % shards_of
    return jnp.where((block_of(source) == near) | (block_of(source) == far), factor * values, values)


def block_scale(stream_key, extent, cuts, least, largest):
    loudness, own = 1.0, jax.random.fold_in(stream_key, 6)
    for axis_at, shards_of in cuts:
        heights = jnp.exp(jax.random.uniform(jax.random.fold_in(own, axis_at), (shards_of,), jnp.float32, least / len(cuts), largest / len(cuts)))
        loudness = loudness * jnp.repeat(heights, extent[axis_at] // shards_of).reshape([-1 if axis == axis_at else 1 for axis in range(len(extent))])
    return loudness


def heavy_noise(stream_key, extent, scale, limit, cuts, heavy, held_as=jnp.bfloat16):
    values = scale * jax.random.normal(stream_key, extent, jnp.float32)
    if cuts:
        values = values * block_scale(stream_key, extent, cuts, -0.22, 0.18)
    return jnp.clip(strengthened(values, jax.random.fold_in(stream_key, 3), *heavy), -limit, limit).astype(held_as)


def setup_inputs(seed: int = 0) -> dict:
    key_of = jax.random.split(jax.random.key(seed), 7)
    activations = draw_activations(jax.random.fold_in(key_of[6], 71), 0)
    cotangent = heavy_noise(key_of[1], (FRAMES, POS, C), 1.0, 6.0, ((0, 16), (1, 2)), (0, 2, 16, 2.0))
    spatial_weights = draw_spatial_weights(jax.random.fold_in(key_of[6], 71), 0)
    spatial_gain = jnp.clip(1.0 + 0.18 * jax.random.normal(key_of[3], (C,), jnp.float32), 0.1, 1.9)
    motion_weights = draw_motion_weights(jax.random.fold_in(key_of[6], 71), 0)
    motion_gain = jnp.clip(1.0 + 0.18 * jax.random.normal(key_of[5], (C,), jnp.float32), 0.1, 1.9)
    return {"activations": activations, "cotangent": cotangent, "spatial_weights": spatial_weights, "spatial_gain": spatial_gain, "motion_weights": motion_weights, "motion_gain": motion_gain}


EPSILON = 1e-05

def normalize(values, gain):
    average = lax.optimization_barrier(jnp.mean(values, axis=-1, keepdims=True))
    centred = values - average
    inv_scale = lax.rsqrt(lax.optimization_barrier(jnp.mean(centred * centred, axis=-1, keepdims=True)) + EPSILON)
    unit_rows = centred * inv_scale
    return (unit_rows * gain, unit_rows, inv_scale)

def normalize_back(grad_rows, unit_rows, inv_scale, gain):
    scaled = grad_rows * gain
    first_mean = lax.optimization_barrier(jnp.mean(scaled, axis=-1, keepdims=True))
    second_mean = lax.optimization_barrier(jnp.mean(scaled * unit_rows, axis=-1, keepdims=True))
    return inv_scale * (scaled - first_mean - unit_rows * second_mean)

def positional(frames, channels):
    frame_pos = jnp.arange(frames).astype(jnp.float32)[:, None]
    freq_index = jnp.arange(channels // 2).astype(jnp.float32)[None, :]
    phases = frame_pos * jnp.exp(freq_index * (-2.0 * math.log(10000.0) / channels))
    return jnp.stack([jnp.sin(phases), jnp.cos(phases)], axis=-1).reshape(frames, channels)

def project(row_block, weight):
    flattened = row_block.reshape(-1, row_block.shape[-1])
    result = jnp.dot(flattened, weight, preferred_element_type=jnp.float32)
    return result.reshape(row_block.shape[:-1] + (weight.shape[-1],))

def project_back(row_block, weight):
    flattened = row_block.reshape(-1, row_block.shape[-1])
    result = jnp.dot(flattened, weight.T, preferred_element_type=jnp.float32)
    return result.reshape(row_block.shape[:-1] + (weight.shape[0],))

def outer_sum(left_rows, right_rows):
    left_flat = left_rows.reshape(-1, left_rows.shape[-1])
    right_flat = right_rows.reshape(-1, right_rows.shape[-1])
    return jnp.dot(left_flat.T, right_flat, preferred_element_type=jnp.float32)

def split_heads(tensor):
    return tensor.reshape(tensor.shape[:-1] + (HEADS, HEAD_DIM)).astype(jnp.float32)

def attend(queries, key_rows, value_rows):
    query_heads = split_heads(queries)
    key_heads = split_heads(key_rows)
    value_heads = split_heads(value_rows)
    scores = jnp.einsum('bqhd,bkhd->bhqk', query_heads, key_heads) * HEAD_DIM ** (-0.5)
    highest = lax.optimization_barrier(jnp.max(scores, axis=-1, keepdims=True))
    expo_rows = jnp.exp(scores - highest)
    probs = (expo_rows / lax.optimization_barrier(jnp.sum(expo_rows, axis=-1, keepdims=True))).astype(jnp.bfloat16)
    result = jnp.einsum('bhqk,bkhd->bqhd', probs.astype(jnp.float32), value_heads)
    return result.reshape(queries.shape).astype(jnp.bfloat16)

def score_grads(queries, key_rows, value_rows, grad_rows):
    query_heads = split_heads(queries)
    key_heads = split_heads(key_rows)
    value_heads = split_heads(value_rows)
    grad_heads = split_heads(grad_rows)
    scores = jnp.einsum('bqhd,bkhd->bhqk', query_heads, key_heads) * HEAD_DIM ** (-0.5)
    highest = lax.optimization_barrier(jnp.max(scores, axis=-1, keepdims=True))
    log_total = highest + jnp.log(lax.optimization_barrier(jnp.sum(jnp.exp(scores - highest), axis=-1, keepdims=True)))
    probs = jnp.exp(scores - log_total)
    grad_probs = jnp.einsum('bqhd,bkhd->bhqk', grad_heads, value_heads)
    inner_sum = lax.optimization_barrier(jnp.sum(probs * grad_probs, axis=-1, keepdims=True))
    grad_scores = (probs * (grad_probs - inner_sum) * HEAD_DIM ** (-0.5)).astype(jnp.bfloat16)
    return (probs.astype(jnp.bfloat16), grad_scores)

def attend_back(queries, key_rows, value_rows, grad_rows):
    probs, grad_scores = score_grads(queries, key_rows, value_rows, grad_rows)
    query_heads = split_heads(queries)
    key_heads = split_heads(key_rows)
    grad_heads = split_heads(grad_rows)
    grad_query = jnp.einsum('bhqk,bkhd->bqhd', grad_scores.astype(jnp.float32), key_heads)
    grad_key = jnp.einsum('bhqk,bqhd->bkhd', grad_scores.astype(jnp.float32), query_heads)
    grad_value = jnp.einsum('bhqk,bqhd->bkhd', probs.astype(jnp.float32), grad_heads)
    return (grad_query.reshape(queries.shape).astype(jnp.bfloat16), grad_key.reshape(key_rows.shape).astype(jnp.bfloat16), grad_value.reshape(key_rows.shape).astype(jnp.bfloat16))

def blocked(function, arrays, block_size):
    groups = arrays[0].shape[0] // block_size
    grouped = tuple((member.reshape((groups, block_size) + member.shape[1:]) for member in arrays))
    results = lax.map(lambda members: function(*members), grouped)
    return jax.tree.map(lambda piece: piece.reshape((groups * block_size,) + piece.shape[2:]), results)

def reference(activations, cotangent, spatial_weights, spatial_gain, motion_weights, motion_gain):
    frames, cells, channels = activations.shape
    input_wide = activations.astype(jnp.float32)
    normed, unit_one, scale_one = normalize(input_wide, spatial_gain)
    normed_one = normed.astype(jnp.bfloat16)
    spatial_query = project(normed_one, spatial_weights[0]).astype(jnp.bfloat16)
    spatial_keys = project(normed_one, spatial_weights[1]).astype(jnp.bfloat16)
    spatial_values = project(normed_one, spatial_weights[2]).astype(jnp.bfloat16)
    spatial_out = blocked(attend, (spatial_query, spatial_keys, spatial_values), 8)
    hidden = (input_wide + project_back(spatial_out, spatial_weights[3])).astype(jnp.bfloat16)
    by_cell = jnp.swapaxes(hidden, 0, 1)
    cell_wide = by_cell.astype(jnp.float32)
    normed_t, unit_two, scale_two = normalize(cell_wide, motion_gain)
    normed_two = (normed_t + positional(frames, channels)[None]).astype(jnp.bfloat16)
    motion_query = project(normed_two, motion_weights[0]).astype(jnp.bfloat16)
    motion_keys = project(normed_two, motion_weights[1]).astype(jnp.bfloat16)
    motion_values = project(normed_two, motion_weights[2]).astype(jnp.bfloat16)
    motion_out = blocked(attend, (motion_query, motion_keys, motion_values), 8)
    result_cells = (cell_wide + project_back(motion_out, motion_weights[3])).astype(jnp.bfloat16)
    block_output = jnp.swapaxes(result_cells, 0, 1)
    grad_by_cell = jnp.swapaxes(cotangent, 0, 1)
    grad_motion_out = project(grad_by_cell, motion_weights[3]).astype(jnp.bfloat16)
    grad_out_proj = outer_sum(grad_by_cell, motion_out)
    grad_mq, grad_mk, grad_mv = blocked(attend_back, (motion_query, motion_keys, motion_values, grad_motion_out), 8)
    weight_terms = jnp.stack([outer_sum(normed_two, grad_mq), outer_sum(normed_two, grad_mk), outer_sum(normed_two, grad_mv), grad_out_proj])
    grad_normed_two = project_back(grad_mq, motion_weights[0]) + project_back(grad_mk, motion_weights[1]) + project_back(grad_mv, motion_weights[2])
    gain_terms = lax.optimization_barrier(jnp.sum((grad_normed_two * unit_two).reshape(-1, channels), axis=0))
    grad_hidden_cells = (grad_by_cell.astype(jnp.float32) + normalize_back(grad_normed_two, unit_two, scale_two, motion_gain)).astype(jnp.bfloat16)
    grad_hidden = jnp.swapaxes(grad_hidden_cells, 0, 1)
    grad_spatial_out = project(grad_hidden, spatial_weights[3]).astype(jnp.bfloat16)
    grad_sq, grad_sk, grad_sv = blocked(attend_back, (spatial_query, spatial_keys, spatial_values, grad_spatial_out), 8)
    grad_normed_one = project_back(grad_sq, spatial_weights[0]) + project_back(grad_sk, spatial_weights[1]) + project_back(grad_sv, spatial_weights[2])
    input_grad = (grad_hidden.astype(jnp.float32) + normalize_back(grad_normed_one, unit_one, scale_one, spatial_gain)).astype(jnp.bfloat16)
    factor = 1.0 / math.sqrt(frames * cells)
    return (block_output, input_grad, weight_terms * factor, gain_terms * factor)
```

```python
import functools
import math

import jax
import jax.numpy as jnp
from jax import lax
from jax.experimental import pallas as pl
from jax.experimental.pallas import tpu as pltpu
from jax.sharding import PartitionSpec as P

HEADS = 4
HEAD_DIM = 160
EPSILON = 1e-05
SCALE = HEAD_DIM ** (-0.5)
F32 = jnp.float32
BF16 = jnp.bfloat16


def log2(n):
    return int(n).bit_length() - 1


def dot(a, b):
    return jnp.dot(a, b, preferred_element_type=F32)


def dot_t(a, b):
    return lax.dot_general(a, b, (((1,), (1,)), ((), ())), preferred_element_type=F32)


def t_dot(a, b):
    return lax.dot_general(a, b, (((0,), (0,)), ((), ())), preferred_element_type=F32)


def normalize(values):
    average = jnp.mean(values, axis=-1, keepdims=True)
    centred = values - average
    inv_scale = lax.rsqrt(jnp.mean(centred * centred, axis=-1, keepdims=True) + EPSILON)
    return centred * inv_scale, inv_scale


def normalize_back(grad_rows, unit_rows, inv_scale, gain):
    scaled = grad_rows * gain
    first_mean = jnp.mean(scaled, axis=-1, keepdims=True)
    second_mean = jnp.mean(scaled * unit_rows, axis=-1, keepdims=True)
    return inv_scale * (scaled - first_mean - unit_rows * second_mean)


def iota(shape, dim):
    return lax.broadcasted_iota(jnp.int32, shape, dim)


def head_mask(dtype):
    lane = iota((1, HEADS * HEAD_DIM), 1)
    return [
        jnp.where((lane >= h * HEAD_DIM) & (lane < (h + 1) * HEAD_DIM), 1.0, 0.0).astype(dtype)
        for h in range(HEADS)
    ]


def stack_heads(rows):
    return jnp.concatenate([rows * mask for mask in head_mask(rows.dtype)], axis=0)


def fold_heads(stacked):
    rows = stacked.shape[0] // HEADS
    total = None
    for h, mask in enumerate(head_mask(F32)):
        piece = stacked[h * rows : (h + 1) * rows] * mask
        total = piece if total is None else total + piece
    return total


def probabilities(query_stack, keys, same):
    scores = dot_t(query_stack, keys) * SCALE
    if same is not None:
        scores = jnp.where(same, scores, -1e30)
    highest = jnp.max(scores, axis=-1, keepdims=True)
    expo = jnp.exp(scores - highest)
    return expo / jnp.sum(expo, axis=-1, keepdims=True)


def attend(query, keys, values, same):
    probs = probabilities(stack_heads(query), keys, same)
    return fold_heads(dot(probs.astype(BF16), values)).astype(BF16)


def attend_back(query, keys, values, grad, same, probs=None):
    query_stack = stack_heads(query)
    grad_stack = stack_heads(grad)
    if probs is None:
        probs = probabilities(query_stack, keys, same)
    grad_probs = dot_t(grad_stack, values)
    inner = jnp.sum(probs * grad_probs, axis=-1, keepdims=True)
    grad_scores = (probs * (grad_probs - inner) * SCALE).astype(BF16)
    grad_query = fold_heads(dot(grad_scores, keys)).astype(BF16)
    grad_key = t_dot(grad_scores, query_stack).astype(BF16)
    grad_value = t_dot(probs.astype(BF16), grad_stack).astype(BF16)
    return grad_query, grad_key, grad_value


def rows_to_sent(quad, nq, fr, pq, transposed):
    rows = nq * fr * pq
    out_dim = 1 if transposed else 0
    out = iota((rows, rows), out_dim)
    src = iota((rows, rows), 1 - out_dim)
    cell = out >> log2(nq * fr)
    other = (out >> log2(fr)) & (nq - 1)
    frame = out & (fr - 1)
    want = (((other - quad) & (nq - 1)) << log2(fr * pq)) + (frame << log2(pq)) + cell
    return jnp.where(want == src, 1.0, 0.0).astype(BF16)


def received_to_rows(quad, nq, nf, fr, transposed):
    rows = nq * nf * fr
    out_dim = 1 if transposed else 0
    out = iota((rows, rows), out_dim)
    src = iota((rows, rows), 1 - out_dim)
    step = out >> log2(nf * fr)
    device = (out >> log2(fr)) & (nf - 1)
    frame = out & (fr - 1)
    want = (device << log2(nq * fr)) + (((step + quad) & (nq - 1)) << log2(fr)) + frame
    return jnp.where(want == src, 1.0, 0.0).astype(BF16)


def own_lanes(values, quad, nq):
    width = values.shape[1] // nq
    picked = values[:, :width]
    for t in range(1, nq):
        picked = jnp.where(quad == t, values[:, t * width : (t + 1) * width], picked)
    return picked


def place_lanes(parts, quad, nq):
    placed = []
    for t in range(nq):
        piece = parts[t]
        for q in range(1, nq):
            piece = jnp.where(quad == q, parts[(t - q) % nq], piece)
        placed.append(piece)
    return jnp.concatenate(placed, axis=1)


def frame_groups(nq, fr, pq):
    size = max(1, min(fr, 128 // (nq * pq)))
    return [(start, size) for start in range(0, fr, size)]


def pick_group(rows, group, nq, fr, pq):
    start, size = group
    if size == fr:
        return rows
    cut = rows.reshape(nq, fr, pq, rows.shape[-1])[:, start : start + size]
    return cut.reshape(nq * size * pq, rows.shape[-1])


def join_groups(pieces, nq, fr, pq):
    if len(pieces) == 1:
        return pieces[0]
    size = fr // len(pieces)
    width = pieces[0].shape[-1]
    joined = jnp.concatenate([p.reshape(nq, size, pq, width) for p in pieces], axis=1)
    return joined.reshape(nq * fr * pq, width)


def same_frame(nq, size, pq):
    if size == 1:
        return None
    rows = nq * size * pq
    shape = (HEADS * rows, rows)
    left = (iota(shape, 0) >> log2(pq)) & (size - 1)
    right = (iota(shape, 1) >> log2(pq)) & (size - 1)
    return left == right


def flat(ref):
    value = ref[...]
    return value.reshape(-1, value.shape[-1])


def flat_wide(ref):
    value = ref[...].astype(F32)
    return value.reshape(-1, value.shape[-1])


def spread(rows, like):
    return rows.reshape(like.shape).astype(like.dtype)


def weight_loader(hbm, vmem, sems):
    copies = [pltpu.make_async_copy(hbm.at[k], vmem.at[k], sems.at[k]) for k in range(hbm.shape[0])]
    for copy in copies:
        copy.start()

    def load(k):
        copies[k].wait()
        return vmem[k]

    return load


def spatial_kernel(dims, *refs):
    nq, nf, fr, pq = dims
    quad_ref, xs = refs[0], refs[1 : 1 + nq]
    gain1, gain2, pos, w_hbm, q_out, k_out, v_out, hid_out, send_out, w_vmem, sems = refs[1 + nq :]
    load = weight_loader(w_hbm, w_vmem, sems)
    quad = quad_ref[0]
    wide = jnp.concatenate([flat_wide(x) for x in xs], axis=0)
    unit, _ = normalize(wide)
    normed = (unit * gain1[...]).astype(BF16)
    query = dot(normed, load(0)).astype(BF16)
    keys = dot(normed, load(1)).astype(BF16)
    values = dot(normed, load(2)).astype(BF16)
    q_out[...], k_out[...], v_out[...] = query, keys, values
    pieces = []
    for group in frame_groups(nq, fr, pq):
        same = same_frame(nq, group[1], pq)
        cut = [pick_group(part, group, nq, fr, pq) for part in (query, keys, values)]
        pieces.append(attend(*cut, same))
    out = join_groups(pieces, nq, fr, pq)
    hidden = (wide + dot_t(out, load(3))).astype(BF16)
    hid_out[...] = hidden
    unit_two, _ = normalize(hidden.astype(F32))
    table = jnp.broadcast_to(pos[...][:, None, :], (fr, pq, pos.shape[-1]))
    table = table.reshape(fr * pq, pos.shape[-1])
    table = jnp.concatenate([table] * nq, axis=0)
    normed_two = own_lanes(unit_two * gain2[...] + table, quad, nq).astype(BF16)
    send_out[...] = spread(dot(rows_to_sent(quad, nq, fr, pq, False), normed_two), send_out)


def order_kernel(dims, *refs):
    nq, nf, fr, pq = dims
    quad_ref, xs, send_out = refs[0], refs[1 : 1 + nq], refs[1 + nq]
    quad = quad_ref[0]
    picked = own_lanes(jnp.concatenate([flat(x) for x in xs], axis=0), quad, nq)
    send_out[...] = spread(dot(rows_to_sent(quad, nq, fr, pq, False), picked), send_out)


def partial_kernel(dims, quad_ref, received, w_hbm, rows_out, own_out, *rest):
    nq, nf, fr, pq = dims
    sends, (w_vmem, sems) = rest[: nq - 1], rest[nq - 1 :]
    load = weight_loader(w_hbm, w_vmem, sems)
    order = received_to_rows(quad_ref[0], nq, nf, fr, False)
    rows = dot(order, flat_wide(received).astype(BF16)).astype(BF16)
    rows_out[...] = rows
    tokens = nf * fr
    for k in range(w_hbm.shape[0]):
        width = w_hbm.shape[-1]
        lanes = slice(k * width, (k + 1) * width)
        product = dot(rows, load(k))
        own_out[:, lanes] = product[:tokens]
        for s in range(1, nq):
            sends[s - 1][:, lanes] = product[s * tokens : (s + 1) * tokens].astype(BF16)


def temporal_kernel(dims, *refs):
    nq, nf, fr, pq = dims
    qkv_own, qkv_in = refs[0], refs[1:nq]
    grad_own, grad_in = refs[nq], refs[nq + 1 : 2 * nq]
    out = refs[2 * nq]
    width = HEADS * HEAD_DIM
    total = qkv_own[...]
    for part in qkv_in:
        total = total + part[...].astype(F32)
    grad = grad_own[...]
    for part in grad_in:
        grad = grad + part[...].astype(F32)
    query, keys, values = [total[:, k * width : (k + 1) * width].astype(BF16) for k in range(3)]
    grad = grad.astype(BF16)
    probs = probabilities(stack_heads(query), keys, None)
    motion_out = fold_heads(dot(probs.astype(BF16), values)).astype(BF16)
    grads = attend_back(query, keys, values, grad, None, probs)
    for k, piece in enumerate(grads + (motion_out,)):
        out[:, k * width : (k + 1) * width] = piece


def back_kernel(dims, quad_ref, *refs):
    nq, nf, fr, pq = dims
    terms, (w_hbm, gn_out, delta_out, w_vmem, sems) = refs[:nq], refs[nq:]
    load = weight_loader(w_hbm, w_vmem, sems)
    width = HEADS * HEAD_DIM
    order = received_to_rows(quad_ref[0], nq, nf, fr, True)

    def part(k):
        return jnp.concatenate([t[:, k * width : (k + 1) * width] for t in terms], axis=0)

    grad = dot_t(part(0), load(0)) + dot_t(part(1), load(1)) + dot_t(part(2), load(2))
    gn_out[...] = spread(dot(order, grad.astype(BF16)), gn_out)
    delta = dot_t(part(3), load(3)).astype(BF16)
    delta_out[...] = spread(dot(order, delta), delta_out)


def weight_kernel(dims, cut, core_ref, rows, cot_rows, *refs):
    nq, nf, fr, pq = dims
    terms, (keep_out, send_out) = refs[:nq], refs[nq:]
    width = HEADS * HEAD_DIM
    split, cross, stage, block = cut
    core = core_ref[0]
    for k in range(4):
        right = jnp.concatenate([t[:, k * width : (k + 1) * width] for t in terms], axis=0)
        left = (rows if k < 3 else cot_rows)[...]
        product = t_dot(left, right)
        for x in range(cross):
            for z in range(stage):
                low, high = [
                    product[j * block : (j + 1) * block] for j in (split(x, 0, z), split(x, 1, z))
                ]
                keep_out[x, z, k] = jnp.where(core == 0, low, high).astype(BF16)
                send_out[x, z, k] = jnp.where(core == 0, high, low).astype(BF16)


def tail_kernel(dims, *refs):
    nq, nf, fr, pq = dims
    quad_ref, xs, cots, hid = refs[0], refs[1], refs[2 : 2 + nq], refs[2 + nq]
    refs = refs[3 + nq :]
    gns, refs = refs[:nq], refs[nq:]
    q_in, k_in, v_in, gain1, gain2, w_hbm, in_grad, gain_out, w_vmem, sems = refs
    load = weight_loader(w_hbm, w_vmem, sems)
    quad = quad_ref[0]
    own = fr * pq
    order = rows_to_sent(quad, nq, fr, pq, True)
    parts = [dot(order, flat_wide(g).astype(BF16)) for g in gns]
    grad_normed = place_lanes(parts, quad, nq)
    unit_two, inv_two = normalize(hid[...].astype(F32))
    gain_out[...] = jnp.sum(grad_normed[:own] * unit_two[:own], axis=0, keepdims=True)
    cot = jnp.concatenate([flat_wide(c) for c in cots], axis=0)
    grad_hidden = (cot + normalize_back(grad_normed, unit_two, inv_two, gain2[...])).astype(BF16)
    grad_out = dot(grad_hidden, load(3)).astype(BF16)
    query, keys, values = q_in[...], k_in[...], v_in[...]
    pieces = []
    for group in frame_groups(nq, fr, pq):
        same = same_frame(nq, group[1], pq)
        cut = [pick_group(part, group, nq, fr, pq) for part in (query, keys, values, grad_out)]
        pieces.append(attend_back(*cut, same))
    grads = [join_groups([p[i] for p in pieces], nq, fr, pq)[:own] for i in range(3)]
    grad_one = dot_t(grads[0], load(0)) + dot_t(grads[1], load(1)) + dot_t(grads[2], load(2))
    unit_one, inv_one = normalize(flat_wide(xs))
    result = grad_hidden[:own].astype(F32) + normalize_back(grad_one, unit_one, inv_one, gain1[...])
    in_grad[...] = spread(result, in_grad)


def block_kernel(dims, *refs):
    nq, nf, fr, pq = dims
    quad_ref, hid, deltas, out = refs[0], refs[1], refs[2 : 2 + nq], refs[2 + nq]
    quad = quad_ref[0]
    own = fr * pq
    order = rows_to_sent(quad, nq, fr, pq, True)[:own]
    parts = [dot(order, flat_wide(d).astype(BF16)) for d in deltas]
    out[...] = spread(hid[...][:own].astype(F32) + place_lanes(parts, quad, nq), out)


def call(kernel, name, outs, args, weights=None, vmem=40):
    in_specs = []
    for i, arg in enumerate(args):
        if arg.dtype == jnp.int32:
            in_specs.append(pl.BlockSpec(memory_space=pltpu.SMEM))
        elif i == weights:
            in_specs.append(pl.BlockSpec(memory_space=pl.ANY))
        else:
            in_specs.append(pl.BlockSpec(memory_space=pltpu.VMEM))
    scratch = []
    if weights is not None:
        shape = args[weights].shape
        scratch = [pltpu.VMEM(shape, BF16), pltpu.SemaphoreType.DMA((shape[0],))]
    return pl.pallas_call(
        kernel,
        out_shape=outs,
        in_specs=in_specs,
        out_specs=jax.tree.map(lambda _: pl.BlockSpec(memory_space=pltpu.VMEM), outs),
        scratch_shapes=scratch,
        compiler_params=pltpu.CompilerParams(vmem_limit_bytes=vmem * 1024 * 1024),
        name=name,
    )(*args)


def sds(*shape, dtype=BF16):
    return jax.ShapeDtypeStruct(shape, dtype)


def positional(first, frames, channels):
    frame_pos = (first + jnp.arange(frames)).astype(F32)[:, None]
    freq_index = jnp.arange(channels // 2).astype(F32)[None, :]
    phases = frame_pos * jnp.exp(freq_index * (-2.0 * math.log(10000.0) / channels))
    return jnp.stack([jnp.sin(phases), jnp.cos(phases)], axis=-1).reshape(frames, channels)


def local(nq, nf, activations, cotangent, spatial_weights, spatial_gain, motion_weights, motion_gain):
    fr, pq, channels = activations.shape
    dims = (nq, nf, fr, pq)
    width = spatial_weights.shape[-1]
    half = channels // nq
    rows = nq * fr * pq
    tokens = nf * fr
    big = 40 if rows <= 256 else 60
    quad = lax.axis_index("quad")
    frame = lax.axis_index("frame")
    quad_arr = quad.astype(jnp.int32).reshape(1)

    def from_quad(x, s):
        return lax.ppermute(x, "quad", [((d + s) % nq, d) for d in range(nq)])

    def to_quad(x, s):
        return lax.ppermute(x, "quad", [(d, (d + s) % nq) for d in range(nq)])

    def swap(x):
        return lax.all_to_all(x, "frame", split_axis=0, concat_axis=0, tiled=True)

    def bound(kernel):
        return functools.partial(kernel, dims)

    gain1 = spatial_gain.reshape(1, channels)
    gain2 = motion_gain.reshape(1, channels)
    acts = [activations] + [from_quad(activations, s) for s in range(1, nq)]
    cots = [cotangent] + [from_quad(cotangent, s) for s in range(1, nq)]
    pos = positional(frame * fr, fr, channels)

    sent = sds(nf, nq * fr, half)
    cot_send = call(bound(order_kernel), "order_cotangent", sent, [quad_arr] + cots)
    cot_recv = swap(cot_send)

    query, keys, values, hidden, send = call(
        bound(spatial_kernel),
        "spatial_forward",
        [sds(rows, width)] * 3 + [sds(rows, channels), sent],
        [quad_arr] + acts + [gain1, gain2, pos, spatial_weights],
        weights=4 + nq,
        vmem=big,
    )
    received = swap(send)

    def partial(name, recv, weights):
        n = weights.shape[0]
        outs = [sds(rows, half), sds(tokens, n * width, dtype=F32)]
        outs = outs + [sds(tokens, n * width)] * (nq - 1)
        got = call(bound(partial_kernel), name, outs, [quad_arr, recv, weights], weights=2)
        moved = [to_quad(part, s + 1) for s, part in enumerate(got[2:])]
        return got[0], [got[1]] + moved

    cot_rows, grad_parts = partial("cotangent_projection", cot_recv, motion_weights[3:])
    normed_rows, qkv_parts = partial("motion_projection", received, motion_weights[:3])

    terms = call(
        bound(temporal_kernel), "temporal_attention", sds(tokens, 4 * width), qkv_parts + grad_parts
    )
    all_terms = [terms] + [from_quad(terms, s) for s in range(1, nq)]
    gn_send, delta_send = call(
        bound(back_kernel),
        "temporal_back_projection",
        [sent, sent],
        [quad_arr] + all_terms + [motion_weights],
        weights=1 + nq,
    )
    gn_recv = swap(gn_send)

    cross = 2
    stage = nf // 4
    block = half // nf

    def split(x, c, z):
        e, a = z // 2, z % 2
        return ((a * 2 + x) * 2 + c) * (stage // 2) + e

    core = frame % 2
    mid = (frame // 2) % 2
    turn = frame // 4
    core_arr = core.astype(jnp.int32).reshape(1)
    keep, other = call(
        functools.partial(weight_kernel, dims, (split, cross, stage, block)),
        "weight_terms",
        [sds(cross, stage, 4, block, width)] * 2,
        [core_arr, normed_rows, cot_rows] + all_terms,
    )
    flip_core = [(g, g ^ 1) for g in range(nf)]
    flip_mid = [(g, g ^ 2) for g in range(nf)]
    ring = [(g, (g + 4) % nf) for g in range(nf)]
    got = lax.ppermute(other, "frame", flip_core)

    def pick(x, index):
        return lax.dynamic_index_in_dim(x, index, 0, keepdims=False)

    def add(a, b):
        return (a.astype(F32) + b.astype(F32)).astype(BF16)

    mine = add(pick(keep, mid), pick(got, mid))
    theirs = add(pick(keep, 1 - mid), pick(got, 1 - mid))
    mine = add(mine, lax.ppermute(theirs, "frame", flip_mid))
    total = pick(mine, (turn - 1) % stage)
    for step in range(1, stage):
        moved = lax.ppermute(total, "frame", ring)
        total = add(moved, pick(mine, (turn - 1 - step) % stage))
    final = []
    for g in range(nf):
        z, x, c = g // 4, (g // 2) % 2, g % 2
        for q in range(nq):
            final.append((g * nq + q, nf * q + split(x, c, z)))
    total = lax.ppermute(total, ("frame", "quad"), final)

    gns = [gn_recv] + [from_quad(gn_recv, s) for s in range(1, nq)]
    delta_recv = swap(delta_send)
    deltas = [delta_recv] + [from_quad(delta_recv, s) for s in range(1, nq)]
    input_grad, gain_terms = call(
        bound(tail_kernel),
        "spatial_backward",
        [sds(fr, pq, channels), sds(1, channels, dtype=F32)],
        [quad_arr, activations]
        + cots
        + [hidden]
        + gns
        + [query, keys, values, gain1, gain2, spatial_weights],
        weights=2 + nq + 1 + nq + 5,
        vmem=big,
    )
    block_output = call(
        bound(block_kernel), "block_output", sds(fr, pq, channels), [quad_arr, hidden] + deltas
    )
    everyone = nf * nq
    gain_moved = lax.all_to_all(
        gain_terms.reshape(everyone, channels // everyone),
        ("frame", "quad"),
        split_axis=0,
        concat_axis=0,
        tiled=True,
    )
    factor = 1.0 / math.sqrt(everyone * fr * pq)
    weight_grad = total.astype(F32) * factor
    gain_grad = jnp.sum(gain_moved, axis=0) * factor
    return block_output, input_grad, weight_grad, gain_grad


def solution(mesh):
    in_specs = (
        P("frame", "quad", None),
        P("frame", "quad", None),
        P(),
        P(),
        P(None, "quad", None),
        P(),
    )
    out_specs = (
        P("frame", "quad", None),
        P("frame", "quad", None),
        P(None, ("frame", "quad"), None),
        P(("frame", "quad")),
    )
    body = functools.partial(local, mesh.shape["quad"], mesh.shape["frame"])
    return jax.shard_map(
        body, mesh=mesh, in_specs=in_specs, out_specs=out_specs, check_vma=False
    )
```

```python
import functools
import math

import jax
import jax.numpy as jnp
from jax import lax
from jax.experimental import pallas as pl
from jax.experimental.pallas import tpu as pltpu
from jax.sharding import PartitionSpec as P

HEADS = 4
HEAD_DIM = 160
EPSILON = 1e-05
SCALE = HEAD_DIM ** (-0.5)
F32 = jnp.float32
BF16 = jnp.bfloat16


def log2(n):
    return int(n).bit_length() - 1


def dot(a, b):
    return jnp.dot(a, b, preferred_element_type=F32)


def dot_t(a, b):
    return lax.dot_general(a, b, (((1,), (1,)), ((), ())), preferred_element_type=F32)


def t_dot(a, b):
    return lax.dot_general(a, b, (((0,), (0,)), ((), ())), preferred_element_type=F32)


def normalize(values):
    average = jnp.mean(values, axis=-1, keepdims=True)
    centred = values - average
    inv_scale = lax.rsqrt(jnp.mean(centred * centred, axis=-1, keepdims=True) + EPSILON)
    return centred * inv_scale, inv_scale


def normalize_back(grad_rows, unit_rows, inv_scale, gain):
    scaled = grad_rows * gain
    first_mean = jnp.mean(scaled, axis=-1, keepdims=True)
    second_mean = jnp.mean(scaled * unit_rows, axis=-1, keepdims=True)
    return inv_scale * (scaled - first_mean - unit_rows * second_mean)


def iota(shape, dim):
    return lax.broadcasted_iota(jnp.int32, shape, dim)


def head_mask(dtype):
    lane = iota((1, HEADS * HEAD_DIM), 1)
    return [
        jnp.where((lane >= h * HEAD_DIM) & (lane < (h + 1) * HEAD_DIM), 1.0, 0.0).astype(dtype)
        for h in range(HEADS)
    ]


def stack_heads(rows):
    return jnp.concatenate([rows * mask for mask in head_mask(rows.dtype)], axis=0)


def fold_heads(stacked):
    rows = stacked.shape[0] // HEADS
    total = None
    for h, mask in enumerate(head_mask(F32)):
        piece = stacked[h * rows : (h + 1) * rows] * mask
        total = piece if total is None else total + piece
    return total


def probabilities(query_stack, keys, same):
    scores = dot_t(query_stack, keys) * SCALE
    if same is not None:
        scores = jnp.where(same, scores, -1e30)
    highest = jnp.max(scores, axis=-1, keepdims=True)
    expo = jnp.exp(scores - highest)
    return expo / jnp.sum(expo, axis=-1, keepdims=True)


def attend(query, keys, values, same):
    probs = probabilities(stack_heads(query), keys, same)
    return fold_heads(dot(probs.astype(BF16), values)).astype(BF16)


def attend_back(query, keys, values, grad, same, probs=None):
    query_stack = stack_heads(query)
    grad_stack = stack_heads(grad)
    if probs is None:
        probs = probabilities(query_stack, keys, same)
    grad_probs = dot_t(grad_stack, values)
    inner = jnp.sum(probs * grad_probs, axis=-1, keepdims=True)
    grad_scores = (probs * (grad_probs - inner) * SCALE).astype(BF16)
    grad_query = fold_heads(dot(grad_scores, keys)).astype(BF16)
    grad_key = t_dot(grad_scores, query_stack).astype(BF16)
    grad_value = t_dot(probs.astype(BF16), grad_stack).astype(BF16)
    return grad_query, grad_key, grad_value


def rows_to_sent(quad, nq, fr, pq, transposed):
    rows = nq * fr * pq
    out_dim = 1 if transposed else 0
    out = iota((rows, rows), out_dim)
    src = iota((rows, rows), 1 - out_dim)
    cell = out >> log2(nq * fr)
    other = (out >> log2(fr)) & (nq - 1)
    frame = out & (fr - 1)
    want = (((other - quad) & (nq - 1)) << log2(fr * pq)) + (frame << log2(pq)) + cell
    return jnp.where(want == src, 1.0, 0.0).astype(BF16)


def received_to_rows(quad, nq, nf, fr, transposed):
    rows = nq * nf * fr
    out_dim = 1 if transposed else 0
    out = iota((rows, rows), out_dim)
    src = iota((rows, rows), 1 - out_dim)
    step = out >> log2(nf * fr)
    device = (out >> log2(fr)) & (nf - 1)
    frame = out & (fr - 1)
    want = (device << log2(nq * fr)) + (((step + quad) & (nq - 1)) << log2(fr)) + frame
    return jnp.where(want == src, 1.0, 0.0).astype(BF16)


def own_lanes(values, quad, nq):
    width = values.shape[1] // nq
    picked = values[:, :width]
    for t in range(1, nq):
        picked = jnp.where(quad == t, values[:, t * width : (t + 1) * width], picked)
    return picked


def place_lanes(parts, quad, nq):
    placed = []
    for t in range(nq):
        piece = parts[t]
        for q in range(1, nq):
            piece = jnp.where(quad == q, parts[(t - q) % nq], piece)
        placed.append(piece)
    return jnp.concatenate(placed, axis=1)


def frame_groups(nq, fr, pq):
    size = max(1, min(fr, 128 // (nq * pq)))
    return [(start, size) for start in range(0, fr, size)]


def pick_group(rows, group, nq, fr, pq):
    start, size = group
    if size == fr:
        return rows
    cut = rows.reshape(nq, fr, pq, rows.shape[-1])[:, start : start + size]
    return cut.reshape(nq * size * pq, rows.shape[-1])


def join_groups(pieces, nq, fr, pq):
    if len(pieces) == 1:
        return pieces[0]
    size = fr // len(pieces)
    width = pieces[0].shape[-1]
    joined = jnp.concatenate([p.reshape(nq, size, pq, width) for p in pieces], axis=1)
    return joined.reshape(nq * fr * pq, width)


def same_frame(nq, size, pq):
    if size == 1:
        return None
    rows = nq * size * pq
    shape = (HEADS * rows, rows)
    left = (iota(shape, 0) >> log2(pq)) & (size - 1)
    right = (iota(shape, 1) >> log2(pq)) & (size - 1)
    return left == right


def flat(ref):
    value = ref[...]
    return value.reshape(-1, value.shape[-1])


def flat_wide(ref):
    value = ref[...].astype(F32)
    return value.reshape(-1, value.shape[-1])


def spread(rows, like):
    return rows.reshape(like.shape).astype(like.dtype)


def spatial_kernel(dims, *refs):
    nq, nf, fr, pq = dims
    quad_ref, xs = refs[0], refs[1 : 1 + nq]
    gain1, gain2, pos, weights, q_out, k_out, v_out, hid_out, send_out = refs[1 + nq :]
    quad = quad_ref[0]
    wide = jnp.concatenate([flat_wide(x) for x in xs], axis=0)
    unit, _ = normalize(wide)
    normed = (unit * gain1[...]).astype(BF16)
    query = dot(normed, weights[0]).astype(BF16)
    keys = dot(normed, weights[1]).astype(BF16)
    values = dot(normed, weights[2]).astype(BF16)
    q_out[...], k_out[...], v_out[...] = query, keys, values
    pieces = []
    for group in frame_groups(nq, fr, pq):
        same = same_frame(nq, group[1], pq)
        cut = [pick_group(part, group, nq, fr, pq) for part in (query, keys, values)]
        pieces.append(attend(*cut, same))
    out = join_groups(pieces, nq, fr, pq)
    hidden = (wide + dot_t(out, weights[3])).astype(BF16)
    hid_out[...] = hidden
    unit_two, _ = normalize(hidden.astype(F32))
    table = jnp.broadcast_to(pos[...][:, None, :], (fr, pq, pos.shape[-1]))
    table = table.reshape(fr * pq, pos.shape[-1])
    table = jnp.concatenate([table] * nq, axis=0)
    normed_two = own_lanes(unit_two * gain2[...] + table, quad, nq).astype(BF16)
    send_out[...] = spread(dot(rows_to_sent(quad, nq, fr, pq, False), normed_two), send_out)


def order_kernel(dims, cot, send_out):
    nq, nf, fr, pq = dims
    rows = flat(cot)
    width = rows.shape[1] // nq
    shape = (nq * fr * pq, fr * pq)
    out, src = iota(shape, 0), iota(shape, 1)
    want = ((out & (fr - 1)) << log2(pq)) + (out >> log2(nq * fr))
    part = (out >> log2(fr)) & (nq - 1)
    total = None
    for t in range(nq):
        pick = jnp.where((want == src) & (part == t), 1.0, 0.0).astype(BF16)
        piece = dot(pick, rows[:, t * width : (t + 1) * width])
        total = piece if total is None else total + piece
    send_out[...] = spread(total, send_out)


def split_kernel(dims, quad_ref, received, *outs):
    nq, nf, fr, pq = dims
    order = received_to_rows(quad_ref[0], nq, nf, fr, False)
    rows = dot(order, flat_wide(received).astype(BF16)).astype(BF16)
    tokens = nf * fr
    for s in range(nq):
        outs[s][...] = rows[s * tokens : (s + 1) * tokens]


def project_parts(rows, weights, which, own_out, sends, tokens):
    for place, k in enumerate(which):
        width = weights.shape[-1]
        lanes = slice(place * width, (place + 1) * width)
        product = dot(rows, weights[k])
        own_out[:, lanes] = product[:tokens]
        for s, send in enumerate(sends):
            send[:, lanes] = product[(s + 1) * tokens : (s + 2) * tokens].astype(BF16)


def motion_kernel(dims, quad_ref, received, weights, rows_out, own_out, *sends):
    nq, nf, fr, pq = dims
    order = received_to_rows(quad_ref[0], nq, nf, fr, False)
    rows = dot(order, flat_wide(received).astype(BF16)).astype(BF16)
    rows_out[...] = rows
    project_parts(rows, weights, (0, 1, 2), own_out, sends, nf * fr)


def cotangent_kernel(dims, *refs):
    nq, nf, fr, pq = dims
    rows = jnp.concatenate([ref[...] for ref in refs[:nq]], axis=0)
    project_parts(rows, refs[nq], (3,), refs[nq + 1], refs[nq + 2 :], nf * fr)


def temporal_kernel(dims, *refs):
    nq, nf, fr, pq = dims
    qkv_own, qkv_in = refs[0], refs[1:nq]
    grad_own, grad_in = refs[nq], refs[nq + 1 : 2 * nq]
    out = refs[2 * nq]
    width = HEADS * HEAD_DIM
    total = qkv_own[...]
    for part in qkv_in:
        total = total + part[...].astype(F32)
    grad = grad_own[...]
    for part in grad_in:
        grad = grad + part[...].astype(F32)
    query, keys, values = [total[:, k * width : (k + 1) * width].astype(BF16) for k in range(3)]
    grad = grad.astype(BF16)
    probs = probabilities(stack_heads(query), keys, None)
    motion_out = fold_heads(dot(probs.astype(BF16), values)).astype(BF16)
    grads = attend_back(query, keys, values, grad, None, probs)
    for k, piece in enumerate(grads + (motion_out,)):
        out[:, k * width : (k + 1) * width] = piece


def back_kernel(dims, quad_ref, *refs):
    nq, nf, fr, pq = dims
    terms, (weights, gn_out, delta_out) = refs[:nq], refs[nq:]
    width = HEADS * HEAD_DIM
    order = received_to_rows(quad_ref[0], nq, nf, fr, True)

    def part(k):
        return jnp.concatenate([t[:, k * width : (k + 1) * width] for t in terms], axis=0)

    grad = dot_t(part(0), weights[0]) + dot_t(part(1), weights[1]) + dot_t(part(2), weights[2])
    gn_out[...] = spread(dot(order, grad.astype(BF16)), gn_out)
    delta = dot_t(part(3), weights[3]).astype(BF16)
    delta_out[...] = spread(dot(order, delta), delta_out)


def weight_kernel(dims, cut, core_ref, rows, *refs):
    nq, nf, fr, pq = dims
    cots, refs = refs[:nq], refs[nq:]
    terms, outs = refs[:nq], refs[nq:]
    width = HEADS * HEAD_DIM
    split, cross, stage, block = cut
    core = core_ref[0]
    cot_rows = jnp.concatenate([ref[...] for ref in cots], axis=0)
    for k in (3, 2, 1, 0):
        right = jnp.concatenate([t[:, k * width : (k + 1) * width] for t in terms], axis=0)
        product = t_dot(rows[...] if k < 3 else cot_rows, right)
        keep_out, send_out = outs[0 if k >= 2 else 2], outs[1 if k >= 2 else 3]
        for x in range(cross):
            for z in range(stage):
                low, high = [
                    product[j * block : (j + 1) * block] for j in (split(x, 0, z), split(x, 1, z))
                ]
                keep_out[x, z, k % 2] = jnp.where(core == 0, low, high).astype(BF16)
                send_out[x, z, k % 2] = jnp.where(core == 0, high, low).astype(BF16)


def tail_kernel(dims, *refs):
    nq, nf, fr, pq = dims
    quad_ref, xs, cots, hid = refs[0], refs[1], refs[2 : 2 + nq], refs[2 + nq]
    refs = refs[3 + nq :]
    gns, refs = refs[:nq], refs[nq:]
    q_in, k_in, v_in, gain1, gain2, weights, in_grad, gain_out = refs
    quad = quad_ref[0]
    own = fr * pq
    order = rows_to_sent(quad, nq, fr, pq, True)
    parts = [dot(order, flat_wide(g).astype(BF16)) for g in gns]
    grad_normed = place_lanes(parts, quad, nq)
    unit_two, inv_two = normalize(hid[...].astype(F32))
    gain_out[...] = jnp.sum(grad_normed[:own] * unit_two[:own], axis=0, keepdims=True)
    cot = jnp.concatenate([flat_wide(c) for c in cots], axis=0)
    grad_hidden = (cot + normalize_back(grad_normed, unit_two, inv_two, gain2[...])).astype(BF16)
    grad_out = dot(grad_hidden, weights[3]).astype(BF16)
    query, keys, values = q_in[...], k_in[...], v_in[...]
    pieces = []
    for group in frame_groups(nq, fr, pq):
        same = same_frame(nq, group[1], pq)
        cut = [pick_group(part, group, nq, fr, pq) for part in (query, keys, values, grad_out)]
        pieces.append(attend_back(*cut, same))
    grads = [join_groups([p[i] for p in pieces], nq, fr, pq)[:own] for i in range(3)]
    grad_one = dot_t(grads[0], weights[0]) + dot_t(grads[1], weights[1]) + dot_t(grads[2], weights[2])
    unit_one, inv_one = normalize(flat_wide(xs))
    result = grad_hidden[:own].astype(F32) + normalize_back(grad_one, unit_one, inv_one, gain1[...])
    in_grad[...] = spread(result, in_grad)


def block_kernel(dims, *refs):
    nq, nf, fr, pq = dims
    quad_ref, hid, deltas, out = refs[0], refs[1], refs[2 : 2 + nq], refs[2 + nq]
    quad = quad_ref[0]
    own = fr * pq
    order = rows_to_sent(quad, nq, fr, pq, True)[:own]
    parts = [dot(order, flat_wide(d).astype(BF16)) for d in deltas]
    out[...] = spread(hid[...][:own].astype(F32) + place_lanes(parts, quad, nq), out)


def call(kernel, name, outs, args, vmem=16):
    in_specs = []
    for arg in args:
        space = pltpu.SMEM if arg.dtype == jnp.int32 else pltpu.VMEM
        in_specs.append(pl.BlockSpec(memory_space=space))
    return pl.pallas_call(
        kernel,
        out_shape=outs,
        in_specs=in_specs,
        out_specs=jax.tree.map(lambda _: pl.BlockSpec(memory_space=pltpu.VMEM), outs),
        compiler_params=pltpu.CompilerParams(vmem_limit_bytes=vmem * 1024 * 1024),
        name=name,
    )(*args)


def after(value, *others):
    return lax.optimization_barrier((value,) + others)[0]


def sds(*shape, dtype=BF16):
    return jax.ShapeDtypeStruct(shape, dtype)


def positional(first, frames, channels):
    frame_pos = (first + jnp.arange(frames)).astype(F32)[:, None]
    freq_index = jnp.arange(channels // 2).astype(F32)[None, :]
    phases = frame_pos * jnp.exp(freq_index * (-2.0 * math.log(10000.0) / channels))
    return jnp.stack([jnp.sin(phases), jnp.cos(phases)], axis=-1).reshape(frames, channels)


def local(nq, nf, activations, cotangent, spatial_weights, spatial_gain, motion_weights, motion_gain):
    fr, pq, channels = activations.shape
    dims = (nq, nf, fr, pq)
    width = spatial_weights.shape[-1]
    half = channels // nq
    rows = nq * fr * pq
    tokens = nf * fr
    small = 16 if rows <= 256 else 40
    big = 16 if rows <= 256 else 52
    quad = lax.axis_index("quad")
    frame = lax.axis_index("frame")
    quad_arr = quad.astype(jnp.int32).reshape(1)

    def from_quad(x, s):
        return lax.ppermute(x, "quad", [((d + s) % nq, d) for d in range(nq)])

    def to_quad(x, s):
        return lax.ppermute(x, "quad", [(d, (d + s) % nq) for d in range(nq)])

    def swap(x):
        return lax.all_to_all(x, "frame", split_axis=0, concat_axis=0, tiled=True)

    def run(kernel, name, outs, args, vmem=small):
        return call(functools.partial(kernel, dims), name, outs, args, vmem)

    gain1 = spatial_gain.reshape(1, channels)
    gain2 = motion_gain.reshape(1, channels)
    sent = sds(nf, nq * fr, half)
    acts = [activations] + [from_quad(activations, s) for s in range(1, nq)]
    cot_send = run(order_kernel, "order_cotangent", sent, [cotangent])
    cot_recv = swap(cot_send)
    cot_later = after(cotangent, acts[-1])
    cots = [cotangent] + [from_quad(cot_later, s) for s in range(1, nq)]
    pos = positional(frame * fr, fr, channels)

    query, keys, values, hidden, send = run(
        spatial_kernel,
        "spatial_forward",
        [sds(rows, width)] * 3 + [sds(rows, channels), sent],
        [quad_arr] + acts + [gain1, gain2, pos, spatial_weights],
        big,
    )
    received = swap(send)

    cot_parts = run(
        split_kernel, "split_cotangent", [sds(tokens, half)] * nq, [quad_arr, after(cot_recv, send)]
    )
    cot_parts = [cot_parts[0]] + [to_quad(cot_parts[nq - s], nq - s) for s in range(1, nq)]

    def partial_outs(n):
        return [sds(tokens, n * width, dtype=F32)] + [sds(tokens, n * width)] * (nq - 1)

    normed_rows, *qkv_parts = run(
        motion_kernel,
        "motion_projection",
        [sds(rows, half)] + partial_outs(3),
        [quad_arr, after(received, cot_parts[0]), motion_weights],
    )
    grad_parts = run(
        cotangent_kernel,
        "cotangent_projection",
        partial_outs(1),
        [after(cot_parts[0], normed_rows)] + cot_parts[1:] + [motion_weights],
    )
    qkv_parts[1:] = [to_quad(part, s + 1) for s, part in enumerate(qkv_parts[1:])]
    grad_parts = [grad_parts[0]] + [to_quad(p, s + 1) for s, p in enumerate(grad_parts[1:])]

    terms = run(
        temporal_kernel, "temporal_attention", sds(tokens, 4 * width), qkv_parts + grad_parts
    )
    all_terms = [terms] + [from_quad(terms, s) for s in range(1, nq)]

    cross, stage, block = 2, nf // 4, half // nf

    def split(x, c, z):
        return (((z % 2) * 2 + x) * 2 + c) * (stage // 2) + z // 2

    core, mid, turn = frame % 2, (frame // 2) % 2, frame // 4
    core_arr = core.astype(jnp.int32).reshape(1)
    halves = run(
        lambda d, *refs: weight_kernel(d, (split, cross, stage, block), *refs),
        "weight_terms",
        [sds(cross, stage, 2, block, width)] * 4,
        [core_arr, normed_rows] + cot_parts + all_terms,
    )
    late_terms = after(all_terms[0], halves[0])
    gn_send, delta_send = run(
        back_kernel,
        "temporal_back_projection",
        [sent, sent],
        [quad_arr, late_terms] + all_terms[1:] + [motion_weights],
    )
    flip_core = [(g, g ^ 1) for g in range(nf)]
    flip_mid = [(g, g ^ 2) for g in range(nf)]
    ring = [(g, (g + 4) % nf) for g in range(nf)]

    def move(x, pairs):
        return lax.ppermute(x, "frame", pairs)

    def pick(x, index, axis):
        return lax.dynamic_index_in_dim(x, index, axis, keepdims=False)

    def add(a, b):
        return (a.astype(F32) + b.astype(F32)).astype(BF16)

    keep_a, other_a, keep_b, other_b = halves
    got_a = move(other_a, flip_core)
    got_b = move(other_b, flip_core)
    theirs_a = add(pick(keep_a, 1 - mid, 0), pick(got_a, 1 - mid, 0))
    sum_b = add(keep_b, got_b)
    gn_recv = swap(after(gn_send, theirs_a, sum_b))
    mine_a = add(pick(keep_a, mid, 0), pick(got_a, mid, 0))
    pair_a = add(mine_a, move(theirs_a, flip_mid))

    def around(total, mine, axis, step):
        moved = move(total, ring)
        return add(moved, pick(mine, (turn - 1 - step) % stage, axis))

    total_b = around(pick(sum_b, (turn - 1) % stage, 1), sum_b, 1, 1)
    total_a = pick(pair_a, (turn - 1) % stage, 0)
    gns = [gn_recv] + [from_quad(gn_recv, s) for s in range(1, nq)]
    gns[0] = after(gns[0], total_b, total_a)
    for step in range(1, stage):
        total_a = around(total_a, pair_a, 0, step)
        if step > 1:
            total_b = around(total_b, sum_b, 1, step)
    total_b = add(pick(total_b, mid, 0), move(pick(total_b, 1 - mid, 0), flip_mid))
    total = jnp.concatenate([total_b, total_a], axis=0)
    final = []
    for g in range(nf):
        z, x, c = g // 4, (g // 2) % 2, g % 2
        for q in range(nq):
            final.append((g * nq + q, nf * q + split(x, c, z)))
    total = lax.ppermute(total, ("frame", "quad"), final)

    input_grad, gain_terms = run(
        tail_kernel,
        "spatial_backward",
        [sds(fr, pq, channels), sds(1, channels, dtype=F32)],
        [quad_arr, activations]
        + cots
        + [hidden]
        + gns
        + [query, keys, values, gain1, gain2, spatial_weights],
        big,
    )
    delta_recv = swap(after(delta_send, gain_terms))
    deltas = [delta_recv] + [from_quad(delta_recv, s) for s in range(1, nq)]
    block_output = run(
        block_kernel, "block_output", sds(fr, pq, channels), [quad_arr, hidden] + deltas
    )
    everyone = nf * nq
    gain_moved = lax.all_to_all(
        gain_terms.reshape(everyone, channels // everyone),
        ("frame", "quad"),
        split_axis=0,
        concat_axis=0,
        tiled=True,
    )
    factor = 1.0 / math.sqrt(everyone * fr * pq)
    weight_grad = total.astype(F32) * factor
    gain_grad = jnp.sum(gain_moved, axis=0) * factor
    return block_output, input_grad, weight_grad, gain_grad


def solution(mesh):
    in_specs = (
        P("frame", "quad", None),
        P("frame", "quad", None),
        P(),
        P(),
        P(None, "quad", None),
        P(),
    )
    out_specs = (
        P("frame", "quad", None),
        P("frame", "quad", None),
        P(None, ("frame", "quad"), None),
        P(("frame", "quad")),
    )
    body = functools.partial(local, mesh.shape["quad"], mesh.shape["frame"])
    return jax.shard_map(
        body, mesh=mesh, in_specs=in_specs, out_specs=out_specs, check_vma=False
    )
```

```python
import functools
import math

import jax
import jax.numpy as jnp
from jax import lax
from jax.experimental import pallas as pl
from jax.experimental.pallas import tpu as pltpu
from jax.sharding import PartitionSpec as P

HEADS = 4
HEAD_DIM = 160
EPSILON = 1e-05
SCALE = HEAD_DIM ** (-0.5)
F32 = jnp.float32
BF16 = jnp.bfloat16


def log2(n):
    return int(n).bit_length() - 1


def dot(a, b):
    return jnp.dot(a, b, preferred_element_type=F32)


def dot_t(a, b):
    return lax.dot_general(a, b, (((1,), (1,)), ((), ())), preferred_element_type=F32)


def t_dot(a, b):
    return lax.dot_general(a, b, (((0,), (0,)), ((), ())), preferred_element_type=F32)


def normalize(values):
    average = jnp.mean(values, axis=-1, keepdims=True)
    centred = values - average
    inv_scale = lax.rsqrt(jnp.mean(centred * centred, axis=-1, keepdims=True) + EPSILON)
    return centred * inv_scale, inv_scale


def normalize_back(grad_rows, unit_rows, inv_scale, gain):
    scaled = grad_rows * gain
    first_mean = jnp.mean(scaled, axis=-1, keepdims=True)
    second_mean = jnp.mean(scaled * unit_rows, axis=-1, keepdims=True)
    return inv_scale * (scaled - first_mean - unit_rows * second_mean)


def iota(shape, dim):
    return lax.broadcasted_iota(jnp.int32, shape, dim)


def head_mask(dtype):
    lane = iota((1, HEADS * HEAD_DIM), 1)
    return [
        jnp.where((lane >= h * HEAD_DIM) & (lane < (h + 1) * HEAD_DIM), 1.0, 0.0).astype(dtype)
        for h in range(HEADS)
    ]


def stack_heads(rows):
    return jnp.concatenate([rows * mask for mask in head_mask(rows.dtype)], axis=0)


def fold_heads(stacked):
    rows = stacked.shape[0] // HEADS
    total = None
    for h, mask in enumerate(head_mask(F32)):
        piece = stacked[h * rows : (h + 1) * rows] * mask
        total = piece if total is None else total + piece
    return total


def probabilities(query_stack, keys, same):
    scores = dot_t(query_stack, keys) * SCALE
    if same is not None:
        scores = jnp.where(same, scores, -1e30)
    highest = jnp.max(scores, axis=-1, keepdims=True)
    expo = jnp.exp(scores - highest)
    return expo / jnp.sum(expo, axis=-1, keepdims=True)


def attend(query, keys, values, same):
    probs = probabilities(stack_heads(query), keys, same)
    return fold_heads(dot(probs.astype(BF16), values)).astype(BF16)


def attend_back(query, keys, values, grad, same, probs=None):
    query_stack = stack_heads(query)
    grad_stack = stack_heads(grad)
    if probs is None:
        probs = probabilities(query_stack, keys, same)
    grad_probs = dot_t(grad_stack, values)
    inner = jnp.sum(probs * grad_probs, axis=-1, keepdims=True)
    grad_scores = (probs * (grad_probs - inner) * SCALE).astype(BF16)
    grad_query = fold_heads(dot(grad_scores, keys)).astype(BF16)
    grad_key = t_dot(grad_scores, query_stack).astype(BF16)
    grad_value = t_dot(probs.astype(BF16), grad_stack).astype(BF16)
    return grad_query, grad_key, grad_value


def rows_to_sent(quad, nq, fr, pq, transposed):
    rows = nq * fr * pq
    out_dim = 1 if transposed else 0
    out = iota((rows, rows), out_dim)
    src = iota((rows, rows), 1 - out_dim)
    cell = out >> log2(nq * fr)
    other = (out >> log2(fr)) & (nq - 1)
    frame = out & (fr - 1)
    want = (((other - quad) & (nq - 1)) << log2(fr * pq)) + (frame << log2(pq)) + cell
    return jnp.where(want == src, 1.0, 0.0).astype(BF16)


def received_to_rows(quad, nq, nf, fr, transposed):
    rows = nq * nf * fr
    out_dim = 1 if transposed else 0
    out = iota((rows, rows), out_dim)
    src = iota((rows, rows), 1 - out_dim)
    step = out >> log2(nf * fr)
    device = (out >> log2(fr)) & (nf - 1)
    frame = out & (fr - 1)
    want = (device << log2(nq * fr)) + (((step + quad) & (nq - 1)) << log2(fr)) + frame
    return jnp.where(want == src, 1.0, 0.0).astype(BF16)


def own_lanes(values, quad, nq):
    width = values.shape[1] // nq
    picked = values[:, :width]
    for t in range(1, nq):
        picked = jnp.where(quad == t, values[:, t * width : (t + 1) * width], picked)
    return picked


def place_lanes(parts, quad, nq):
    placed = []
    for t in range(nq):
        piece = parts[t]
        for q in range(1, nq):
            piece = jnp.where(quad == q, parts[(t - q) % nq], piece)
        placed.append(piece)
    return jnp.concatenate(placed, axis=1)


def frame_groups(nq, fr, pq):
    size = max(1, min(fr, 128 // (nq * pq)))
    return [(start, size) for start in range(0, fr, size)]


def pick_group(rows, group, nq, fr, pq):
    start, size = group
    if size == fr:
        return rows
    cut = rows.reshape(nq, fr, pq, rows.shape[-1])[:, start : start + size]
    return cut.reshape(nq * size * pq, rows.shape[-1])


def join_groups(pieces, nq, fr, pq):
    if len(pieces) == 1:
        return pieces[0]
    size = fr // len(pieces)
    width = pieces[0].shape[-1]
    joined = jnp.concatenate([p.reshape(nq, size, pq, width) for p in pieces], axis=1)
    return joined.reshape(nq * fr * pq, width)


def same_frame(nq, size, pq):
    if size == 1:
        return None
    rows = nq * size * pq
    shape = (HEADS * rows, rows)
    left = (iota(shape, 0) >> log2(pq)) & (size - 1)
    right = (iota(shape, 1) >> log2(pq)) & (size - 1)
    return left == right


def flat(ref):
    value = ref[...]
    return value.reshape(-1, value.shape[-1])


def flat_wide(ref):
    value = ref[...].astype(F32)
    return value.reshape(-1, value.shape[-1])


def spread(rows, like):
    return rows.reshape(like.shape).astype(like.dtype)


def spatial_kernel(dims, *refs):
    nq, nf, fr, pq = dims
    quad_ref, xs = refs[0], refs[1 : 1 + nq]
    gain1, gain2, pos, weights, q_out, k_out, v_out, hid_out, send_out = refs[1 + nq :]
    quad = quad_ref[0]
    wide = jnp.concatenate([flat_wide(x) for x in xs], axis=0)
    unit, _ = normalize(wide)
    normed = (unit * gain1[...]).astype(BF16)
    query = dot(normed, weights[0]).astype(BF16)
    keys = dot(normed, weights[1]).astype(BF16)
    values = dot(normed, weights[2]).astype(BF16)
    q_out[...], k_out[...], v_out[...] = query, keys, values
    pieces = []
    for group in frame_groups(nq, fr, pq):
        same = same_frame(nq, group[1], pq)
        cut = [pick_group(part, group, nq, fr, pq) for part in (query, keys, values)]
        pieces.append(attend(*cut, same))
    out = join_groups(pieces, nq, fr, pq)
    hidden = (wide + dot_t(out, weights[3])).astype(BF16)
    hid_out[...] = hidden
    unit_two, _ = normalize(hidden.astype(F32))
    table = jnp.broadcast_to(pos[...][:, None, :], (fr, pq, pos.shape[-1]))
    table = table.reshape(fr * pq, pos.shape[-1])
    table = jnp.concatenate([table] * nq, axis=0)
    normed_two = own_lanes(unit_two * gain2[...] + table, quad, nq).astype(BF16)
    send_out[...] = spread(dot(rows_to_sent(quad, nq, fr, pq, False), normed_two), send_out)


def cotangent_kernel(dims, *refs):
    nq, nf, fr, pq = dims
    quad_ref, cots, (weights, grad_out, cot_out) = refs[0], refs[1 : 1 + nq], refs[1 + nq :]
    quad = quad_ref[0]
    rows = own_lanes(jnp.concatenate([flat(c) for c in cots], axis=0), quad, nq)
    order = rows_to_sent(quad, nq, fr, pq, False)
    product = dot(rows, weights[3]).astype(BF16)
    grad_out[...] = spread(dot(order, product), grad_out)
    cot_out[...] = spread(dot(order, rows), cot_out)


def split_kernel(dims, quad_ref, received, *outs):
    nq, nf, fr, pq = dims
    order = received_to_rows(quad_ref[0], nq, nf, fr, False)
    rows = dot(order, flat_wide(received).astype(BF16)).astype(BF16)
    tokens = nf * fr
    for s in range(nq):
        outs[s][...] = rows[s * tokens : (s + 1) * tokens]


def cut_lanes(rows, core, keep, swap):
    half = rows.shape[1] // 2
    low, high = rows[:, :half].astype(F32), rows[:, half:].astype(F32)
    keep[...] = jnp.where(core == 0, low, high).astype(BF16)
    swap[...] = jnp.where(core == 0, high, low).astype(BF16)


def cut_kernel(dims, quad_ref, core_ref, received, keep, swap):
    nq, nf, fr, pq = dims
    order = received_to_rows(quad_ref[0], nq, nf, fr, False)
    rows = dot(order, flat_wide(received).astype(BF16)).astype(BF16)
    cut_lanes(rows, core_ref[0], keep, swap)


def motion_kernel(dims, quad_ref, core_ref, received, weights, keep, swap, own_out, *sends):
    nq, nf, fr, pq = dims
    order = received_to_rows(quad_ref[0], nq, nf, fr, False)
    rows = dot(order, flat_wide(received).astype(BF16)).astype(BF16)
    tokens = nf * fr
    for k in range(3):
        width = weights.shape[-1]
        lanes = slice(k * width, (k + 1) * width)
        product = dot(rows, weights[k])
        own_out[:, lanes] = product[:tokens]
        for s, send in enumerate(sends):
            send[:, lanes] = product[(s + 1) * tokens : (s + 2) * tokens].astype(BF16)
    cut_lanes(rows, core_ref[0], keep, swap)


def temporal_kernel(dims, *refs):
    nq, nf, fr, pq = dims
    qkv_own, qkv_in = refs[0], refs[1:nq]
    grad_own, grad_in = refs[nq], refs[nq + 1 : 2 * nq]
    out = refs[2 * nq]
    width = HEADS * HEAD_DIM
    total = qkv_own[...]
    for part in qkv_in:
        total = total + part[...].astype(F32)
    grad = grad_own[...].astype(F32)
    for part in grad_in:
        grad = grad + part[...].astype(F32)
    query, keys, values = [total[:, k * width : (k + 1) * width].astype(BF16) for k in range(3)]
    grad = grad.astype(BF16)
    probs = probabilities(stack_heads(query), keys, None)
    motion_out = fold_heads(dot(probs.astype(BF16), values)).astype(BF16)
    grads = attend_back(query, keys, values, grad, None, probs)
    for k, piece in enumerate(grads + (motion_out,)):
        out[:, k * width : (k + 1) * width] = piece


def back_kernel(dims, quad_ref, *refs):
    nq, nf, fr, pq = dims
    terms, (weights, gn_out, delta_out) = refs[:nq], refs[nq:]
    width = HEADS * HEAD_DIM
    order = received_to_rows(quad_ref[0], nq, nf, fr, True)

    def part(k):
        return jnp.concatenate([t[:, k * width : (k + 1) * width] for t in terms], axis=0)

    grad = dot_t(part(0), weights[0]) + dot_t(part(1), weights[1]) + dot_t(part(2), weights[2])
    gn_out[...] = spread(dot(order, grad.astype(BF16)), gn_out)
    delta = dot_t(part(3), weights[3]).astype(BF16)
    delta_out[...] = spread(dot(order, delta), delta_out)


def weight_kernel(dims, place, nt_keep, nt_in, cot_keep, cot_in, *refs):
    nq, nf, fr, pq = dims
    terms, refs = refs[: 2 * nq], refs[2 * nq :]
    keep_a, send_a, outs_b, blocks = refs[0], refs[1], refs[2:-1], refs[-1]
    width = HEADS * HEAD_DIM
    _, stage, block, _ = blocks.shape
    mid, turn = place[0], place[1]
    normed = jnp.concatenate([nt_keep[...], nt_in[...]], axis=0)
    cot = jnp.concatenate([cot_keep[...], cot_in[...]], axis=0)
    for k in (0, 1, 2, 3):
        right = jnp.concatenate([t[:, k * width : (k + 1) * width] for t in terms], axis=0)
        product = t_dot(normed if k < 3 else cot, right)
        for x in range(2):
            for z in range(stage):
                j = x * stage + z
                blocks[x, z] = product[j * block : (j + 1) * block]
        for r in range(stage):
            z = (turn + r) & (stage - 1)
            own, other = blocks[mid, z].astype(BF16), blocks[1 - mid, z].astype(BF16)
            if k < 2:
                keep_a[r, k], send_a[r, k] = own, other
            else:
                outs_b[r][0, k - 2], outs_b[r][1, k - 2] = own, other


def tail_kernel(dims, *refs):
    nq, nf, fr, pq = dims
    quad_ref, xs, cots, hid = refs[0], refs[1], refs[2 : 2 + nq], refs[2 + nq]
    refs = refs[3 + nq :]
    gns, refs = refs[:nq], refs[nq:]
    q_in, k_in, v_in, gain1, gain2, weights, in_grad, gain_out = refs
    quad = quad_ref[0]
    own = fr * pq
    order = rows_to_sent(quad, nq, fr, pq, True)
    parts = [dot(order, flat_wide(g).astype(BF16)) for g in gns]
    grad_normed = place_lanes(parts, quad, nq)
    unit_two, inv_two = normalize(hid[...].astype(F32))
    gain_out[...] = jnp.sum(grad_normed[:own] * unit_two[:own], axis=0, keepdims=True)
    cot = jnp.concatenate([flat_wide(c) for c in cots], axis=0)
    grad_hidden = (cot + normalize_back(grad_normed, unit_two, inv_two, gain2[...])).astype(BF16)
    grad_out = dot(grad_hidden, weights[3]).astype(BF16)
    query, keys, values = q_in[...], k_in[...], v_in[...]
    pieces = []
    for group in frame_groups(nq, fr, pq):
        same = same_frame(nq, group[1], pq)
        cut = [pick_group(part, group, nq, fr, pq) for part in (query, keys, values, grad_out)]
        pieces.append(attend_back(*cut, same))
    grads = [join_groups([p[i] for p in pieces], nq, fr, pq)[:own] for i in range(3)]
    grad_one = dot_t(grads[0], weights[0]) + dot_t(grads[1], weights[1]) + dot_t(grads[2], weights[2])
    unit_one, inv_one = normalize(flat_wide(xs))
    result = grad_hidden[:own].astype(F32) + normalize_back(grad_one, unit_one, inv_one, gain1[...])
    in_grad[...] = spread(result, in_grad)


def block_kernel(dims, *refs):
    nq, nf, fr, pq = dims
    quad_ref, hid, deltas, out = refs[0], refs[1], refs[2 : 2 + nq], refs[2 + nq]
    quad = quad_ref[0]
    own = fr * pq
    order = rows_to_sent(quad, nq, fr, pq, True)[:own]
    parts = [dot(order, flat_wide(d).astype(BF16)) for d in deltas]
    out[...] = spread(hid[...][:own].astype(F32) + place_lanes(parts, quad, nq), out)


class Far:
    def __init__(self, hbm, vmem, sem, parts):
        self.vmem, self.shape, self.dtype = vmem, vmem.shape, vmem.dtype
        if parts is None:
            self.copies = {None: pltpu.make_async_copy(hbm, vmem, sem.at[0])}
        else:
            self.copies = {
                k: pltpu.make_async_copy(hbm.at[k], vmem.at[k], sem.at[i])
                for i, k in enumerate(parts)
            }
        self.waiting = set(self.copies)

    def start(self, part):
        self.copies[part].start()

    def __getitem__(self, key):
        for part in [key] if isinstance(key, int) else list(self.copies):
            if part in self.waiting:
                self.copies[part].wait()
                self.waiting.remove(part)
        return self.vmem[key]


class FarOut:
    def __init__(self, hbm, vmem, sem):
        self.vmem, self.shape, self.dtype = vmem, vmem.shape, vmem.dtype
        self.copy = pltpu.make_async_copy(vmem, hbm, sem.at[0])

    def __setitem__(self, key, value):
        self.vmem[key] = value
        self.copy.start()


def call(kernel, name, outs, args, vmem, far=(), far_outs=(), scratch=()):
    outs = list(outs)
    far_at = dict(far)
    hbm, vm = pl.BlockSpec(memory_space=pltpu.HBM), pl.BlockSpec(memory_space=pltpu.VMEM)
    in_specs = []
    for i, arg in enumerate(args):
        if arg.dtype == jnp.int32:
            in_specs.append(pl.BlockSpec(memory_space=pltpu.SMEM))
        else:
            in_specs.append(hbm if i in far_at else vm)
    out_specs = [hbm if i in far_outs else vm for i in range(len(outs))]
    spaces = []
    for i, parts in far:
        count = 1 if parts is None else len(parts)
        spaces += [pltpu.VMEM(args[i].shape, args[i].dtype), pltpu.SemaphoreType.DMA((count,))]
    for i in far_outs:
        spaces += [pltpu.VMEM(outs[i].shape, outs[i].dtype), pltpu.SemaphoreType.DMA((1,))]

    def body(*refs):
        ins = list(refs[: len(args)])
        results = list(refs[len(args) : len(args) + len(outs)])
        extra = refs[len(args) + len(outs) :]
        own, extra = extra[: len(scratch)], extra[len(scratch) :]
        for n, (i, parts) in enumerate(far):
            ins[i] = Far(ins[i], extra[2 * n], extra[2 * n + 1], parts)
        for i, parts in far:
            for part in ins[i].copies:
                ins[i].start(part)
        extra = extra[2 * len(far) :]
        for n, i in enumerate(far_outs):
            results[i] = FarOut(results[i], extra[2 * n], extra[2 * n + 1])
        kernel(*ins, *results, *own)
        for i in far_outs:
            results[i].copy.wait()
        for i, _ in far:
            for part in sorted(ins[i].waiting, key=str):
                ins[i].copies[part].wait()

    return pl.pallas_call(
        body,
        out_shape=outs,
        in_specs=in_specs,
        out_specs=out_specs,
        scratch_shapes=list(scratch) + spaces,
        compiler_params=pltpu.CompilerParams(vmem_limit_bytes=vmem * 1024 * 1024),
        name=name,
    )(*args)


def after(value, *others):
    return lax.optimization_barrier((value,) + others)[0]


def sds(*shape, dtype=BF16):
    return jax.ShapeDtypeStruct(shape, dtype)


def positional(first, frames, channels):
    frame_pos = (first + jnp.arange(frames)).astype(F32)[:, None]
    freq_index = jnp.arange(channels // 2).astype(F32)[None, :]
    phases = frame_pos * jnp.exp(freq_index * (-2.0 * math.log(10000.0) / channels))
    return jnp.stack([jnp.sin(phases), jnp.cos(phases)], axis=-1).reshape(frames, channels)


def local(nq, nf, activations, cotangent, spatial_weights, spatial_gain, motion_weights, motion_gain):
    fr, pq, channels = activations.shape
    dims = (nq, nf, fr, pq)
    width = spatial_weights.shape[-1]
    half = channels // nq
    rows = nq * fr * pq
    tokens = nf * fr
    small = 16 if rows <= 256 else 40
    big = 28 if rows <= 256 else 60
    quad = lax.axis_index("quad")
    frame = lax.axis_index("frame")
    quad_arr = quad.astype(jnp.int32).reshape(1)

    def from_quad(x, s):
        return lax.ppermute(x, "quad", [((d + s) % nq, d) for d in range(nq)])

    def to_quad(x, s):
        return lax.ppermute(x, "quad", [(d, (d + s) % nq) for d in range(nq)])

    def swap(x):
        return lax.all_to_all(x, "frame", split_axis=0, concat_axis=0, tiled=True)

    def run(kernel, name, outs, args, vmem=small, **options):
        return call(functools.partial(kernel, dims), name, outs, args, vmem, **options)

    def move(x, pairs):
        return lax.ppermute(x, "frame", pairs)

    def add(a, b):
        return (a.astype(F32) + b.astype(F32)).astype(BF16)

    core, mid, turn = frame % 2, (frame // 2) % 2, frame // 4
    core_arr = core.astype(jnp.int32).reshape(1)
    place_arr = jnp.stack([mid, turn]).astype(jnp.int32)
    flip_core = [(g, g ^ 1) for g in range(nf)]
    flip_mid = [(g, g ^ 2) for g in range(nf)]
    ring = [(g, (g + 4) % nf) for g in range(nf)]

    gain1 = spatial_gain.reshape(1, channels)
    gain2 = motion_gain.reshape(1, channels)
    sent = sds(nf, nq * fr, half)
    acts = [activations] + [from_quad(activations, s) for s in range(1, nq)]
    cot_later = after(cotangent, acts[-1])
    cots = [cotangent] + [from_quad(cot_later, s) for s in range(1, nq)]
    pos = positional(frame * fr, fr, channels)

    query, keys, values, hidden, send = run(
        spatial_kernel,
        "spatial_forward",
        [sds(rows, width)] * 3 + [sds(rows, channels), sent],
        [quad_arr] + acts + [gain1, gain2, pos, spatial_weights],
        big,
        far=[(1 + s, None) for s in range(nq)] + [(4 + nq, (0, 1, 2, 3))],
        far_outs=(0, 1, 2, 3, 4),
    )
    received = swap(send)

    grad_send, cot_send = run(
        cotangent_kernel,
        "cotangent_projection",
        [sds(nf, nq * fr, width), sent],
        [quad_arr, after(cots[0], send)] + cots[1:] + [motion_weights],
        far=[(1 + s, None) for s in range(nq)] + [(1 + nq, (3,))],
        far_outs=(0, 1),
    )
    grad_recv = swap(grad_send)
    cot_recv = swap(cot_send)

    nt_keep, nt_swap, *qkv_parts = run(
        motion_kernel,
        "motion_projection",
        [sds(rows, half // 2)] * 2
        + [sds(tokens, 3 * width, dtype=F32)]
        + [sds(tokens, 3 * width)] * (nq - 1),
        [quad_arr, core_arr, after(received, grad_send), motion_weights],
        far_outs=(0, 1),
    )
    qkv_parts = [qkv_parts[0]] + [to_quad(part, s + 1) for s, part in enumerate(qkv_parts[1:])]
    grad_parts = run(
        split_kernel,
        "split_projected_cotangent",
        [sds(tokens, width)] * nq,
        [quad_arr, after(grad_recv, qkv_parts[0])],
    )
    grad_parts = [grad_parts[0]] + [to_quad(p, s + 1) for s, p in enumerate(grad_parts[1:])]
    nt_in = move(nt_swap, flip_core)

    (terms,) = run(
        temporal_kernel, "temporal_attention", [sds(tokens, 4 * width)], qkv_parts + grad_parts
    )
    all_terms = [terms] + [from_quad(terms, s) for s in range(1, nq)]
    swapped = [move(t, flip_core) for t in all_terms]
    cot_keep, cot_swap = run(
        cut_kernel,
        "cut_cotangent",
        [sds(rows, half // 2)] * 2,
        [quad_arr, core_arr, after(cot_recv, terms)],
        far_outs=(0, 1),
    )
    cot_in = move(cot_swap, flip_core)

    gn_send, delta_send = run(
        back_kernel,
        "temporal_back_projection",
        [sent, sent],
        [quad_arr] + all_terms + [motion_weights],
        far_outs=(0, 1),
    )

    stage, block = nf // 4, half // nf
    keep_a, send_a, *parts_b = run(
        weight_kernel,
        "weight_terms",
        [sds(stage, 2, block, width)] * 2 + [sds(2, 2, block, width)] * stage,
        [place_arr, nt_keep, nt_in, cot_keep, cot_in] + all_terms + swapped,
        far=[(i, None) for i in (1, 2, 3, 4)],
        scratch=[pltpu.VMEM((2, stage, block, width), F32)],
    )
    gn_recv = swap(after(gn_send, send_a))
    pair_a = add(keep_a, move(send_a, flip_mid))
    total_a, total_b = pair_a[stage - 1], parts_b[stage - 1]
    gns = [gn_recv] + [from_quad(gn_recv, s) for s in range(1, nq)]
    for step in range(1, stage):
        total_b = add(move(total_b, ring), parts_b[stage - 1 - step])
        total_a = add(move(total_a, ring), pair_a[stage - 1 - step])
        if step == 1:
            gns[0] = after(gns[0], total_b)
    total_b = add(total_b[0], move(total_b[1], flip_mid))
    final = []
    for g in range(nf):
        z, x, c = g // 4, (g // 2) % 2, g % 2
        for q in range(nq):
            final.append((g * nq + q, nf * q + c * (nf // 2) + x * stage + z))
    totals = [lax.ppermute(t, ("frame", "quad"), final) for t in (total_a, total_b)]

    input_grad, gain_terms = run(
        tail_kernel,
        "spatial_backward",
        [sds(fr, pq, channels), sds(1, channels, dtype=F32)],
        [quad_arr, activations]
        + cots
        + [hidden]
        + gns
        + [query, keys, values, gain1, gain2, spatial_weights],
        big,
        far=[(2 + nq, None)]
        + [(2 + s, None) for s in range(nq)]
        + [(8 + 2 * nq, (3, 0, 1, 2))]
        + [(3 + 2 * nq + i, None) for i in range(3)]
        + [(1, None)],
        far_outs=(0,),
    )
    delta_recv = swap(after(delta_send, gn_recv))
    deltas = [delta_recv] + [from_quad(delta_recv, s) for s in range(1, nq)]
    (block_output,) = run(
        block_kernel, "block_output", [sds(fr, pq, channels)], [quad_arr, hidden] + deltas, far=[(1, None)]
    )
    everyone = nf * nq
    gain_moved = lax.all_to_all(
        gain_terms.reshape(everyone, channels // everyone),
        ("frame", "quad"),
        split_axis=0,
        concat_axis=0,
        tiled=True,
    )
    factor = 1.0 / math.sqrt(everyone * fr * pq)
    weight_grad = jnp.concatenate(totals, axis=0).astype(F32) * factor
    gain_grad = jnp.sum(gain_moved, axis=0) * factor
    return block_output, input_grad, weight_grad, gain_grad


def solution(mesh):
    in_specs = (
        P("frame", "quad", None),
        P("frame", "quad", None),
        P(),
        P(),
        P(None, "quad", None),
        P(),
    )
    out_specs = (
        P("frame", "quad", None),
        P("frame", "quad", None),
        P(None, ("frame", "quad"), None),
        P(("frame", "quad")),
    )
    body = functools.partial(local, mesh.shape["quad"], mesh.shape["frame"])
    return jax.shard_map(
        body, mesh=mesh, in_specs=in_specs, out_specs=out_specs, check_vma=False
    )
```

```python
import functools
import math

import jax
import jax.numpy as jnp
from jax import lax
from jax.experimental import pallas as pl
from jax.experimental.pallas import tpu as pltpu
from jax.sharding import PartitionSpec as P

HEADS = 4
HEAD_DIM = 160
EPSILON = 1e-05
SCALE = HEAD_DIM ** (-0.5)
F32 = jnp.float32
BF16 = jnp.bfloat16


def log2(n):
    return int(n).bit_length() - 1


def dot(a, b):
    return jnp.dot(a, b, preferred_element_type=F32)


def dot_t(a, b):
    return lax.dot_general(a, b, (((1,), (1,)), ((), ())), preferred_element_type=F32)


def t_dot(a, b):
    return lax.dot_general(a, b, (((0,), (0,)), ((), ())), preferred_element_type=F32)


def normalize(values):
    average = jnp.mean(values, axis=-1, keepdims=True)
    centred = values - average
    inv_scale = lax.rsqrt(jnp.mean(centred * centred, axis=-1, keepdims=True) + EPSILON)
    return centred * inv_scale, inv_scale


def normalize_back(grad_rows, unit_rows, inv_scale, gain):
    scaled = grad_rows * gain
    first_mean = jnp.mean(scaled, axis=-1, keepdims=True)
    second_mean = jnp.mean(scaled * unit_rows, axis=-1, keepdims=True)
    return inv_scale * (scaled - first_mean - unit_rows * second_mean)


def iota(shape, dim):
    return lax.broadcasted_iota(jnp.int32, shape, dim)


def head_mask(dtype):
    lane = iota((1, HEADS * HEAD_DIM), 1)
    return [
        jnp.where((lane >= h * HEAD_DIM) & (lane < (h + 1) * HEAD_DIM), 1.0, 0.0).astype(dtype)
        for h in range(HEADS)
    ]


def stack_heads(rows):
    return jnp.concatenate([rows * mask for mask in head_mask(rows.dtype)], axis=0)


def fold_heads(stacked):
    rows = stacked.shape[0] // HEADS
    total = None
    for h, mask in enumerate(head_mask(F32)):
        piece = stacked[h * rows : (h + 1) * rows] * mask
        total = piece if total is None else total + piece
    return total


def probabilities(query_stack, keys, same):
    scores = dot_t(query_stack, keys) * SCALE
    if same is not None:
        scores = jnp.where(same, scores, -1e30)
    highest = jnp.max(scores, axis=-1, keepdims=True)
    expo = jnp.exp(scores - highest)
    return expo / jnp.sum(expo, axis=-1, keepdims=True)


def attend(query, keys, values, same):
    probs = probabilities(stack_heads(query), keys, same)
    return fold_heads(dot(probs.astype(BF16), values)).astype(BF16)


def attend_back(query, keys, values, grad, same, probs=None):
    query_stack = stack_heads(query)
    grad_stack = stack_heads(grad)
    if probs is None:
        probs = probabilities(query_stack, keys, same)
    grad_probs = dot_t(grad_stack, values)
    inner = jnp.sum(probs * grad_probs, axis=-1, keepdims=True)
    grad_scores = (probs * (grad_probs - inner) * SCALE).astype(BF16)
    grad_query = fold_heads(dot(grad_scores, keys)).astype(BF16)
    grad_key = t_dot(grad_scores, query_stack).astype(BF16)
    grad_value = t_dot(probs.astype(BF16), grad_stack).astype(BF16)
    return grad_query, grad_key, grad_value


def at_frames(fr, pq):
    return lambda s, other, frame: (s << log2(fr * pq)) + (frame << log2(pq)) + other


def at_positions(nf, fr):
    return lambda s, other, frame: (s << log2(nf * fr)) + (other << log2(fr)) + frame


def one_hot(rows, want):
    shape = (rows, rows)
    return jnp.where(want(iota(shape, 0)) == iota(shape, 1), 1.0, 0.0).astype(BF16)


def to_send(geo, n, nf, fr, row):
    quad, four, turn = geo

    def want(out):
        frame = out & (fr - 1)
        other = (out >> log2(fr)) & (n - 1)
        flip = (out >> log2(n * fr)) & 3
        shift = out >> log2(4 * n * fr)
        device = (((turn + shift) & (nf // 4 - 1)) << 2) + (four ^ flip)
        return row((other - quad) & (n - 1), device, frame)

    return one_hot(n * nf * fr, want)


def regroup(n, nf, fr):
    def want(out):
        rest = out & (n * fr - 1)
        shift = (out >> log2(n * fr)) & (nf // 4 - 1)
        flip = out >> log2(nf // 4 * n * fr)
        return (((shift << 2) + flip) << log2(n * fr)) + rest

    return one_hot(n * nf * fr, want)


def from_received(geo, n, nf, fr, pq=None):
    quad, four, turn = geo

    def want(out):
        if pq is None:
            frame, device = out & (fr - 1), (out >> log2(fr)) & (nf - 1)
        else:
            device, frame = out & (pq - 1), (out >> log2(pq)) & (fr - 1)
        other = ((out >> log2(nf * fr)) + quad) & (n - 1)
        shift = (turn - (device >> 2)) & (nf // 4 - 1)
        flip = (device & 3) ^ four
        return (((((flip << log2(nf // 4)) + shift) << log2(n)) + other) << log2(fr)) + frame

    return one_hot(n * nf * fr, want)


def read_geo(ref):
    return ref[0], ref[1], ref[2]


def join(refs):
    return jnp.concatenate([ref[...] for ref in refs], axis=0)


def share(rows, outs):
    step = rows.shape[0] // len(outs)
    for i, out in enumerate(outs):
        out[...] = rows[i * step : (i + 1) * step].astype(out.dtype)


def own_lanes(values, quad, nq):
    width = values.shape[1] // nq
    picked = values[:, :width]
    for t in range(1, nq):
        picked = jnp.where(quad == t, values[:, t * width : (t + 1) * width], picked)
    return picked


def place_lanes(parts, quad, nq):
    placed = []
    for t in range(nq):
        piece = parts[t]
        for q in range(1, nq):
            piece = jnp.where(quad == q, parts[(t - q) % nq], piece)
        placed.append(piece)
    return jnp.concatenate(placed, axis=1)


def frame_groups(nq, fr, pq):
    size = max(1, min(fr, 128 // (nq * pq)))
    return [(start, size) for start in range(0, fr, size)]


def pick_group(rows, group, nq, fr, pq):
    start, size = group
    if size == fr:
        return rows
    cut = rows.reshape(nq, fr, pq, rows.shape[-1])[:, start : start + size]
    return cut.reshape(nq * size * pq, rows.shape[-1])


def join_groups(pieces, nq, fr, pq):
    if len(pieces) == 1:
        return pieces[0]
    size = fr // len(pieces)
    width = pieces[0].shape[-1]
    joined = jnp.concatenate([p.reshape(nq, size, pq, width) for p in pieces], axis=1)
    return joined.reshape(nq * fr * pq, width)


def same_frame(nq, size, pq):
    if size == 1:
        return None
    rows = nq * size * pq
    shape = (HEADS * rows, rows)
    left = (iota(shape, 0) >> log2(pq)) & (size - 1)
    right = (iota(shape, 1) >> log2(pq)) & (size - 1)
    return left == right


def flat(ref):
    value = ref[...]
    return value.reshape(-1, value.shape[-1])


def flat_wide(ref):
    value = ref[...].astype(F32)
    return value.reshape(-1, value.shape[-1])


def spread(rows, like):
    return rows.reshape(like.shape).astype(like.dtype)


def spatial_kernel(dims, *refs):
    nq, nf, fr, pq = dims
    geo, xs, refs = read_geo(refs[0]), refs[1 : 1 + nq], refs[1 + nq :]
    gain1, gain2, pos, weights, q_out, k_out, v_out, hid_out, *sends = refs
    wide = jnp.concatenate([flat_wide(x) for x in xs], axis=0)
    unit, _ = normalize(wide)
    normed = (unit * gain1[...]).astype(BF16)
    query = dot(normed, weights[0]).astype(BF16)
    q_out[...] = query
    keys = dot(normed, weights[1]).astype(BF16)
    k_out[...] = keys
    values = dot(normed, weights[2]).astype(BF16)
    v_out[...] = values
    pieces = []
    for group in frame_groups(nq, fr, pq):
        same = same_frame(nq, group[1], pq)
        cut = [pick_group(part, group, nq, fr, pq) for part in (query, keys, values)]
        pieces.append(attend(*cut, same))
    out = join_groups(pieces, nq, fr, pq)
    hidden = (wide + dot_t(out, weights[3])).astype(BF16)
    hid_out[...] = hidden
    unit_two, _ = normalize(hidden.astype(F32))
    table = jnp.broadcast_to(pos[...][:, None, :], (fr, pq, pos.shape[-1]))
    table = table.reshape(fr * pq, pos.shape[-1])
    table = jnp.concatenate([table] * nq, axis=0)
    normed_two = own_lanes(unit_two * gain2[...] + table, geo[0], nq).astype(BF16)
    share(dot(to_send(geo, nq, nf, fr, at_frames(fr, pq)), normed_two), sends)


def cut_lanes(rows, four, keep, swap):
    half = rows.shape[1] // 2
    low, high = rows[:, :half].astype(F32), rows[:, half:].astype(F32)
    keep[...] = jnp.where(four & 1 == 0, low, high).astype(BF16)
    swap[...] = jnp.where(four & 1 == 0, high, low).astype(BF16)


def cotangent_kernel(dims, *refs):
    nq, nf, fr, pq = dims
    geo, cots, refs = read_geo(refs[0]), refs[1 : 1 + nq], refs[1 + nq :]
    weights, keep, swap, own_out, *sends = refs
    rows = own_lanes(jnp.concatenate([flat(c) for c in cots], axis=0), geo[0], nq)
    share(dot(rows, weights[3]), [own_out] + sends)
    cut_lanes(rows, geo[1], keep, swap)


def total_of(parts):
    total = parts[0][...].astype(F32)
    for part in parts[1:]:
        total = total + part[...].astype(F32)
    return total


def sum_kernel(dims, geo_ref, *refs):
    nq, nf, fr, pq = dims
    parts, sends = refs[:nq], refs[nq:]
    order = to_send(read_geo(geo_ref), 1, nf, fr, at_frames(fr, pq))
    share(dot(order, total_of(parts).astype(BF16)), sends)


def regroup_kernel(dims, n, *refs):
    nq, nf, fr, pq = dims
    ins, outs = refs[: nf // 4], refs[nf // 4 :]
    share(dot(regroup(n, nf, fr), join(ins)), outs)


def motion_kernel(dims, geo_ref, *refs):
    nq, nf, fr, pq = dims
    received, weights, own_out, sends = refs[:4], refs[4], refs[5], refs[6:]
    order = from_received(read_geo(geo_ref), nq, nf, fr)
    rows = dot(order, join(received)).astype(BF16)
    tokens = nf * fr
    for k in range(3):
        width = weights.shape[-1]
        lanes = slice(k * width, (k + 1) * width)
        product = dot(rows, weights[k])
        own_out[:, lanes] = product[:tokens]
        for s, send in enumerate(sends):
            send[:, lanes] = product[(s + 1) * tokens : (s + 2) * tokens].astype(BF16)


def cut_kernel(dims, geo_ref, *refs):
    nq, nf, fr, pq = dims
    geo = read_geo(geo_ref)
    rows = dot(from_received(geo, nq, nf, fr), join(refs[:4])).astype(BF16)
    cut_lanes(rows, geo[1], refs[4], refs[5])


def temporal_kernel(dims, geo_ref, *refs):
    nq, nf, fr, pq = dims
    geo = read_geo(geo_ref)
    qkv, received, refs = refs[:nq], refs[nq : nq + 4], refs[nq + 4 :]
    grads_out, sends = refs[0], refs[1:]
    width = HEADS * HEAD_DIM
    total = total_of(qkv)
    grad = dot(from_received(geo, 1, nf, fr), join(received)).astype(BF16)
    query, keys, values = [total[:, k * width : (k + 1) * width].astype(BF16) for k in range(3)]
    probs = probabilities(stack_heads(query), keys, None)
    motion = fold_heads(dot(probs.astype(BF16), values)).astype(BF16)
    grads = attend_back(query, keys, values, grad, None, probs)
    for k, piece in enumerate(grads):
        grads_out[:, k * width : (k + 1) * width] = piece
    share(dot(to_send(geo, 1, nf, fr, at_positions(nf, fr)), motion), sends)


def back_kernel(dims, geo_ref, *refs):
    nq, nf, fr, pq = dims
    terms, weights, sends = refs[:nq], refs[nq], refs[nq + 1 :]
    width = HEADS * HEAD_DIM
    order = to_send(read_geo(geo_ref), nq, nf, fr, at_positions(nf, fr))

    def part(k):
        return jnp.concatenate([t[:, k * width : (k + 1) * width] for t in terms], axis=0)

    grad = dot_t(part(0), weights[0]) + dot_t(part(1), weights[1]) + dot_t(part(2), weights[2])
    share(dot(order, grad.astype(BF16)), sends)


def result_kernel(dims, geo_ref, *refs):
    nq, nf, fr, pq = dims
    order = from_received(read_geo(geo_ref), 1, nf, fr, pq)
    refs[4][...] = dot(order, join(refs[:4])).astype(BF16)


def delta_kernel(dims, *refs):
    nq, nf, fr, pq = dims
    share(dot_t(join(refs[:nq]), refs[nq][3]), refs[nq + 1 :])


def relative_blocks(product, blocks, place):
    _, stage, block, _ = blocks.shape
    for x in range(2):
        for z in range(stage):
            j = x * stage + z
            blocks[x, z] = product[j * block : (j + 1) * block]
    mid, turn = place[1] >> 1, place[2]

    def get(x, r):
        return blocks[mid ^ x, (turn + r) & (stage - 1)].astype(BF16)

    return get


def first_weight_kernel(dims, place, nt_keep, nt_in, *refs):
    nq, nf, fr, pq = dims
    terms, (keep, send, blocks) = refs[: 2 * nq], refs[2 * nq :]
    width = HEADS * HEAD_DIM
    normed = join((nt_keep, nt_in))
    for k in range(2):
        right = jnp.concatenate([t[:, k * width : (k + 1) * width] for t in terms], axis=0)
        get = relative_blocks(t_dot(normed, right), blocks, place)
        for r in range(nf // 4):
            keep[r, k], send[r, k] = get(0, r), get(1, r)


def second_weight_kernel(dims, place, nt_keep, nt_in, cot_keep, cot_in, *refs):
    nq, nf, fr, pq = dims
    terms, motion, refs = refs[: 2 * nq], refs[2 * nq : 4 * nq], refs[4 * nq :]
    outs, blocks = refs[:-1], refs[-1]
    width = HEADS * HEAD_DIM
    values = jnp.concatenate([t[:, 2 * width : 3 * width] for t in terms], axis=0)
    pairs = ((join((nt_keep, nt_in)), values), (join((cot_keep, cot_in)), join(motion)))
    for k, (left, right) in enumerate(pairs):
        get = relative_blocks(t_dot(left, right), blocks, place)
        for r in range(nf // 4):
            outs[r][0, k], outs[r][1, k] = get(0, r), get(1, r)


def tail_kernel(dims, *refs):
    nq, nf, fr, pq = dims
    geo, xs, cots, hid = read_geo(refs[0]), refs[1], refs[2 : 2 + nq], refs[2 + nq]
    refs = refs[3 + nq :]
    gns, refs = refs[: 4 * nq], refs[4 * nq :]
    q_in, k_in, v_in, gain1, gain2, weights, in_grad, gain_out = refs
    own = fr * pq
    order = from_received(geo, nq, nf, fr, pq)
    parts = [dot(order, join(gns[4 * s : 4 * s + 4])) for s in range(nq)]
    grad_normed = place_lanes(parts, geo[0], nq)
    unit_two, inv_two = normalize(hid[...].astype(F32))
    gain_out[...] = jnp.sum(grad_normed[:own] * unit_two[:own], axis=0, keepdims=True)
    cot = jnp.concatenate([flat_wide(c) for c in cots], axis=0)
    grad_hidden = (cot + normalize_back(grad_normed, unit_two, inv_two, gain2[...])).astype(BF16)
    grad_out = dot(grad_hidden, weights[3]).astype(BF16)
    query, keys, values = q_in[...], k_in[...], v_in[...]
    pieces = []
    for group in frame_groups(nq, fr, pq):
        same = same_frame(nq, group[1], pq)
        cut = [pick_group(part, group, nq, fr, pq) for part in (query, keys, values, grad_out)]
        pieces.append(attend_back(*cut, same))
    grads = [join_groups([p[i] for p in pieces], nq, fr, pq)[:own] for i in range(3)]
    grad_one = dot_t(grads[0], weights[0]) + dot_t(grads[1], weights[1]) + dot_t(grads[2], weights[2])
    unit_one, inv_one = normalize(flat_wide(xs))
    result = grad_hidden[:own].astype(F32) + normalize_back(grad_one, unit_one, inv_one, gain1[...])
    in_grad[...] = spread(result, in_grad)


def block_kernel(dims, *refs):
    nq, nf, fr, pq = dims
    geo, hid, deltas, out = read_geo(refs[0]), refs[1], refs[2 : 2 + nq], refs[2 + nq]
    parts = [d[...].astype(F32) for d in deltas]
    rows = hid[...][: fr * pq].astype(F32) + place_lanes(parts, geo[0], nq)
    out[...] = spread(rows, out)


class Far:
    def __init__(self, hbm, vmem, sem, parts):
        self.vmem, self.shape, self.dtype = vmem, vmem.shape, vmem.dtype
        if parts is None:
            self.copies = {None: pltpu.make_async_copy(hbm, vmem, sem.at[0])}
        else:
            self.copies = {
                k: pltpu.make_async_copy(hbm.at[k], vmem.at[k], sem.at[i])
                for i, k in enumerate(parts)
            }
        self.waiting = set(self.copies)

    def start(self, part):
        self.copies[part].start()

    def __getitem__(self, key):
        for part in [key] if isinstance(key, int) else list(self.copies):
            if part in self.waiting:
                self.copies[part].wait()
                self.waiting.remove(part)
        return self.vmem[key]


class FarOut:
    def __init__(self, hbm, vmem, sem):
        self.vmem, self.shape, self.dtype = vmem, vmem.shape, vmem.dtype
        self.copy = pltpu.make_async_copy(vmem, hbm, sem.at[0])

    def __setitem__(self, key, value):
        self.vmem[key] = value
        self.copy.start()


def call(kernel, name, outs, args, vmem, far=(), far_outs=(), scratch=()):
    outs = list(outs)
    far_at = dict(far)
    hbm, vm = pl.BlockSpec(memory_space=pltpu.HBM), pl.BlockSpec(memory_space=pltpu.VMEM)
    in_specs = []
    for i, arg in enumerate(args):
        if arg.dtype == jnp.int32:
            in_specs.append(pl.BlockSpec(memory_space=pltpu.SMEM))
        else:
            in_specs.append(hbm if i in far_at else vm)
    out_specs = [hbm if i in far_outs else vm for i in range(len(outs))]
    spaces = []
    for i, parts in far:
        count = 1 if parts is None else len(parts)
        spaces += [pltpu.VMEM(args[i].shape, args[i].dtype), pltpu.SemaphoreType.DMA((count,))]
    for i in far_outs:
        spaces += [pltpu.VMEM(outs[i].shape, outs[i].dtype), pltpu.SemaphoreType.DMA((1,))]

    def body(*refs):
        ins = list(refs[: len(args)])
        results = list(refs[len(args) : len(args) + len(outs)])
        extra = refs[len(args) + len(outs) :]
        own, extra = extra[: len(scratch)], extra[len(scratch) :]
        for n, (i, parts) in enumerate(far):
            ins[i] = Far(ins[i], extra[2 * n], extra[2 * n + 1], parts)
        for i, parts in far:
            for part in ins[i].copies:
                ins[i].start(part)
        extra = extra[2 * len(far) :]
        for n, i in enumerate(far_outs):
            results[i] = FarOut(results[i], extra[2 * n], extra[2 * n + 1])
        kernel(*ins, *results, *own)
        for i in far_outs:
            results[i].copy.wait()
        for i, _ in far:
            for part in sorted(ins[i].waiting, key=str):
                ins[i].copies[part].wait()

    return pl.pallas_call(
        body,
        out_shape=outs,
        in_specs=in_specs,
        out_specs=out_specs,
        scratch_shapes=list(scratch) + spaces,
        compiler_params=pltpu.CompilerParams(vmem_limit_bytes=vmem * 1024 * 1024),
        name=name,
    )(*args)


def after(value, *others):
    return lax.optimization_barrier((value,) + others)[0]


def sds(*shape, dtype=BF16):
    return jax.ShapeDtypeStruct(shape, dtype)


def positional(first, frames, channels):
    frame_pos = (first + jnp.arange(frames)).astype(F32)[:, None]
    freq_index = jnp.arange(channels // 2).astype(F32)[None, :]
    phases = frame_pos * jnp.exp(freq_index * (-2.0 * math.log(10000.0) / channels))
    return jnp.stack([jnp.sin(phases), jnp.cos(phases)], axis=-1).reshape(frames, channels)


def local(nq, nf, activations, cotangent, spatial_weights, spatial_gain, motion_weights, motion_gain):
    fr, pq, channels = activations.shape
    dims = (nq, nf, fr, pq)
    width = spatial_weights.shape[-1]
    half = channels // nq
    rows = nq * fr * pq
    tokens = nf * fr
    small = 16 if rows <= 256 else 40
    big = 62
    quad = lax.axis_index("quad")
    frame = lax.axis_index("frame")

    def from_quad(x, s):
        return lax.ppermute(x, "quad", [((d + s) % nq, d) for d in range(nq)])

    def to_quad(x, s):
        return lax.ppermute(x, "quad", [(d, (d + s) % nq) for d in range(nq)])

    def run(kernel, name, outs, args, vmem=small, **options):
        return call(functools.partial(kernel, dims), name, outs, args, vmem, **options)

    def move(x, pairs):
        return lax.ppermute(x, "frame", pairs)

    def add(a, b):
        return (a.astype(F32) + b.astype(F32)).astype(BF16)

    stage, block = nf // 4, half // nf
    geo = jnp.stack([quad, frame % 4, frame // 4]).astype(jnp.int32)

    def shifted(by):
        return [(g, (g + 4 * by) % nf) for g in range(nf)]

    def flipped(bits):
        return [(g, g ^ bits) for g in range(nf)]

    def over_ring(sends, n, name, *first):
        got = [sends[0]] + [move(sends[s], shifted(s)) for s in range(1, stage)]
        got[0] = after(got[0], *first) if first else got[0]
        shape = sds(stage * n * fr, sends[0].shape[-1])
        return list(run(lambda d, *refs: regroup_kernel(d, n, *refs), name, [shape] * 4, got))

    def over_four(ready):
        return [ready[0]] + [move(ready[d], flipped(d)) for d in range(1, 4)]

    def over_four_quads(ready):
        got = [over_four(ready)]
        for s in range(1, nq):
            lists = []
            for d in range(4):
                pairs = [
                    (g * nq + (q + s) % nq, (g ^ d) * nq + q) for g in range(nf) for q in range(nq)
                ]
                lists.append(lax.ppermute(ready[d], ("frame", "quad"), pairs))
            got.append(lists)
        return got

    gain1 = spatial_gain.reshape(1, channels)
    gain2 = motion_gain.reshape(1, channels)
    acts = [activations] + [from_quad(activations, s) for s in range(1, nq)]
    cot_later = after(cotangent, acts[-1])
    cots = [cotangent] + [from_quad(cot_later, s) for s in range(1, nq)]
    pos = positional(frame * fr, fr, channels)
    own = fr * pq

    query, keys, values, hidden, *sends = run(
        spatial_kernel,
        "spatial_forward",
        [sds(rows, width)] * 3 + [sds(rows, channels)] + [sds(4 * nq * fr, half)] * stage,
        [geo] + acts + [gain1, gain2, pos, spatial_weights],
        big,
        far=[(1 + s, None) for s in range(nq)] + [(4 + nq, (0, 1, 2, 3))],
        far_outs=(0, 1, 2, 3),
    )

    cot_keep, cot_swap, *grad_parts = run(
        cotangent_kernel,
        "cotangent_projection",
        [sds(rows, half // 2)] * 2 + [sds(own, width, dtype=F32)] + [sds(own, width)] * (nq - 1),
        [geo, after(cots[0], hidden)] + cots[1:] + [motion_weights],
    )
    received = over_four(over_ring(sends, nq, "regroup_normed", grad_parts[0]))
    grad_parts = [grad_parts[0]] + [to_quad(p, s + 1) for s, p in enumerate(grad_parts[1:])]
    grad_sends = run(
        sum_kernel, "sum_projected_cotangent", [sds(4 * fr, width)] * stage, [geo] + grad_parts
    )
    grad_recv = over_four(over_ring(grad_sends, 1, "regroup_projected_cotangent"))
    cot_in = move(cot_swap, flipped(1))

    qkv_parts = run(
        motion_kernel,
        "motion_projection",
        [sds(tokens, 3 * width, dtype=F32)] + [sds(tokens, 3 * width)] * (nq - 1),
        [geo, after(received[0], grad_sends[0])] + received[1:] + [motion_weights],
    )
    nt_keep, nt_swap = run(
        cut_kernel,
        "cut_normed",
        [sds(rows, half // 2)] * 2,
        [geo, after(received[0], qkv_parts[0])] + received[1:],
    )
    qkv_parts = [qkv_parts[0]] + [to_quad(part, s + 1) for s, part in enumerate(qkv_parts[1:])]
    nt_in = move(nt_swap, flipped(1))

    terms, *motion_sends = run(
        temporal_kernel,
        "temporal_attention",
        [sds(tokens, 3 * width)] + [sds(4 * fr, width)] * stage,
        [geo] + qkv_parts + grad_recv,
    )
    all_terms = [terms] + [from_quad(terms, s) for s in range(1, nq)]
    swapped = [move(t, flipped(1)) for t in all_terms]

    motion_ready = over_ring(motion_sends, 1, "regroup_motion")
    gn_sends = run(
        back_kernel,
        "temporal_back_projection",
        [sds(4 * nq * fr, half)] * stage,
        [geo, after(all_terms[0], motion_ready[0])] + all_terms[1:] + [motion_weights],
    )
    scratch = [pltpu.VMEM((2, stage, block, width), F32)]
    keep_a, send_a = run(
        first_weight_kernel,
        "weight_terms_query_key",
        [sds(stage, 2, block, width)] * 2,
        [geo, after(nt_keep, gn_sends[0]), nt_in] + all_terms + swapped,
        scratch=scratch,
    )
    gn_ready = over_ring(gn_sends, nq, "regroup_back", send_a)
    gns = sum(over_four_quads(gn_ready), [])
    motion_recv = over_four(motion_ready)
    motion_recv[0] = after(motion_recv[0], gn_ready[0])
    (motion_own,) = run(
        result_kernel, "motion_at_frames", [sds(own, width)], [geo] + motion_recv
    )
    motion = [motion_own] + [from_quad(motion_own, s) for s in range(1, nq)]
    motion_swapped = [move(m, flipped(1)) for m in motion]
    parts_b = run(
        second_weight_kernel,
        "weight_terms_value_output",
        [sds(2, 2, block, width)] * stage,
        [geo, after(nt_keep, gns[1]), nt_in, cot_keep, cot_in]
        + all_terms
        + swapped
        + motion
        + motion_swapped,
        scratch=scratch,
    )
    pair_a = add(keep_a, move(send_a, flipped(2)))
    total_a, total_b = pair_a[stage - 1], parts_b[stage - 1]
    gns[0] = after(gns[0], total_a, total_b)
    for step in range(1, stage):
        total_b = add(move(total_b, shifted(1)), parts_b[stage - 1 - step])
        total_a = add(move(total_a, shifted(1)), pair_a[stage - 1 - step])
    total_b = add(total_b[0], move(total_b[1], flipped(2)))
    final = []
    for g in range(nf):
        z, x, c = g // 4, (g // 2) % 2, g % 2
        for q in range(nq):
            final.append((g * nq + q, nf * q + c * (nf // 2) + x * stage + z))
    totals = [lax.ppermute(t, ("frame", "quad"), final) for t in (total_a, total_b)]

    base = 3 + nq + 4 * nq
    input_grad, gain_terms = run(
        tail_kernel,
        "spatial_backward",
        [sds(fr, pq, channels), sds(1, channels, dtype=F32)],
        [geo, activations]
        + cots
        + [hidden]
        + gns
        + [query, keys, values, gain1, gain2, spatial_weights],
        big,
        far=[(3 + nq + i, None) for i in range(4 * nq)]
        + [(2 + nq, None)]
        + [(2 + s, None) for s in range(nq)]
        + [(base + 5, (3, 0, 1, 2))]
        + [(base + i, None) for i in range(3)]
        + [(1, None)],
        far_outs=(0,),
    )
    delta_parts = run(
        delta_kernel,
        "block_projection",
        [sds(own, half, dtype=F32)] + [sds(own, half)] * (nq - 1),
        [after(motion[0], parts_b[0])] + motion[1:] + [motion_weights],
    )
    moved = [None] + [to_quad(p, s + 1) for s, p in enumerate(delta_parts[1:])]
    deltas = [delta_parts[0]] + [moved[nq - s] for s in range(1, nq)]
    (block_output,) = run(
        block_kernel, "block_output", [sds(fr, pq, channels)], [geo, hidden] + deltas
    )
    everyone = nf * nq
    gain_moved = lax.all_to_all(
        gain_terms.reshape(everyone, channels // everyone),
        ("frame", "quad"),
        split_axis=0,
        concat_axis=0,
        tiled=True,
    )
    factor = 1.0 / math.sqrt(everyone * fr * pq)
    weight_grad = jnp.concatenate(totals, axis=0).astype(F32) * factor
    gain_grad = jnp.sum(gain_moved, axis=0) * factor
    return block_output, input_grad, weight_grad, gain_grad


def solution(mesh):
    in_specs = (
        P("frame", "quad", None),
        P("frame", "quad", None),
        P(),
        P(),
        P(None, "quad", None),
        P(),
    )
    out_specs = (
        P("frame", "quad", None),
        P("frame", "quad", None),
        P(None, ("frame", "quad"), None),
        P(("frame", "quad")),
    )
    body = functools.partial(local, mesh.shape["quad"], mesh.shape["frame"])
    return jax.shard_map(
        body, mesh=mesh, in_specs=in_specs, out_specs=out_specs, check_vma=False
    )
```

```python
import functools
import math

import jax
import jax.numpy as jnp
from jax import lax
from jax.experimental import pallas as pl
from jax.experimental.pallas import tpu as pltpu
from jax.sharding import PartitionSpec as P

HEADS = 4
HEAD_DIM = 160
EPSILON = 1e-05
SCALE = HEAD_DIM ** (-0.5)
F32 = jnp.float32
BF16 = jnp.bfloat16


def log2(n):
    return int(n).bit_length() - 1


def dot(a, b):
    return jnp.dot(a, b, preferred_element_type=F32)


def dot_t(a, b):
    return lax.dot_general(a, b, (((1,), (1,)), ((), ())), preferred_element_type=F32)


def t_dot(a, b):
    return lax.dot_general(a, b, (((0,), (0,)), ((), ())), preferred_element_type=F32)


def normalize(values):
    average = jnp.mean(values, axis=-1, keepdims=True)
    centred = values - average
    inv_scale = lax.rsqrt(jnp.mean(centred * centred, axis=-1, keepdims=True) + EPSILON)
    return centred * inv_scale, inv_scale


def normalize_back(grad_rows, unit_rows, inv_scale, gain):
    scaled = grad_rows * gain
    first_mean = jnp.mean(scaled, axis=-1, keepdims=True)
    second_mean = jnp.mean(scaled * unit_rows, axis=-1, keepdims=True)
    return inv_scale * (scaled - first_mean - unit_rows * second_mean)


def iota(shape, dim):
    return lax.broadcasted_iota(jnp.int32, shape, dim)


def head_mask(dtype):
    lane = iota((1, HEADS * HEAD_DIM), 1)
    return [
        jnp.where((lane >= h * HEAD_DIM) & (lane < (h + 1) * HEAD_DIM), 1.0, 0.0).astype(dtype)
        for h in range(HEADS)
    ]


def stack_heads(rows):
    return jnp.concatenate([rows * mask for mask in head_mask(rows.dtype)], axis=0)


def fold_heads(stacked):
    rows = stacked.shape[0] // HEADS
    total = None
    for h, mask in enumerate(head_mask(F32)):
        piece = stacked[h * rows : (h + 1) * rows] * mask
        total = piece if total is None else total + piece
    return total


def probabilities(query_stack, keys, same):
    scores = dot_t(query_stack, keys) * SCALE
    if same is not None:
        scores = jnp.where(same, scores, -1e30)
    highest = jnp.max(scores, axis=-1, keepdims=True)
    expo = jnp.exp(scores - highest)
    return expo / jnp.sum(expo, axis=-1, keepdims=True)


def attend(query, keys, values, same):
    probs = probabilities(stack_heads(query), keys, same)
    return fold_heads(dot(probs.astype(BF16), values)).astype(BF16)


def attend_back(query, keys, values, grad, same, probs=None):
    query_stack = stack_heads(query)
    grad_stack = stack_heads(grad)
    if probs is None:
        probs = probabilities(query_stack, keys, same)
    grad_probs = dot_t(grad_stack, values)
    inner = jnp.sum(probs * grad_probs, axis=-1, keepdims=True)
    grad_scores = (probs * (grad_probs - inner) * SCALE).astype(BF16)
    grad_query = fold_heads(dot(grad_scores, keys)).astype(BF16)
    grad_key = t_dot(grad_scores, query_stack).astype(BF16)
    grad_value = t_dot(probs.astype(BF16), grad_stack).astype(BF16)
    return grad_query, grad_key, grad_value


def rows_to_sent(quad, nq, fr, pq, transposed):
    rows = nq * fr * pq
    out_dim = 1 if transposed else 0
    out = iota((rows, rows), out_dim)
    src = iota((rows, rows), 1 - out_dim)
    cell = out >> log2(nq * fr)
    other = (out >> log2(fr)) & (nq - 1)
    frame = out & (fr - 1)
    want = (((other - quad) & (nq - 1)) << log2(fr * pq)) + (frame << log2(pq)) + cell
    return jnp.where(want == src, 1.0, 0.0).astype(BF16)


def received_to_rows(quad, nq, nf, fr, transposed):
    rows = nq * nf * fr
    out_dim = 1 if transposed else 0
    out = iota((rows, rows), out_dim)
    src = iota((rows, rows), 1 - out_dim)
    step = out >> log2(nf * fr)
    device = (out >> log2(fr)) & (nf - 1)
    frame = out & (fr - 1)
    want = (device << log2(nq * fr)) + (((step + quad) & (nq - 1)) << log2(fr)) + frame
    return jnp.where(want == src, 1.0, 0.0).astype(BF16)


def own_lanes(values, quad, nq):
    width = values.shape[1] // nq
    picked = values[:, :width]
    for t in range(1, nq):
        picked = jnp.where(quad == t, values[:, t * width : (t + 1) * width], picked)
    return picked


def place_lanes(parts, quad, nq):
    placed = []
    for t in range(nq):
        piece = parts[t]
        for q in range(1, nq):
            piece = jnp.where(quad == q, parts[(t - q) % nq], piece)
        placed.append(piece)
    return jnp.concatenate(placed, axis=1)


def frame_groups(nq, fr, pq):
    size = max(1, min(fr, 128 // (nq * pq)))
    return [(start, size) for start in range(0, fr, size)]


def pick_group(rows, group, nq, fr, pq):
    start, size = group
    if size == fr:
        return rows
    cut = rows.reshape(nq, fr, pq, rows.shape[-1])[:, start : start + size]
    return cut.reshape(nq * size * pq, rows.shape[-1])


def join_groups(pieces, nq, fr, pq):
    if len(pieces) == 1:
        return pieces[0]
    size = fr // len(pieces)
    width = pieces[0].shape[-1]
    joined = jnp.concatenate([p.reshape(nq, size, pq, width) for p in pieces], axis=1)
    return joined.reshape(nq * fr * pq, width)


def same_frame(nq, size, pq):
    if size == 1:
        return None
    rows = nq * size * pq
    shape = (HEADS * rows, rows)
    left = (iota(shape, 0) >> log2(pq)) & (size - 1)
    right = (iota(shape, 1) >> log2(pq)) & (size - 1)
    return left == right


def flat(ref):
    value = ref[...]
    return value.reshape(-1, value.shape[-1])


def flat_wide(ref):
    value = ref[...].astype(F32)
    return value.reshape(-1, value.shape[-1])


def spread(rows, like):
    return rows.reshape(like.shape).astype(like.dtype)


def spatial_kernel(dims, *refs):
    nq, nf, fr, pq = dims
    quad, xs, refs = refs[0][0], refs[1 : 1 + nq], refs[1 + nq :]
    gain1, gain2, pos, weights, kept_out, send_out = refs
    width = HEADS * HEAD_DIM
    wide = jnp.concatenate([flat_wide(x) for x in xs], axis=0)
    unit, _ = normalize(wide)
    normed = (unit * gain1[...]).astype(BF16)
    query = dot(normed, weights[0]).astype(BF16)
    keys = dot(normed, weights[1]).astype(BF16)
    values = dot(normed, weights[2]).astype(BF16)
    for i, part in enumerate((query, keys, values)):
        kept_out[:, i * width : (i + 1) * width] = part
    pieces = []
    for group in frame_groups(nq, fr, pq):
        same = same_frame(nq, group[1], pq)
        cut = [pick_group(part, group, nq, fr, pq) for part in (query, keys, values)]
        pieces.append(attend(*cut, same))
    out = join_groups(pieces, nq, fr, pq)
    hidden = (wide + dot_t(out, weights[3])).astype(BF16)
    kept_out[:, 3 * width :] = hidden
    unit_two, _ = normalize(hidden.astype(F32))
    table = jnp.broadcast_to(pos[...][:, None, :], (fr, pq, pos.shape[-1]))
    table = table.reshape(fr * pq, pos.shape[-1])
    table = jnp.concatenate([table] * nq, axis=0)
    normed_two = own_lanes(unit_two * gain2[...] + table, quad, nq).astype(BF16)
    send_out[...] = spread(dot(rows_to_sent(quad, nq, fr, pq, False), normed_two), send_out)


def order_kernel(dims, cot, send_out):
    nq, nf, fr, pq = dims
    rows = flat(cot)
    width = rows.shape[1] // nq
    shape = (nq * fr * pq, fr * pq)
    out, src = iota(shape, 0), iota(shape, 1)
    want = ((out & (fr - 1)) << log2(pq)) + (out >> log2(nq * fr))
    part = (out >> log2(fr)) & (nq - 1)
    total = None
    for t in range(nq):
        pick = jnp.where((want == src) & (part == t), 1.0, 0.0).astype(BF16)
        piece = dot(pick, rows[:, t * width : (t + 1) * width])
        total = piece if total is None else total + piece
    send_out[...] = spread(total, send_out)


def split_kernel(dims, quad_ref, received, *outs):
    nq, nf, fr, pq = dims
    order = received_to_rows(quad_ref[0], nq, nf, fr, False)
    rows = dot(order, flat_wide(received).astype(BF16)).astype(BF16)
    tokens = nf * fr
    for s in range(nq):
        outs[s][...] = rows[s * tokens : (s + 1) * tokens]


def join(refs):
    return jnp.concatenate([ref[...] for ref in refs], axis=0)


def cotangent_kernel(dims, *refs):
    nq, nf, fr, pq = dims
    weights, own_out, *sends = refs[nq:]
    product = dot(join(refs[:nq]), weights[3])
    tokens = nf * fr
    own_out[...] = product[:tokens]
    for s, send in enumerate(sends):
        send[...] = product[(s + 1) * tokens : (s + 2) * tokens].astype(BF16)


def motion_kernel(dims, quad_ref, received, weights, own_out, *sends):
    nq, nf, fr, pq = dims
    order = received_to_rows(quad_ref[0], nq, nf, fr, False)
    rows = dot(order, flat_wide(received).astype(BF16)).astype(BF16)
    tokens = nf * fr
    for k in range(3):
        width = weights.shape[-1]
        lanes = slice(k * width, (k + 1) * width)
        product = dot(rows, weights[k])
        own_out[:, lanes] = product[:tokens]
        for s, send in enumerate(sends):
            send[:, lanes] = product[(s + 1) * tokens : (s + 2) * tokens].astype(BF16)


def cut_kernel(dims, quad_ref, core_ref, received, *refs):
    nq, nf, fr, pq = dims
    cots, (keep, swap) = refs[:nq], refs[nq:]
    order = received_to_rows(quad_ref[0], nq, nf, fr, False)
    normed = dot(order, flat_wide(received).astype(BF16))
    for i, rows in enumerate((normed, join(cots).astype(F32))):
        half = rows.shape[1] // 2
        low, high = rows[:, :half], rows[:, half:]
        keep[i] = jnp.where(core_ref[0] == 0, low, high).astype(BF16)
        swap[i] = jnp.where(core_ref[0] == 0, high, low).astype(BF16)


def temporal_kernel(dims, *refs):
    nq, nf, fr, pq = dims
    qkv_own, qkv_in = refs[0], refs[1:nq]
    grad_own, grad_in = refs[nq], refs[nq + 1 : 2 * nq]
    out = refs[2 * nq]
    width = HEADS * HEAD_DIM
    total = qkv_own[...]
    for part in qkv_in:
        total = total + part[...].astype(F32)
    grad = grad_own[...].astype(F32)
    for part in grad_in:
        grad = grad + part[...].astype(F32)
    query, keys, values = [total[:, k * width : (k + 1) * width].astype(BF16) for k in range(3)]
    grad = grad.astype(BF16)
    probs = probabilities(stack_heads(query), keys, None)
    motion_out = fold_heads(dot(probs.astype(BF16), values)).astype(BF16)
    grads = attend_back(query, keys, values, grad, None, probs)
    for k, piece in enumerate(grads + (motion_out,)):
        out[:, k * width : (k + 1) * width] = piece


def back_kernel(dims, quad_ref, *refs):
    nq, nf, fr, pq = dims
    terms, (weights, out) = refs[:nq], refs[nq:]
    width = HEADS * HEAD_DIM
    order = received_to_rows(quad_ref[0], nq, nf, fr, True)

    def part(k):
        return jnp.concatenate([t[:, k * width : (k + 1) * width] for t in terms], axis=0)

    grad = dot_t(part(0), weights[0]) + dot_t(part(1), weights[1]) + dot_t(part(2), weights[2])
    delta = dot_t(part(3), weights[3])
    for i, rows in enumerate((grad, delta)):
        rows = dot(order, rows.astype(BF16))
        out[:, i * nq * fr : (i + 1) * nq * fr, :] = rows.reshape(nf, nq * fr, -1).astype(BF16)


def weight_kernel(dims, place, keep, swapped, *refs):
    nq, nf, fr, pq = dims
    terms, refs = refs[: 2 * nq], refs[2 * nq :]
    keep_a, send_a, outs_b, blocks = refs[0], refs[1], refs[2:-1], refs[-1]
    width = HEADS * HEAD_DIM
    _, stage, block, _ = blocks.shape
    mid, turn = place[0], place[1]
    normed = jnp.concatenate([keep[0], swapped[0]], axis=0)
    cot = jnp.concatenate([keep[1], swapped[1]], axis=0)
    for k in range(4):
        right = jnp.concatenate([t[:, k * width : (k + 1) * width] for t in terms], axis=0)
        product = t_dot(normed if k < 3 else cot, right)
        for x in range(2):
            for z in range(stage):
                j = x * stage + z
                blocks[x, z] = product[j * block : (j + 1) * block]
        for r in range(stage):
            z = (turn + r) & (stage - 1)
            own, other = blocks[mid, z].astype(BF16), blocks[1 - mid, z].astype(BF16)
            if k < 2:
                keep_a[r, k], send_a[r, k] = own, other
            else:
                outs_b[r][0, k - 2], outs_b[r][1, k - 2] = own, other


def middle_kernel(dims, *refs):
    nq, nf, fr, pq = dims
    quad, received, cots = refs[0][0], refs[1 : 1 + nq], refs[1 + nq : 1 + 2 * nq]
    kept, gain2, block_out, gain_out, grad_out = refs[1 + 2 * nq :]
    own = fr * pq
    order = rows_to_sent(quad, nq, fr, pq, True)

    def lanes(i):
        parts = []
        for r in received:
            rows = r[:, i * nq * fr : (i + 1) * nq * fr, :].astype(F32)
            parts.append(dot(order, rows.reshape(nf * nq * fr, -1).astype(BF16)))
        return place_lanes(parts, quad, nq)

    hidden = kept[:, 3 * HEADS * HEAD_DIM :].astype(F32)
    grad_normed, delta = lanes(0), lanes(1)
    block_out[...] = spread(hidden[:own] + delta[:own], block_out)
    unit_two, inv_two = normalize(hidden)
    gain_out[...] = jnp.sum(grad_normed[:own] * unit_two[:own], axis=0, keepdims=True)
    cot = jnp.concatenate([flat_wide(c) for c in cots], axis=0)
    back = normalize_back(grad_normed, unit_two, inv_two, gain2[...])
    grad_out[...] = (cot + back).astype(BF16)


def tail_kernel(dims, grad_hidden, xs, kept, gain1, weights, in_grad):
    nq, nf, fr, pq = dims
    own, width = fr * pq, HEADS * HEAD_DIM
    grad_out = dot(grad_hidden[...], weights[3]).astype(BF16)
    parts = [kept[:, i * width : (i + 1) * width] for i in range(3)] + [grad_out]
    pieces = []
    for group in frame_groups(nq, fr, pq):
        same = same_frame(nq, group[1], pq)
        pieces.append(attend_back(*[pick_group(p, group, nq, fr, pq) for p in parts], same))
    grads = [join_groups([p[i] for p in pieces], nq, fr, pq)[:own] for i in range(3)]
    grad_one = dot_t(grads[0], weights[0]) + dot_t(grads[1], weights[1]) + dot_t(grads[2], weights[2])
    unit_one, inv_one = normalize(flat_wide(xs))
    back = normalize_back(grad_one, unit_one, inv_one, gain1[...])
    in_grad[...] = spread(grad_hidden[...][:own].astype(F32) + back, in_grad)


def call(kernel, name, outs, args, vmem, micros, scratch=()):
    in_specs = []
    for arg in args:
        space = pltpu.SMEM if arg.dtype == jnp.int32 else pltpu.VMEM
        in_specs.append(pl.BlockSpec(memory_space=space))
    return list(
        pl.pallas_call(
            kernel,
            out_shape=outs,
            in_specs=in_specs,
            out_specs=[pl.BlockSpec(memory_space=pltpu.VMEM) for _ in outs],
            scratch_shapes=list(scratch),
            compiler_params=pltpu.CompilerParams(vmem_limit_bytes=vmem * 1024 * 1024),
            cost_estimate=pl.CostEstimate(
                flops=int(micros * 1e9), bytes_accessed=2**20, transcendentals=0
            ),
            name=name,
        )(*args)
    )


def after(value, *others):
    return lax.optimization_barrier((value,) + others)[0]


def sds(*shape, dtype=BF16):
    return jax.ShapeDtypeStruct(shape, dtype)


def positional(first, frames, channels):
    frame_pos = (first + jnp.arange(frames)).astype(F32)[:, None]
    freq_index = jnp.arange(channels // 2).astype(F32)[None, :]
    phases = frame_pos * jnp.exp(freq_index * (-2.0 * math.log(10000.0) / channels))
    return jnp.stack([jnp.sin(phases), jnp.cos(phases)], axis=-1).reshape(frames, channels)


def local(nq, nf, activations, cotangent, spatial_weights, spatial_gain, motion_weights, motion_gain):
    fr, pq, channels = activations.shape
    dims = (nq, nf, fr, pq)
    width = spatial_weights.shape[-1]
    half = channels // nq
    rows = nq * fr * pq
    tokens = nf * fr
    small = 16 if rows <= 256 else 40
    big = 16 if rows <= 256 else 52
    quad = lax.axis_index("quad")
    frame = lax.axis_index("frame")
    quad_arr = quad.astype(jnp.int32).reshape(1)

    def from_quad(x, s):
        return lax.ppermute(x, "quad", [((d + s) % nq, d) for d in range(nq)])

    def to_quad(x, s):
        return lax.ppermute(x, "quad", [(d, (d + s) % nq) for d in range(nq)])

    def swap(x):
        return lax.all_to_all(x, "frame", split_axis=0, concat_axis=0, tiled=True)

    def run(kernel, name, outs, args, micros, vmem=small, **options):
        kernel = functools.partial(kernel, dims)
        return call(kernel, name, outs, args, vmem, micros, **options)

    def move(x, pairs):
        return lax.ppermute(x, "frame", pairs)

    def add(a, b):
        return (a.astype(F32) + b.astype(F32)).astype(BF16)

    core, mid, turn = frame % 2, (frame // 2) % 2, frame // 4
    core_arr = core.astype(jnp.int32).reshape(1)
    place_arr = jnp.stack([mid, turn]).astype(jnp.int32)
    flip_core = [(g, g ^ 1) for g in range(nf)]
    flip_mid = [(g, g ^ 2) for g in range(nf)]
    ring = [(g, (g + 4) % nf) for g in range(nf)]

    gain1 = spatial_gain.reshape(1, channels)
    gain2 = motion_gain.reshape(1, channels)
    sent = sds(nf, nq * fr, half)
    acts = [activations] + [from_quad(activations, s) for s in range(1, nq)]
    (cot_send,) = run(order_kernel, "order_cotangent", [sent], [cotangent], 5)
    cot_recv = swap(cot_send)
    cot_later = after(cotangent, acts[-1])
    cots = [cotangent] + [from_quad(cot_later, s) for s in range(1, nq)]
    pos = positional(frame * fr, fr, channels)

    kept, send = run(
        spatial_kernel,
        "spatial_forward",
        [sds(rows, 3 * width + channels), sent],
        [quad_arr] + acts + [gain1, gain2, pos, spatial_weights],
        3,
        big,
    )
    received = swap(send)

    cot_parts = run(
        split_kernel,
        "split_cotangent",
        [sds(tokens, half)] * nq,
        [quad_arr, after(cot_recv, send)],
        0.3,
    )
    cot_parts = [cot_parts[0]] + [to_quad(cot_parts[nq - s], nq - s) for s in range(1, nq)]
    grad_parts = run(
        cotangent_kernel,
        "cotangent_projection",
        [sds(tokens, width, dtype=F32)] + [sds(tokens, width)] * (nq - 1),
        cot_parts + [motion_weights],
        0.4,
    )
    grad_parts = [grad_parts[0]] + [to_quad(p, s + 1) for s, p in enumerate(grad_parts[1:])]

    qkv_parts = run(
        motion_kernel,
        "motion_projection",
        [sds(tokens, 3 * width, dtype=F32)] + [sds(tokens, 3 * width)] * (nq - 1),
        [quad_arr, after(received, grad_parts[-1]), motion_weights],
        0.8,
    )
    factors, factors_out = run(
        cut_kernel,
        "cut_factors",
        [sds(2, rows, half // 2)] * 2,
        [quad_arr, core_arr, after(received, qkv_parts[0])] + cot_parts,
        0.5,
    )
    qkv_parts = [qkv_parts[0]] + [to_quad(part, s + 1) for s, part in enumerate(qkv_parts[1:])]
    factors_in = move(factors_out, flip_core)

    (terms,) = run(
        temporal_kernel,
        "temporal_attention",
        [sds(tokens, 4 * width)],
        qkv_parts + grad_parts,
        2,
    )
    all_terms = [terms] + [from_quad(terms, s) for s in range(1, nq)]
    swapped = [move(t, flip_core) for t in all_terms]

    (back_send,) = run(
        back_kernel,
        "temporal_back_projection",
        [sds(nf, 2 * nq * fr, half)],
        [quad_arr] + all_terms + [motion_weights],
        2,
    )

    stage, block = nf // 4, half // nf
    keep_a, send_a, *parts_b = run(
        weight_kernel,
        "weight_terms",
        [sds(stage, 2, block, width)] * 2 + [sds(2, 2, block, width)] * stage,
        [place_arr, after(factors, back_send), factors_in] + all_terms + swapped,
        2,
        scratch=[pltpu.VMEM((2, stage, block, width), F32)],
    )
    back_recv = swap(after(back_send, send_a))
    backs = [back_recv] + [from_quad(back_recv, s) for s in range(1, nq)]
    pair_a = add(keep_a, move(send_a, flip_mid))
    total_a, total_b = pair_a[stage - 1], parts_b[stage - 1]
    for step in range(1, stage):
        total_b = add(move(total_b, ring), parts_b[stage - 1 - step])
        total_a = add(move(total_a, ring), pair_a[stage - 1 - step])
        if step == 1:
            backs[0] = after(backs[0], total_b, total_a)
    total_b = add(total_b[0], move(total_b[1], flip_mid))
    final = []
    for g in range(nf):
        z, x, c = g // 4, (g // 2) % 2, g % 2
        for q in range(nq):
            final.append((g * nq + q, nf * q + c * (nf // 2) + x * stage + z))
    totals = [lax.ppermute(t, ("frame", "quad"), final) for t in (total_a, total_b)]

    block_output, gain_terms, grad_hidden = run(
        middle_kernel,
        "block_output_hidden_gradient",
        [sds(fr, pq, channels), sds(1, channels, dtype=F32), sds(rows, channels)],
        [quad_arr] + backs + cots + [kept, gain2],
        1.5,
        big,
    )
    (input_grad,) = run(
        tail_kernel,
        "spatial_backward",
        [sds(fr, pq, channels)],
        [grad_hidden, activations, kept, gain1, spatial_weights],
        3.5,
        big,
    )
    everyone = nf * nq
    gain_moved = lax.all_to_all(
        gain_terms.reshape(everyone, channels // everyone),
        ("frame", "quad"),
        split_axis=0,
        concat_axis=0,
        tiled=True,
    )
    factor = 1.0 / math.sqrt(everyone * fr * pq)
    weight_grad = jnp.concatenate(totals, axis=0).astype(F32) * factor
    gain_grad = jnp.sum(gain_moved, axis=0) * factor
    return block_output, input_grad, weight_grad, gain_grad


def solution(mesh):
    in_specs = (
        P("frame", "quad", None),
        P("frame", "quad", None),
        P(),
        P(),
        P(None, "quad", None),
        P(),
    )
    out_specs = (
        P("frame", "quad", None),
        P("frame", "quad", None),
        P(None, ("frame", "quad"), None),
        P(("frame", "quad")),
    )
    body = functools.partial(local, mesh.shape["quad"], mesh.shape["frame"])
    return jax.shard_map(
        body, mesh=mesh, in_specs=in_specs, out_specs=out_specs, check_vma=False
    )
```

```python
import functools
import math

import jax
import jax.numpy as jnp
from jax import lax
from jax.experimental import pallas as pl
from jax.experimental.pallas import tpu as pltpu
from jax.sharding import PartitionSpec as P

HEADS = 4
HEAD_DIM = 160
EPSILON = 1e-05
SCALE = HEAD_DIM ** (-0.5)
F32 = jnp.float32
BF16 = jnp.bfloat16


def log2(n):
    return int(n).bit_length() - 1


def dot(a, b):
    return jnp.dot(a, b, preferred_element_type=F32)


def dot_t(a, b):
    return lax.dot_general(a, b, (((1,), (1,)), ((), ())), preferred_element_type=F32)


def t_dot(a, b):
    return lax.dot_general(a, b, (((0,), (0,)), ((), ())), preferred_element_type=F32)


def normalize(values):
    average = jnp.mean(values, axis=-1, keepdims=True)
    centred = values - average
    inv_scale = lax.rsqrt(jnp.mean(centred * centred, axis=-1, keepdims=True) + EPSILON)
    return centred * inv_scale, inv_scale


def normalize_back(grad_rows, unit_rows, inv_scale, gain):
    scaled = grad_rows * gain
    first_mean = jnp.mean(scaled, axis=-1, keepdims=True)
    second_mean = jnp.mean(scaled * unit_rows, axis=-1, keepdims=True)
    return inv_scale * (scaled - first_mean - unit_rows * second_mean)


def iota(shape, dim):
    return lax.broadcasted_iota(jnp.int32, shape, dim)


def head_mask(dtype):
    lane = iota((1, HEADS * HEAD_DIM), 1)
    return [
        jnp.where((lane >= h * HEAD_DIM) & (lane < (h + 1) * HEAD_DIM), 1.0, 0.0).astype(dtype)
        for h in range(HEADS)
    ]


def stack_heads(rows):
    return jnp.concatenate([rows * mask for mask in head_mask(rows.dtype)], axis=0)


def fold_heads(stacked):
    rows = stacked.shape[0] // HEADS
    total = None
    for h, mask in enumerate(head_mask(F32)):
        piece = stacked[h * rows : (h + 1) * rows] * mask
        total = piece if total is None else total + piece
    return total


def probabilities(query_stack, keys, same):
    scores = dot_t(query_stack, keys) * SCALE
    if same is not None:
        scores = jnp.where(same, scores, -1e30)
    highest = jnp.max(scores, axis=-1, keepdims=True)
    expo = jnp.exp(scores - highest)
    return expo / jnp.sum(expo, axis=-1, keepdims=True)


def attend(query, keys, values, same):
    probs = probabilities(stack_heads(query), keys, same)
    return fold_heads(dot(probs.astype(BF16), values)).astype(BF16)


def attend_back(query, keys, values, grad, same, probs=None):
    query_stack = stack_heads(query)
    grad_stack = stack_heads(grad)
    if probs is None:
        probs = probabilities(query_stack, keys, same)
    grad_probs = dot_t(grad_stack, values)
    inner = jnp.sum(probs * grad_probs, axis=-1, keepdims=True)
    grad_scores = (probs * (grad_probs - inner) * SCALE).astype(BF16)
    grad_query = fold_heads(dot(grad_scores, keys)).astype(BF16)
    grad_key = t_dot(grad_scores, query_stack).astype(BF16)
    grad_value = t_dot(probs.astype(BF16), grad_stack).astype(BF16)
    return grad_query, grad_key, grad_value


def rows_to_sent(quad, nq, fr, pq, transposed):
    rows = nq * fr * pq
    out_dim = 1 if transposed else 0
    out = iota((rows, rows), out_dim)
    src = iota((rows, rows), 1 - out_dim)
    cell = out >> log2(nq * fr)
    other = (out >> log2(fr)) & (nq - 1)
    frame = out & (fr - 1)
    want = (((other - quad) & (nq - 1)) << log2(fr * pq)) + (frame << log2(pq)) + cell
    return jnp.where(want == src, 1.0, 0.0).astype(BF16)


def received_to_rows(quad, nq, nf, fr, transposed):
    rows = nq * nf * fr
    out_dim = 1 if transposed else 0
    out = iota((rows, rows), out_dim)
    src = iota((rows, rows), 1 - out_dim)
    step = out >> log2(nf * fr)
    device = (out >> log2(fr)) & (nf - 1)
    frame = out & (fr - 1)
    want = (device << log2(nq * fr)) + (((step + quad) & (nq - 1)) << log2(fr)) + frame
    return jnp.where(want == src, 1.0, 0.0).astype(BF16)


def own_lanes(values, quad, nq):
    width = values.shape[1] // nq
    picked = values[:, :width]
    for t in range(1, nq):
        picked = jnp.where(quad == t, values[:, t * width : (t + 1) * width], picked)
    return picked


def place_lanes(parts, quad, nq):
    placed = []
    for t in range(nq):
        piece = parts[t]
        for q in range(1, nq):
            piece = jnp.where(quad == q, parts[(t - q) % nq], piece)
        placed.append(piece)
    return jnp.concatenate(placed, axis=1)


def frame_groups(nq, fr, pq):
    size = max(1, min(fr, 128 // (nq * pq)))
    return [(start, size) for start in range(0, fr, size)]


def pick_group(rows, group, nq, fr, pq):
    start, size = group
    if size == fr:
        return rows
    cut = rows.reshape(nq, fr, pq, rows.shape[-1])[:, start : start + size]
    return cut.reshape(nq * size * pq, rows.shape[-1])


def join_groups(pieces, nq, fr, pq):
    if len(pieces) == 1:
        return pieces[0]
    size = fr // len(pieces)
    width = pieces[0].shape[-1]
    joined = jnp.concatenate([p.reshape(nq, size, pq, width) for p in pieces], axis=1)
    return joined.reshape(nq * fr * pq, width)


def same_frame(nq, size, pq):
    if size == 1:
        return None
    rows = nq * size * pq
    shape = (HEADS * rows, rows)
    left = (iota(shape, 0) >> log2(pq)) & (size - 1)
    right = (iota(shape, 1) >> log2(pq)) & (size - 1)
    return left == right


def flat(ref):
    value = ref[...]
    return value.reshape(-1, value.shape[-1])


def flat_wide(ref):
    value = ref[...].astype(F32)
    return value.reshape(-1, value.shape[-1])


def spread(rows, like):
    return rows.reshape(like.shape).astype(like.dtype)


def spatial_kernel(dims, *refs):
    nq, nf, fr, pq = dims
    quad, xs, refs = refs[0][0], refs[1 : 1 + nq], refs[1 + nq :]
    gain1, gain2, pos, weights, kept_out, send_out = refs
    width = HEADS * HEAD_DIM
    wide = jnp.concatenate([flat_wide(x) for x in xs], axis=0)
    unit, _ = normalize(wide)
    normed = (unit * gain1[...]).astype(BF16)
    query = dot(normed, weights[0]).astype(BF16)
    keys = dot(normed, weights[1]).astype(BF16)
    values = dot(normed, weights[2]).astype(BF16)
    for i, part in enumerate((query, keys, values)):
        kept_out[:, i * width : (i + 1) * width] = part
    pieces = []
    for group in frame_groups(nq, fr, pq):
        same = same_frame(nq, group[1], pq)
        cut = [pick_group(part, group, nq, fr, pq) for part in (query, keys, values)]
        pieces.append(attend(*cut, same))
    out = join_groups(pieces, nq, fr, pq)
    hidden = (wide + dot_t(out, weights[3])).astype(BF16)
    kept_out[:, 3 * width :] = hidden
    unit_two, _ = normalize(hidden.astype(F32))
    table = jnp.broadcast_to(pos[...][:, None, :], (fr, pq, pos.shape[-1]))
    table = table.reshape(fr * pq, pos.shape[-1])
    table = jnp.concatenate([table] * nq, axis=0)
    normed_two = own_lanes(unit_two * gain2[...] + table, quad, nq).astype(BF16)
    send_out[...] = spread(dot(rows_to_sent(quad, nq, fr, pq, False), normed_two), send_out)


def order_kernel(dims, cot, send_out):
    nq, nf, fr, pq = dims
    rows = flat(cot)
    width = rows.shape[1] // nq
    shape = (nq * fr * pq, fr * pq)
    out, src = iota(shape, 0), iota(shape, 1)
    want = ((out & (fr - 1)) << log2(pq)) + (out >> log2(nq * fr))
    part = (out >> log2(fr)) & (nq - 1)
    total = None
    for t in range(nq):
        pick = jnp.where((want == src) & (part == t), 1.0, 0.0).astype(BF16)
        piece = dot(pick, rows[:, t * width : (t + 1) * width])
        total = piece if total is None else total + piece
    send_out[...] = spread(total, send_out)


def split_kernel(dims, quad_ref, received, *outs):
    nq, nf, fr, pq = dims
    order = received_to_rows(quad_ref[0], nq, nf, fr, False)
    rows = dot(order, flat_wide(received).astype(BF16)).astype(BF16)
    tokens = nf * fr
    for s in range(nq):
        outs[s][...] = rows[s * tokens : (s + 1) * tokens]


def join(refs):
    return jnp.concatenate([ref[...] for ref in refs], axis=0)


def cotangent_kernel(dims, *refs):
    nq, nf, fr, pq = dims
    weights, own_out, *sends = refs[nq:]
    product = dot(join(refs[:nq]), weights[3])
    tokens = nf * fr
    own_out[...] = product[:tokens]
    for s, send in enumerate(sends):
        send[...] = product[(s + 1) * tokens : (s + 2) * tokens].astype(BF16)


def motion_kernel(dims, quad_ref, received, weights, own_out, *sends):
    nq, nf, fr, pq = dims
    order = received_to_rows(quad_ref[0], nq, nf, fr, False)
    rows = dot(order, flat_wide(received).astype(BF16)).astype(BF16)
    tokens = nf * fr
    for k in range(3):
        width = weights.shape[-1]
        lanes = slice(k * width, (k + 1) * width)
        product = dot(rows, weights[k])
        own_out[:, lanes] = product[:tokens]
        for s, send in enumerate(sends):
            send[:, lanes] = product[(s + 1) * tokens : (s + 2) * tokens].astype(BF16)


def cut_kernel(dims, quad_ref, core_ref, received, *refs):
    nq, nf, fr, pq = dims
    cots, (keep, swap) = refs[:nq], refs[nq:]
    order = received_to_rows(quad_ref[0], nq, nf, fr, False)
    normed = dot(order, flat_wide(received).astype(BF16))
    for i, rows in enumerate((normed, join(cots).astype(F32))):
        half = rows.shape[1] // 2
        low, high = rows[:, :half], rows[:, half:]
        keep[i] = jnp.where(core_ref[0] == 0, low, high).astype(BF16)
        swap[i] = jnp.where(core_ref[0] == 0, high, low).astype(BF16)


def temporal_kernel(dims, *refs):
    nq, nf, fr, pq = dims
    qkv_own, qkv_in = refs[0], refs[1:nq]
    grad_own, grad_in = refs[nq], refs[nq + 1 : 2 * nq]
    out = refs[2 * nq]
    width = HEADS * HEAD_DIM
    total = qkv_own[...]
    for part in qkv_in:
        total = total + part[...].astype(F32)
    grad = grad_own[...].astype(F32)
    for part in grad_in:
        grad = grad + part[...].astype(F32)
    query, keys, values = [total[:, k * width : (k + 1) * width].astype(BF16) for k in range(3)]
    grad = grad.astype(BF16)
    probs = probabilities(stack_heads(query), keys, None)
    motion_out = fold_heads(dot(probs.astype(BF16), values)).astype(BF16)
    grads = attend_back(query, keys, values, grad, None, probs)
    for k, piece in enumerate(grads + (motion_out,)):
        out[:, k * width : (k + 1) * width] = piece


def back_kernel(dims, quad_ref, *refs):
    nq, nf, fr, pq = dims
    terms, (weights, received, pos, gain2, out, gain_out) = refs[:nq], refs[nq:]
    width = HEADS * HEAD_DIM
    order = received_to_rows(quad_ref[0], nq, nf, fr, True)

    def part(k):
        return jnp.concatenate([t[:, k * width : (k + 1) * width] for t in terms], axis=0)

    grad = dot_t(part(0), weights[0]) + dot_t(part(1), weights[1]) + dot_t(part(2), weights[2])
    delta = dot_t(part(3), weights[3])
    quad = quad_ref[0]
    normed = dot(received_to_rows(quad, nq, nf, fr, False), flat_wide(received).astype(BF16))
    table = jnp.concatenate([own_lanes(pos[...], quad, nq)] * nq, axis=0)
    unit = jnp.sum(grad * (normed - table), axis=0, keepdims=True)
    gain_out[...] = unit / own_lanes(gain2[...], quad, nq)
    for i, rows in enumerate((grad, delta)):
        rows = dot(order, rows.astype(BF16))
        out[:, i * nq * fr : (i + 1) * nq * fr, :] = rows.reshape(nf, nq * fr, -1).astype(BF16)


def weight_kernel(dims, place, keep, swapped, *refs):
    nq, nf, fr, pq = dims
    terms, refs = refs[: 2 * nq], refs[2 * nq :]
    keep_a, send_a, outs_b, blocks = refs[0], refs[1], refs[2:-1], refs[-1]
    width = HEADS * HEAD_DIM
    _, stage, block, _ = blocks.shape
    mid, turn = place[0], place[1]
    normed = jnp.concatenate([keep[0], swapped[0]], axis=0)
    cot = jnp.concatenate([keep[1], swapped[1]], axis=0)
    for k in range(4):
        right = jnp.concatenate([t[:, k * width : (k + 1) * width] for t in terms], axis=0)
        product = t_dot(normed if k < 3 else cot, right)
        for x in range(2):
            for z in range(stage):
                j = x * stage + z
                blocks[x, z] = product[j * block : (j + 1) * block]
        for r in range(stage):
            z = (turn + r) & (stage - 1)
            own, other = blocks[mid, z].astype(BF16), blocks[1 - mid, z].astype(BF16)
            if k < 2:
                keep_a[r, k], send_a[r, k] = own, other
            else:
                outs_b[r][0, k - 2], outs_b[r][1, k - 2] = own, other


def middle_kernel(dims, *refs):
    nq, nf, fr, pq = dims
    quad, received, cots = refs[0][0], refs[1 : 1 + nq], refs[1 + nq : 1 + 2 * nq]
    kept, gain2, block_out, grad_out = refs[1 + 2 * nq :]
    own = fr * pq
    order = rows_to_sent(quad, nq, fr, pq, True)

    def lanes(i):
        parts = []
        for r in received:
            rows = r[:, i * nq * fr : (i + 1) * nq * fr, :].astype(F32)
            parts.append(dot(order, rows.reshape(nf * nq * fr, -1).astype(BF16)))
        return place_lanes(parts, quad, nq)

    hidden = kept[:, 3 * HEADS * HEAD_DIM :].astype(F32)
    grad_normed, delta = lanes(0), lanes(1)
    block_out[...] = spread(hidden[:own] + delta[:own], block_out)
    unit_two, inv_two = normalize(hidden)
    cot = jnp.concatenate([flat_wide(c) for c in cots], axis=0)
    back = normalize_back(grad_normed, unit_two, inv_two, gain2[...])
    grad_out[...] = (cot + back).astype(BF16)


def tail_kernel(dims, grad_hidden, xs, kept, gain1, weights, in_grad):
    nq, nf, fr, pq = dims
    own, width = fr * pq, HEADS * HEAD_DIM
    grad_out = dot(grad_hidden[...], weights[3]).astype(BF16)
    parts = [kept[:, i * width : (i + 1) * width] for i in range(3)] + [grad_out]
    pieces = []
    for group in frame_groups(nq, fr, pq):
        same = same_frame(nq, group[1], pq)
        pieces.append(attend_back(*[pick_group(p, group, nq, fr, pq) for p in parts], same))
    grads = [join_groups([p[i] for p in pieces], nq, fr, pq)[:own] for i in range(3)]
    grad_one = dot_t(grads[0], weights[0]) + dot_t(grads[1], weights[1]) + dot_t(grads[2], weights[2])
    unit_one, inv_one = normalize(flat_wide(xs))
    back = normalize_back(grad_one, unit_one, inv_one, gain1[...])
    in_grad[...] = spread(grad_hidden[...][:own].astype(F32) + back, in_grad)


def call(kernel, name, outs, args, vmem, micros, scratch=()):
    in_specs = []
    for arg in args:
        space = pltpu.SMEM if arg.dtype == jnp.int32 else pltpu.VMEM
        in_specs.append(pl.BlockSpec(memory_space=space))
    return list(
        pl.pallas_call(
            kernel,
            out_shape=outs,
            in_specs=in_specs,
            out_specs=[pl.BlockSpec(memory_space=pltpu.VMEM) for _ in outs],
            scratch_shapes=list(scratch),
            compiler_params=pltpu.CompilerParams(vmem_limit_bytes=vmem * 1024 * 1024),
            cost_estimate=pl.CostEstimate(
                flops=int(micros * 1e9), bytes_accessed=2**20, transcendentals=0
            ),
            name=name,
        )(*args)
    )


def after(value, *others):
    return lax.optimization_barrier((value,) + others)[0]


def sds(*shape, dtype=BF16):
    return jax.ShapeDtypeStruct(shape, dtype)


def positional(first, frames, channels):
    frame_pos = (first + lax.broadcasted_iota(jnp.int32, (frames, channels), 0)).astype(F32)
    lane = lax.broadcasted_iota(jnp.int32, (frames, channels), 1)
    freq_index = (lane >> 1).astype(F32)
    phases = frame_pos * jnp.exp(freq_index * (-2.0 * math.log(10000.0) / channels))
    return jnp.sin(phases + (lane & 1).astype(F32) * (0.5 * math.pi))


def local(nq, nf, activations, cotangent, spatial_weights, spatial_gain, motion_weights, motion_gain):
    fr, pq, channels = activations.shape
    dims = (nq, nf, fr, pq)
    width = spatial_weights.shape[-1]
    half = channels // nq
    rows = nq * fr * pq
    tokens = nf * fr
    small = 16 if rows <= 256 else 40
    big = 16 if rows <= 256 else 52
    quad = lax.axis_index("quad")
    frame = lax.axis_index("frame")
    quad_arr = quad.astype(jnp.int32).reshape(1)

    def from_quad(x, s):
        return lax.ppermute(x, "quad", [((d + s) % nq, d) for d in range(nq)])

    def to_quad(x, s):
        return lax.ppermute(x, "quad", [(d, (d + s) % nq) for d in range(nq)])

    def swap(x):
        return lax.all_to_all(x, "frame", split_axis=0, concat_axis=0, tiled=True)

    def run(kernel, name, outs, args, micros, vmem=small, **options):
        kernel = functools.partial(kernel, dims)
        return call(kernel, name, outs, args, vmem, micros, **options)

    def move(x, pairs):
        return lax.ppermute(x, "frame", pairs)

    def add(a, b):
        return (a.astype(F32) + b.astype(F32)).astype(BF16)

    core, mid, turn = frame % 2, (frame // 2) % 2, frame // 4
    core_arr = core.astype(jnp.int32).reshape(1)
    place_arr = jnp.stack([mid, turn]).astype(jnp.int32)
    flip_core = [(g, g ^ 1) for g in range(nf)]
    flip_mid = [(g, g ^ 2) for g in range(nf)]
    ring = [(g, (g + 4) % nf) for g in range(nf)]

    gain1 = spatial_gain.reshape(1, channels)
    gain2 = motion_gain.reshape(1, channels)
    sent = sds(nf, nq * fr, half)
    acts = [activations] + [from_quad(activations, s) for s in range(1, nq)]
    (cot_send,) = run(order_kernel, "order_cotangent", [sent], [cotangent], 0.3)
    cot_recv = swap(cot_send)
    cot_later = after(cotangent, acts[-1])
    cots = [cotangent] + [from_quad(cot_later, s) for s in range(1, nq)]
    pos = positional(frame * fr, fr, channels)

    kept, send = run(
        spatial_kernel,
        "spatial_forward",
        [sds(rows, 3 * width + channels), sent],
        [quad_arr] + acts + [gain1, gain2, pos, spatial_weights],
        3,
        big,
    )
    received = swap(send)

    cot_parts = run(
        split_kernel,
        "split_cotangent",
        [sds(tokens, half)] * nq,
        [quad_arr, after(cot_recv, send)],
        0.3,
    )
    cot_parts = [cot_parts[0]] + [to_quad(cot_parts[nq - s], nq - s) for s in range(1, nq)]
    grad_parts = run(
        cotangent_kernel,
        "cotangent_projection",
        [sds(tokens, width, dtype=F32)] + [sds(tokens, width)] * (nq - 1),
        [after(cot_parts[0], cots[-1])] + cot_parts[1:] + [motion_weights],
        0.4,
    )
    grad_own = grad_parts[0]
    grad_parts = [grad_own] + [to_quad(p, s + 1) for s, p in enumerate(grad_parts[1:])]

    qkv_parts = run(
        motion_kernel,
        "motion_projection",
        [sds(tokens, 3 * width, dtype=F32)] + [sds(tokens, 3 * width)] * (nq - 1),
        [quad_arr, after(received, grad_own), motion_weights],
        0.8,
    )
    factors, factors_out = run(
        cut_kernel,
        "cut_factors",
        [sds(2, rows, half // 2)] * 2,
        [quad_arr, core_arr, after(received, qkv_parts[0])] + cot_parts,
        0.5,
    )
    qkv_parts = [qkv_parts[0]] + [to_quad(part, s + 1) for s, part in enumerate(qkv_parts[1:])]
    factors_in = move(factors_out, flip_core)

    (terms,) = run(
        temporal_kernel,
        "temporal_attention",
        [sds(tokens, 4 * width)],
        [after(qkv_parts[0], factors)] + qkv_parts[1:] + grad_parts,
        2,
    )
    all_terms = [terms] + [from_quad(terms, s) for s in range(1, nq)]
    swapped = [move(t, flip_core) for t in all_terms]

    back_send, gain_terms = run(
        back_kernel,
        "temporal_back_projection",
        [sds(nf, 2 * nq * fr, half), sds(1, half, dtype=F32)],
        [quad_arr]
        + all_terms
        + [motion_weights, received, positional(0, tokens, channels), gain2],
        3,
    )

    stage, block = nf // 4, half // nf
    keep_a, send_a, *parts_b = run(
        weight_kernel,
        "weight_terms",
        [sds(stage, 2, block, width)] * 2 + [sds(2, 2, block, width)] * stage,
        [place_arr, after(factors, back_send), factors_in] + all_terms + swapped,
        2,
        scratch=[pltpu.VMEM((2, stage, block, width), F32)],
    )
    back_recv = swap(after(back_send, send_a))
    pair_a = add(keep_a, move(send_a, flip_mid))
    total_b = add(move(parts_b[stage - 1], ring), parts_b[stage - 2])
    back_recv = after(back_recv, pair_a, total_b)
    backs = [back_recv] + [from_quad(back_recv, s) for s in range(1, nq)]
    block_output, grad_hidden = run(
        middle_kernel,
        "block_output_hidden_gradient",
        [sds(fr, pq, channels), sds(rows, channels)],
        [quad_arr] + backs + cots + [kept, gain2],
        1.5,
        big,
    )
    total_a = pair_a[stage - 1]
    for step in range(2, stage):
        if step == stage - 1:
            total_b = after(total_b, back_recv)
            total_a = after(total_a, back_recv)
        total_a = add(move(total_a, ring), pair_a[stage - step])
        moved_b = move(total_b, ring)
        if step == stage - 1:
            moved_b = after(moved_b, grad_hidden)
        total_b = add(moved_b, parts_b[stage - 1 - step])
    give_b = total_b[1]
    grad_hidden = after(grad_hidden, total_a, give_b)
    (input_grad,) = run(
        tail_kernel,
        "spatial_backward",
        [sds(fr, pq, channels)],
        [grad_hidden, activations, kept, gain1, spatial_weights],
        3.5,
        big,
    )
    moved_a, moved_b = move(total_a, ring), move(give_b, flip_mid)
    total_a = add(after(moved_a, input_grad), pair_a[0])
    total_b = add(total_b[0], after(moved_b, input_grad))
    final = []
    for g in range(nf):
        z, x, c = g // 4, (g // 2) % 2, g % 2
        for q in range(nq):
            final.append((g * nq + q, nf * q + c * (nf // 2) + x * stage + z))
    totals = [lax.ppermute(t, ("frame", "quad"), final) for t in (total_a, total_b)]

    everyone = nf * nq
    shares = gain_terms.reshape(1, nf, half // nf)
    at_quad = lax.broadcasted_iota(jnp.int32, (nq, 1, 1), 0) == quad
    shares = jnp.where(at_quad, shares, 0.0).reshape(everyone, 1, half // nf)
    gain_moved = lax.all_to_all(
        after(shares, back_recv), ("frame", "quad"), split_axis=0, concat_axis=0, tiled=True
    )
    factor = 1.0 / math.sqrt(everyone * fr * pq)
    weight_grad = jnp.concatenate(totals, axis=0).astype(F32) * factor
    gain_grad = jnp.sum(gain_moved, axis=(0, 1)) * factor
    return block_output, input_grad, weight_grad, gain_grad


def solution(mesh):
    in_specs = (
        P("frame", "quad", None),
        P("frame", "quad", None),
        P(),
        P(),
        P(None, "quad", None),
        P(),
    )
    out_specs = (
        P("frame", "quad", None),
        P("frame", "quad", None),
        P(None, ("frame", "quad"), None),
        P(("frame", "quad")),
    )
    body = functools.partial(local, mesh.shape["quad"], mesh.shape["frame"])
    return jax.shard_map(
        body, mesh=mesh, in_specs=in_specs, out_specs=out_specs, check_vma=False
    )
```

```python
import functools
import math

import jax
import jax.numpy as jnp
from jax import lax
from jax.experimental import pallas as pl
from jax.experimental.pallas import tpu as pltpu
from jax.sharding import PartitionSpec as P

HEADS = 4
HEAD_DIM = 160
EPSILON = 1e-05
SCALE = HEAD_DIM ** (-0.5)
F32 = jnp.float32
BF16 = jnp.bfloat16


def log2(n):
    return int(n).bit_length() - 1


def dot(a, b):
    return jnp.dot(a, b, preferred_element_type=F32)


def dot_t(a, b):
    return lax.dot_general(a, b, (((1,), (1,)), ((), ())), preferred_element_type=F32)


def t_dot(a, b):
    return lax.dot_general(a, b, (((0,), (0,)), ((), ())), preferred_element_type=F32)


def normalize(values):
    average = jnp.mean(values, axis=-1, keepdims=True)
    centred = values - average
    inv_scale = lax.rsqrt(jnp.mean(centred * centred, axis=-1, keepdims=True) + EPSILON)
    return centred * inv_scale, inv_scale


def normalize_back(grad_rows, unit_rows, inv_scale, gain):
    scaled = grad_rows * gain
    first_mean = jnp.mean(scaled, axis=-1, keepdims=True)
    second_mean = jnp.mean(scaled * unit_rows, axis=-1, keepdims=True)
    return inv_scale * (scaled - first_mean - unit_rows * second_mean)


def iota(shape, dim):
    return lax.broadcasted_iota(jnp.int32, shape, dim)


def head_mask(dtype):
    lane = iota((1, HEADS * HEAD_DIM), 1)
    return [
        jnp.where((lane >= h * HEAD_DIM) & (lane < (h + 1) * HEAD_DIM), 1.0, 0.0).astype(dtype)
        for h in range(HEADS)
    ]


def stack_heads(rows):
    return jnp.concatenate([rows * mask for mask in head_mask(rows.dtype)], axis=0)


def fold_heads(stacked):
    rows = stacked.shape[0] // HEADS
    total = None
    for h, mask in enumerate(head_mask(F32)):
        piece = stacked[h * rows : (h + 1) * rows] * mask
        total = piece if total is None else total + piece
    return total


def probabilities(query_stack, keys, same):
    scores = dot_t(query_stack, keys) * SCALE
    if same is not None:
        scores = jnp.where(same, scores, -1e30)
    highest = jnp.max(scores, axis=-1, keepdims=True)
    expo = jnp.exp(scores - highest)
    return expo / jnp.sum(expo, axis=-1, keepdims=True)


def attend(query, keys, values, same):
    probs = probabilities(stack_heads(query), keys, same)
    return fold_heads(dot(probs.astype(BF16), values)).astype(BF16)


def attend_back(query, keys, values, grad, same, probs=None):
    query_stack = stack_heads(query)
    grad_stack = stack_heads(grad)
    if probs is None:
        probs = probabilities(query_stack, keys, same)
    grad_probs = dot_t(grad_stack, values)
    inner = jnp.sum(probs * grad_probs, axis=-1, keepdims=True)
    grad_scores = (probs * (grad_probs - inner) * SCALE).astype(BF16)
    grad_query = fold_heads(dot(grad_scores, keys)).astype(BF16)
    grad_key = t_dot(grad_scores, query_stack).astype(BF16)
    grad_value = t_dot(probs.astype(BF16), grad_stack).astype(BF16)
    return grad_query, grad_key, grad_value


def rows_to_sent(quad, nq, fr, pq, transposed):
    rows = nq * fr * pq
    out_dim = 1 if transposed else 0
    out = iota((rows, rows), out_dim)
    src = iota((rows, rows), 1 - out_dim)
    cell = out >> log2(nq * fr)
    other = (out >> log2(fr)) & (nq - 1)
    frame = out & (fr - 1)
    want = (((other - quad) & (nq - 1)) << log2(fr * pq)) + (frame << log2(pq)) + cell
    return jnp.where(want == src, 1.0, 0.0).astype(BF16)


def received_to_rows(quad, nq, nf, fr, transposed):
    rows = nq * nf * fr
    out_dim = 1 if transposed else 0
    out = iota((rows, rows), out_dim)
    src = iota((rows, rows), 1 - out_dim)
    step = out >> log2(nf * fr)
    device = (out >> log2(fr)) & (nf - 1)
    frame = out & (fr - 1)
    want = (device << log2(nq * fr)) + (((step + quad) & (nq - 1)) << log2(fr)) + frame
    return jnp.where(want == src, 1.0, 0.0).astype(BF16)


def own_lanes(values, quad, nq):
    width = values.shape[1] // nq
    picked = values[:, :width]
    for t in range(1, nq):
        picked = jnp.where(quad == t, values[:, t * width : (t + 1) * width], picked)
    return picked


def place_lanes(parts, quad, nq):
    placed = []
    for t in range(nq):
        piece = parts[t]
        for q in range(1, nq):
            piece = jnp.where(quad == q, parts[(t - q) % nq], piece)
        placed.append(piece)
    return jnp.concatenate(placed, axis=1)


def frame_groups(nq, fr, pq):
    size = max(1, min(fr, 128 // (nq * pq)))
    return [(start, size) for start in range(0, fr, size)]


def pick_group(rows, group, nq, fr, pq):
    start, size = group
    if size == fr:
        return rows
    cut = rows.reshape(nq, fr, pq, rows.shape[-1])[:, start : start + size]
    return cut.reshape(nq * size * pq, rows.shape[-1])


def join_groups(pieces, nq, fr, pq):
    if len(pieces) == 1:
        return pieces[0]
    size = fr // len(pieces)
    width = pieces[0].shape[-1]
    joined = jnp.concatenate([p.reshape(nq, size, pq, width) for p in pieces], axis=1)
    return joined.reshape(nq * fr * pq, width)


def same_frame(nq, size, pq):
    if size == 1:
        return None
    rows = nq * size * pq
    shape = (HEADS * rows, rows)
    left = (iota(shape, 0) >> log2(pq)) & (size - 1)
    right = (iota(shape, 1) >> log2(pq)) & (size - 1)
    return left == right


def row_of(ref):
    return ref[...].reshape(1, -1)


def flat(ref):
    value = ref[...]
    return value.reshape(-1, value.shape[-1])


def flat_wide(ref):
    value = ref[...].astype(F32)
    return value.reshape(-1, value.shape[-1])


def spread(rows, like):
    return rows.reshape(like.shape).astype(like.dtype)


def spatial_kernel(dims, *refs):
    nq, nf, fr, pq = dims
    quad, xs, refs = refs[0][0], refs[1 : 1 + nq], refs[1 + nq :]
    gain1, gain2, pos, weights, kept_out, send_out = refs
    width = HEADS * HEAD_DIM
    wide = jnp.concatenate([flat_wide(x) for x in xs], axis=0)
    unit, _ = normalize(wide)
    normed = (unit * row_of(gain1)).astype(BF16)
    query = dot(normed, weights[0]).astype(BF16)
    keys = dot(normed, weights[1]).astype(BF16)
    values = dot(normed, weights[2]).astype(BF16)
    for i, part in enumerate((query, keys, values)):
        kept_out[:, i * width : (i + 1) * width] = part
    pieces = []
    for group in frame_groups(nq, fr, pq):
        same = same_frame(nq, group[1], pq)
        cut = [pick_group(part, group, nq, fr, pq) for part in (query, keys, values)]
        pieces.append(attend(*cut, same))
    out = join_groups(pieces, nq, fr, pq)
    hidden = (wide + dot_t(out, weights[3])).astype(BF16)
    kept_out[:, 3 * width :] = hidden
    unit_two, _ = normalize(hidden.astype(F32))
    table = jnp.broadcast_to(pos[...][:, None, :], (fr, pq, pos.shape[-1]))
    table = table.reshape(fr * pq, pos.shape[-1])
    table = jnp.concatenate([table] * nq, axis=0)
    normed_two = own_lanes(unit_two * row_of(gain2) + table, quad, nq).astype(BF16)
    send_out[...] = spread(dot(rows_to_sent(quad, nq, fr, pq, False), normed_two), send_out)


def order_kernel(dims, cot, send_out):
    nq, nf, fr, pq = dims
    rows = flat(cot)
    width = rows.shape[1] // nq
    shape = (nq * fr * pq, fr * pq)
    out, src = iota(shape, 0), iota(shape, 1)
    want = ((out & (fr - 1)) << log2(pq)) + (out >> log2(nq * fr))
    part = (out >> log2(fr)) & (nq - 1)
    total = None
    for t in range(nq):
        pick = jnp.where((want == src) & (part == t), 1.0, 0.0).astype(BF16)
        piece = dot(pick, rows[:, t * width : (t + 1) * width])
        total = piece if total is None else total + piece
    send_out[...] = spread(total, send_out)


def split_kernel(dims, quad_ref, received, *outs):
    nq, nf, fr, pq = dims
    order = received_to_rows(quad_ref[0], nq, nf, fr, False)
    rows = dot(order, flat_wide(received).astype(BF16)).astype(BF16)
    tokens = nf * fr
    for s in range(nq):
        outs[s][...] = rows[s * tokens : (s + 1) * tokens]


def join(refs):
    return jnp.concatenate([ref[...] for ref in refs], axis=0)


def cotangent_kernel(dims, *refs):
    nq, nf, fr, pq = dims
    weights, own_out, *sends = refs[nq:]
    product = dot(join(refs[:nq]), weights[3])
    tokens = nf * fr
    own_out[...] = product[:tokens]
    for s, send in enumerate(sends):
        send[...] = product[(s + 1) * tokens : (s + 2) * tokens].astype(BF16)


def motion_kernel(dims, quad_ref, received, weights, own_out, *sends):
    nq, nf, fr, pq = dims
    order = received_to_rows(quad_ref[0], nq, nf, fr, False)
    rows = dot(order, flat_wide(received).astype(BF16)).astype(BF16)
    tokens = nf * fr
    for k in range(3):
        width = weights.shape[-1]
        lanes = slice(k * width, (k + 1) * width)
        product = dot(rows, weights[k])
        own_out[:, lanes] = product[:tokens]
        for s, send in enumerate(sends):
            send[:, lanes] = product[(s + 1) * tokens : (s + 2) * tokens].astype(BF16)


def cut_kernel(dims, geo, received, *refs):
    nq, nf, fr, pq = dims
    cots, (keep, swap) = refs[:nq], refs[nq:]
    order = received_to_rows(geo[0], nq, nf, fr, False)
    normed = dot(order, flat_wide(received).astype(BF16))
    for i, rows in enumerate((normed, join(cots).astype(F32))):
        half = rows.shape[1] // 2
        low, high = rows[:, :half], rows[:, half:]
        keep[i] = jnp.where(geo[1] == 0, low, high).astype(BF16)
        swap[i] = jnp.where(geo[1] == 0, high, low).astype(BF16)


def temporal_kernel(dims, *refs):
    nq, nf, fr, pq = dims
    qkv_own, qkv_in = refs[0], refs[1:nq]
    grad_own, grad_in = refs[nq], refs[nq + 1 : 2 * nq]
    out = refs[2 * nq]
    width = HEADS * HEAD_DIM
    total = qkv_own[...]
    for part in qkv_in:
        total = total + part[...].astype(F32)
    grad = grad_own[...].astype(F32)
    for part in grad_in:
        grad = grad + part[...].astype(F32)
    query, keys, values = [total[:, k * width : (k + 1) * width].astype(BF16) for k in range(3)]
    grad = grad.astype(BF16)
    probs = probabilities(stack_heads(query), keys, None)
    motion_out = fold_heads(dot(probs.astype(BF16), values)).astype(BF16)
    grads = attend_back(query, keys, values, grad, None, probs)
    for k, piece in enumerate(grads + (motion_out,)):
        out[:, k * width : (k + 1) * width] = piece


def part_of(terms, k):
    width = HEADS * HEAD_DIM
    return jnp.concatenate([t[:, k * width : (k + 1) * width] for t in terms], axis=0)


def back_kernel(dims, quad_ref, *refs):
    nq, nf, fr, pq = dims
    terms, (weights, out) = refs[:nq], refs[nq:]
    order = received_to_rows(quad_ref[0], nq, nf, fr, True)
    grad = None
    for k in range(3):
        product = dot_t(part_of(terms, k), weights[k])
        grad = product if grad is None else grad + product
    delta = dot_t(part_of(terms, 3), weights[3])
    for i, rows in enumerate((grad, delta)):
        rows = dot(order, rows.astype(BF16))
        out[:, i * nq * fr : (i + 1) * nq * fr, :] = rows.reshape(nf, nq * fr, -1).astype(BF16)


def weight_kernel(dims, geo, keep, swapped, weights, pos, gain2, *refs):
    nq, nf, fr, pq = dims
    terms, refs = refs[: 2 * nq], refs[2 * nq :]
    keep_a, send_a, outs_b, (first, second) = refs[0], refs[1], refs[2:-2], refs[-2:]
    _, stage, block, width = first.shape
    quad, core, mid, turn = [geo[i] for i in range(4)]
    normed = jnp.concatenate([keep[0], swapped[0]], axis=0)
    cot = jnp.concatenate([keep[1], swapped[1]], axis=0)
    rows = normed.shape[1]
    grad = None
    for k in range(4):
        right = part_of(terms, k)
        product = t_dot(normed if k < 3 else cot, right)
        blocks = second if k == 3 else first
        for x in range(2):
            for z in range(stage):
                j = x * stage + z
                blocks[x, z] = product[j * block : (j + 1) * block]
        if k < 3:
            back = dot_t(right, weights[k, pl.ds(pl.multiple_of(core * rows, 16), rows), :])
            grad = back if grad is None else grad + back
        if k < 2:
            for r in range(stage):
                z = (turn + r) & (stage - 1)
                keep_a[r, k] = blocks[mid, z].astype(BF16)
                send_a[r, k] = blocks[1 - mid, z].astype(BF16)

    def core_lanes(values):
        values = own_lanes(values, quad, nq)
        return jnp.where(core == 0, values[:, :rows], values[:, rows:])

    table = jnp.concatenate([core_lanes(pos[...])] * (2 * nq), axis=0)
    gain = jnp.sum(grad * (normed.astype(F32) - table), axis=0, keepdims=True)
    gain = gain / core_lanes(row_of(gain2))
    extra = jnp.concatenate([gain, jnp.zeros((1, width - rows), F32)], axis=1)
    extra = jnp.where(iota((8, width), 0) == 0, extra, 0.0)
    for r in range(stage):
        z = (turn + r) & (stage - 1)
        for x, at in enumerate((mid, 1 - mid)):
            rows_out = jnp.concatenate([first[at, z], second[at, z], extra], axis=0)
            outs_b[r][x] = rows_out.astype(BF16)


def pair_kernel(dims, keep, moved, *outs):
    for r, out in enumerate(outs):
        out[...] = (keep[r].astype(F32) + moved[r].astype(F32)).astype(BF16)


def add_kernel(dims, left, right, *outs):
    total = (left[...].astype(F32) + right[...].astype(F32)).astype(BF16)
    if len(outs) == 1:
        outs[0][...] = total
    else:
        for i, out in enumerate(outs):
            out[...] = total[i]


def middle_kernel(dims, *refs):
    nq, nf, fr, pq = dims
    quad, received, cots = refs[0][0], refs[1 : 1 + nq], refs[1 + nq : 1 + 2 * nq]
    kept, gain2, block_out, grad_out = refs[1 + 2 * nq :]
    own = fr * pq
    order = rows_to_sent(quad, nq, fr, pq, True)

    def lanes(i):
        parts = []
        for r in received:
            rows = r[:, i * nq * fr : (i + 1) * nq * fr, :].astype(F32)
            parts.append(dot(order, rows.reshape(nf * nq * fr, -1).astype(BF16)))
        return place_lanes(parts, quad, nq)

    hidden = kept[:, 3 * HEADS * HEAD_DIM :].astype(F32)
    grad_normed, delta = lanes(0), lanes(1)
    block_out[...] = spread(hidden[:own] + delta[:own], block_out)
    unit_two, inv_two = normalize(hidden)
    cot = jnp.concatenate([flat_wide(c) for c in cots], axis=0)
    back = normalize_back(grad_normed, unit_two, inv_two, row_of(gain2))
    grad_out[...] = (cot + back).astype(BF16)


def tail_kernel(dims, grad_hidden, xs, kept, gain1, weights, in_grad):
    nq, nf, fr, pq = dims
    own, width = fr * pq, HEADS * HEAD_DIM
    grad_out = dot(grad_hidden[...], weights[3]).astype(BF16)
    parts = [kept[:, i * width : (i + 1) * width] for i in range(3)] + [grad_out]
    pieces = []
    for group in frame_groups(nq, fr, pq):
        same = same_frame(nq, group[1], pq)
        pieces.append(attend_back(*[pick_group(p, group, nq, fr, pq) for p in parts], same))
    grads = [join_groups([p[i] for p in pieces], nq, fr, pq)[:own] for i in range(3)]
    grad_one = dot_t(grads[0], weights[0]) + dot_t(grads[1], weights[1]) + dot_t(grads[2], weights[2])
    unit_one, inv_one = normalize(flat_wide(xs))
    back = normalize_back(grad_one, unit_one, inv_one, row_of(gain1))
    in_grad[...] = spread(grad_hidden[...][:own].astype(F32) + back, in_grad)


def call(kernel, name, outs, args, vmem, micros, scratch=()):
    in_specs = []
    for arg in args:
        space = pltpu.SMEM if arg.dtype == jnp.int32 else pltpu.VMEM
        in_specs.append(pl.BlockSpec(memory_space=space))
    return list(
        pl.pallas_call(
            kernel,
            out_shape=outs,
            in_specs=in_specs,
            out_specs=[pl.BlockSpec(memory_space=pltpu.VMEM) for _ in outs],
            scratch_shapes=list(scratch),
            compiler_params=pltpu.CompilerParams(vmem_limit_bytes=vmem * 1024 * 1024),
            cost_estimate=pl.CostEstimate(
                flops=int(micros * 1e9), bytes_accessed=2**20, transcendentals=0
            ),
            name=name,
        )(*args)
    )


def after(value, *others):
    return lax.optimization_barrier((value,) + others)[0]


def sds(*shape, dtype=BF16):
    return jax.ShapeDtypeStruct(shape, dtype)


def positional(first, frames, channels):
    frame_pos = (first + lax.broadcasted_iota(jnp.int32, (frames, channels), 0)).astype(F32)
    lane = lax.broadcasted_iota(jnp.int32, (frames, channels), 1)
    freq_index = (lane >> 1).astype(F32)
    phases = frame_pos * jnp.exp(freq_index * (-2.0 * math.log(10000.0) / channels))
    return jnp.sin(phases + (lane & 1).astype(F32) * (0.5 * math.pi))


def local(nq, nf, activations, cotangent, spatial_weights, spatial_gain, motion_weights, motion_gain):
    fr, pq, channels = activations.shape
    dims = (nq, nf, fr, pq)
    width = spatial_weights.shape[-1]
    half = channels // nq
    rows = nq * fr * pq
    tokens = nf * fr
    small = 16 if rows <= 256 else 40
    big = 16 if rows <= 256 else 52
    quad = lax.axis_index("quad")
    frame = lax.axis_index("frame")


    def from_quad(x, s):
        return lax.ppermute(x, "quad", [((d + s) % nq, d) for d in range(nq)])

    def to_quad(x, s):
        return lax.ppermute(x, "quad", [(d, (d + s) % nq) for d in range(nq)])

    def swap(x):
        return lax.all_to_all(x, "frame", split_axis=0, concat_axis=0, tiled=True)

    def run(kernel, name, outs, args, micros, vmem=small, **options):
        kernel = functools.partial(kernel, dims)
        return call(kernel, name, outs, args, vmem, micros, **options)

    def move(x, pairs):
        return lax.ppermute(x, "frame", pairs)

    core, mid, turn = frame % 2, (frame // 2) % 2, frame // 4
    geo = jnp.stack([quad, core, mid, turn]).astype(jnp.int32)
    flip_core = [(g, g ^ 1) for g in range(nf)]
    flip_mid = [(g, g ^ 2) for g in range(nf)]
    ring = [(g, (g + 4) % nf) for g in range(nf)]

    gain1, gain2 = spatial_gain, motion_gain
    sent = sds(nf, nq * fr, half)
    acts = [activations] + [from_quad(activations, s) for s in range(1, nq)]
    (cot_send,) = run(order_kernel, "order_cotangent", [sent], [cotangent], 0.3)
    cot_recv = swap(cot_send)
    cot_later = after(cotangent, acts[-1])
    cots = [cotangent] + [from_quad(cot_later, s) for s in range(1, nq)]
    pos = positional(frame * fr, fr, channels)

    kept, send = run(
        spatial_kernel,
        "spatial_forward",
        [sds(rows, 3 * width + channels), sent],
        [geo] + acts + [gain1, gain2, pos, spatial_weights],
        3,
        big,
    )
    received = swap(send)

    cot_parts = run(
        split_kernel,
        "split_cotangent",
        [sds(tokens, half)] * nq,
        [geo, after(cot_recv, send)],
        0.3,
    )
    cot_parts = [cot_parts[0]] + [to_quad(cot_parts[nq - s], nq - s) for s in range(1, nq)]
    grad_parts = run(
        cotangent_kernel,
        "cotangent_projection",
        [sds(tokens, width, dtype=F32)] + [sds(tokens, width)] * (nq - 1),
        [after(cot_parts[0], cots[-1])] + cot_parts[1:] + [motion_weights],
        0.4,
    )
    grad_own = grad_parts[0]
    table = positional(after(frame * 0, cot_parts[0]), tokens, channels)
    grad_parts = [grad_own] + [to_quad(p, s + 1) for s, p in enumerate(grad_parts[1:])]

    qkv_parts = run(
        motion_kernel,
        "motion_projection",
        [sds(tokens, 3 * width, dtype=F32)] + [sds(tokens, 3 * width)] * (nq - 1),
        [geo, after(received, grad_own, table), motion_weights],
        0.8,
    )
    factors, factors_out = run(
        cut_kernel,
        "cut_factors",
        [sds(2, rows, half // 2)] * 2,
        [geo, after(received, qkv_parts[0])] + cot_parts,
        0.5,
    )
    qkv_parts = [qkv_parts[0]] + [to_quad(part, s + 1) for s, part in enumerate(qkv_parts[1:])]
    factors_in = move(factors_out, flip_core)

    (terms,) = run(
        temporal_kernel,
        "temporal_attention",
        [sds(tokens, 4 * width)],
        [after(qkv_parts[0], factors)] + qkv_parts[1:] + grad_parts,
        2,
    )
    all_terms = [terms] + [from_quad(terms, s) for s in range(1, nq)]
    swapped = [move(t, flip_core) for t in all_terms]

    (back_send,) = run(
        back_kernel,
        "temporal_back_projection",
        [sds(nf, 2 * nq * fr, half)],
        [geo] + all_terms + [motion_weights],
        2,
    )

    stage, block = nf // 4, half // nf
    keep_a, send_a, *parts_b = run(
        weight_kernel,
        "weight_terms",
        [sds(stage, 2, block, width)] * 2 + [sds(2, 2 * block + 8, width)] * stage,
        [geo, after(factors, back_send), factors_in, motion_weights, table, gain2]
        + all_terms
        + swapped,
        3,
        scratch=[pltpu.VMEM((2, stage, block, width), F32)] * 2,
    )

    def add(a, b, cut=False):
        outs = [sds(*a.shape[1:])] * a.shape[0] if cut else [sds(*a.shape)]
        outs = run(add_kernel, "add", outs, [a, b], 0.2)
        return outs if cut else outs[0]

    back_recv = swap(after(back_send, send_a))
    pair_a = run(
        pair_kernel,
        "add_pair",
        [sds(2, block, width)] * stage,
        [keep_a, move(send_a, flip_mid)],
        0.3,
    )
    total_a = pair_a[stage - 1]
    total_b = add(move(parts_b[stage - 1], ring), parts_b[stage - 2])
    back_recv = after(back_recv, total_a, total_b)
    backs = [back_recv] + [from_quad(back_recv, s) for s in range(1, nq)]
    for step in range(2, stage):
        last = step == stage - 1
        if last:
            total_b = after(total_b, back_recv)
            total_a = after(total_a, back_recv)
        total_a = add(move(total_a, ring), pair_a[stage - step])
        total_b = add(move(total_b, ring), parts_b[stage - 1 - step], last)
    own_b, give_b = total_b
    backs[0] = after(backs[0], total_a, give_b)
    block_output, grad_hidden = run(
        middle_kernel,
        "block_output_hidden_gradient",
        [sds(fr, pq, channels), sds(rows, channels)],
        [geo] + backs + cots + [kept, gain2],
        1.5,
        big,
    )
    total_a = add(after(move(total_a, ring), grad_hidden), pair_a[0])
    total_b = add(after(move(give_b, flip_mid), grad_hidden), own_b)
    final = []
    for g in range(nf):
        z, x, c = g // 4, (g // 2) % 2, g % 2
        for q in range(nq):
            final.append((g * nq + q, nf * q + c * (nf // 2) + x * stage + z))
    grad_hidden = after(grad_hidden, total_a, total_b)
    total_a, total_b = [lax.ppermute(t, ("frame", "quad"), final) for t in (total_a, total_b)]
    (input_grad,) = run(
        tail_kernel,
        "spatial_backward",
        [sds(fr, pq, channels)],
        [grad_hidden, activations, kept, gain1, spatial_weights],
        3.5,
        big,
    )
    everyone = nf * nq
    factor = 1.0 / math.sqrt(everyone * fr * pq)
    total_b, extra = total_b[: 2 * block], total_b[2 * block]
    weight_grad = jnp.concatenate([total_a, total_b.reshape(total_a.shape)], axis=0)
    weight_grad = weight_grad.astype(F32) * factor
    place = ((frame * nq + quad) % (nf // 2)) * block
    gain_grad = lax.dynamic_slice(extra, (place,), (block,)).astype(F32) * factor
    return block_output, input_grad, weight_grad, gain_grad


def solution(mesh):
    in_specs = (
        P("frame", "quad", None),
        P("frame", "quad", None),
        P(),
        P(),
        P(None, "quad", None),
        P(),
    )
    out_specs = (
        P("frame", "quad", None),
        P("frame", "quad", None),
        P(None, ("frame", "quad"), None),
        P(("frame", "quad")),
    )
    body = functools.partial(local, mesh.shape["quad"], mesh.shape["frame"])
    return jax.shard_map(
        body, mesh=mesh, in_specs=in_specs, out_specs=out_specs, check_vma=False
    )
```

```python
import functools
import math

import jax
import jax.numpy as jnp
from jax import lax
from jax.experimental import pallas as pl
from jax.experimental.pallas import tpu as pltpu
from jax.sharding import PartitionSpec as P

HEADS = 4
HEAD_DIM = 160
EPSILON = 1e-05
SCALE = HEAD_DIM ** (-0.5)
F32 = jnp.float32
BF16 = jnp.bfloat16


def log2(n):
    return int(n).bit_length() - 1


def dot(a, b):
    return jnp.dot(a, b, preferred_element_type=F32)


def dot_t(a, b):
    return lax.dot_general(a, b, (((1,), (1,)), ((), ())), preferred_element_type=F32)


def t_dot(a, b):
    return lax.dot_general(a, b, (((0,), (0,)), ((), ())), preferred_element_type=F32)


def normalize(values):
    average = jnp.mean(values, axis=-1, keepdims=True)
    centred = values - average
    inv_scale = lax.rsqrt(jnp.mean(centred * centred, axis=-1, keepdims=True) + EPSILON)
    return centred * inv_scale, inv_scale


def normalize_back(grad_rows, unit_rows, inv_scale, gain):
    scaled = grad_rows * gain
    first_mean = jnp.mean(scaled, axis=-1, keepdims=True)
    second_mean = jnp.mean(scaled * unit_rows, axis=-1, keepdims=True)
    return inv_scale * (scaled - first_mean - unit_rows * second_mean)


def iota(shape, dim):
    return lax.broadcasted_iota(jnp.int32, shape, dim)


def head_mask(dtype):
    lane = iota((1, HEADS * HEAD_DIM), 1)
    return [
        jnp.where((lane >= h * HEAD_DIM) & (lane < (h + 1) * HEAD_DIM), 1.0, 0.0).astype(dtype)
        for h in range(HEADS)
    ]


def stack_heads(rows):
    return jnp.concatenate([rows * mask for mask in head_mask(rows.dtype)], axis=0)


def fold_heads(stacked):
    rows = stacked.shape[0] // HEADS
    total = None
    for h, mask in enumerate(head_mask(F32)):
        piece = stacked[h * rows : (h + 1) * rows] * mask
        total = piece if total is None else total + piece
    return total


def probabilities(query_stack, keys, same):
    scores = dot_t(query_stack, keys) * SCALE
    if same is not None:
        scores = jnp.where(same, scores, -1e30)
    highest = jnp.max(scores, axis=-1, keepdims=True)
    expo = jnp.exp(scores - highest)
    return expo / jnp.sum(expo, axis=-1, keepdims=True)


def attend(query, keys, values, same):
    probs = probabilities(stack_heads(query), keys, same)
    return fold_heads(dot(probs.astype(BF16), values)).astype(BF16)


def attend_back(query, keys, values, grad, same, probs=None):
    query_stack = stack_heads(query)
    grad_stack = stack_heads(grad)
    if probs is None:
        probs = probabilities(query_stack, keys, same)
    grad_probs = dot_t(grad_stack, values)
    inner = jnp.sum(probs * grad_probs, axis=-1, keepdims=True)
    grad_scores = (probs * (grad_probs - inner) * SCALE).astype(BF16)
    grad_query = fold_heads(dot(grad_scores, keys)).astype(BF16)
    grad_key = t_dot(grad_scores, query_stack).astype(BF16)
    grad_value = t_dot(probs.astype(BF16), grad_stack).astype(BF16)
    return grad_query, grad_key, grad_value


def rows_to_sent(quad, nq, fr, pq, transposed):
    rows = nq * fr * pq
    out_dim = 1 if transposed else 0
    out = iota((rows, rows), out_dim)
    src = iota((rows, rows), 1 - out_dim)
    cell = out >> log2(nq * fr)
    other = (out >> log2(fr)) & (nq - 1)
    frame = out & (fr - 1)
    want = (((other - quad) & (nq - 1)) << log2(fr * pq)) + (frame << log2(pq)) + cell
    return jnp.where(want == src, 1.0, 0.0).astype(BF16)


def received_to_rows(quad, nq, nf, fr, transposed):
    rows = nq * nf * fr
    out_dim = 1 if transposed else 0
    out = iota((rows, rows), out_dim)
    src = iota((rows, rows), 1 - out_dim)
    step = out >> log2(nf * fr)
    device = (out >> log2(fr)) & (nf - 1)
    frame = out & (fr - 1)
    want = (device << log2(nq * fr)) + (((step + quad) & (nq - 1)) << log2(fr)) + frame
    return jnp.where(want == src, 1.0, 0.0).astype(BF16)


def own_lanes(values, quad, nq):
    width = values.shape[1] // nq
    picked = values[:, :width]
    for t in range(1, nq):
        picked = jnp.where(quad == t, values[:, t * width : (t + 1) * width], picked)
    return picked


def place_lanes(parts, quad, nq):
    placed = []
    for t in range(nq):
        piece = parts[t]
        for q in range(1, nq):
            piece = jnp.where(quad == q, parts[(t - q) % nq], piece)
        placed.append(piece)
    return jnp.concatenate(placed, axis=1)


def frame_groups(nq, fr, pq):
    size = max(1, min(fr, 128 // (nq * pq)))
    return [(start, size) for start in range(0, fr, size)]


def pick_group(rows, group, nq, fr, pq):
    start, size = group
    if size == fr:
        return rows
    cut = rows.reshape(nq, fr, pq, rows.shape[-1])[:, start : start + size]
    return cut.reshape(nq * size * pq, rows.shape[-1])


def join_groups(pieces, nq, fr, pq):
    if len(pieces) == 1:
        return pieces[0]
    size = fr // len(pieces)
    width = pieces[0].shape[-1]
    joined = jnp.concatenate([p.reshape(nq, size, pq, width) for p in pieces], axis=1)
    return joined.reshape(nq * fr * pq, width)


def same_frame(nq, size, pq):
    if size == 1:
        return None
    rows = nq * size * pq
    shape = (HEADS * rows, rows)
    left = (iota(shape, 0) >> log2(pq)) & (size - 1)
    right = (iota(shape, 1) >> log2(pq)) & (size - 1)
    return left == right


def row_of(ref):
    return ref[...].reshape(1, -1)


def flat(ref):
    value = ref[...]
    return value.reshape(-1, value.shape[-1])


def flat_wide(ref):
    value = ref[...].astype(F32)
    return value.reshape(-1, value.shape[-1])


def spread(rows, like):
    return rows.reshape(like.shape).astype(like.dtype)


def spatial_kernel(dims, *refs):
    nq, nf, fr, pq = dims
    quad, xs, refs = refs[0][0], refs[1 : 1 + nq], refs[1 + nq :]
    gain1, gain2, pos, weights, kept_out, send_out = refs
    width = HEADS * HEAD_DIM
    wide = jnp.concatenate([flat_wide(x) for x in xs], axis=0)
    unit, _ = normalize(wide)
    normed = (unit * row_of(gain1)).astype(BF16)
    query = dot(normed, weights[0]).astype(BF16)
    keys = dot(normed, weights[1]).astype(BF16)
    values = dot(normed, weights[2]).astype(BF16)
    for i, part in enumerate((query, keys, values)):
        kept_out[:, i * width : (i + 1) * width] = part
    pieces = []
    for group in frame_groups(nq, fr, pq):
        same = same_frame(nq, group[1], pq)
        cut = [pick_group(part, group, nq, fr, pq) for part in (query, keys, values)]
        pieces.append(attend(*cut, same))
    out = join_groups(pieces, nq, fr, pq)
    hidden = (wide + dot_t(out, weights[3])).astype(BF16)
    kept_out[:, 3 * width :] = hidden
    unit_two, _ = normalize(hidden.astype(F32))
    table = jnp.broadcast_to(pos[...][:, None, :], (fr, pq, pos.shape[-1]))
    table = table.reshape(fr * pq, pos.shape[-1])
    table = jnp.concatenate([table] * nq, axis=0)
    normed_two = own_lanes(unit_two * row_of(gain2) + table, quad, nq).astype(BF16)
    send_out[...] = spread(dot(rows_to_sent(quad, nq, fr, pq, False), normed_two), send_out)


def order_kernel(dims, geo, cot, weights, send_out):
    nq, nf, fr, pq = dims
    order = rows_to_sent(geo[0], nq, fr, pq, False)[:, : fr * pq]
    send_out[...] = spread(dot(order, own_lanes(flat(cot), geo[0], nq)), send_out)


def join_kernel(dims, geo, normed, own_part, *refs):
    nq, nf, fr, pq = dims
    cots, send_out = refs[:-1], refs[-1]
    order = rows_to_sent(geo[0], nq, fr, pq, False)[:, fr * pq :]
    rows = own_lanes(jnp.concatenate([flat(c) for c in cots], axis=0), geo[0], nq)
    total = own_part[...].astype(F32) + dot(order, rows).reshape(own_part.shape)
    send_out[:, : nq * fr, :] = normed[...]
    send_out[:, nq * fr :, :] = total.astype(BF16)


def sent_part(received, i, rows):
    part = received[:, i * rows : (i + 1) * rows, :].astype(F32)
    return part.reshape(-1, part.shape[-1]).astype(BF16)


def motion_kernel(dims, geo, received, weights, own_out, *sends):
    nq, nf, fr, pq = dims
    order = received_to_rows(geo[0], nq, nf, fr, False)
    normed, cot = [dot(order, sent_part(received, i, nq * fr)).astype(BF16) for i in range(2)]
    tokens = nf * fr
    for k in range(4):
        width = weights.shape[-1]
        lanes = slice(k * width, (k + 1) * width)
        product = dot(normed if k < 3 else cot, weights[k])
        own_out[:, lanes] = product[:tokens]
        for s, send in enumerate(sends):
            send[:, lanes] = product[(s + 1) * tokens : (s + 2) * tokens].astype(BF16)


def cut_kernel(dims, geo, received, keep, swap):
    nq, nf, fr, pq = dims
    order = received_to_rows(geo[0], nq, nf, fr, False)
    for i in range(2):
        rows = dot(order, sent_part(received, i, nq * fr))
        half = rows.shape[1] // 2
        low, high = rows[:, :half], rows[:, half:]
        keep[i] = jnp.where(geo[1] == 0, low, high).astype(BF16)
        swap[i] = jnp.where(geo[1] == 0, high, low).astype(BF16)


def temporal_kernel(dims, *refs):
    nq, nf, fr, pq = dims
    parts, out = refs[:nq], refs[nq]
    width = HEADS * HEAD_DIM
    total = parts[0][...]
    for part in parts[1:]:
        total = total + part[...].astype(F32)
    query, keys, values, grad = [
        total[:, k * width : (k + 1) * width].astype(BF16) for k in range(4)
    ]
    probs = probabilities(stack_heads(query), keys, None)
    motion_out = fold_heads(dot(probs.astype(BF16), values)).astype(BF16)
    grads = attend_back(query, keys, values, grad, None, probs)
    for k, piece in enumerate(grads + (motion_out,)):
        out[:, k * width : (k + 1) * width] = piece


def part_of(terms, k):
    width = HEADS * HEAD_DIM
    return jnp.concatenate([t[:, k * width : (k + 1) * width] for t in terms], axis=0)


def back_kernel(dims, quad_ref, *refs):
    nq, nf, fr, pq = dims
    terms, (weights, out) = refs[:nq], refs[nq:]
    order = received_to_rows(quad_ref[0], nq, nf, fr, True)
    grad = None
    for k in range(3):
        product = dot_t(part_of(terms, k), weights[k])
        grad = product if grad is None else grad + product
    delta = dot_t(part_of(terms, 3), weights[3])
    for i, rows in enumerate((grad, delta)):
        rows = dot(order, rows.astype(BF16))
        out[:, i * nq * fr : (i + 1) * nq * fr, :] = rows.reshape(nf, nq * fr, -1).astype(BF16)


def weight_kernel(dims, geo, keep, swapped, weights, pos, gain2, *refs):
    nq, nf, fr, pq = dims
    terms, refs = refs[: 2 * nq], refs[2 * nq :]
    keep_a, send_a, outs_b, (first, second) = refs[0], refs[1], refs[2:-2], refs[-2:]
    _, stage, block, width = first.shape
    quad, core, mid, turn = [geo[i] for i in range(4)]
    normed = jnp.concatenate([keep[0], swapped[0]], axis=0)
    cot = jnp.concatenate([keep[1], swapped[1]], axis=0)
    rows = normed.shape[1]
    grad = None
    for k in range(4):
        right = part_of(terms, k)
        product = t_dot(normed if k < 3 else cot, right)
        blocks = second if k == 3 else first
        for x in range(2):
            for z in range(stage):
                j = x * stage + z
                blocks[x, z] = product[j * block : (j + 1) * block]
        if k < 3:
            back = dot_t(right, weights[k, pl.ds(pl.multiple_of(core * rows, 16), rows), :])
            grad = back if grad is None else grad + back
        if k < 2:
            for r in range(stage):
                z = (turn + r) & (stage - 1)
                keep_a[r, k] = blocks[mid, z].astype(BF16)
                send_a[r, k] = blocks[1 - mid, z].astype(BF16)

    def core_lanes(values):
        values = own_lanes(values, quad, nq)
        return jnp.where(core == 0, values[:, :rows], values[:, rows:])

    table = jnp.concatenate([core_lanes(pos[...])] * (2 * nq), axis=0)
    gain = jnp.sum(grad * (normed.astype(F32) - table), axis=0, keepdims=True)
    gain = gain / core_lanes(row_of(gain2))
    extra = jnp.concatenate([gain, jnp.zeros((1, width - rows), F32)], axis=1)
    extra = jnp.where(iota((8, width), 0) == 0, extra, 0.0)
    for r in range(stage):
        z = (turn + r) & (stage - 1)
        for x, at in enumerate((mid, 1 - mid)):
            rows_out = jnp.concatenate([first[at, z], second[at, z], extra], axis=0)
            outs_b[r][x] = rows_out.astype(BF16)


def middle_kernel(dims, *refs):
    nq, nf, fr, pq = dims
    quad, received, cots = refs[0][0], refs[1 : 1 + nq], refs[1 + nq : 1 + 2 * nq]
    kept, gain2, block_out, grad_out = refs[1 + 2 * nq :]
    own = fr * pq
    order = rows_to_sent(quad, nq, fr, pq, True)

    def lanes(i):
        parts = []
        for r in received:
            parts.append(dot(order, sent_part(r, i, nq * fr)))
        return place_lanes(parts, quad, nq)

    hidden = kept[:, 3 * HEADS * HEAD_DIM :].astype(F32)
    grad_normed, delta = lanes(0), lanes(1)
    block_out[...] = spread(hidden[:own] + delta[:own], block_out)
    unit_two, inv_two = normalize(hidden)
    cot = jnp.concatenate([flat_wide(c) for c in cots], axis=0)
    back = normalize_back(grad_normed, unit_two, inv_two, row_of(gain2))
    grad_out[...] = (cot + back).astype(BF16)


def tail_kernel(dims, grad_hidden, xs, kept, gain1, weights, in_grad):
    nq, nf, fr, pq = dims
    own, width = fr * pq, HEADS * HEAD_DIM
    grad_out = dot(grad_hidden[...], weights[3]).astype(BF16)
    parts = [kept[:, i * width : (i + 1) * width] for i in range(3)] + [grad_out]
    pieces = []
    for group in frame_groups(nq, fr, pq):
        same = same_frame(nq, group[1], pq)
        pieces.append(attend_back(*[pick_group(p, group, nq, fr, pq) for p in parts], same))
    grads = [join_groups([p[i] for p in pieces], nq, fr, pq)[:own] for i in range(3)]
    grad_one = dot_t(grads[0], weights[0]) + dot_t(grads[1], weights[1]) + dot_t(grads[2], weights[2])
    unit_one, inv_one = normalize(flat_wide(xs))
    back = normalize_back(grad_one, unit_one, inv_one, row_of(gain1))
    in_grad[...] = spread(grad_hidden[...][:own].astype(F32) + back, in_grad)


def call(kernel, name, outs, args, vmem, micros, scratch=()):
    in_specs = []
    for arg in args:
        space = pltpu.SMEM if arg.dtype == jnp.int32 else pltpu.VMEM
        in_specs.append(pl.BlockSpec(memory_space=space))
    return list(
        pl.pallas_call(
            kernel,
            out_shape=outs,
            in_specs=in_specs,
            out_specs=[pl.BlockSpec(memory_space=pltpu.VMEM) for _ in outs],
            scratch_shapes=list(scratch),
            compiler_params=pltpu.CompilerParams(vmem_limit_bytes=vmem * 1024 * 1024),
            cost_estimate=pl.CostEstimate(
                flops=int(micros * 1e9), bytes_accessed=2**20, transcendentals=0
            ),
            name=name,
        )(*args)
    )


def after(value, *others):
    return lax.optimization_barrier((value,) + others)[0]


def sds(*shape, dtype=BF16):
    return jax.ShapeDtypeStruct(shape, dtype)


def positional(first, frames, channels):
    frame_pos = (first + lax.broadcasted_iota(jnp.int32, (frames, channels), 0)).astype(F32)
    lane = lax.broadcasted_iota(jnp.int32, (frames, channels), 1)
    freq_index = (lane >> 1).astype(F32)
    phases = frame_pos * jnp.exp(freq_index * (-2.0 * math.log(10000.0) / channels))
    return jnp.sin(phases + (lane & 1).astype(F32) * (0.5 * math.pi))


def local(nq, nf, activations, cotangent, spatial_weights, spatial_gain, motion_weights, motion_gain):
    fr, pq, channels = activations.shape
    dims = (nq, nf, fr, pq)
    width = spatial_weights.shape[-1]
    half = channels // nq
    rows = nq * fr * pq
    tokens = nf * fr
    small = 16 if rows <= 256 else 40
    big = 16 if rows <= 256 else 52
    quad = lax.axis_index("quad")
    frame = lax.axis_index("frame")


    def from_quad(x, s):
        return lax.ppermute(x, "quad", [((d + s) % nq, d) for d in range(nq)])

    def to_quad(x, s):
        return lax.ppermute(x, "quad", [(d, (d + s) % nq) for d in range(nq)])

    def swap(x):
        return lax.all_to_all(x, "frame", split_axis=0, concat_axis=0, tiled=True)

    def run(kernel, name, outs, args, micros, vmem=small, **options):
        kernel = functools.partial(kernel, dims)
        return call(kernel, name, outs, args, vmem, micros, **options)

    def move(x, pairs):
        return lax.ppermute(x, "frame", pairs)

    core, mid, turn = frame % 2, (frame // 2) % 2, frame // 4
    geo = jnp.stack([quad, core, mid, turn]).astype(jnp.int32)
    flip_core = [(g, g ^ 1) for g in range(nf)]
    flip_mid = [(g, g ^ 2) for g in range(nf)]
    ring = [(g, (g + 4) % nf) for g in range(nf)]

    gain1, gain2 = spatial_gain, motion_gain
    sent = sds(nf, nq * fr, half)
    acts = [activations] + [from_quad(activations, s) for s in range(1, nq)]
    both = sds(nf, 2 * nq * fr, half)
    (own_part,) = run(
        order_kernel, "order_cotangent", [sent], [geo, cotangent, spatial_weights], 0.5, big
    )
    cot_later = after(cotangent, acts[-1])
    cots = [cotangent] + [from_quad(cot_later, s) for s in range(1, nq)]
    pos = positional(frame * fr, fr, channels)
    kept, normed = run(
        spatial_kernel,
        "spatial_forward",
        [sds(rows, 3 * width + channels), sent],
        [geo] + acts + [gain1, gain2, pos, spatial_weights],
        3,
        big,
    )
    (send,) = run(join_kernel, "join_sent", [both], [geo, normed, own_part] + cots[1:], 0.5)
    received = swap(send)
    table = positional(after(frame * 0, send), tokens, channels)

    parts = run(
        motion_kernel,
        "motion_projection",
        [sds(tokens, 4 * width, dtype=F32)] + [sds(tokens, 4 * width)] * (nq - 1),
        [geo, after(received, table), motion_weights],
        1.5,
    )
    factors, factors_out = run(
        cut_kernel,
        "cut_factors",
        [sds(2, rows, half // 2)] * 2,
        [geo, after(received, parts[0])],
        0.5,
    )
    factors_in = move(factors_out, flip_core)
    parts = [after(parts[0], factors_in)] + [to_quad(p, s + 1) for s, p in enumerate(parts[1:])]

    (terms,) = run(temporal_kernel, "temporal_attention", [sds(tokens, 4 * width)], parts, 2)
    all_terms = [terms] + [from_quad(terms, s) for s in range(1, nq)]
    swapped = [move(t, flip_core) for t in all_terms]

    stage, block = nf // 4, half // nf
    keep_a, send_a, *parts_b = run(
        weight_kernel,
        "weight_terms",
        [sds(stage, 2, block, width)] * 2 + [sds(2, 2 * block + 8, width)] * stage,
        [geo, factors, factors_in, motion_weights, table, gain2]
        + all_terms
        + swapped,
        3,
        scratch=[pltpu.VMEM((2, stage, block, width), F32)] * 2,
    )

    (back_send,) = run(
        back_kernel,
        "temporal_back_projection",
        [sds(nf, 2 * nq * fr, half)],
        [geo, after(all_terms[0], send_a)] + all_terms[1:] + [motion_weights],
        2,
    )

    def add(a, b):
        return (a.astype(F32) + b.astype(F32)).astype(BF16)

    back_recv = swap(back_send)
    pair_a = add(keep_a, move(send_a, flip_mid))
    total_a = pair_a[stage - 1]
    total_b = add(move(parts_b[stage - 1], ring), parts_b[stage - 2])
    back_recv = after(back_recv, total_a, total_b)
    backs = [back_recv] + [from_quad(back_recv, s) for s in range(1, nq)]
    for step in range(2, stage):
        last = step == stage - 1
        if last:
            total_b = after(total_b, back_recv)
            total_a = after(total_a, back_recv)
        total_a = add(move(total_a, ring), pair_a[stage - step])
        total_b = add(move(total_b, ring), parts_b[stage - 1 - step])
    own_b, give_b = total_b[0], total_b[1]
    backs[0] = after(backs[0], total_a, give_b)
    block_output, grad_hidden = run(
        middle_kernel,
        "block_output_hidden_gradient",
        [sds(fr, pq, channels), sds(rows, channels)],
        [geo] + backs + cots + [kept, gain2],
        1.5,
        big,
    )
    total_a = add(after(move(total_a, ring), grad_hidden), pair_a[0])
    total_b = add(after(move(give_b, flip_mid), grad_hidden), own_b)
    final = []
    for g in range(nf):
        z, x, c = g // 4, (g // 2) % 2, g % 2
        for q in range(nq):
            final.append((g * nq + q, nf * q + c * (nf // 2) + x * stage + z))
    grad_hidden = after(grad_hidden, total_a, total_b)
    total_a, total_b = [lax.ppermute(t, ("frame", "quad"), final) for t in (total_a, total_b)]
    (input_grad,) = run(
        tail_kernel,
        "spatial_backward",
        [sds(fr, pq, channels)],
        [grad_hidden, activations, kept, gain1, spatial_weights],
        3.5,
        big,
    )
    everyone = nf * nq
    factor = 1.0 / math.sqrt(everyone * fr * pq)
    total_b, extra = total_b[: 2 * block], total_b[2 * block]
    weight_grad = jnp.concatenate([total_a, total_b.reshape(total_a.shape)], axis=0)
    weight_grad = weight_grad.astype(F32) * factor
    place = ((frame * nq + quad) % (nf // 2)) * block
    gain_grad = lax.dynamic_slice(extra, (place,), (block,)).astype(F32) * factor
    return block_output, input_grad, weight_grad, gain_grad


def solution(mesh):
    in_specs = (
        P("frame", "quad", None),
        P("frame", "quad", None),
        P(),
        P(),
        P(None, "quad", None),
        P(),
    )
    out_specs = (
        P("frame", "quad", None),
        P("frame", "quad", None),
        P(None, ("frame", "quad"), None),
        P(("frame", "quad")),
    )
    body = functools.partial(local, mesh.shape["quad"], mesh.shape["frame"])
    return jax.shard_map(
        body, mesh=mesh, in_specs=in_specs, out_specs=out_specs, check_vma=False
    )
```

```python
import functools
import math

import jax
import jax.numpy as jnp
from jax import lax
from jax.experimental import pallas as pl
from jax.experimental.pallas import tpu as pltpu
from jax.sharding import PartitionSpec as P

HEADS = 4
HEAD_DIM = 160
EPSILON = 1e-05
SCALE = HEAD_DIM ** (-0.5)
F32 = jnp.float32
BF16 = jnp.bfloat16


def log2(n):
    return int(n).bit_length() - 1


def dot(a, b):
    return jnp.dot(a, b, preferred_element_type=F32)


def dot_t(a, b):
    return lax.dot_general(a, b, (((1,), (1,)), ((), ())), preferred_element_type=F32)


def t_dot(a, b):
    return lax.dot_general(a, b, (((0,), (0,)), ((), ())), preferred_element_type=F32)


def normalize(values):
    average = jnp.mean(values, axis=-1, keepdims=True)
    centred = values - average
    inv_scale = lax.rsqrt(jnp.mean(centred * centred, axis=-1, keepdims=True) + EPSILON)
    return centred * inv_scale, inv_scale


def normalize_back(grad_rows, unit_rows, inv_scale, gain):
    scaled = grad_rows * gain
    first_mean = jnp.mean(scaled, axis=-1, keepdims=True)
    second_mean = jnp.mean(scaled * unit_rows, axis=-1, keepdims=True)
    return inv_scale * (scaled - first_mean - unit_rows * second_mean)


def iota(shape, dim):
    return lax.broadcasted_iota(jnp.int32, shape, dim)


def head_mask(dtype):
    lane = iota((1, HEADS * HEAD_DIM), 1)
    return [
        jnp.where((lane >= h * HEAD_DIM) & (lane < (h + 1) * HEAD_DIM), 1.0, 0.0).astype(dtype)
        for h in range(HEADS)
    ]


def stack_heads(rows):
    return jnp.concatenate([rows * mask for mask in head_mask(rows.dtype)], axis=0)


def fold_heads(stacked):
    rows = stacked.shape[0] // HEADS
    total = None
    for h, mask in enumerate(head_mask(F32)):
        piece = stacked[h * rows : (h + 1) * rows] * mask
        total = piece if total is None else total + piece
    return total


def probabilities(query_stack, keys, same):
    scores = dot_t(query_stack, keys) * SCALE
    if same is not None:
        scores = jnp.where(same, scores, -1e30)
    highest = jnp.max(scores, axis=-1, keepdims=True)
    expo = jnp.exp(scores - highest)
    return expo / jnp.sum(expo, axis=-1, keepdims=True)


def attend(query, keys, values, same):
    probs = probabilities(stack_heads(query), keys, same)
    return fold_heads(dot(probs.astype(BF16), values)).astype(BF16)


def attend_back(query, keys, values, grad, same, probs=None):
    query_stack = stack_heads(query)
    grad_stack = stack_heads(grad)
    if probs is None:
        probs = probabilities(query_stack, keys, same)
    grad_probs = dot_t(grad_stack, values)
    inner = jnp.sum(probs * grad_probs, axis=-1, keepdims=True)
    grad_scores = (probs * (grad_probs - inner) * SCALE).astype(BF16)
    grad_query = fold_heads(dot(grad_scores, keys)).astype(BF16)
    grad_key = t_dot(grad_scores, query_stack).astype(BF16)
    grad_value = t_dot(probs.astype(BF16), grad_stack).astype(BF16)
    return grad_query, grad_key, grad_value


def rows_to_sent(quad, nq, fr, pq, transposed):
    rows = nq * fr * pq
    out_dim = 1 if transposed else 0
    out = iota((rows, rows), out_dim)
    src = iota((rows, rows), 1 - out_dim)
    cell = out >> log2(nq * fr)
    other = (out >> log2(fr)) & (nq - 1)
    frame = out & (fr - 1)
    want = (((other - quad) & (nq - 1)) << log2(fr * pq)) + (frame << log2(pq)) + cell
    return jnp.where(want == src, 1.0, 0.0).astype(BF16)


def received_to_rows(quad, nq, nf, fr, transposed):
    rows = nq * nf * fr
    out_dim = 1 if transposed else 0
    out = iota((rows, rows), out_dim)
    src = iota((rows, rows), 1 - out_dim)
    step = out >> log2(nf * fr)
    device = (out >> log2(fr)) & (nf - 1)
    frame = out & (fr - 1)
    want = (device << log2(nq * fr)) + (((step + quad) & (nq - 1)) << log2(fr)) + frame
    return jnp.where(want == src, 1.0, 0.0).astype(BF16)


def own_lanes(values, quad, nq):
    width = values.shape[1] // nq
    picked = values[:, :width]
    for t in range(1, nq):
        picked = jnp.where(quad == t, values[:, t * width : (t + 1) * width], picked)
    return picked


def place_lanes(parts, quad, nq):
    placed = []
    for t in range(nq):
        piece = parts[t]
        for q in range(1, nq):
            piece = jnp.where(quad == q, parts[(t - q) % nq], piece)
        placed.append(piece)
    return jnp.concatenate(placed, axis=1)


def frame_groups(nq, fr, pq):
    size = max(1, min(fr, 128 // (nq * pq)))
    return [(start, size) for start in range(0, fr, size)]


def pick_group(rows, group, nq, fr, pq):
    start, size = group
    if size == fr:
        return rows
    cut = rows.reshape(nq, fr, pq, rows.shape[-1])[:, start : start + size]
    return cut.reshape(nq * size * pq, rows.shape[-1])


def join_groups(pieces, nq, fr, pq):
    if len(pieces) == 1:
        return pieces[0]
    size = fr // len(pieces)
    width = pieces[0].shape[-1]
    joined = jnp.concatenate([p.reshape(nq, size, pq, width) for p in pieces], axis=1)
    return joined.reshape(nq * fr * pq, width)


def same_frame(nq, size, pq):
    if size == 1:
        return None
    rows = nq * size * pq
    shape = (HEADS * rows, rows)
    left = (iota(shape, 0) >> log2(pq)) & (size - 1)
    right = (iota(shape, 1) >> log2(pq)) & (size - 1)
    return left == right


def row_of(ref):
    return ref[...].reshape(1, -1)


def flat(ref):
    value = ref[...]
    return value.reshape(-1, value.shape[-1])


def flat_wide(ref):
    value = ref[...].astype(F32)
    return value.reshape(-1, value.shape[-1])


def spread(rows, like):
    return rows.reshape(like.shape).astype(like.dtype)


def spatial_kernel(dims, *refs):
    nq, nf, fr, pq = dims
    quad, xs, refs = refs[0][0], refs[1 : 1 + nq], refs[1 + nq :]
    gain1, gain2, pos, weights, kept_out, send_out = refs
    width = HEADS * HEAD_DIM
    wide = jnp.concatenate([flat_wide(x) for x in xs], axis=0)
    unit, _ = normalize(wide)
    normed = (unit * row_of(gain1)).astype(BF16)
    query = dot(normed, weights[0]).astype(BF16)
    keys = dot(normed, weights[1]).astype(BF16)
    values = dot(normed, weights[2]).astype(BF16)
    for i, part in enumerate((query, keys, values)):
        kept_out[:, i * width : (i + 1) * width] = part
    pieces = []
    for group in frame_groups(nq, fr, pq):
        same = same_frame(nq, group[1], pq)
        cut = [pick_group(part, group, nq, fr, pq) for part in (query, keys, values)]
        pieces.append(attend(*cut, same))
    out = join_groups(pieces, nq, fr, pq)
    hidden = (wide + dot_t(out, weights[3])).astype(BF16)
    kept_out[:, 3 * width :] = hidden
    unit_two, _ = normalize(hidden.astype(F32))
    table = jnp.broadcast_to(pos[...][:, None, :], (fr, pq, pos.shape[-1]))
    table = table.reshape(fr * pq, pos.shape[-1])
    table = jnp.concatenate([table] * nq, axis=0)
    normed_two = own_lanes(unit_two * row_of(gain2) + table, quad, nq).astype(BF16)
    send_out[...] = spread(dot(rows_to_sent(quad, nq, fr, pq, False), normed_two), send_out)


def order_kernel(dims, geo, cot, weights, send_out):
    nq, nf, fr, pq = dims
    order = rows_to_sent(geo[0], nq, fr, pq, False)[:, : fr * pq]
    send_out[...] = spread(dot(order, own_lanes(flat(cot), geo[0], nq)), send_out)


def join_kernel(dims, geo, normed, own_part, *refs):
    nq, nf, fr, pq = dims
    cots, send_out = refs[:-1], refs[-1]
    order = rows_to_sent(geo[0], nq, fr, pq, False)[:, fr * pq :]
    rows = own_lanes(jnp.concatenate([flat(c) for c in cots], axis=0), geo[0], nq)
    total = own_part[...].astype(F32) + dot(order, rows).reshape(own_part.shape)
    send_out[:, : nq * fr, :] = normed[...]
    send_out[:, nq * fr :, :] = total.astype(BF16)


def sent_part(received, i, rows):
    part = received[:, i * rows : (i + 1) * rows, :].astype(F32)
    return part.reshape(-1, part.shape[-1]).astype(BF16)


def motion_kernel(dims, geo, received, weights, own_out, *sends):
    nq, nf, fr, pq = dims
    order = received_to_rows(geo[0], nq, nf, fr, False)
    normed, cot = [dot(order, sent_part(received, i, nq * fr)).astype(BF16) for i in range(2)]
    tokens = nf * fr
    for k in range(4):
        width = weights.shape[-1]
        lanes = slice(k * width, (k + 1) * width)
        product = dot(normed if k < 3 else cot, weights[k])
        own_out[:, lanes] = product[:tokens]
        for s, send in enumerate(sends):
            send[:, lanes] = product[(s + 1) * tokens : (s + 2) * tokens].astype(BF16)


def quarter_of(four):
    return ((four & 1) << 1) | (four >> 1)


def quarter_lanes(values, quarter):
    width = values.shape[1] // 4
    picked = values[:, :width]
    for t in range(1, 4):
        picked = jnp.where(quarter == t, values[:, t * width : (t + 1) * width], picked)
    return picked


def cut_kernel(dims, geo, received, *outs):
    nq, nf, fr, pq = dims
    order = received_to_rows(geo[0], nq, nf, fr, False)
    for i in range(2):
        rows = dot(order, sent_part(received, i, nq * fr))
        for d in range(4):
            outs[d][i] = quarter_lanes(rows, quarter_of(geo[1] ^ d)).astype(BF16)


def table_kernel(dims, geo, out):
    shape = out.shape
    lane = iota(shape, 1)
    freq = jnp.exp((lane >> 1).astype(F32) * (-2.0 * math.log(10000.0) / shape[1]))
    turn = (lane & 1).astype(F32) * (0.5 * math.pi)
    out[...] = jnp.sin(iota(shape, 0).astype(F32) * freq + turn)


def temporal_kernel(dims, *refs):
    nq, nf, fr, pq = dims
    parts, out = refs[:nq], refs[nq]
    width = HEADS * HEAD_DIM
    total = parts[0][...]
    for part in parts[1:]:
        total = total + part[...].astype(F32)
    query, keys, values, grad = [
        total[:, k * width : (k + 1) * width].astype(BF16) for k in range(4)
    ]
    probs = probabilities(stack_heads(query), keys, None)
    motion_out = fold_heads(dot(probs.astype(BF16), values)).astype(BF16)
    grads = attend_back(query, keys, values, grad, None, probs)
    for k, piece in enumerate(grads + (motion_out,)):
        out[:, k * width : (k + 1) * width] = piece


def part_of(terms, k):
    width = HEADS * HEAD_DIM
    return jnp.concatenate([t[:, k * width : (k + 1) * width] for t in terms], axis=0)


def back_kernel(dims, quad_ref, *refs):
    nq, nf, fr, pq = dims
    terms, (weights, out) = refs[:nq], refs[nq:]
    order = received_to_rows(quad_ref[0], nq, nf, fr, True)
    grad = None
    for k in range(3):
        product = dot_t(part_of(terms, k), weights[k])
        grad = product if grad is None else grad + product
    delta = dot_t(part_of(terms, 3), weights[3])
    for i, rows in enumerate((grad, delta)):
        rows = dot(order, rows.astype(BF16))
        out[:, i * nq * fr : (i + 1) * nq * fr, :] = rows.reshape(nf, nq * fr, -1).astype(BF16)


def weight_kernel(dims, geo, *refs):
    nq, nf, fr, pq = dims
    factors, (weights, pos, gain2), refs = refs[:4], refs[4:7], refs[7:]
    terms, outs, blocks = refs[: 4 * nq], refs[4 * nq : -1], refs[-1]
    _, stage, block, width = blocks.shape
    quad, quarter, turn = geo[0], quarter_of(geo[1]), geo[2]
    normed = jnp.concatenate([f[0] for f in factors], axis=0)
    cot = jnp.concatenate([f[1] for f in factors], axis=0)
    rows = normed.shape[1]
    grad = None
    for k in range(4):
        right = part_of(terms, k)
        product = t_dot(normed if k < 3 else cot, right)
        for z in range(stage):
            blocks[k, z] = product[z * block : (z + 1) * block]
        if k < 3:
            if rows % 16 == 0:
                own = weights[k, pl.ds(pl.multiple_of(quarter * rows, 16), rows), :]
            else:
                wide = weights[k].astype(F32)
                own = wide[:rows]
                for t in range(1, 4):
                    own = jnp.where(quarter == t, wide[t * rows : (t + 1) * rows], own)
                own = own.astype(BF16)
            back = dot_t(right, own)
            grad = back if grad is None else grad + back
    table = quarter_lanes(own_lanes(pos[...], quad, nq), quarter)
    table = jnp.concatenate([table] * (4 * nq), axis=0)
    gain = jnp.sum(grad * (normed.astype(F32) - table), axis=0, keepdims=True)
    gain = gain / quarter_lanes(own_lanes(row_of(gain2), quad, nq), quarter)
    extra = jnp.concatenate([gain, jnp.zeros((1, width - rows), F32)], axis=1)
    extra = jnp.where(iota((8, width), 0) == 0, extra, 0.0)
    for r in range(stage):
        z = (turn + r) & (stage - 1)
        rows_out = jnp.concatenate([blocks[k, z] for k in range(4)] + [extra], axis=0)
        outs[r][...] = rows_out.astype(BF16)


def middle_kernel(dims, *refs):
    nq, nf, fr, pq = dims
    quad, received, cots = refs[0][0], refs[1 : 1 + nq], refs[1 + nq : 1 + 2 * nq]
    kept, gain2, block_out, grad_out = refs[1 + 2 * nq :]
    own = fr * pq
    order = rows_to_sent(quad, nq, fr, pq, True)

    def lanes(i):
        parts = []
        for r in received:
            parts.append(dot(order, sent_part(r, i, nq * fr)))
        return place_lanes(parts, quad, nq)

    hidden = kept[:, 3 * HEADS * HEAD_DIM :].astype(F32)
    grad_normed, delta = lanes(0), lanes(1)
    block_out[...] = spread(hidden[:own] + delta[:own], block_out)
    unit_two, inv_two = normalize(hidden)
    cot = jnp.concatenate([flat_wide(c) for c in cots], axis=0)
    back = normalize_back(grad_normed, unit_two, inv_two, row_of(gain2))
    grad_out[...] = (cot + back).astype(BF16)


def tail_kernel(dims, grad_hidden, xs, kept, gain1, weights, in_grad):
    nq, nf, fr, pq = dims
    own, width = fr * pq, HEADS * HEAD_DIM
    grad_out = dot(grad_hidden[...], weights[3]).astype(BF16)
    parts = [kept[:, i * width : (i + 1) * width] for i in range(3)] + [grad_out]
    pieces = []
    for group in frame_groups(nq, fr, pq):
        same = same_frame(nq, group[1], pq)
        pieces.append(attend_back(*[pick_group(p, group, nq, fr, pq) for p in parts], same))
    grads = [join_groups([p[i] for p in pieces], nq, fr, pq)[:own] for i in range(3)]
    grad_one = dot_t(grads[0], weights[0]) + dot_t(grads[1], weights[1]) + dot_t(grads[2], weights[2])
    unit_one, inv_one = normalize(flat_wide(xs))
    back = normalize_back(grad_one, unit_one, inv_one, row_of(gain1))
    in_grad[...] = spread(grad_hidden[...][:own].astype(F32) + back, in_grad)


def call(kernel, name, outs, args, vmem, micros, scratch=()):
    in_specs = []
    for arg in args:
        space = pltpu.SMEM if arg.dtype == jnp.int32 else pltpu.VMEM
        in_specs.append(pl.BlockSpec(memory_space=space))
    return list(
        pl.pallas_call(
            kernel,
            out_shape=outs,
            in_specs=in_specs,
            out_specs=[pl.BlockSpec(memory_space=pltpu.VMEM) for _ in outs],
            scratch_shapes=list(scratch),
            compiler_params=pltpu.CompilerParams(vmem_limit_bytes=vmem * 1024 * 1024),
            cost_estimate=pl.CostEstimate(
                flops=int(micros * 1e9), bytes_accessed=2**20, transcendentals=0
            ),
            name=name,
        )(*args)
    )


def after(value, *others):
    return lax.optimization_barrier((value,) + others)[0]


def sds(*shape, dtype=BF16):
    return jax.ShapeDtypeStruct(shape, dtype)


def positional(first, frames, channels):
    frame_pos = (first + lax.broadcasted_iota(jnp.int32, (frames, channels), 0)).astype(F32)
    lane = lax.broadcasted_iota(jnp.int32, (frames, channels), 1)
    freq_index = (lane >> 1).astype(F32)
    phases = frame_pos * jnp.exp(freq_index * (-2.0 * math.log(10000.0) / channels))
    return jnp.sin(phases + (lane & 1).astype(F32) * (0.5 * math.pi))


def local(nq, nf, activations, cotangent, spatial_weights, spatial_gain, motion_weights, motion_gain):
    fr, pq, channels = activations.shape
    dims = (nq, nf, fr, pq)
    width = spatial_weights.shape[-1]
    half = channels // nq
    rows = nq * fr * pq
    tokens = nf * fr
    small = 16 if rows <= 256 else 40
    big = 16 if rows <= 256 else 52
    quad = lax.axis_index("quad")
    frame = lax.axis_index("frame")


    def from_quad(x, s):
        return lax.ppermute(x, "quad", [((d + s) % nq, d) for d in range(nq)])

    def to_quad(x, s):
        return lax.ppermute(x, "quad", [(d, (d + s) % nq) for d in range(nq)])

    def swap(x):
        return lax.all_to_all(x, "frame", split_axis=0, concat_axis=0, tiled=True)

    def run(kernel, name, outs, args, micros, vmem=small, **options):
        kernel = functools.partial(kernel, dims)
        return call(kernel, name, outs, args, vmem, micros, **options)

    def move(x, pairs):
        return lax.ppermute(x, "frame", pairs)

    geo = jnp.stack([quad, frame % 4, frame // 4]).astype(jnp.int32)

    def flipped(bits):
        return [(g, g ^ bits) for g in range(nf)]

    ring = [(g, (g + 4) % nf) for g in range(nf)]

    gain1, gain2 = spatial_gain, motion_gain
    sent = sds(nf, nq * fr, half)
    acts = [activations] + [from_quad(activations, s) for s in range(1, nq)]
    both = sds(nf, 2 * nq * fr, half)
    (own_part,) = run(
        order_kernel, "order_cotangent", [sent], [geo, cotangent, spatial_weights], 0.5, big
    )
    cot_later = after(cotangent, acts[-1])
    cots = [cotangent] + [from_quad(cot_later, s) for s in range(1, nq)]
    pos = positional(frame * fr, fr, channels)
    kept, normed = run(
        spatial_kernel,
        "spatial_forward",
        [sds(rows, 3 * width + channels), sent],
        [geo] + acts + [gain1, gain2, pos, spatial_weights],
        3,
        big,
    )
    (send,) = run(join_kernel, "join_sent", [both], [geo, normed, own_part] + cots[1:], 0.5)
    received = swap(send)
    (table,) = run(
        table_kernel,
        "positional_table",
        [sds(tokens, channels, dtype=F32)],
        [after(geo, send)],
        5,
    )

    parts = run(
        motion_kernel,
        "motion_projection",
        [sds(tokens, 4 * width, dtype=F32)] + [sds(tokens, 4 * width)] * (nq - 1),
        [geo, after(received, table), motion_weights],
        1.5,
    )
    factors = run(
        cut_kernel,
        "cut_factors",
        [sds(2, rows, half // 4)] * 4,
        [geo, after(received, parts[0])],
        0.5,
    )
    factors = [factors[0]] + [move(factors[d], flipped(d)) for d in range(1, 4)]
    parts = [after(parts[0], *factors)] + [to_quad(p, s + 1) for s, p in enumerate(parts[1:])]

    (terms,) = run(temporal_kernel, "temporal_attention", [sds(tokens, 4 * width)], parts, 2)
    all_terms = [terms] + [from_quad(terms, s) for s in range(1, nq)]
    pair_terms = [move(t, flipped(2)) for t in all_terms]
    core_terms = [move(t, flipped(1)) for t in all_terms]
    last_terms = [move(t, flipped(1)) for t in pair_terms]

    (back_send,) = run(
        back_kernel,
        "temporal_back_projection",
        [sds(nf, 2 * nq * fr, half)],
        [geo] + all_terms + [motion_weights],
        3,
    )
    stage, block = nf // 4, half // nf
    parts_w = run(
        weight_kernel,
        "weight_terms",
        [sds(4 * block + 8, width)] * stage,
        [geo, after(factors[0], back_send)]
        + factors[1:]
        + [motion_weights, table, gain2]
        + all_terms
        + core_terms
        + pair_terms
        + last_terms,
        3,
        scratch=[pltpu.VMEM((4, stage, block, width), F32)],
    )

    def add(a, b):
        return (a.astype(F32) + b.astype(F32)).astype(BF16)

    back_recv = swap(back_send)
    backs = [back_recv] + [from_quad(back_recv, s) for s in range(1, nq)]
    block_output, grad_hidden = run(
        middle_kernel,
        "block_output_hidden_gradient",
        [sds(fr, pq, channels), sds(rows, channels)],
        [geo] + backs + cots + [kept, gain2],
        6,
        big,
    )
    total = parts_w[stage - 1]
    for step in range(1, stage):
        if step == stage - 2:
            total = after(total, back_recv)
        moved = move(total, ring)
        if step == stage - 1:
            moved = after(moved, grad_hidden)
        total = add(moved, parts_w[stage - 1 - step])
    final = []
    for g in range(nf):
        for q in range(nq):
            j = quarter_of(g % 4) * stage + g // 4
            final.append((g * nq + q, nf * q + j))
    grad_hidden = after(grad_hidden, total)
    total = lax.ppermute(total, ("frame", "quad"), final)
    (input_grad,) = run(
        tail_kernel,
        "spatial_backward",
        [sds(fr, pq, channels)],
        [grad_hidden, activations, kept, gain1, spatial_weights],
        3.5,
        big,
    )
    everyone = nf * nq
    factor = 1.0 / math.sqrt(everyone * fr * pq)
    weight_grad = total[: 4 * block].reshape(4, block, width).astype(F32) * factor
    place = ((frame * nq + quad) % stage) * block
    gain_grad = lax.dynamic_slice(total[4 * block], (place,), (block,)).astype(F32) * factor
    return block_output, input_grad, weight_grad, gain_grad


def solution(mesh):
    in_specs = (
        P("frame", "quad", None),
        P("frame", "quad", None),
        P(),
        P(),
        P(None, "quad", None),
        P(),
    )
    out_specs = (
        P("frame", "quad", None),
        P("frame", "quad", None),
        P(None, ("frame", "quad"), None),
        P(("frame", "quad")),
    )
    body = functools.partial(local, mesh.shape["quad"], mesh.shape["frame"])
    return jax.shard_map(
        body, mesh=mesh, in_specs=in_specs, out_specs=out_specs, check_vma=False
    )
```

```python
import functools
import math

import jax
import jax.numpy as jnp
from jax import lax
from jax.experimental import pallas as pl
from jax.experimental.pallas import tpu as pltpu
from jax.sharding import PartitionSpec as P

HEADS = 4
HEAD_DIM = 160
EPSILON = 1e-05
SCALE = HEAD_DIM ** (-0.5)
F32 = jnp.float32
BF16 = jnp.bfloat16


def log2(n):
    return int(n).bit_length() - 1


def dot(a, b):
    return jnp.dot(a, b, preferred_element_type=F32)


def dot_t(a, b):
    return lax.dot_general(a, b, (((1,), (1,)), ((), ())), preferred_element_type=F32)


def t_dot(a, b):
    return lax.dot_general(a, b, (((0,), (0,)), ((), ())), preferred_element_type=F32)


def normalize(values):
    average = jnp.mean(values, axis=-1, keepdims=True)
    centred = values - average
    inv_scale = lax.rsqrt(jnp.mean(centred * centred, axis=-1, keepdims=True) + EPSILON)
    return centred * inv_scale, inv_scale


def normalize_back(grad_rows, unit_rows, inv_scale, gain):
    scaled = grad_rows * gain
    first_mean = jnp.mean(scaled, axis=-1, keepdims=True)
    second_mean = jnp.mean(scaled * unit_rows, axis=-1, keepdims=True)
    return inv_scale * (scaled - first_mean - unit_rows * second_mean)


def iota(shape, dim):
    return lax.broadcasted_iota(jnp.int32, shape, dim)


def head_mask(dtype):
    lane = iota((1, HEADS * HEAD_DIM), 1)
    return [
        jnp.where((lane >= h * HEAD_DIM) & (lane < (h + 1) * HEAD_DIM), 1.0, 0.0).astype(dtype)
        for h in range(HEADS)
    ]


def stack_heads(rows):
    return jnp.concatenate([rows * mask for mask in head_mask(rows.dtype)], axis=0)


def fold_heads(stacked):
    rows = stacked.shape[0] // HEADS
    total = None
    for h, mask in enumerate(head_mask(F32)):
        piece = stacked[h * rows : (h + 1) * rows] * mask
        total = piece if total is None else total + piece
    return total


def probabilities(query_stack, keys, same):
    scores = dot_t(query_stack, keys) * SCALE
    if same is not None:
        scores = jnp.where(same, scores, -1e30)
    highest = jnp.max(scores, axis=-1, keepdims=True)
    expo = jnp.exp(scores - highest)
    return expo / jnp.sum(expo, axis=-1, keepdims=True)


def attend(query, keys, values, same):
    probs = probabilities(stack_heads(query), keys, same)
    return fold_heads(dot(probs.astype(BF16), values)).astype(BF16)


def attend_back(query, keys, values, grad, same, probs=None):
    query_stack = stack_heads(query)
    grad_stack = stack_heads(grad)
    if probs is None:
        probs = probabilities(query_stack, keys, same)
    grad_probs = dot_t(grad_stack, values)
    inner = jnp.sum(probs * grad_probs, axis=-1, keepdims=True)
    grad_scores = (probs * (grad_probs - inner) * SCALE).astype(BF16)
    grad_query = fold_heads(dot(grad_scores, keys)).astype(BF16)
    grad_key = t_dot(grad_scores, query_stack).astype(BF16)
    grad_value = t_dot(probs.astype(BF16), grad_stack).astype(BF16)
    return grad_query, grad_key, grad_value


def rows_to_sent(quad, nq, fr, pq, transposed):
    rows = nq * fr * pq
    out_dim = 1 if transposed else 0
    out = iota((rows, rows), out_dim)
    src = iota((rows, rows), 1 - out_dim)
    cell = out >> log2(nq * fr)
    other = (out >> log2(fr)) & (nq - 1)
    frame = out & (fr - 1)
    want = (((other - quad) & (nq - 1)) << log2(fr * pq)) + (frame << log2(pq)) + cell
    return jnp.where(want == src, 1.0, 0.0).astype(BF16)


def received_to_rows(quad, nq, nf, fr, transposed):
    rows = nq * nf * fr
    out_dim = 1 if transposed else 0
    out = iota((rows, rows), out_dim)
    src = iota((rows, rows), 1 - out_dim)
    step = out >> log2(nf * fr)
    device = (out >> log2(fr)) & (nf - 1)
    frame = out & (fr - 1)
    want = (device << log2(nq * fr)) + (((step + quad) & (nq - 1)) << log2(fr)) + frame
    return jnp.where(want == src, 1.0, 0.0).astype(BF16)


def own_lanes(values, quad, nq):
    width = values.shape[1] // nq
    picked = values[:, :width]
    for t in range(1, nq):
        picked = jnp.where(quad == t, values[:, t * width : (t + 1) * width], picked)
    return picked


def place_lanes(parts, quad, nq):
    placed = []
    for t in range(nq):
        piece = parts[t]
        for q in range(1, nq):
            piece = jnp.where(quad == q, parts[(t - q) % nq], piece)
        placed.append(piece)
    return jnp.concatenate(placed, axis=1)


def frame_groups(nq, fr, pq):
    size = max(1, min(fr, 128 // (nq * pq)))
    return [(start, size) for start in range(0, fr, size)]


def pick_group(rows, group, nq, fr, pq):
    start, size = group
    if size == fr:
        return rows
    cut = rows.reshape(nq, fr, pq, rows.shape[-1])[:, start : start + size]
    return cut.reshape(nq * size * pq, rows.shape[-1])


def join_groups(pieces, nq, fr, pq):
    if len(pieces) == 1:
        return pieces[0]
    size = fr // len(pieces)
    width = pieces[0].shape[-1]
    joined = jnp.concatenate([p.reshape(nq, size, pq, width) for p in pieces], axis=1)
    return joined.reshape(nq * fr * pq, width)


def same_frame(nq, size, pq):
    if size == 1:
        return None
    rows = nq * size * pq
    shape = (HEADS * rows, rows)
    left = (iota(shape, 0) >> log2(pq)) & (size - 1)
    right = (iota(shape, 1) >> log2(pq)) & (size - 1)
    return left == right


def row_of(ref):
    return ref[...].reshape(1, -1)


def flat(ref):
    value = ref[...]
    return value.reshape(-1, value.shape[-1])


def flat_wide(ref):
    value = ref[...].astype(F32)
    return value.reshape(-1, value.shape[-1])


def spread(rows, like):
    return rows.reshape(like.shape).astype(like.dtype)


def spatial_kernel(dims, *refs):
    nq, nf, fr, pq = dims
    quad, xs, refs = refs[0][0], refs[1 : 1 + nq], refs[1 + nq :]
    gain1, gain2, pos, weights, kept_out, send_out = refs
    width = HEADS * HEAD_DIM
    wide = jnp.concatenate([flat_wide(x) for x in xs], axis=0)
    unit, _ = normalize(wide)
    normed = (unit * row_of(gain1)).astype(BF16)
    query = dot(normed, weights[0]).astype(BF16)
    keys = dot(normed, weights[1]).astype(BF16)
    values = dot(normed, weights[2]).astype(BF16)
    for i, part in enumerate((query, keys, values)):
        kept_out[:, i * width : (i + 1) * width] = part
    pieces = []
    for group in frame_groups(nq, fr, pq):
        same = same_frame(nq, group[1], pq)
        cut = [pick_group(part, group, nq, fr, pq) for part in (query, keys, values)]
        pieces.append(attend(*cut, same))
    out = join_groups(pieces, nq, fr, pq)
    hidden = (wide + dot_t(out, weights[3])).astype(BF16)
    kept_out[:, 3 * width :] = hidden
    unit_two, _ = normalize(hidden.astype(F32))
    table = jnp.broadcast_to(pos[...][:, None, :], (fr, pq, pos.shape[-1]))
    table = table.reshape(fr * pq, pos.shape[-1])
    table = jnp.concatenate([table] * nq, axis=0)
    normed_two = own_lanes(unit_two * row_of(gain2) + table, quad, nq).astype(BF16)
    send_out[...] = spread(dot(rows_to_sent(quad, nq, fr, pq, False), normed_two), send_out)


def order_kernel(dims, geo, cot, weights, send_out):
    nq, nf, fr, pq = dims
    order = rows_to_sent(geo[0], nq, fr, pq, False)[:, : fr * pq]
    send_out[...] = spread(dot(order, own_lanes(flat(cot), geo[0], nq)), send_out)


def join_kernel(dims, geo, normed, own_part, *refs):
    nq, nf, fr, pq = dims
    cots, send_out = refs[:-1], refs[-1]
    order = rows_to_sent(geo[0], nq, fr, pq, False)[:, fr * pq :]
    rows = own_lanes(jnp.concatenate([flat(c) for c in cots], axis=0), geo[0], nq)
    total = own_part[...].astype(F32) + dot(order, rows).reshape(own_part.shape)
    send_out[:, : nq * fr, :] = normed[...]
    send_out[:, nq * fr :, :] = total.astype(BF16)


def sent_part(received, i, rows):
    part = received[:, i * rows : (i + 1) * rows, :].astype(F32)
    return part.reshape(-1, part.shape[-1]).astype(BF16)


def motion_kernel(dims, geo, received, weights, own_out, *sends):
    nq, nf, fr, pq = dims
    order = received_to_rows(geo[0], nq, nf, fr, False)
    normed, cot = [dot(order, sent_part(received, i, nq * fr)).astype(BF16) for i in range(2)]
    tokens = nf * fr
    for k in range(4):
        width = weights.shape[-1]
        lanes = slice(k * width, (k + 1) * width)
        product = dot(normed if k < 3 else cot, weights[k])
        own_out[:, lanes] = product[:tokens]
        for s, send in enumerate(sends):
            send[:, lanes] = product[(s + 1) * tokens : (s + 2) * tokens].astype(BF16)


def quarter_of(four):
    return ((four & 1) << 1) | (four >> 1)


def quarter_lanes(values, quarter):
    width = values.shape[1] // 4
    picked = values[:, :width]
    for t in range(1, 4):
        picked = jnp.where(quarter == t, values[:, t * width : (t + 1) * width], picked)
    return picked


def cut_kernel(dims, geo, received, *outs):
    nq, nf, fr, pq = dims
    order = received_to_rows(geo[0], nq, nf, fr, False)
    for i in range(2):
        rows = dot(order, sent_part(received, i, nq * fr))
        for d in range(4):
            outs[d][i] = quarter_lanes(rows, quarter_of(geo[1] ^ d)).astype(BF16)


def table_kernel(dims, geo, weights, out):
    shape = out.shape
    lane = iota(shape, 1)
    freq = jnp.exp((lane >> 1).astype(F32) * (-2.0 * math.log(10000.0) / shape[1]))
    turn = (lane & 1).astype(F32) * (0.5 * math.pi)
    out[...] = jnp.sin(iota(shape, 0).astype(F32) * freq + turn)


def temporal_kernel(dims, *refs):
    nq, nf, fr, pq = dims
    parts, out = refs[:nq], refs[nq]
    width = HEADS * HEAD_DIM
    total = parts[0][...]
    for part in parts[1:]:
        total = total + part[...].astype(F32)
    query, keys, values, grad = [
        total[:, k * width : (k + 1) * width].astype(BF16) for k in range(4)
    ]
    probs = probabilities(stack_heads(query), keys, None)
    motion_out = fold_heads(dot(probs.astype(BF16), values)).astype(BF16)
    grads = attend_back(query, keys, values, grad, None, probs)
    for k, piece in enumerate(grads + (motion_out,)):
        out[:, k * width : (k + 1) * width] = piece


def part_of(terms, k):
    width = HEADS * HEAD_DIM
    return jnp.concatenate([t[:, k * width : (k + 1) * width] for t in terms], axis=0)


def back_kernel(dims, quad_ref, *refs):
    nq, nf, fr, pq = dims
    terms, (weights, out) = refs[:nq], refs[nq:]
    order = received_to_rows(quad_ref[0], nq, nf, fr, True)
    grad = None
    for k in range(3):
        product = dot_t(part_of(terms, k), weights[k])
        grad = product if grad is None else grad + product
    delta = dot_t(part_of(terms, 3), weights[3])
    for i, rows in enumerate((grad, delta)):
        rows = dot(order, rows.astype(BF16))
        out[:, i * nq * fr : (i + 1) * nq * fr, :] = rows.reshape(nf, nq * fr, -1).astype(BF16)


def weight_kernel(dims, geo, *refs):
    nq, nf, fr, pq = dims
    factors, (weights, pos, gain2), refs = refs[:4], refs[4:7], refs[7:]
    terms, outs, blocks = refs[: 4 * nq], refs[4 * nq : -1], refs[-1]
    _, stage, block, width = blocks.shape
    quad, quarter, turn = geo[0], quarter_of(geo[1]), geo[2]
    normed = jnp.concatenate([f[0] for f in factors], axis=0)
    cot = jnp.concatenate([f[1] for f in factors], axis=0)
    rows = normed.shape[1]
    grad = None
    for k in range(4):
        right = part_of(terms, k)
        product = t_dot(normed if k < 3 else cot, right)
        for z in range(stage):
            blocks[k, z] = product[z * block : (z + 1) * block]
        if k < 3:
            if rows % 16 == 0:
                own = weights[k, pl.ds(pl.multiple_of(quarter * rows, 16), rows), :]
            else:
                wide = weights[k].astype(F32)
                own = wide[:rows]
                for t in range(1, 4):
                    own = jnp.where(quarter == t, wide[t * rows : (t + 1) * rows], own)
                own = own.astype(BF16)
            back = dot_t(right, own)
            grad = back if grad is None else grad + back
    table = quarter_lanes(own_lanes(pos[...], quad, nq), quarter)
    table = jnp.concatenate([table] * (4 * nq), axis=0)
    gain = jnp.sum(grad * (normed.astype(F32) - table), axis=0, keepdims=True)
    gain = gain / quarter_lanes(own_lanes(row_of(gain2), quad, nq), quarter)
    extra = jnp.concatenate([gain, jnp.zeros((1, width - rows), F32)], axis=1)
    extra = jnp.where(iota((8, width), 0) == 0, extra, 0.0)
    for r in range(stage):
        z = (turn + r) & (stage - 1)
        rows_out = jnp.concatenate([blocks[k, z] for k in range(4)] + [extra], axis=0)
        outs[r][...] = rows_out.astype(BF16)


def middle_kernel(dims, *refs):
    nq, nf, fr, pq = dims
    quad, received, cots = refs[0][0], refs[1 : 1 + nq], refs[1 + nq : 1 + 2 * nq]
    kept, gain2, block_out, grad_out = refs[1 + 2 * nq :]
    own = fr * pq
    order = rows_to_sent(quad, nq, fr, pq, True)

    def lanes(i):
        parts = []
        for r in received:
            parts.append(dot(order, sent_part(r, i, nq * fr)))
        return place_lanes(parts, quad, nq)

    hidden = kept[:, 3 * HEADS * HEAD_DIM :].astype(F32)
    grad_normed, delta = lanes(0), lanes(1)
    block_out[...] = spread(hidden[:own] + delta[:own], block_out)
    unit_two, inv_two = normalize(hidden)
    cot = jnp.concatenate([flat_wide(c) for c in cots], axis=0)
    back = normalize_back(grad_normed, unit_two, inv_two, row_of(gain2))
    grad_out[...] = (cot + back).astype(BF16)


def tail_kernel(dims, grad_hidden, xs, kept, gain1, weights, in_grad):
    nq, nf, fr, pq = dims
    own, width = fr * pq, HEADS * HEAD_DIM
    grad_out = dot(grad_hidden[...], weights[3]).astype(BF16)
    parts = [kept[:, i * width : (i + 1) * width] for i in range(3)] + [grad_out]
    pieces = []
    for group in frame_groups(nq, fr, pq):
        same = same_frame(nq, group[1], pq)
        pieces.append(attend_back(*[pick_group(p, group, nq, fr, pq) for p in parts], same))
    grads = [join_groups([p[i] for p in pieces], nq, fr, pq)[:own] for i in range(3)]
    grad_one = dot_t(grads[0], weights[0]) + dot_t(grads[1], weights[1]) + dot_t(grads[2], weights[2])
    unit_one, inv_one = normalize(flat_wide(xs))
    back = normalize_back(grad_one, unit_one, inv_one, row_of(gain1))
    in_grad[...] = spread(grad_hidden[...][:own].astype(F32) + back, in_grad)


class Far:
    def __init__(self, hbm, vmem, sem):
        self.vmem, self.shape, self.dtype = vmem, vmem.shape, vmem.dtype
        self.copy = pltpu.make_async_copy(hbm, vmem, sem.at[0])
        self.copy.start()
        self.waiting = True

    def wait(self):
        if self.waiting:
            self.copy.wait()
            self.waiting = False

    def __getitem__(self, key):
        self.wait()
        return self.vmem[key]


def call(kernel, name, outs, args, vmem, micros, scratch=(), far=()):
    in_specs, fetched = [], []
    for i, arg in enumerate(args):
        space = pltpu.SMEM if arg.dtype == jnp.int32 else pltpu.VMEM
        in_specs.append(pl.BlockSpec(memory_space=pl.ANY if i in far else space))
    for i in far:
        fetched += [pltpu.VMEM(args[i].shape, args[i].dtype), pltpu.SemaphoreType.DMA((1,))]

    def body(*refs):
        refs = list(refs)
        first = len(args) + len(outs) + len(scratch)
        extra = refs[first:]
        for n, i in enumerate(far):
            refs[i] = Far(refs[i], extra[2 * n], extra[2 * n + 1])
        kernel(*refs[:first])
        for i in far:
            refs[i].wait()

    return list(
        pl.pallas_call(
            body,
            out_shape=outs,
            in_specs=in_specs,
            out_specs=[pl.BlockSpec(memory_space=pltpu.VMEM) for _ in outs],
            scratch_shapes=list(scratch) + fetched,
            compiler_params=pltpu.CompilerParams(vmem_limit_bytes=vmem * 1024 * 1024),
            cost_estimate=pl.CostEstimate(
                flops=int(micros * 1e9), bytes_accessed=2**20, transcendentals=0
            ),
            name=name,
        )(*args)
    )


def after(value, *others):
    return lax.optimization_barrier((value,) + others)[0]


def sds(*shape, dtype=BF16):
    return jax.ShapeDtypeStruct(shape, dtype)


def positional(first, frames, channels):
    frame_pos = (first + lax.broadcasted_iota(jnp.int32, (frames, channels), 0)).astype(F32)
    lane = lax.broadcasted_iota(jnp.int32, (frames, channels), 1)
    freq_index = (lane >> 1).astype(F32)
    phases = frame_pos * jnp.exp(freq_index * (-2.0 * math.log(10000.0) / channels))
    return jnp.sin(phases + (lane & 1).astype(F32) * (0.5 * math.pi))


def local(nq, nf, activations, cotangent, spatial_weights, spatial_gain, motion_weights, motion_gain):
    fr, pq, channels = activations.shape
    dims = (nq, nf, fr, pq)
    width = spatial_weights.shape[-1]
    half = channels // nq
    rows = nq * fr * pq
    tokens = nf * fr
    small = 16 if rows <= 256 else 40
    big = 16 if rows <= 256 else 52
    quad = lax.axis_index("quad")
    frame = lax.axis_index("frame")


    def from_quad(x, s):
        return lax.ppermute(x, "quad", [((d + s) % nq, d) for d in range(nq)])

    def to_quad(x, s):
        return lax.ppermute(x, "quad", [(d, (d + s) % nq) for d in range(nq)])

    def swap(x):
        return lax.all_to_all(x, "frame", split_axis=0, concat_axis=0, tiled=True)

    def run(kernel, name, outs, args, micros, vmem=small, **options):
        kernel = functools.partial(kernel, dims)
        return call(kernel, name, outs, args, vmem, micros, **options)

    def move(x, pairs):
        return lax.ppermute(x, "frame", pairs)

    geo = jnp.stack([quad, frame % 4, frame // 4]).astype(jnp.int32)

    def flipped(bits):
        return [(g, g ^ bits) for g in range(nf)]

    ring = [(g, (g + 4) % nf) for g in range(nf)]

    gain1, gain2 = spatial_gain, motion_gain
    sent = sds(nf, nq * fr, half)
    acts = [activations] + [from_quad(activations, s) for s in range(1, nq)]
    both = sds(nf, 2 * nq * fr, half)
    (own_part,) = run(
        order_kernel, "order_cotangent", [sent], [geo, cotangent, spatial_weights], 0.5, big
    )
    cot_later = after(cotangent, acts[-1])
    cots = [cotangent] + [from_quad(cot_later, s) for s in range(1, nq)]
    pos = positional(frame * fr, fr, channels)
    kept, normed = run(
        spatial_kernel,
        "spatial_forward",
        [sds(rows, 3 * width + channels), sent],
        [geo] + acts + [gain1, gain2, pos, spatial_weights],
        3,
        big,
    )
    (send,) = run(join_kernel, "join_sent", [both], [geo, normed, own_part] + cots[1:], 0.5)
    received = swap(send)
    (table,) = run(
        table_kernel,
        "positional_table",
        [sds(tokens, channels, dtype=F32)],
        [after(geo, send), motion_weights],
        5,
    )

    parts = run(
        motion_kernel,
        "motion_projection",
        [sds(tokens, 4 * width, dtype=F32)] + [sds(tokens, 4 * width)] * (nq - 1),
        [geo, after(received, table), motion_weights],
        1.5,
    )
    factors = run(
        cut_kernel,
        "cut_factors",
        [sds(2, rows, half // 4)] * 4,
        [geo, after(received, parts[0])],
        0.5,
    )
    factors = [factors[0]] + [move(factors[d], flipped(d)) for d in range(1, 4)]
    parts = [after(parts[0], factors[0])] + [to_quad(p, s + 1) for s, p in enumerate(parts[1:])]

    (terms,) = run(temporal_kernel, "temporal_attention", [sds(tokens, 4 * width)], parts, 2)
    terms = after(terms, *factors)
    all_terms = [terms] + [from_quad(terms, s) for s in range(1, nq)]
    pair_terms = [move(t, flipped(2)) for t in all_terms]
    core_terms = [move(t, flipped(1)) for t in all_terms]
    (back_send,) = run(
        back_kernel,
        "temporal_back_projection",
        [sds(nf, 2 * nq * fr, half)],
        [geo] + all_terms + [motion_weights],
        3,
    )
    last_terms = [move(after(t, back_send), flipped(1)) for t in pair_terms]
    stage, block = nf // 4, half // nf
    parts_w = run(
        weight_kernel,
        "weight_terms",
        [sds(4 * block + 8, width)] * stage,
        [geo, after(factors[0], back_send)]
        + factors[1:]
        + [motion_weights, table, gain2]
        + all_terms
        + core_terms
        + pair_terms
        + last_terms,
        3,
        62,
        scratch=[pltpu.VMEM((4, stage, block, width), F32)],
        far=[1, 2, 3, 4] + list(range(8, 8 + 4 * nq)) + [5, 6],
    )

    def add(a, b):
        return (a.astype(F32) + b.astype(F32)).astype(BF16)

    back_recv = swap(back_send)
    backs = [back_recv] + [from_quad(back_recv, s) for s in range(1, nq)]
    block_output, grad_hidden = run(
        middle_kernel,
        "block_output_hidden_gradient",
        [sds(fr, pq, channels), sds(rows, channels)],
        [geo] + backs + cots + [kept, gain2],
        6,
        big,
    )
    total = parts_w[stage - 1]
    for step in range(1, stage):
        if step == stage - 2:
            total = after(total, back_recv)
        moved = move(total, ring)
        if step == stage - 1:
            moved = after(moved, grad_hidden)
        total = add(moved, parts_w[stage - 1 - step])
    final = []
    for g in range(nf):
        for q in range(nq):
            j = quarter_of(g % 4) * stage + g // 4
            final.append((g * nq + q, nf * q + j))
    grad_hidden = after(grad_hidden, total)
    total = lax.ppermute(total, ("frame", "quad"), final)
    (input_grad,) = run(
        tail_kernel,
        "spatial_backward",
        [sds(fr, pq, channels)],
        [grad_hidden, activations, kept, gain1, spatial_weights],
        3.5,
        big,
    )
    everyone = nf * nq
    factor = 1.0 / math.sqrt(everyone * fr * pq)
    weight_grad = total[: 4 * block].reshape(4, block, width).astype(F32) * factor
    place = ((frame * nq + quad) % stage) * block
    gain_grad = lax.dynamic_slice(total[4 * block], (place,), (block,)).astype(F32) * factor
    return block_output, input_grad, weight_grad, gain_grad


def solution(mesh):
    in_specs = (
        P("frame", "quad", None),
        P("frame", "quad", None),
        P(),
        P(),
        P(None, "quad", None),
        P(),
    )
    out_specs = (
        P("frame", "quad", None),
        P("frame", "quad", None),
        P(None, ("frame", "quad"), None),
        P(("frame", "quad")),
    )
    body = functools.partial(local, mesh.shape["quad"], mesh.shape["frame"])
    return jax.shard_map(
        body, mesh=mesh, in_specs=in_specs, out_specs=out_specs, check_vma=False
    )
```

```python
import functools
import math

import jax
import jax.numpy as jnp
from jax import lax
from jax.experimental import pallas as pl
from jax.experimental.pallas import tpu as pltpu
from jax.sharding import PartitionSpec as P

HEADS = 4
HEAD_DIM = 160
EPSILON = 1e-05
SCALE = HEAD_DIM ** (-0.5)
F32 = jnp.float32
BF16 = jnp.bfloat16


def log2(n):
    return int(n).bit_length() - 1


def dot(a, b):
    return jnp.dot(a, b, preferred_element_type=F32)


def dot_t(a, b):
    return lax.dot_general(a, b, (((1,), (1,)), ((), ())), preferred_element_type=F32)


def t_dot(a, b):
    return lax.dot_general(a, b, (((0,), (0,)), ((), ())), preferred_element_type=F32)


def normalize(values):
    average = jnp.mean(values, axis=-1, keepdims=True)
    centred = values - average
    inv_scale = lax.rsqrt(jnp.mean(centred * centred, axis=-1, keepdims=True) + EPSILON)
    return centred * inv_scale, inv_scale


def normalize_back(grad_rows, unit_rows, inv_scale, gain):
    scaled = grad_rows * gain
    first_mean = jnp.mean(scaled, axis=-1, keepdims=True)
    second_mean = jnp.mean(scaled * unit_rows, axis=-1, keepdims=True)
    return inv_scale * (scaled - first_mean - unit_rows * second_mean)


def iota(shape, dim):
    return lax.broadcasted_iota(jnp.int32, shape, dim)


def head_mask(dtype):
    lane = iota((1, HEADS * HEAD_DIM), 1)
    return [
        jnp.where((lane >= h * HEAD_DIM) & (lane < (h + 1) * HEAD_DIM), 1.0, 0.0).astype(dtype)
        for h in range(HEADS)
    ]


def stack_heads(rows):
    return jnp.concatenate([rows * mask for mask in head_mask(rows.dtype)], axis=0)


def fold_heads(stacked):
    rows = stacked.shape[0] // HEADS
    total = None
    for h, mask in enumerate(head_mask(F32)):
        piece = stacked[h * rows : (h + 1) * rows] * mask
        total = piece if total is None else total + piece
    return total


def probabilities(query_stack, keys, same):
    scores = dot_t(query_stack, keys) * SCALE
    if same is not None:
        scores = jnp.where(same, scores, -1e30)
    highest = jnp.max(scores, axis=-1, keepdims=True)
    expo = jnp.exp(scores - highest)
    return expo / jnp.sum(expo, axis=-1, keepdims=True)


def attend(query, keys, values, same):
    probs = probabilities(stack_heads(query), keys, same)
    return fold_heads(dot(probs.astype(BF16), values)).astype(BF16)


def attend_back(query, keys, values, grad, same, probs=None):
    query_stack = stack_heads(query)
    grad_stack = stack_heads(grad)
    if probs is None:
        probs = probabilities(query_stack, keys, same)
    grad_probs = dot_t(grad_stack, values)
    inner = jnp.sum(probs * grad_probs, axis=-1, keepdims=True)
    grad_scores = (probs * (grad_probs - inner) * SCALE).astype(BF16)
    grad_query = fold_heads(dot(grad_scores, keys)).astype(BF16)
    grad_key = t_dot(grad_scores, query_stack).astype(BF16)
    grad_value = t_dot(probs.astype(BF16), grad_stack).astype(BF16)
    return grad_query, grad_key, grad_value


def rows_to_sent(quad, nq, fr, pq, transposed):
    rows = nq * fr * pq
    out_dim = 1 if transposed else 0
    out = iota((rows, rows), out_dim)
    src = iota((rows, rows), 1 - out_dim)
    cell = out >> log2(nq * fr)
    other = (out >> log2(fr)) & (nq - 1)
    frame = out & (fr - 1)
    want = (((other - quad) & (nq - 1)) << log2(fr * pq)) + (frame << log2(pq)) + cell
    return jnp.where(want == src, 1.0, 0.0).astype(BF16)


def received_to_rows(quad, nq, nf, fr, transposed):
    rows = nq * nf * fr
    out_dim = 1 if transposed else 0
    out = iota((rows, rows), out_dim)
    src = iota((rows, rows), 1 - out_dim)
    step = out >> log2(nf * fr)
    device = (out >> log2(fr)) & (nf - 1)
    frame = out & (fr - 1)
    want = (device << log2(nq * fr)) + (((step + quad) & (nq - 1)) << log2(fr)) + frame
    return jnp.where(want == src, 1.0, 0.0).astype(BF16)


def own_lanes(values, quad, nq):
    width = values.shape[1] // nq
    picked = values[:, :width]
    for t in range(1, nq):
        picked = jnp.where(quad == t, values[:, t * width : (t + 1) * width], picked)
    return picked


def place_lanes(parts, quad, nq):
    placed = []
    for t in range(nq):
        piece = parts[t]
        for q in range(1, nq):
            piece = jnp.where(quad == q, parts[(t - q) % nq], piece)
        placed.append(piece)
    return jnp.concatenate(placed, axis=1)


def frame_groups(nq, fr, pq):
    size = max(1, min(fr, 128 // (nq * pq)))
    return [(start, size) for start in range(0, fr, size)]


def pick_group(rows, group, nq, fr, pq):
    start, size = group
    if size == fr:
        return rows
    cut = rows.reshape(nq, fr, pq, rows.shape[-1])[:, start : start + size]
    return cut.reshape(nq * size * pq, rows.shape[-1])


def join_groups(pieces, nq, fr, pq):
    if len(pieces) == 1:
        return pieces[0]
    size = fr // len(pieces)
    width = pieces[0].shape[-1]
    joined = jnp.concatenate([p.reshape(nq, size, pq, width) for p in pieces], axis=1)
    return joined.reshape(nq * fr * pq, width)


def same_frame(nq, size, pq):
    if size == 1:
        return None
    rows = nq * size * pq
    shape = (HEADS * rows, rows)
    left = (iota(shape, 0) >> log2(pq)) & (size - 1)
    right = (iota(shape, 1) >> log2(pq)) & (size - 1)
    return left == right


def row_of(ref):
    return ref[...].reshape(1, -1)


def flat(ref):
    value = ref[...]
    return value.reshape(-1, value.shape[-1])


def flat_wide(ref):
    value = ref[...].astype(F32)
    return value.reshape(-1, value.shape[-1])


def spread(rows, like):
    return rows.reshape(like.shape).astype(like.dtype)


def spatial_kernel(dims, *refs):
    nq, nf, fr, pq = dims
    quad, xs, refs = refs[0][0], refs[1 : 1 + nq], refs[1 + nq :]
    gain1, gain2, pos, weights, kept_out, send_out = refs
    width = HEADS * HEAD_DIM
    wide = jnp.concatenate([flat_wide(x) for x in xs], axis=0)
    unit, _ = normalize(wide)
    normed = (unit * row_of(gain1)).astype(BF16)
    query = dot(normed, weights[0]).astype(BF16)
    keys = dot(normed, weights[1]).astype(BF16)
    values = dot(normed, weights[2]).astype(BF16)
    for i, part in enumerate((query, keys, values)):
        kept_out[:, i * width : (i + 1) * width] = part
    pieces = []
    for group in frame_groups(nq, fr, pq):
        same = same_frame(nq, group[1], pq)
        cut = [pick_group(part, group, nq, fr, pq) for part in (query, keys, values)]
        pieces.append(attend(*cut, same))
    out = join_groups(pieces, nq, fr, pq)
    hidden = (wide + dot_t(out, weights[3])).astype(BF16)
    kept_out[:, 3 * width :] = hidden
    unit_two, _ = normalize(hidden.astype(F32))
    table = jnp.broadcast_to(pos[...][:, None, :], (fr, pq, pos.shape[-1]))
    table = table.reshape(fr * pq, pos.shape[-1])
    table = jnp.concatenate([table] * nq, axis=0)
    normed_two = own_lanes(unit_two * row_of(gain2) + table, quad, nq).astype(BF16)
    send_out[...] = spread(dot(rows_to_sent(quad, nq, fr, pq, False), normed_two), send_out)


def order_kernel(dims, geo, cot, weights, send_out):
    nq, nf, fr, pq = dims
    order = rows_to_sent(geo[0], nq, fr, pq, False)[:, : fr * pq]
    send_out[...] = spread(dot(order, own_lanes(flat(cot), geo[0], nq)), send_out)


def join_kernel(dims, geo, normed, own_part, *refs):
    nq, nf, fr, pq = dims
    cots, send_out = refs[:-1], refs[-1]
    order = rows_to_sent(geo[0], nq, fr, pq, False)[:, fr * pq :]
    rows = own_lanes(jnp.concatenate([flat(c) for c in cots], axis=0), geo[0], nq)
    total = own_part[...].astype(F32) + dot(order, rows).reshape(own_part.shape)
    send_out[:, : nq * fr, :] = normed[...]
    send_out[:, nq * fr :, :] = total.astype(BF16)


def sent_part(received, i, rows):
    part = received[:, i * rows : (i + 1) * rows, :].astype(F32)
    return part.reshape(-1, part.shape[-1]).astype(BF16)


def motion_kernel(dims, geo, received, weights, own_out, *sends):
    nq, nf, fr, pq = dims
    order = received_to_rows(geo[0], nq, nf, fr, False)
    normed, cot = [dot(order, sent_part(received, i, nq * fr)).astype(BF16) for i in range(2)]
    tokens = nf * fr
    for k in range(4):
        width = weights.shape[-1]
        lanes = slice(k * width, (k + 1) * width)
        product = dot(normed if k < 3 else cot, weights[k])
        own_out[:, lanes] = product[:tokens]
        for s, send in enumerate(sends):
            send[:, lanes] = product[(s + 1) * tokens : (s + 2) * tokens].astype(BF16)


def quarter_of(four):
    return ((four & 1) << 1) | (four >> 1)


def quarter_lanes(values, quarter):
    width = values.shape[1] // 4
    picked = values[:, :width]
    for t in range(1, 4):
        picked = jnp.where(quarter == t, values[:, t * width : (t + 1) * width], picked)
    return picked


def cut_kernel(dims, geo, received, *outs):
    nq, nf, fr, pq = dims
    order = received_to_rows(geo[0], nq, nf, fr, False)
    for i in range(2):
        rows = dot(order, sent_part(received, i, nq * fr))
        for d in range(4):
            outs[d][i] = quarter_lanes(rows, quarter_of(geo[1] ^ d)).astype(BF16)


def table_kernel(dims, geo, out):
    shape = out.shape
    lane = iota(shape, 1)
    freq = jnp.exp((lane >> 1).astype(F32) * (-2.0 * math.log(10000.0) / shape[1]))
    turn = (lane & 1).astype(F32) * (0.5 * math.pi)
    out[...] = jnp.sin(iota(shape, 0).astype(F32) * freq + turn)


def temporal_kernel(dims, *refs):
    nq, nf, fr, pq = dims
    parts, out = refs[:nq], refs[nq]
    width = HEADS * HEAD_DIM
    total = parts[0][...]
    for part in parts[1:]:
        total = total + part[...].astype(F32)
    query, keys, values, grad = [
        total[:, k * width : (k + 1) * width].astype(BF16) for k in range(4)
    ]
    probs = probabilities(stack_heads(query), keys, None)
    motion_out = fold_heads(dot(probs.astype(BF16), values)).astype(BF16)
    grads = attend_back(query, keys, values, grad, None, probs)
    for k, piece in enumerate(grads + (motion_out,)):
        out[:, k * width : (k + 1) * width] = piece


def part_of(terms, k):
    width = HEADS * HEAD_DIM
    return jnp.concatenate([t[:, k * width : (k + 1) * width] for t in terms], axis=0)


def back_kernel(dims, quad_ref, *refs):
    nq, nf, fr, pq = dims
    terms, (weights, out, quarter_out) = refs[:nq], refs[nq:]
    order = received_to_rows(quad_ref[0], nq, nf, fr, True)
    quarter, rows = quarter_of(quad_ref[1]), quarter_out.shape[1]
    for k in range(3):
        if rows % 16 == 0:
            own = weights[k, pl.ds(pl.multiple_of(quarter * rows, 16), rows), :]
        else:
            wide = weights[k].astype(F32)
            own = wide[:rows]
            for t in range(1, 4):
                own = jnp.where(quarter == t, wide[t * rows : (t + 1) * rows], own)
            own = own.astype(BF16)
        quarter_out[k] = own
    grad = None
    for k in range(3):
        product = dot_t(part_of(terms, k), weights[k])
        grad = product if grad is None else grad + product
    delta = dot_t(part_of(terms, 3), weights[3])
    for i, rows in enumerate((grad, delta)):
        rows = dot(order, rows.astype(BF16))
        out[:, i * nq * fr : (i + 1) * nq * fr, :] = rows.reshape(nf, nq * fr, -1).astype(BF16)


def weight_sums(geo, nq, normed, cot, weights, pos, terms):
    products, grad = [], None
    for k in range(4):
        right = part_of(terms, k)
        products.append(t_dot(normed if k < 3 else cot, right))
        if k < 3:
            back = dot_t(right, weights[k])
            grad = back if grad is None else grad + back
    table = quarter_lanes(own_lanes(pos[...], geo[0], nq), quarter_of(geo[1]))
    table = jnp.concatenate([table] * len(terms), axis=0)
    return products, jnp.sum(grad * (normed.astype(F32) - table), axis=0, keepdims=True)


def first_weight_kernel(dims, geo, *refs):
    nq, nf, fr, pq = dims
    factors, (weights, pos), refs = refs[:4], refs[4:6], refs[6:]
    terms, (blocks, gain_out, late_out) = refs[: 2 * nq + 2], refs[2 * nq + 2 :]
    _, stage, block, _ = blocks.shape
    tokens = nf * fr
    left = []
    for i in range(2):
        early = [factors[0][i], factors[1][i], factors[2][i, :tokens], factors[3][i, :tokens]]
        left.append(jnp.concatenate(early, axis=0))
        late = [factors[2][i, tokens:], factors[3][i, tokens:]]
        late_out[i] = jnp.concatenate(late, axis=0)
    products, gain_out[...] = weight_sums(geo, nq, *left, weights, pos, terms)
    for k in range(4):
        for z in range(stage):
            blocks[k, z] = products[k][z * block : (z + 1) * block]


def second_weight_kernel(dims, geo, sums, gain_sum, left, weights, pos, gain2, *refs):
    nq, nf, fr, pq = dims
    terms, outs, blocks = refs[: 2 * nq - 2], refs[2 * nq - 2 : -1], refs[-1]
    _, stage, block, width = blocks.shape
    products, gain = weight_sums(geo, nq, left[0], left[1], weights, pos, terms)
    for k in range(4):
        for z in range(stage):
            blocks[k, z] = sums[k, z] + products[k][z * block : (z + 1) * block]
    gain = gain + gain_sum[...]
    rows = gain.shape[1]
    gain = gain / quarter_lanes(own_lanes(row_of(gain2), geo[0], nq), quarter_of(geo[1]))
    extra = jnp.concatenate([gain, jnp.zeros((1, width - rows), F32)], axis=1)
    extra = jnp.where(iota((8, width), 0) == 0, extra, 0.0)
    for r in range(stage):
        z = (geo[2] + r) & (stage - 1)
        rows_out = jnp.concatenate([blocks[k, z] for k in range(4)] + [extra], axis=0)
        outs[r][...] = rows_out.astype(BF16)


def middle_kernel(dims, *refs):
    nq, nf, fr, pq = dims
    quad, received, cots = refs[0][0], refs[1 : 1 + nq], refs[1 + nq : 1 + 2 * nq]
    kept, gain2, block_out, grad_out = refs[1 + 2 * nq :]
    own = fr * pq
    order = rows_to_sent(quad, nq, fr, pq, True)

    def lanes(i):
        parts = []
        for r in received:
            parts.append(dot(order, sent_part(r, i, nq * fr)))
        return place_lanes(parts, quad, nq)

    hidden = kept[:, 3 * HEADS * HEAD_DIM :].astype(F32)
    grad_normed, delta = lanes(0), lanes(1)
    block_out[...] = spread(hidden[:own] + delta[:own], block_out)
    unit_two, inv_two = normalize(hidden)
    cot = jnp.concatenate([flat_wide(c) for c in cots], axis=0)
    back = normalize_back(grad_normed, unit_two, inv_two, row_of(gain2))
    grad_out[...] = (cot + back).astype(BF16)


def tail_kernel(dims, grad_hidden, xs, kept, gain1, weights, in_grad):
    nq, nf, fr, pq = dims
    own, width = fr * pq, HEADS * HEAD_DIM
    grad_out = dot(grad_hidden[...], weights[3]).astype(BF16)
    parts = [kept[:, i * width : (i + 1) * width] for i in range(3)] + [grad_out]
    pieces = []
    for group in frame_groups(nq, fr, pq):
        same = same_frame(nq, group[1], pq)
        pieces.append(attend_back(*[pick_group(p, group, nq, fr, pq) for p in parts], same))
    grads = [join_groups([p[i] for p in pieces], nq, fr, pq)[:own] for i in range(3)]
    grad_one = dot_t(grads[0], weights[0]) + dot_t(grads[1], weights[1]) + dot_t(grads[2], weights[2])
    unit_one, inv_one = normalize(flat_wide(xs))
    back = normalize_back(grad_one, unit_one, inv_one, row_of(gain1))
    in_grad[...] = spread(grad_hidden[...][:own].astype(F32) + back, in_grad)


def call(kernel, name, outs, args, vmem, micros, scratch=()):
    in_specs = []
    for arg in args:
        space = pltpu.SMEM if arg.dtype == jnp.int32 else pltpu.VMEM
        in_specs.append(pl.BlockSpec(memory_space=space))
    return list(
        pl.pallas_call(
            kernel,
            out_shape=outs,
            in_specs=in_specs,
            out_specs=[pl.BlockSpec(memory_space=pltpu.VMEM) for _ in outs],
            scratch_shapes=list(scratch),
            compiler_params=pltpu.CompilerParams(vmem_limit_bytes=vmem * 1024 * 1024),
            cost_estimate=pl.CostEstimate(
                flops=int(micros * 1e9), bytes_accessed=2**20, transcendentals=0
            ),
            name=name,
        )(*args)
    )


def after(value, *others):
    return lax.optimization_barrier((value,) + others)[0]


def sds(*shape, dtype=BF16):
    return jax.ShapeDtypeStruct(shape, dtype)


def positional(first, frames, channels):
    frame_pos = (first + lax.broadcasted_iota(jnp.int32, (frames, channels), 0)).astype(F32)
    lane = lax.broadcasted_iota(jnp.int32, (frames, channels), 1)
    freq_index = (lane >> 1).astype(F32)
    phases = frame_pos * jnp.exp(freq_index * (-2.0 * math.log(10000.0) / channels))
    return jnp.sin(phases + (lane & 1).astype(F32) * (0.5 * math.pi))


def local(nq, nf, activations, cotangent, spatial_weights, spatial_gain, motion_weights, motion_gain):
    fr, pq, channels = activations.shape
    dims = (nq, nf, fr, pq)
    width = spatial_weights.shape[-1]
    half = channels // nq
    rows = nq * fr * pq
    tokens = nf * fr
    small = 16 if rows <= 256 else 40
    big = 16 if rows <= 256 else 52
    quad = lax.axis_index("quad")
    frame = lax.axis_index("frame")


    def from_quad(x, s):
        return lax.ppermute(x, "quad", [((d + s) % nq, d) for d in range(nq)])

    def to_quad(x, s):
        return lax.ppermute(x, "quad", [(d, (d + s) % nq) for d in range(nq)])

    def swap(x):
        return lax.all_to_all(x, "frame", split_axis=0, concat_axis=0, tiled=True)

    def run(kernel, name, outs, args, micros, vmem=small, **options):
        kernel = functools.partial(kernel, dims)
        return call(kernel, name, outs, args, vmem, micros, **options)

    def move(x, pairs):
        return lax.ppermute(x, "frame", pairs)

    geo = jnp.stack([quad, frame % 4, frame // 4]).astype(jnp.int32)

    def flipped(bits):
        return [(g, g ^ bits) for g in range(nf)]

    ring = [(g, (g + 4) % nf) for g in range(nf)]

    gain1, gain2 = spatial_gain, motion_gain
    sent = sds(nf, nq * fr, half)
    acts = [activations] + [from_quad(activations, s) for s in range(1, nq)]
    both = sds(nf, 2 * nq * fr, half)
    (own_part,) = run(
        order_kernel, "order_cotangent", [sent], [geo, cotangent, spatial_weights], 0.5, big
    )
    cot_later = after(cotangent, acts[-1])
    cots = [cotangent] + [from_quad(cot_later, s) for s in range(1, nq)]
    pos = positional(frame * fr, fr, channels)
    kept, normed = run(
        spatial_kernel,
        "spatial_forward",
        [sds(rows, 3 * width + channels), sent],
        [geo] + acts + [gain1, gain2, pos, spatial_weights],
        3,
        big,
    )
    (send,) = run(join_kernel, "join_sent", [both], [geo, normed, own_part] + cots[1:], 0.5)
    received = swap(send)
    parts = run(
        motion_kernel,
        "motion_projection",
        [sds(tokens, 4 * width, dtype=F32)] + [sds(tokens, 4 * width)] * (nq - 1),
        [geo, received, motion_weights],
        1.5,
    )
    parts = [parts[0]] + [to_quad(p, s + 1) for s, p in enumerate(parts[1:])]
    (terms,) = run(temporal_kernel, "temporal_attention", [sds(tokens, 4 * width)], parts, 2)
    factors = run(
        cut_kernel,
        "cut_factors",
        [sds(2, rows, half // 4)] * 4,
        [geo, after(received, terms)],
        0.5,
    )
    (table,) = run(
        table_kernel,
        "positional_table",
        [sds(tokens, channels, dtype=F32)],
        [after(geo, terms)],
        1.5,
    )
    all_terms = [terms] + [after(from_quad(terms, s), factors[0], table) for s in range(1, nq)]
    pair_terms = [move(t, flipped(2)) for t in all_terms]
    core_terms = [move(t, flipped(1)) for t in all_terms]
    factors = [factors[0]] + [move(factors[d], flipped(d)) for d in range(1, 4)]
    back_send, quarter = run(
        back_kernel,
        "temporal_back_projection",
        [sds(nf, 2 * nq * fr, half), sds(3, half // 4, width)],
        [geo] + all_terms + [motion_weights],
        3,
    )
    last_terms = [move(t, flipped(1)) for t in pair_terms[:1]]

    stage, block = nf // 4, half // nf
    sums, gain_sum, late_left = run(
        first_weight_kernel,
        "weight_terms_first_tokens",
        [
            sds(4, stage, block, width, dtype=F32),
            sds(1, half // 4, dtype=F32),
            sds(2, 2 * (nq - 1) * tokens, half // 4),
        ],
        [geo] + factors + [quarter, table] + all_terms + core_terms
        + pair_terms[:1] + last_terms,
        3,
    )
    late_terms = [after(t, back_send, sums) for t in pair_terms[1:]]
    late_terms += [move(t, flipped(1)) for t in late_terms]
    parts_w = run(
        second_weight_kernel,
        "weight_terms_last_tokens",
        [sds(4 * block + 8, width)] * stage,
        [geo, sums, gain_sum, late_left, quarter, table, gain2] + late_terms,
        2,
        scratch=[pltpu.VMEM((4, stage, block, width), F32)],
    )

    def add(a, b):
        return (a.astype(F32) + b.astype(F32)).astype(BF16)

    back_recv = swap(back_send)
    backs = [back_recv] + [from_quad(back_recv, s) for s in range(1, nq)]
    block_output, grad_hidden = run(
        middle_kernel,
        "block_output_hidden_gradient",
        [sds(fr, pq, channels), sds(rows, channels)],
        [geo] + backs + cots + [kept, gain2],
        6,
        big,
    )
    total = parts_w[stage - 1]
    for step in range(1, stage):
        if step == stage - 2:
            total = after(total, back_recv)
        moved = move(total, ring)
        if step == stage - 1:
            moved = after(moved, grad_hidden)
        total = add(moved, parts_w[stage - 1 - step])
    final = []
    for g in range(nf):
        for q in range(nq):
            j = quarter_of(g % 4) * stage + g // 4
            final.append((g * nq + q, nf * q + j))
    grad_hidden = after(grad_hidden, total)
    total = lax.ppermute(total, ("frame", "quad"), final)
    (input_grad,) = run(
        tail_kernel,
        "spatial_backward",
        [sds(fr, pq, channels)],
        [grad_hidden, activations, kept, gain1, spatial_weights],
        3.5,
        big,
    )
    everyone = nf * nq
    factor = 1.0 / math.sqrt(everyone * fr * pq)
    weight_grad = total[: 4 * block].reshape(4, block, width).astype(F32) * factor
    place = ((frame * nq + quad) % stage) * block
    gain_grad = lax.dynamic_slice(total[4 * block], (place,), (block,)).astype(F32) * factor
    return block_output, input_grad, weight_grad, gain_grad


def solution(mesh):
    in_specs = (
        P("frame", "quad", None),
        P("frame", "quad", None),
        P(),
        P(),
        P(None, "quad", None),
        P(),
    )
    out_specs = (
        P("frame", "quad", None),
        P("frame", "quad", None),
        P(None, ("frame", "quad"), None),
        P(("frame", "quad")),
    )
    body = functools.partial(local, mesh.shape["quad"], mesh.shape["frame"])
    return jax.shard_map(
        body, mesh=mesh, in_specs=in_specs, out_specs=out_specs, check_vma=False
    )
```

```python
import functools
import math

import jax
import jax.numpy as jnp
from jax import lax
from jax.experimental import pallas as pl
from jax.experimental.pallas import tpu as pltpu
from jax.sharding import PartitionSpec as P

HEADS = 4
HEAD_DIM = 160
EPSILON = 1e-05
SCALE = HEAD_DIM ** (-0.5)
F32 = jnp.float32
BF16 = jnp.bfloat16


def log2(n):
    return int(n).bit_length() - 1


def dot(a, b):
    return jnp.dot(a, b, preferred_element_type=F32)


def dot_t(a, b):
    return lax.dot_general(a, b, (((1,), (1,)), ((), ())), preferred_element_type=F32)


def t_dot(a, b):
    return lax.dot_general(a, b, (((0,), (0,)), ((), ())), preferred_element_type=F32)


def normalize(values):
    average = jnp.mean(values, axis=-1, keepdims=True)
    centred = values - average
    inv_scale = lax.rsqrt(jnp.mean(centred * centred, axis=-1, keepdims=True) + EPSILON)
    return centred * inv_scale, inv_scale


def normalize_back(grad_rows, unit_rows, inv_scale, gain):
    scaled = grad_rows * gain
    first_mean = jnp.mean(scaled, axis=-1, keepdims=True)
    second_mean = jnp.mean(scaled * unit_rows, axis=-1, keepdims=True)
    return inv_scale * (scaled - first_mean - unit_rows * second_mean)


def iota(shape, dim):
    return lax.broadcasted_iota(jnp.int32, shape, dim)


def head_mask(dtype):
    lane = iota((1, HEADS * HEAD_DIM), 1)
    return [
        jnp.where((lane >= h * HEAD_DIM) & (lane < (h + 1) * HEAD_DIM), 1.0, 0.0).astype(dtype)
        for h in range(HEADS)
    ]


def stack_heads(rows):
    return jnp.concatenate([rows * mask for mask in head_mask(rows.dtype)], axis=0)


def fold_heads(stacked):
    rows = stacked.shape[0] // HEADS
    total = None
    for h, mask in enumerate(head_mask(F32)):
        piece = stacked[h * rows : (h + 1) * rows] * mask
        total = piece if total is None else total + piece
    return total


def probabilities(query_stack, keys, same):
    scores = dot_t(query_stack, keys) * SCALE
    if same is not None:
        scores = jnp.where(same, scores, -1e30)
    highest = jnp.max(scores, axis=-1, keepdims=True)
    expo = jnp.exp(scores - highest)
    return expo / jnp.sum(expo, axis=-1, keepdims=True)


def attend(query, keys, values, same):
    probs = probabilities(stack_heads(query), keys, same)
    return fold_heads(dot(probs.astype(BF16), values)).astype(BF16)


def attend_back(query, keys, values, grad, same, probs=None):
    query_stack = stack_heads(query)
    grad_stack = stack_heads(grad)
    if probs is None:
        probs = probabilities(query_stack, keys, same)
    grad_probs = dot_t(grad_stack, values)
    inner = jnp.sum(probs * grad_probs, axis=-1, keepdims=True)
    grad_scores = (probs * (grad_probs - inner) * SCALE).astype(BF16)
    grad_query = fold_heads(dot(grad_scores, keys)).astype(BF16)
    grad_key = t_dot(grad_scores, query_stack).astype(BF16)
    grad_value = t_dot(probs.astype(BF16), grad_stack).astype(BF16)
    return grad_query, grad_key, grad_value


def rows_to_sent(quad, nq, fr, pq, transposed):
    rows = nq * fr * pq
    out_dim = 1 if transposed else 0
    out = iota((rows, rows), out_dim)
    src = iota((rows, rows), 1 - out_dim)
    cell = out >> log2(nq * fr)
    other = (out >> log2(fr)) & (nq - 1)
    frame = out & (fr - 1)
    want = (((other - quad) & (nq - 1)) << log2(fr * pq)) + (frame << log2(pq)) + cell
    return jnp.where(want == src, 1.0, 0.0).astype(BF16)


def received_to_rows(quad, nq, nf, fr, transposed):
    rows = nq * nf * fr
    out_dim = 1 if transposed else 0
    out = iota((rows, rows), out_dim)
    src = iota((rows, rows), 1 - out_dim)
    step = out >> log2(nf * fr)
    device = (out >> log2(fr)) & (nf - 1)
    frame = out & (fr - 1)
    want = (device << log2(nq * fr)) + (((step + quad) & (nq - 1)) << log2(fr)) + frame
    return jnp.where(want == src, 1.0, 0.0).astype(BF16)


def own_lanes(values, quad, nq):
    width = values.shape[1] // nq
    picked = values[:, :width]
    for t in range(1, nq):
        picked = jnp.where(quad == t, values[:, t * width : (t + 1) * width], picked)
    return picked


def place_lanes(parts, quad, nq):
    placed = []
    for t in range(nq):
        piece = parts[t]
        for q in range(1, nq):
            piece = jnp.where(quad == q, parts[(t - q) % nq], piece)
        placed.append(piece)
    return jnp.concatenate(placed, axis=1)


def frame_groups(nq, fr, pq):
    size = max(1, min(fr, 128 // (nq * pq)))
    return [(start, size) for start in range(0, fr, size)]


def pick_group(rows, group, nq, fr, pq):
    start, size = group
    if size == fr:
        return rows
    cut = rows.reshape(nq, fr, pq, rows.shape[-1])[:, start : start + size]
    return cut.reshape(nq * size * pq, rows.shape[-1])


def join_groups(pieces, nq, fr, pq):
    if len(pieces) == 1:
        return pieces[0]
    size = fr // len(pieces)
    width = pieces[0].shape[-1]
    joined = jnp.concatenate([p.reshape(nq, size, pq, width) for p in pieces], axis=1)
    return joined.reshape(nq * fr * pq, width)


def same_frame(nq, size, pq):
    if size == 1:
        return None
    rows = nq * size * pq
    shape = (HEADS * rows, rows)
    left = (iota(shape, 0) >> log2(pq)) & (size - 1)
    right = (iota(shape, 1) >> log2(pq)) & (size - 1)
    return left == right


def row_of(ref):
    return ref[...].reshape(1, -1)


def flat(ref):
    value = ref[...]
    return value.reshape(-1, value.shape[-1])


def flat_wide(ref):
    value = ref[...].astype(F32)
    return value.reshape(-1, value.shape[-1])


def spread(rows, like):
    return rows.reshape(like.shape).astype(like.dtype)


def spatial_kernel(dims, *refs):
    nq, nf, fr, pq = dims
    quad, xs, refs = refs[0][0], refs[1 : 1 + nq], refs[1 + nq :]
    gain1, gain2, pos, weights, kept_out, send_out = refs
    width = HEADS * HEAD_DIM
    wide = jnp.concatenate([flat_wide(x) for x in xs], axis=0)
    unit, _ = normalize(wide)
    normed = (unit * row_of(gain1)).astype(BF16)
    query = dot(normed, weights[0]).astype(BF16)
    keys = dot(normed, weights[1]).astype(BF16)
    values = dot(normed, weights[2]).astype(BF16)
    for i, part in enumerate((query, keys, values)):
        kept_out[:, i * width : (i + 1) * width] = part
    pieces = []
    for group in frame_groups(nq, fr, pq):
        same = same_frame(nq, group[1], pq)
        cut = [pick_group(part, group, nq, fr, pq) for part in (query, keys, values)]
        pieces.append(attend(*cut, same))
    out = join_groups(pieces, nq, fr, pq)
    hidden = (wide + dot_t(out, weights[3])).astype(BF16)
    kept_out[:, 3 * width :] = hidden
    unit_two, _ = normalize(hidden.astype(F32))
    table = jnp.broadcast_to(pos[...][:, None, :], (fr, pq, pos.shape[-1]))
    table = table.reshape(fr * pq, pos.shape[-1])
    table = jnp.concatenate([table] * nq, axis=0)
    normed_two = own_lanes(unit_two * row_of(gain2) + table, quad, nq).astype(BF16)
    send_out[...] = spread(dot(rows_to_sent(quad, nq, fr, pq, False), normed_two), send_out)


def order_kernel(dims, geo, cot, weights, send_out):
    nq, nf, fr, pq = dims
    order = rows_to_sent(geo[0], nq, fr, pq, False)[:, : fr * pq]
    send_out[...] = spread(dot(order, own_lanes(flat(cot), geo[0], nq)), send_out)


def join_kernel(dims, geo, normed, own_part, *refs):
    nq, nf, fr, pq = dims
    cots, send_out = refs[:-1], refs[-1]
    order = rows_to_sent(geo[0], nq, fr, pq, False)[:, fr * pq :]
    rows = own_lanes(jnp.concatenate([flat(c) for c in cots], axis=0), geo[0], nq)
    total = own_part[...].astype(F32) + dot(order, rows).reshape(own_part.shape)
    send_out[:, : nq * fr, :] = normed[...]
    send_out[:, nq * fr :, :] = total.astype(BF16)


def sent_part(received, i, rows):
    part = received[:, i * rows : (i + 1) * rows, :].astype(F32)
    return part.reshape(-1, part.shape[-1]).astype(BF16)


def motion_kernel(dims, geo, received, weights, own_out, *sends):
    nq, nf, fr, pq = dims
    order = received_to_rows(geo[0], nq, nf, fr, False)
    normed, cot = [dot(order, sent_part(received, i, nq * fr)).astype(BF16) for i in range(2)]
    tokens = nf * fr
    for k in range(4):
        width = weights.shape[-1]
        lanes = slice(k * width, (k + 1) * width)
        product = dot(normed if k < 3 else cot, weights[k])
        own_out[:, lanes] = product[:tokens]
        for s, send in enumerate(sends):
            send[:, lanes] = product[(s + 1) * tokens : (s + 2) * tokens].astype(BF16)


def quarter_of(four):
    return ((four & 1) << 1) | (four >> 1)


def quarter_lanes(values, quarter):
    width = values.shape[1] // 4
    picked = values[:, :width]
    for t in range(1, 4):
        picked = jnp.where(quarter == t, values[:, t * width : (t + 1) * width], picked)
    return picked


def cut_kernel(dims, geo, received, *outs):
    nq, nf, fr, pq = dims
    order = received_to_rows(geo[0], nq, nf, fr, False)
    for i in range(2):
        rows = dot(order, sent_part(received, i, nq * fr))
        for d in range(4):
            outs[d][i] = quarter_lanes(rows, quarter_of(geo[1] ^ d)).astype(BF16)


def table_kernel(dims, geo, out):
    shape = out.shape
    lane = iota(shape, 1)
    freq = jnp.exp((lane >> 1).astype(F32) * (-2.0 * math.log(10000.0) / shape[1]))
    turn = (lane & 1).astype(F32) * (0.5 * math.pi)
    out[...] = jnp.sin(iota(shape, 0).astype(F32) * freq + turn)


def temporal_kernel(dims, *refs):
    nq, nf, fr, pq = dims
    parts, out = refs[:nq], refs[nq]
    width = HEADS * HEAD_DIM
    total = parts[0][...]
    for part in parts[1:]:
        total = total + part[...].astype(F32)
    query, keys, values, grad = [
        total[:, k * width : (k + 1) * width].astype(BF16) for k in range(4)
    ]
    probs = probabilities(stack_heads(query), keys, None)
    motion_out = fold_heads(dot(probs.astype(BF16), values)).astype(BF16)
    grads = attend_back(query, keys, values, grad, None, probs)
    for k, piece in enumerate(grads + (motion_out,)):
        out[:, k * width : (k + 1) * width] = piece


def part_of(terms, k):
    width = HEADS * HEAD_DIM
    return jnp.concatenate([t[:, k * width : (k + 1) * width] for t in terms], axis=0)


def back_kernel(dims, quad_ref, *refs):
    nq, nf, fr, pq = dims
    terms, (weights, out, quarter_out) = refs[:nq], refs[nq:]
    order = received_to_rows(quad_ref[0], nq, nf, fr, True)
    quarter, rows = quarter_of(quad_ref[1]), quarter_out.shape[1]
    for k in range(3):
        if rows % 16 == 0:
            own = weights[k, pl.ds(pl.multiple_of(quarter * rows, 16), rows), :]
        else:
            wide = weights[k].astype(F32)
            own = wide[:rows]
            for t in range(1, 4):
                own = jnp.where(quarter == t, wide[t * rows : (t + 1) * rows], own)
            own = own.astype(BF16)
        quarter_out[k] = own
    grad = None
    for k in range(3):
        product = dot_t(part_of(terms, k), weights[k])
        grad = product if grad is None else grad + product
    delta = dot_t(part_of(terms, 3), weights[3])
    for i, rows in enumerate((grad, delta)):
        rows = dot(order, rows.astype(BF16))
        out[:, i * nq * fr : (i + 1) * nq * fr, :] = rows.reshape(nf, nq * fr, -1).astype(BF16)


def weight_sums(geo, nq, normed, cot, weights, pos, terms):
    products, grad = [], None
    for k in range(4):
        right = part_of(terms, k)
        products.append(t_dot(normed if k < 3 else cot, right))
        if k < 3:
            back = dot_t(right, weights[k])
            grad = back if grad is None else grad + back
    table = quarter_lanes(own_lanes(pos[...], geo[0], nq), quarter_of(geo[1]))
    table = jnp.concatenate([table] * len(terms), axis=0)
    return products, jnp.sum(grad * (normed.astype(F32) - table), axis=0, keepdims=True)


def first_weight_kernel(dims, geo, *refs):
    nq, nf, fr, pq = dims
    factors, (weights, pos), refs = refs[:4], refs[4:6], refs[6:]
    terms, (blocks, gain_out, late_out) = refs[: 2 * nq + 2], refs[2 * nq + 2 :]
    _, stage, block, _ = blocks.shape
    tokens = nf * fr
    left = []
    for i in range(2):
        early = [factors[0][i], factors[1][i], factors[2][i, :tokens], factors[3][i, :tokens]]
        left.append(jnp.concatenate(early, axis=0))
        late = [factors[2][i, tokens:], factors[3][i, tokens:]]
        late_out[i] = jnp.concatenate(late, axis=0)
    products, gain_out[...] = weight_sums(geo, nq, *left, weights, pos, terms)
    for k in range(4):
        for z in range(stage):
            blocks[k, z] = products[k][z * block : (z + 1) * block]


def second_weight_kernel(dims, geo, sums, gain_sum, left, weights, pos, gain2, *refs):
    nq, nf, fr, pq = dims
    terms, outs, blocks = refs[: 2 * nq - 2], refs[2 * nq - 2 : -1], refs[-1]
    _, stage, block, width = blocks.shape
    products, gain = weight_sums(geo, nq, left[0], left[1], weights, pos, terms)
    for k in range(4):
        for z in range(stage):
            blocks[k, z] = sums[k, z] + products[k][z * block : (z + 1) * block]
    gain = gain + gain_sum[...]
    rows = gain.shape[1]
    gain = gain / quarter_lanes(own_lanes(row_of(gain2), geo[0], nq), quarter_of(geo[1]))
    extra = jnp.concatenate([gain, jnp.zeros((1, width - rows), F32)], axis=1)
    extra = jnp.where(iota((8, width), 0) == 0, extra, 0.0)
    for r in range(stage):
        z = (geo[2] + r) & (stage - 1)
        rows_out = jnp.concatenate([blocks[0, z], blocks[1, z], extra], axis=0)
        outs[r][...] = rows_out.astype(BF16)
        rows_out = jnp.concatenate([blocks[2, z], blocks[3, z]], axis=0)
        outs[stage + r][...] = rows_out.astype(BF16)


def middle_kernel(dims, *refs):
    nq, nf, fr, pq = dims
    quad, received, cots = refs[0][0], refs[1 : 1 + nq], refs[1 + nq : 1 + 2 * nq]
    kept, gain2, block_out, grad_out = refs[1 + 2 * nq :]
    own = fr * pq
    order = rows_to_sent(quad, nq, fr, pq, True)

    def lanes(i):
        parts = []
        for r in received:
            parts.append(dot(order, sent_part(r, i, nq * fr)))
        return place_lanes(parts, quad, nq)

    hidden = kept[:, 3 * HEADS * HEAD_DIM :].astype(F32)
    grad_normed, delta = lanes(0), lanes(1)
    block_out[...] = spread(hidden[:own] + delta[:own], block_out)
    unit_two, inv_two = normalize(hidden)
    cot = jnp.concatenate([flat_wide(c) for c in cots], axis=0)
    back = normalize_back(grad_normed, unit_two, inv_two, row_of(gain2))
    grad_out[...] = (cot + back).astype(BF16)


def tail_kernel(dims, grad_hidden, xs, kept, gain1, weights, in_grad):
    nq, nf, fr, pq = dims
    own, width = fr * pq, HEADS * HEAD_DIM
    grad_out = dot(grad_hidden[...], weights[3]).astype(BF16)
    parts = [kept[:, i * width : (i + 1) * width] for i in range(3)] + [grad_out]
    pieces = []
    for group in frame_groups(nq, fr, pq):
        same = same_frame(nq, group[1], pq)
        pieces.append(attend_back(*[pick_group(p, group, nq, fr, pq) for p in parts], same))
    grads = [join_groups([p[i] for p in pieces], nq, fr, pq)[:own] for i in range(3)]
    grad_one = dot_t(grads[0], weights[0]) + dot_t(grads[1], weights[1]) + dot_t(grads[2], weights[2])
    unit_one, inv_one = normalize(flat_wide(xs))
    back = normalize_back(grad_one, unit_one, inv_one, row_of(gain1))
    in_grad[...] = spread(grad_hidden[...][:own].astype(F32) + back, in_grad)


def call(kernel, name, outs, args, vmem, micros, scratch=()):
    in_specs = []
    for arg in args:
        space = pltpu.SMEM if arg.dtype == jnp.int32 else pltpu.VMEM
        in_specs.append(pl.BlockSpec(memory_space=space))
    return list(
        pl.pallas_call(
            kernel,
            out_shape=outs,
            in_specs=in_specs,
            out_specs=[pl.BlockSpec(memory_space=pltpu.VMEM) for _ in outs],
            scratch_shapes=list(scratch),
            compiler_params=pltpu.CompilerParams(vmem_limit_bytes=vmem * 1024 * 1024),
            cost_estimate=pl.CostEstimate(
                flops=int(micros * 1e9), bytes_accessed=2**20, transcendentals=0
            ),
            name=name,
        )(*args)
    )


def after(value, *others):
    return lax.optimization_barrier((value,) + others)[0]


def sds(*shape, dtype=BF16):
    return jax.ShapeDtypeStruct(shape, dtype)


def positional(first, frames, channels):
    frame_pos = (first + lax.broadcasted_iota(jnp.int32, (frames, channels), 0)).astype(F32)
    lane = lax.broadcasted_iota(jnp.int32, (frames, channels), 1)
    freq_index = (lane >> 1).astype(F32)
    phases = frame_pos * jnp.exp(freq_index * (-2.0 * math.log(10000.0) / channels))
    return jnp.sin(phases + (lane & 1).astype(F32) * (0.5 * math.pi))


def local(nq, nf, activations, cotangent, spatial_weights, spatial_gain, motion_weights, motion_gain):
    fr, pq, channels = activations.shape
    dims = (nq, nf, fr, pq)
    width = spatial_weights.shape[-1]
    half = channels // nq
    rows = nq * fr * pq
    tokens = nf * fr
    small = 16 if rows <= 256 else 40
    big = 16 if rows <= 256 else 52
    quad = lax.axis_index("quad")
    frame = lax.axis_index("frame")


    def from_quad(x, s):
        return lax.ppermute(x, "quad", [((d + s) % nq, d) for d in range(nq)])

    def to_quad(x, s):
        return lax.ppermute(x, "quad", [(d, (d + s) % nq) for d in range(nq)])

    def swap(x):
        return lax.all_to_all(x, "frame", split_axis=0, concat_axis=0, tiled=True)

    def run(kernel, name, outs, args, micros, vmem=small, **options):
        kernel = functools.partial(kernel, dims)
        return call(kernel, name, outs, args, vmem, micros, **options)

    def move(x, pairs):
        return lax.ppermute(x, "frame", pairs)

    geo = jnp.stack([quad, frame % 4, frame // 4]).astype(jnp.int32)

    def flipped(bits):
        return [(g, g ^ bits) for g in range(nf)]

    ring = [(g, (g + 4) % nf) for g in range(nf)]

    gain1, gain2 = spatial_gain, motion_gain
    sent = sds(nf, nq * fr, half)
    acts = [activations] + [from_quad(activations, s) for s in range(1, nq)]
    both = sds(nf, 2 * nq * fr, half)
    (own_part,) = run(
        order_kernel, "order_cotangent", [sent], [geo, cotangent, spatial_weights], 0.5, big
    )
    cot_later = after(cotangent, acts[-1])
    cots = [cotangent] + [from_quad(cot_later, s) for s in range(1, nq)]
    pos = positional(frame * fr, fr, channels)
    kept, normed = run(
        spatial_kernel,
        "spatial_forward",
        [sds(rows, 3 * width + channels), sent],
        [geo] + acts + [gain1, gain2, pos, spatial_weights],
        3,
        big,
    )
    (send,) = run(join_kernel, "join_sent", [both], [geo, normed, own_part] + cots[1:], 0.5)
    received = swap(send)
    parts = run(
        motion_kernel,
        "motion_projection",
        [sds(tokens, 4 * width, dtype=F32)] + [sds(tokens, 4 * width)] * (nq - 1),
        [geo, received, motion_weights],
        1.5,
    )
    parts = [parts[0]] + [to_quad(p, s + 1) for s, p in enumerate(parts[1:])]
    (terms,) = run(temporal_kernel, "temporal_attention", [sds(tokens, 4 * width)], parts, 2)
    factors = run(
        cut_kernel,
        "cut_factors",
        [sds(2, rows, half // 4)] * 4,
        [geo, after(received, terms)],
        0.5,
    )
    (table,) = run(
        table_kernel,
        "positional_table",
        [sds(tokens, channels, dtype=F32)],
        [after(geo, terms)],
        1.5,
    )
    all_terms = [terms] + [after(from_quad(terms, s), factors[0], table) for s in range(1, nq)]
    pair_terms = [move(t, flipped(2)) for t in all_terms]
    core_terms = [move(t, flipped(1)) for t in all_terms]
    factors = [factors[0]] + [move(factors[d], flipped(d)) for d in range(1, 4)]
    back_send, quarter = run(
        back_kernel,
        "temporal_back_projection",
        [sds(nf, 2 * nq * fr, half), sds(3, half // 4, width)],
        [geo] + all_terms + [motion_weights],
        3,
    )
    pair_terms[0] = after(pair_terms[0], back_send)
    last_terms = [move(pair_terms[0], flipped(1))]

    stage, block = nf // 4, half // nf
    sums, gain_sum, late_left = run(
        first_weight_kernel,
        "weight_terms_first_tokens",
        [
            sds(4, stage, block, width, dtype=F32),
            sds(1, half // 4, dtype=F32),
            sds(2, 2 * (nq - 1) * tokens, half // 4),
        ],
        [geo] + factors + [quarter, table] + all_terms + core_terms
        + pair_terms[:1] + last_terms,
        3,
    )
    late_terms = [after(t, back_send, sums) for t in pair_terms[1:]]
    late_terms += [move(t, flipped(1)) for t in late_terms]
    parts_w = run(
        second_weight_kernel,
        "weight_terms_last_tokens",
        [sds(2 * block + 8, width)] * stage + [sds(2 * block, width)] * stage,
        [geo, sums, gain_sum, late_left, quarter, table, gain2] + late_terms,
        0.01,
        scratch=[pltpu.VMEM((4, stage, block, width), F32)],
    )

    def add(a, b):
        return (a.astype(F32) + b.astype(F32)).astype(BF16)

    back_recv = swap(back_send)
    backs = [back_recv] + [from_quad(back_recv, s) for s in range(1, nq)]
    block_output, grad_hidden = run(
        middle_kernel,
        "block_output_hidden_gradient",
        [sds(fr, pq, channels), sds(rows, channels)],
        [geo] + backs + cots + [kept, gain2],
        6,
        big,
    )
    totals = [parts_w[stage - 1], parts_w[2 * stage - 1]]
    for step in range(1, stage):
        for i in range(2):
            if step == stage - 2:
                totals[i] = after(totals[i], back_recv)
            moved = move(totals[i], ring)
            if step == stage - 1:
                moved = after(moved, grad_hidden)
            totals[i] = add(moved, parts_w[(i + 1) * stage - 1 - step])
    final = []
    for g in range(nf):
        for q in range(nq):
            j = quarter_of(g % 4) * stage + g // 4
            final.append((g * nq + q, nf * q + j))
    grad_hidden = after(grad_hidden, *totals)
    totals = [lax.ppermute(t, ("frame", "quad"), final) for t in totals]
    (input_grad,) = run(
        tail_kernel,
        "spatial_backward",
        [sds(fr, pq, channels)],
        [grad_hidden, activations, kept, gain1, spatial_weights],
        3.5,
        big,
    )
    everyone = nf * nq
    factor = 1.0 / math.sqrt(everyone * fr * pq)
    weight_grad = jnp.concatenate([totals[0][: 2 * block], totals[1]], axis=0)
    weight_grad = weight_grad.reshape(4, block, width).astype(F32) * factor
    place = ((frame * nq + quad) % stage) * block
    gain_grad = lax.dynamic_slice(totals[0][2 * block], (place,), (block,)).astype(F32) * factor
    return block_output, input_grad, weight_grad, gain_grad


def solution(mesh):
    in_specs = (
        P("frame", "quad", None),
        P("frame", "quad", None),
        P(),
        P(),
        P(None, "quad", None),
        P(),
    )
    out_specs = (
        P("frame", "quad", None),
        P("frame", "quad", None),
        P(None, ("frame", "quad"), None),
        P(("frame", "quad")),
    )
    body = functools.partial(local, mesh.shape["quad"], mesh.shape["frame"])
    return jax.shard_map(
        body, mesh=mesh, in_specs=in_specs, out_specs=out_specs, check_vma=False
    )
```

```python
import functools
import math

import jax
import jax.numpy as jnp
from jax import lax
from jax.experimental import pallas as pl
from jax.experimental.pallas import tpu as pltpu
from jax.sharding import PartitionSpec as P

HEADS = 4
HEAD_DIM = 160
EPSILON = 1e-05
SCALE = HEAD_DIM ** (-0.5)
F32 = jnp.float32
BF16 = jnp.bfloat16


def log2(n):
    return int(n).bit_length() - 1


def dot(a, b):
    return jnp.dot(a, b, preferred_element_type=F32)


def dot_t(a, b):
    return lax.dot_general(a, b, (((1,), (1,)), ((), ())), preferred_element_type=F32)


def t_dot(a, b):
    return lax.dot_general(a, b, (((0,), (0,)), ((), ())), preferred_element_type=F32)


def normalize(values):
    average = jnp.mean(values, axis=-1, keepdims=True)
    centred = values - average
    inv_scale = lax.rsqrt(jnp.mean(centred * centred, axis=-1, keepdims=True) + EPSILON)
    return centred * inv_scale, inv_scale


def normalize_back(grad_rows, unit_rows, inv_scale, gain):
    scaled = grad_rows * gain
    first_mean = jnp.mean(scaled, axis=-1, keepdims=True)
    second_mean = jnp.mean(scaled * unit_rows, axis=-1, keepdims=True)
    return inv_scale * (scaled - first_mean - unit_rows * second_mean)


def iota(shape, dim):
    return lax.broadcasted_iota(jnp.int32, shape, dim)


def head_mask(dtype):
    lane = iota((1, HEADS * HEAD_DIM), 1)
    return [
        jnp.where((lane >= h * HEAD_DIM) & (lane < (h + 1) * HEAD_DIM), 1.0, 0.0).astype(dtype)
        for h in range(HEADS)
    ]


def stack_heads(rows):
    return jnp.concatenate([rows * mask for mask in head_mask(rows.dtype)], axis=0)


def fold_heads(stacked):
    rows = stacked.shape[0] // HEADS
    total = None
    for h, mask in enumerate(head_mask(F32)):
        piece = stacked[h * rows : (h + 1) * rows] * mask
        total = piece if total is None else total + piece
    return total


def probabilities(query_stack, keys, same):
    scores = dot_t(query_stack, keys) * SCALE
    if same is not None:
        scores = jnp.where(same, scores, -1e30)
    highest = jnp.max(scores, axis=-1, keepdims=True)
    expo = jnp.exp(scores - highest)
    return expo / jnp.sum(expo, axis=-1, keepdims=True)


def attend(query, keys, values, same):
    probs = probabilities(stack_heads(query), keys, same)
    return fold_heads(dot(probs.astype(BF16), values)).astype(BF16)


def attend_back(query, keys, values, grad, same, probs=None):
    query_stack = stack_heads(query)
    grad_stack = stack_heads(grad)
    if probs is None:
        probs = probabilities(query_stack, keys, same)
    grad_probs = dot_t(grad_stack, values)
    inner = jnp.sum(probs * grad_probs, axis=-1, keepdims=True)
    grad_scores = (probs * (grad_probs - inner) * SCALE).astype(BF16)
    grad_query = fold_heads(dot(grad_scores, keys)).astype(BF16)
    grad_key = t_dot(grad_scores, query_stack).astype(BF16)
    grad_value = t_dot(probs.astype(BF16), grad_stack).astype(BF16)
    return grad_query, grad_key, grad_value


def rows_to_sent(quad, nq, fr, pq, transposed):
    rows = nq * fr * pq
    out_dim = 1 if transposed else 0
    out = iota((rows, rows), out_dim)
    src = iota((rows, rows), 1 - out_dim)
    cell = out >> log2(nq * fr)
    other = (out >> log2(fr)) & (nq - 1)
    frame = out & (fr - 1)
    want = (((other - quad) & (nq - 1)) << log2(fr * pq)) + (frame << log2(pq)) + cell
    return jnp.where(want == src, 1.0, 0.0).astype(BF16)


def received_to_rows(quad, nq, nf, fr, transposed):
    rows = nq * nf * fr
    out_dim = 1 if transposed else 0
    out = iota((rows, rows), out_dim)
    src = iota((rows, rows), 1 - out_dim)
    step = out >> log2(nf * fr)
    device = (out >> log2(fr)) & (nf - 1)
    frame = out & (fr - 1)
    want = (device << log2(nq * fr)) + (((step + quad) & (nq - 1)) << log2(fr)) + frame
    return jnp.where(want == src, 1.0, 0.0).astype(BF16)


def own_lanes(values, quad, nq):
    width = values.shape[1] // nq
    picked = values[:, :width]
    for t in range(1, nq):
        picked = jnp.where(quad == t, values[:, t * width : (t + 1) * width], picked)
    return picked


def place_lanes(parts, quad, nq):
    placed = []
    for t in range(nq):
        piece = parts[t]
        for q in range(1, nq):
            piece = jnp.where(quad == q, parts[(t - q) % nq], piece)
        placed.append(piece)
    return jnp.concatenate(placed, axis=1)


def frame_groups(nq, fr, pq):
    size = max(1, min(fr, 128 // (nq * pq)))
    return [(start, size) for start in range(0, fr, size)]


def pick_group(rows, group, nq, fr, pq):
    start, size = group
    if size == fr:
        return rows
    cut = rows.reshape(nq, fr, pq, rows.shape[-1])[:, start : start + size]
    return cut.reshape(nq * size * pq, rows.shape[-1])


def join_groups(pieces, nq, fr, pq):
    if len(pieces) == 1:
        return pieces[0]
    size = fr // len(pieces)
    width = pieces[0].shape[-1]
    joined = jnp.concatenate([p.reshape(nq, size, pq, width) for p in pieces], axis=1)
    return joined.reshape(nq * fr * pq, width)


def same_frame(nq, size, pq):
    if size == 1:
        return None
    rows = nq * size * pq
    shape = (HEADS * rows, rows)
    left = (iota(shape, 0) >> log2(pq)) & (size - 1)
    right = (iota(shape, 1) >> log2(pq)) & (size - 1)
    return left == right


def row_of(ref):
    return ref[...].reshape(1, -1)


def flat(ref):
    value = ref[...]
    return value.reshape(-1, value.shape[-1])


def flat_wide(ref):
    value = ref[...].astype(F32)
    return value.reshape(-1, value.shape[-1])


def spread(rows, like):
    return rows.reshape(like.shape).astype(like.dtype)


def spatial_kernel(dims, *refs):
    nq, nf, fr, pq = dims
    quad, xs, refs = refs[0][0], refs[1 : 1 + nq], refs[1 + nq :]
    gain1, gain2, pos, weights, kept_out, send_out = refs
    width = HEADS * HEAD_DIM
    wide = jnp.concatenate([flat_wide(x) for x in xs], axis=0)
    unit, _ = normalize(wide)
    normed = (unit * row_of(gain1)).astype(BF16)
    query = dot(normed, weights[0]).astype(BF16)
    keys = dot(normed, weights[1]).astype(BF16)
    values = dot(normed, weights[2]).astype(BF16)
    for i, part in enumerate((query, keys, values)):
        kept_out[:, i * width : (i + 1) * width] = part
    pieces = []
    for group in frame_groups(nq, fr, pq):
        same = same_frame(nq, group[1], pq)
        cut = [pick_group(part, group, nq, fr, pq) for part in (query, keys, values)]
        pieces.append(attend(*cut, same))
    out = join_groups(pieces, nq, fr, pq)
    hidden = (wide + dot_t(out, weights[3])).astype(BF16)
    kept_out[:, 3 * width :] = hidden
    unit_two, _ = normalize(hidden.astype(F32))
    table = jnp.broadcast_to(pos[...][:, None, :], (fr, pq, pos.shape[-1]))
    table = table.reshape(fr * pq, pos.shape[-1])
    table = jnp.concatenate([table] * nq, axis=0)
    normed_two = own_lanes(unit_two * row_of(gain2) + table, quad, nq).astype(BF16)
    send_out[...] = spread(dot(rows_to_sent(quad, nq, fr, pq, False), normed_two), send_out)


def order_kernel(dims, geo, cot, weights, send_out):
    nq, nf, fr, pq = dims
    order = rows_to_sent(geo[0], nq, fr, pq, False)[:, : fr * pq]
    send_out[...] = spread(dot(order, own_lanes(flat(cot), geo[0], nq)), send_out)


def join_kernel(dims, geo, normed, own_part, *refs):
    nq, nf, fr, pq = dims
    cots, send_out = refs[:-1], refs[-1]
    order = rows_to_sent(geo[0], nq, fr, pq, False)[:, fr * pq :]
    rows = own_lanes(jnp.concatenate([flat(c) for c in cots], axis=0), geo[0], nq)
    total = own_part[...].astype(F32) + dot(order, rows).reshape(own_part.shape)
    send_out[:, : nq * fr, :] = normed[...]
    send_out[:, nq * fr :, :] = total.astype(BF16)


def sent_part(received, i, rows):
    part = received[:, i * rows : (i + 1) * rows, :].astype(F32)
    return part.reshape(-1, part.shape[-1]).astype(BF16)


def motion_kernel(dims, geo, received, weights, own_out, *sends):
    nq, nf, fr, pq = dims
    order = received_to_rows(geo[0], nq, nf, fr, False)
    normed, cot = [dot(order, sent_part(received, i, nq * fr)).astype(BF16) for i in range(2)]
    tokens = nf * fr
    for k in range(4):
        width = weights.shape[-1]
        lanes = slice(k * width, (k + 1) * width)
        product = dot(normed if k < 3 else cot, weights[k])
        own_out[:, lanes] = product[:tokens]
        for s, send in enumerate(sends):
            send[:, lanes] = product[(s + 1) * tokens : (s + 2) * tokens].astype(BF16)


def quarter_of(four):
    return ((four & 1) << 1) | (four >> 1)


def quarter_lanes(values, quarter):
    width = values.shape[1] // 4
    picked = values[:, :width]
    for t in range(1, 4):
        picked = jnp.where(quarter == t, values[:, t * width : (t + 1) * width], picked)
    return picked


def cut_kernel(dims, geo, received, *outs):
    nq, nf, fr, pq = dims
    order = received_to_rows(geo[0], nq, nf, fr, False)
    for i in range(2):
        rows = dot(order, sent_part(received, i, nq * fr))
        for d in range(4):
            outs[d][i] = quarter_lanes(rows, quarter_of(geo[1] ^ d)).astype(BF16)


def table_kernel(dims, geo, out):
    shape = out.shape
    lane = iota(shape, 1)
    freq = jnp.exp((lane >> 1).astype(F32) * (-2.0 * math.log(10000.0) / shape[1]))
    turn = (lane & 1).astype(F32) * (0.5 * math.pi)
    out[...] = jnp.sin(iota(shape, 0).astype(F32) * freq + turn)


def temporal_kernel(dims, *refs):
    nq, nf, fr, pq = dims
    parts, out = refs[:nq], refs[nq]
    width = HEADS * HEAD_DIM
    total = parts[0][...]
    for part in parts[1:]:
        total = total + part[...].astype(F32)
    query, keys, values, grad = [
        total[:, k * width : (k + 1) * width].astype(BF16) for k in range(4)
    ]
    probs = probabilities(stack_heads(query), keys, None)
    motion_out = fold_heads(dot(probs.astype(BF16), values)).astype(BF16)
    grads = attend_back(query, keys, values, grad, None, probs)
    for k, piece in enumerate(grads + (motion_out,)):
        out[:, k * width : (k + 1) * width] = piece


def part_of(terms, k):
    width = HEADS * HEAD_DIM
    return jnp.concatenate([t[:, k * width : (k + 1) * width] for t in terms], axis=0)


def back_kernel(dims, quad_ref, *refs):
    nq, nf, fr, pq = dims
    terms, (weights, out, quarter_out) = refs[:nq], refs[nq:]
    order = received_to_rows(quad_ref[0], nq, nf, fr, True)
    quarter, rows = quarter_of(quad_ref[1]), quarter_out.shape[1]
    for k in range(3):
        if rows % 16 == 0:
            own = weights[k, pl.ds(pl.multiple_of(quarter * rows, 16), rows), :]
        else:
            wide = weights[k].astype(F32)
            own = wide[:rows]
            for t in range(1, 4):
                own = jnp.where(quarter == t, wide[t * rows : (t + 1) * rows], own)
            own = own.astype(BF16)
        quarter_out[k] = own
    grad = None
    for k in range(3):
        product = dot_t(part_of(terms, k), weights[k])
        grad = product if grad is None else grad + product
    delta = dot_t(part_of(terms, 3), weights[3])
    for i, rows in enumerate((grad, delta)):
        rows = dot(order, rows.astype(BF16))
        out[:, i * nq * fr : (i + 1) * nq * fr, :] = rows.reshape(nf, nq * fr, -1).astype(BF16)


def weight_sums(geo, nq, normed, cot, weights, pos, terms):
    products, grad = [], None
    for k in range(4):
        right = part_of(terms, k)
        products.append(t_dot(normed if k < 3 else cot, right))
        if k < 3:
            back = dot_t(right, weights[k])
            grad = back if grad is None else grad + back
    table = quarter_lanes(own_lanes(pos[...], geo[0], nq), quarter_of(geo[1]))
    table = jnp.concatenate([table] * len(terms), axis=0)
    return products, jnp.sum(grad * (normed.astype(F32) - table), axis=0, keepdims=True)


def first_weight_kernel(dims, geo, *refs):
    nq, nf, fr, pq = dims
    factors, (weights, pos), refs = refs[:4], refs[4:6], refs[6:]
    terms, (blocks, gain_out, late_out) = refs[: 2 * nq + 2], refs[2 * nq + 2 :]
    _, stage, block, _ = blocks.shape
    tokens = nf * fr
    left = []
    for i in range(2):
        early = [factors[0][i], factors[1][i], factors[2][i, :tokens], factors[3][i, :tokens]]
        left.append(jnp.concatenate(early, axis=0))
        late = [factors[2][i, tokens:], factors[3][i, tokens:]]
        late_out[i] = jnp.concatenate(late, axis=0)
    products, gain_out[...] = weight_sums(geo, nq, *left, weights, pos, terms)
    for k in range(4):
        for z in range(stage):
            blocks[k, z] = products[k][z * block : (z + 1) * block]


def second_weight_kernel(dims, geo, sums, gain_sum, left, weights, pos, gain2, *refs):
    nq, nf, fr, pq = dims
    terms, outs, blocks = refs[: 2 * nq - 2], refs[2 * nq - 2 : -1], refs[-1]
    _, stage, block, width = blocks.shape
    products, gain = weight_sums(geo, nq, left[0], left[1], weights, pos, terms)
    for k in range(4):
        for z in range(stage):
            blocks[k, z] = sums[k, z] + products[k][z * block : (z + 1) * block]
    gain = gain + gain_sum[...]
    rows = gain.shape[1]
    gain = gain / quarter_lanes(own_lanes(row_of(gain2), geo[0], nq), quarter_of(geo[1]))
    extra = jnp.concatenate([gain, jnp.zeros((1, width - rows), F32)], axis=1)
    extra = jnp.where(iota((8, width), 0) == 0, extra, 0.0)
    for r in range(stage):
        z = (geo[2] + r) & (stage - 1)
        rows_out = jnp.concatenate([blocks[0, z], blocks[1, z], extra], axis=0)
        outs[r][...] = rows_out.astype(BF16)
        rows_out = jnp.concatenate([blocks[2, z], blocks[3, z]], axis=0)
        outs[stage + r][...] = rows_out.astype(BF16)


def middle_kernel(dims, *refs):
    nq, nf, fr, pq = dims
    quad, received, cots = refs[0][0], refs[1 : 1 + nq], refs[1 + nq : 1 + 2 * nq]
    kept, gain2, block_out, grad_out = refs[1 + 2 * nq :]
    own = fr * pq
    order = rows_to_sent(quad, nq, fr, pq, True)

    def lanes(i):
        parts = []
        for r in received:
            parts.append(dot(order, sent_part(r, i, nq * fr)))
        return place_lanes(parts, quad, nq)

    hidden = kept[:, 3 * HEADS * HEAD_DIM :].astype(F32)
    grad_normed, delta = lanes(0), lanes(1)
    block_out[...] = spread(hidden[:own] + delta[:own], block_out)
    unit_two, inv_two = normalize(hidden)
    cot = jnp.concatenate([flat_wide(c) for c in cots], axis=0)
    back = normalize_back(grad_normed, unit_two, inv_two, row_of(gain2))
    grad_out[...] = (cot + back).astype(BF16)


def tail_kernel(dims, grad_hidden, xs, kept, gain1, weights, in_grad):
    nq, nf, fr, pq = dims
    own, width = fr * pq, HEADS * HEAD_DIM
    grad_out = dot(grad_hidden[...], weights[3]).astype(BF16)
    parts = [kept[:, i * width : (i + 1) * width] for i in range(3)] + [grad_out]
    pieces = []
    for group in frame_groups(nq, fr, pq):
        same = same_frame(nq, group[1], pq)
        pieces.append(attend_back(*[pick_group(p, group, nq, fr, pq) for p in parts], same))
    grads = [join_groups([p[i] for p in pieces], nq, fr, pq)[:own] for i in range(3)]
    grad_one = dot_t(grads[0], weights[0]) + dot_t(grads[1], weights[1]) + dot_t(grads[2], weights[2])
    unit_one, inv_one = normalize(flat_wide(xs))
    back = normalize_back(grad_one, unit_one, inv_one, row_of(gain1))
    in_grad[...] = spread(grad_hidden[...][:own].astype(F32) + back, in_grad)


def call(kernel, name, outs, args, vmem, micros, scratch=()):
    in_specs = []
    for arg in args:
        space = pltpu.SMEM if arg.dtype == jnp.int32 else pltpu.VMEM
        in_specs.append(pl.BlockSpec(memory_space=space))
    return list(
        pl.pallas_call(
            kernel,
            out_shape=outs,
            in_specs=in_specs,
            out_specs=[pl.BlockSpec(memory_space=pltpu.VMEM) for _ in outs],
            scratch_shapes=list(scratch),
            compiler_params=pltpu.CompilerParams(vmem_limit_bytes=vmem * 1024 * 1024),
            cost_estimate=pl.CostEstimate(
                flops=int(micros * 1e9),
                bytes_accessed=2**20 if micros > 0.1 else 2**12,
                transcendentals=0,
            ),
            name=name,
        )(*args)
    )


def after(value, *others):
    return lax.optimization_barrier((value,) + others)[0]


def sds(*shape, dtype=BF16):
    return jax.ShapeDtypeStruct(shape, dtype)


def positional(first, frames, channels):
    frame_pos = (first + lax.broadcasted_iota(jnp.int32, (frames, channels), 0)).astype(F32)
    lane = lax.broadcasted_iota(jnp.int32, (frames, channels), 1)
    freq_index = (lane >> 1).astype(F32)
    phases = frame_pos * jnp.exp(freq_index * (-2.0 * math.log(10000.0) / channels))
    return jnp.sin(phases + (lane & 1).astype(F32) * (0.5 * math.pi))


def local(nq, nf, activations, cotangent, spatial_weights, spatial_gain, motion_weights, motion_gain):
    fr, pq, channels = activations.shape
    dims = (nq, nf, fr, pq)
    width = spatial_weights.shape[-1]
    half = channels // nq
    rows = nq * fr * pq
    tokens = nf * fr
    small = 16 if rows <= 256 else 40
    big = 16 if rows <= 256 else 52
    quad = lax.axis_index("quad")
    frame = lax.axis_index("frame")


    def from_quad(x, s):
        return lax.ppermute(x, "quad", [((d + s) % nq, d) for d in range(nq)])

    def to_quad(x, s):
        return lax.ppermute(x, "quad", [(d, (d + s) % nq) for d in range(nq)])

    def swap(x):
        return lax.all_to_all(x, "frame", split_axis=0, concat_axis=0, tiled=True)

    def run(kernel, name, outs, args, micros, vmem=small, **options):
        kernel = functools.partial(kernel, dims)
        return call(kernel, name, outs, args, vmem, micros, **options)

    def move(x, pairs):
        return lax.ppermute(x, "frame", pairs)

    geo = jnp.stack([quad, frame % 4, frame // 4]).astype(jnp.int32)

    def flipped(bits):
        return [(g, g ^ bits) for g in range(nf)]

    ring = [(g, (g + 4) % nf) for g in range(nf)]

    gain1, gain2 = spatial_gain, motion_gain
    sent = sds(nf, nq * fr, half)
    acts = [activations] + [from_quad(activations, s) for s in range(1, nq)]
    both = sds(nf, 2 * nq * fr, half)
    (own_part,) = run(
        order_kernel, "order_cotangent", [sent], [geo, cotangent, spatial_weights], 0.5, big
    )
    cot_later = after(cotangent, acts[-1])
    cots = [cotangent] + [from_quad(cot_later, s) for s in range(1, nq)]
    pos = positional(frame * fr, fr, channels)
    kept, normed = run(
        spatial_kernel,
        "spatial_forward",
        [sds(rows, 3 * width + channels), sent],
        [geo] + acts + [gain1, gain2, pos, spatial_weights],
        3,
        big,
    )
    (send,) = run(join_kernel, "join_sent", [both], [geo, normed, own_part] + cots[1:], 0.5)
    received = swap(send)
    parts = run(
        motion_kernel,
        "motion_projection",
        [sds(tokens, 4 * width, dtype=F32)] + [sds(tokens, 4 * width)] * (nq - 1),
        [geo, received, motion_weights],
        1.5,
    )
    parts = [parts[0]] + [to_quad(p, s + 1) for s, p in enumerate(parts[1:])]
    (terms,) = run(temporal_kernel, "temporal_attention", [sds(tokens, 4 * width)], parts, 2)
    factors = run(
        cut_kernel,
        "cut_factors",
        [sds(2, rows, half // 4)] * 4,
        [geo, after(received, terms)],
        0.5,
    )
    (table,) = run(
        table_kernel,
        "positional_table",
        [sds(tokens, channels, dtype=F32)],
        [after(geo, terms)],
        1.5,
    )
    all_terms = [terms] + [after(from_quad(terms, s), factors[0], table) for s in range(1, nq)]
    pair_terms = [move(t, flipped(2)) for t in all_terms]
    core_terms = [move(t, flipped(1)) for t in all_terms]
    factors = [factors[0]] + [move(factors[d], flipped(d)) for d in range(1, 4)]
    back_send, quarter = run(
        back_kernel,
        "temporal_back_projection",
        [sds(nf, 2 * nq * fr, half), sds(3, half // 4, width)],
        [geo] + all_terms + [motion_weights],
        0.01,
    )
    pair_terms[0] = after(pair_terms[0], back_send)
    last_terms = [move(pair_terms[0], flipped(1))]

    stage, block = nf // 4, half // nf
    sums, gain_sum, late_left = run(
        first_weight_kernel,
        "weight_terms_first_tokens",
        [
            sds(4, stage, block, width, dtype=F32),
            sds(1, half // 4, dtype=F32),
            sds(2, 2 * (nq - 1) * tokens, half // 4),
        ],
        [geo] + factors + [quarter, table] + all_terms + core_terms
        + pair_terms[:1] + last_terms,
        0.01,
    )
    late_terms = [after(t, back_send, sums) for t in pair_terms[1:]]
    late_terms += [move(t, flipped(1)) for t in late_terms]
    parts_w = run(
        second_weight_kernel,
        "weight_terms_last_tokens",
        [sds(2 * block + 8, width)] * stage + [sds(2 * block, width)] * stage,
        [geo, sums, gain_sum, late_left, quarter, table, gain2] + late_terms,
        0.01,
        scratch=[pltpu.VMEM((4, stage, block, width), F32)],
    )

    def add(a, b):
        return (a.astype(F32) + b.astype(F32)).astype(BF16)

    back_recv = swap(back_send)
    backs = [back_recv] + [from_quad(back_recv, s) for s in range(1, nq)]
    block_output, grad_hidden = run(
        middle_kernel,
        "block_output_hidden_gradient",
        [sds(fr, pq, channels), sds(rows, channels)],
        [geo] + backs + cots + [kept, gain2],
        6,
        big,
    )
    totals = [parts_w[stage - 1], parts_w[2 * stage - 1]]
    for step in range(1, stage):
        for i in range(2):
            if step == stage - 2:
                totals[i] = after(totals[i], back_recv)
            moved = move(totals[i], ring)
            if step == stage - 1:
                moved = after(moved, grad_hidden)
            totals[i] = add(moved, parts_w[(i + 1) * stage - 1 - step])
    final = []
    for g in range(nf):
        for q in range(nq):
            j = quarter_of(g % 4) * stage + g // 4
            final.append((g * nq + q, nf * q + j))
    grad_hidden = after(grad_hidden, *totals)
    totals = [lax.ppermute(t, ("frame", "quad"), final) for t in totals]
    (input_grad,) = run(
        tail_kernel,
        "spatial_backward",
        [sds(fr, pq, channels)],
        [grad_hidden, activations, kept, gain1, spatial_weights],
        3.5,
        big,
    )
    everyone = nf * nq
    factor = 1.0 / math.sqrt(everyone * fr * pq)
    weight_grad = jnp.concatenate([totals[0][: 2 * block], totals[1]], axis=0)
    weight_grad = weight_grad.reshape(4, block, width).astype(F32) * factor
    place = ((frame * nq + quad) % stage) * block
    gain_grad = lax.dynamic_slice(totals[0][2 * block], (place,), (block,)).astype(F32) * factor
    return block_output, input_grad, weight_grad, gain_grad


def solution(mesh):
    in_specs = (
        P("frame", "quad", None),
        P("frame", "quad", None),
        P(),
        P(),
        P(None, "quad", None),
        P(),
    )
    out_specs = (
        P("frame", "quad", None),
        P("frame", "quad", None),
        P(None, ("frame", "quad"), None),
        P(("frame", "quad")),
    )
    body = functools.partial(local, mesh.shape["quad"], mesh.shape["frame"])
    return jax.shard_map(
        body, mesh=mesh, in_specs=in_specs, out_specs=out_specs, check_vma=False
    )
```

```python
import functools
import math

import jax
import jax.numpy as jnp
from jax import lax
from jax.experimental import pallas as pl
from jax.experimental.pallas import tpu as pltpu
from jax.sharding import PartitionSpec as P

HEADS = 4
HEAD_DIM = 160
EPSILON = 1e-05
SCALE = HEAD_DIM ** (-0.5)
F32 = jnp.float32
BF16 = jnp.bfloat16


def log2(n):
    return int(n).bit_length() - 1


def dot(a, b):
    return jnp.dot(a, b, preferred_element_type=F32)


def dot_t(a, b):
    return lax.dot_general(a, b, (((1,), (1,)), ((), ())), preferred_element_type=F32)


def t_dot(a, b):
    return lax.dot_general(a, b, (((0,), (0,)), ((), ())), preferred_element_type=F32)


def normalize(values):
    average = jnp.mean(values, axis=-1, keepdims=True)
    centred = values - average
    inv_scale = lax.rsqrt(jnp.mean(centred * centred, axis=-1, keepdims=True) + EPSILON)
    return centred * inv_scale, inv_scale


def normalize_back(grad_rows, unit_rows, inv_scale, gain):
    scaled = grad_rows * gain
    first_mean = jnp.mean(scaled, axis=-1, keepdims=True)
    second_mean = jnp.mean(scaled * unit_rows, axis=-1, keepdims=True)
    return inv_scale * (scaled - first_mean - unit_rows * second_mean)


def iota(shape, dim):
    return lax.broadcasted_iota(jnp.int32, shape, dim)


def head_mask(dtype):
    lane = iota((1, HEADS * HEAD_DIM), 1)
    return [
        jnp.where((lane >= h * HEAD_DIM) & (lane < (h + 1) * HEAD_DIM), 1.0, 0.0).astype(dtype)
        for h in range(HEADS)
    ]


def stack_heads(rows):
    return jnp.concatenate([rows * mask for mask in head_mask(rows.dtype)], axis=0)


def fold_heads(stacked):
    rows = stacked.shape[0] // HEADS
    total = None
    for h, mask in enumerate(head_mask(F32)):
        piece = stacked[h * rows : (h + 1) * rows] * mask
        total = piece if total is None else total + piece
    return total


def probabilities(query_stack, keys, same):
    scores = dot_t(query_stack, keys) * SCALE
    if same is not None:
        scores = jnp.where(same, scores, -1e30)
    highest = jnp.max(scores, axis=-1, keepdims=True)
    expo = jnp.exp(scores - highest)
    return expo / jnp.sum(expo, axis=-1, keepdims=True)


def attend(query, keys, values, same):
    probs = probabilities(stack_heads(query), keys, same)
    return fold_heads(dot(probs.astype(BF16), values)).astype(BF16)


def attend_back(query, keys, values, grad, same, probs=None):
    query_stack = stack_heads(query)
    grad_stack = stack_heads(grad)
    if probs is None:
        probs = probabilities(query_stack, keys, same)
    grad_probs = dot_t(grad_stack, values)
    inner = jnp.sum(probs * grad_probs, axis=-1, keepdims=True)
    grad_scores = (probs * (grad_probs - inner) * SCALE).astype(BF16)
    grad_query = fold_heads(dot(grad_scores, keys)).astype(BF16)
    grad_key = t_dot(grad_scores, query_stack).astype(BF16)
    grad_value = t_dot(probs.astype(BF16), grad_stack).astype(BF16)
    return grad_query, grad_key, grad_value


def rows_to_sent(quad, nq, fr, pq, transposed):
    rows = nq * fr * pq
    out_dim = 1 if transposed else 0
    out = iota((rows, rows), out_dim)
    src = iota((rows, rows), 1 - out_dim)
    cell = out >> log2(nq * fr)
    other = (out >> log2(fr)) & (nq - 1)
    frame = out & (fr - 1)
    want = (((other - quad) & (nq - 1)) << log2(fr * pq)) + (frame << log2(pq)) + cell
    return jnp.where(want == src, 1.0, 0.0).astype(BF16)


def received_to_rows(quad, nq, nf, fr, transposed):
    rows = nq * nf * fr
    out_dim = 1 if transposed else 0
    out = iota((rows, rows), out_dim)
    src = iota((rows, rows), 1 - out_dim)
    step = out >> log2(nf * fr)
    device = (out >> log2(fr)) & (nf - 1)
    frame = out & (fr - 1)
    want = (device << log2(nq * fr)) + (((step + quad) & (nq - 1)) << log2(fr)) + frame
    return jnp.where(want == src, 1.0, 0.0).astype(BF16)


def own_lanes(values, quad, nq):
    width = values.shape[1] // nq
    picked = values[:, :width]
    for t in range(1, nq):
        picked = jnp.where(quad == t, values[:, t * width : (t + 1) * width], picked)
    return picked


def place_lanes(parts, quad, nq):
    placed = []
    for t in range(nq):
        piece = parts[t]
        for q in range(1, nq):
            piece = jnp.where(quad == q, parts[(t - q) % nq], piece)
        placed.append(piece)
    return jnp.concatenate(placed, axis=1)


def frame_groups(nq, fr, pq):
    size = max(1, min(fr, 128 // (nq * pq)))
    return [(start, size) for start in range(0, fr, size)]


def pick_group(rows, group, nq, fr, pq):
    start, size = group
    if size == fr:
        return rows
    cut = rows.reshape(nq, fr, pq, rows.shape[-1])[:, start : start + size]
    return cut.reshape(nq * size * pq, rows.shape[-1])


def join_groups(pieces, nq, fr, pq):
    if len(pieces) == 1:
        return pieces[0]
    size = fr // len(pieces)
    width = pieces[0].shape[-1]
    joined = jnp.concatenate([p.reshape(nq, size, pq, width) for p in pieces], axis=1)
    return joined.reshape(nq * fr * pq, width)


def same_frame(nq, size, pq):
    if size == 1:
        return None
    rows = nq * size * pq
    shape = (HEADS * rows, rows)
    left = (iota(shape, 0) >> log2(pq)) & (size - 1)
    right = (iota(shape, 1) >> log2(pq)) & (size - 1)
    return left == right


def row_of(ref):
    return ref[...].reshape(1, -1)


def flat(ref):
    value = ref[...]
    return value.reshape(-1, value.shape[-1])


def flat_wide(ref):
    value = ref[...].astype(F32)
    return value.reshape(-1, value.shape[-1])


def spread(rows, like):
    return rows.reshape(like.shape).astype(like.dtype)


def spatial_kernel(dims, *refs):
    nq, nf, fr, pq = dims
    quad, xs, refs = refs[0][0], refs[1 : 1 + nq], refs[1 + nq :]
    gain1, gain2, pos, weights, kept_out, send_out = refs
    width = HEADS * HEAD_DIM
    wide = jnp.concatenate([flat_wide(x) for x in xs], axis=0)
    unit, _ = normalize(wide)
    normed = (unit * row_of(gain1)).astype(BF16)
    query = dot(normed, weights[0]).astype(BF16)
    keys = dot(normed, weights[1]).astype(BF16)
    values = dot(normed, weights[2]).astype(BF16)
    for i, part in enumerate((query, keys, values)):
        kept_out[:, i * width : (i + 1) * width] = part
    pieces = []
    for group in frame_groups(nq, fr, pq):
        same = same_frame(nq, group[1], pq)
        cut = [pick_group(part, group, nq, fr, pq) for part in (query, keys, values)]
        pieces.append(attend(*cut, same))
    out = join_groups(pieces, nq, fr, pq)
    hidden = (wide + dot_t(out, weights[3])).astype(BF16)
    kept_out[:, 3 * width :] = hidden
    unit_two, _ = normalize(hidden.astype(F32))
    table = jnp.broadcast_to(pos[...][:, None, :], (fr, pq, pos.shape[-1]))
    table = table.reshape(fr * pq, pos.shape[-1])
    table = jnp.concatenate([table] * nq, axis=0)
    normed_two = own_lanes(unit_two * row_of(gain2) + table, quad, nq).astype(BF16)
    send_out[...] = spread(dot(rows_to_sent(quad, nq, fr, pq, False), normed_two), send_out)


def order_kernel(dims, geo, cot, weights, send_out):
    nq, nf, fr, pq = dims
    order = rows_to_sent(geo[0], nq, fr, pq, False)[:, : fr * pq]
    send_out[...] = spread(dot(order, own_lanes(flat(cot), geo[0], nq)), send_out)


def join_kernel(dims, geo, normed, own_part, *refs):
    nq, nf, fr, pq = dims
    cots, send_out = refs[:-1], refs[-1]
    order = rows_to_sent(geo[0], nq, fr, pq, False)[:, fr * pq :]
    rows = own_lanes(jnp.concatenate([flat(c) for c in cots], axis=0), geo[0], nq)
    total = own_part[...].astype(F32) + dot(order, rows).reshape(own_part.shape)
    send_out[:, : nq * fr, :] = normed[...]
    send_out[:, nq * fr :, :] = total.astype(BF16)


def sent_part(received, i, rows):
    part = received[:, i * rows : (i + 1) * rows, :].astype(F32)
    return part.reshape(-1, part.shape[-1]).astype(BF16)


def motion_kernel(dims, geo, received, weights, own_out, *sends):
    nq, nf, fr, pq = dims
    order = received_to_rows(geo[0], nq, nf, fr, False)
    normed, cot = [dot(order, sent_part(received, i, nq * fr)).astype(BF16) for i in range(2)]
    tokens = nf * fr
    for k in range(4):
        width = weights.shape[-1]
        lanes = slice(k * width, (k + 1) * width)
        product = dot(normed if k < 3 else cot, weights[k])
        own_out[:, lanes] = product[:tokens]
        for s, send in enumerate(sends):
            send[:, lanes] = product[(s + 1) * tokens : (s + 2) * tokens].astype(BF16)


def quarter_of(four):
    return ((four & 1) << 1) | (four >> 1)


def quarter_lanes(values, quarter):
    width = values.shape[1] // 4
    picked = values[:, :width]
    for t in range(1, 4):
        picked = jnp.where(quarter == t, values[:, t * width : (t + 1) * width], picked)
    return picked


def cut_kernel(dims, geo, received, *outs):
    nq, nf, fr, pq = dims
    order = received_to_rows(geo[0], nq, nf, fr, False)
    for i in range(2):
        rows = dot(order, sent_part(received, i, nq * fr))
        for d in range(4):
            outs[d][i] = quarter_lanes(rows, quarter_of(geo[1] ^ d)).astype(BF16)


def table_kernel(dims, geo, out):
    shape = out.shape
    lane = iota(shape, 1)
    freq = jnp.exp((lane >> 1).astype(F32) * (-2.0 * math.log(10000.0) / shape[1]))
    turn = (lane & 1).astype(F32) * (0.5 * math.pi)
    out[...] = jnp.sin(iota(shape, 0).astype(F32) * freq + turn)


def temporal_kernel(dims, *refs):
    nq, nf, fr, pq = dims
    parts, out = refs[:nq], refs[nq]
    width = HEADS * HEAD_DIM
    total = parts[0][...]
    for part in parts[1:]:
        total = total + part[...].astype(F32)
    query, keys, values, grad = [
        total[:, k * width : (k + 1) * width].astype(BF16) for k in range(4)
    ]
    probs = probabilities(stack_heads(query), keys, None)
    motion_out = fold_heads(dot(probs.astype(BF16), values)).astype(BF16)
    grads = attend_back(query, keys, values, grad, None, probs)
    for k, piece in enumerate(grads + (motion_out,)):
        out[:, k * width : (k + 1) * width] = piece


def part_of(terms, k):
    width = HEADS * HEAD_DIM
    return jnp.concatenate([t[:, k * width : (k + 1) * width] for t in terms], axis=0)


def back_kernel(dims, quad_ref, *refs):
    nq, nf, fr, pq = dims
    terms, (weights, out, quarter_out) = refs[:nq], refs[nq:]
    order = received_to_rows(quad_ref[0], nq, nf, fr, True)
    quarter, rows = quarter_of(quad_ref[1]), quarter_out.shape[1]
    for k in range(3):
        if rows % 16 == 0:
            own = weights[k, pl.ds(pl.multiple_of(quarter * rows, 16), rows), :]
        else:
            wide = weights[k].astype(F32)
            own = wide[:rows]
            for t in range(1, 4):
                own = jnp.where(quarter == t, wide[t * rows : (t + 1) * rows], own)
            own = own.astype(BF16)
        quarter_out[k] = own
    grad = None
    for k in range(3):
        product = dot_t(part_of(terms, k), weights[k])
        grad = product if grad is None else grad + product
    delta = dot_t(part_of(terms, 3), weights[3])
    for i, rows in enumerate((grad, delta)):
        rows = dot(order, rows.astype(BF16))
        out[:, i * nq * fr : (i + 1) * nq * fr, :] = rows.reshape(nf, nq * fr, -1).astype(BF16)


def weight_sums(geo, nq, normed, cot, weights, pos, terms):
    products, grad = [], None
    for k in range(4):
        right = part_of(terms, k)
        products.append(t_dot(normed if k < 3 else cot, right))
        if k < 3:
            back = dot_t(right, weights[k])
            grad = back if grad is None else grad + back
    table = quarter_lanes(own_lanes(pos[...], geo[0], nq), quarter_of(geo[1]))
    table = jnp.concatenate([table] * len(terms), axis=0)
    return products, jnp.sum(grad * (normed.astype(F32) - table), axis=0, keepdims=True)


def first_weight_kernel(dims, geo, *refs):
    nq, nf, fr, pq = dims
    factors, (weights, pos), refs = refs[:4], refs[4:6], refs[6:]
    terms, (blocks, gain_out, late_out) = refs[: 2 * nq + 2], refs[2 * nq + 2 :]
    _, stage, block, _ = blocks.shape
    tokens = nf * fr
    left = []
    for i in range(2):
        early = [factors[0][i], factors[1][i], factors[2][i, :tokens], factors[3][i, :tokens]]
        left.append(jnp.concatenate(early, axis=0))
        late = [factors[2][i, tokens:], factors[3][i, tokens:]]
        late_out[i] = jnp.concatenate(late, axis=0)
    products, gain_out[...] = weight_sums(geo, nq, *left, weights, pos, terms)
    for k in range(4):
        for z in range(stage):
            blocks[k, z] = products[k][z * block : (z + 1) * block]


def second_weight_kernel(dims, geo, sums, gain_sum, left, weights, pos, gain2, *refs):
    nq, nf, fr, pq = dims
    terms, outs, blocks = refs[: 2 * nq - 2], refs[2 * nq - 2 : -1], refs[-1]
    _, stage, block, width = blocks.shape
    products, gain = weight_sums(geo, nq, left[0], left[1], weights, pos, terms)
    for k in range(4):
        for z in range(stage):
            blocks[k, z] = sums[k, z] + products[k][z * block : (z + 1) * block]
    gain = gain + gain_sum[...]
    rows = gain.shape[1]
    gain = gain / quarter_lanes(own_lanes(row_of(gain2), geo[0], nq), quarter_of(geo[1]))
    extra = jnp.concatenate([gain, jnp.zeros((1, width - rows), F32)], axis=1)
    extra = jnp.where(iota((8, width), 0) == 0, extra, 0.0)
    for r in range(stage):
        z = (geo[2] + r) & (stage - 1)
        rows_out = jnp.concatenate([blocks[0, z], blocks[1, z], extra], axis=0)
        outs[r][...] = rows_out.astype(BF16)
        rows_out = jnp.concatenate([blocks[2, z], blocks[3, z]], axis=0)
        outs[stage + r][...] = rows_out.astype(BF16)


def middle_kernel(dims, *refs):
    nq, nf, fr, pq = dims
    quad, received, cots = refs[0][0], refs[1 : 1 + nq], refs[1 + nq : 1 + 2 * nq]
    kept, gain2, block_out, grad_out = refs[1 + 2 * nq :]
    own = fr * pq
    order = rows_to_sent(quad, nq, fr, pq, True)

    def lanes(i):
        parts = []
        for r in received:
            parts.append(dot(order, sent_part(r, i, nq * fr)))
        return place_lanes(parts, quad, nq)

    hidden = kept[:, 3 * HEADS * HEAD_DIM :].astype(F32)
    grad_normed, delta = lanes(0), lanes(1)
    block_out[...] = spread(hidden[:own] + delta[:own], block_out)
    unit_two, inv_two = normalize(hidden)
    cot = jnp.concatenate([flat_wide(c) for c in cots], axis=0)
    back = normalize_back(grad_normed, unit_two, inv_two, row_of(gain2))
    grad_out[...] = (cot + back).astype(BF16)


def tail_kernel(dims, grad_hidden, xs, kept, gain1, weights, in_grad):
    nq, nf, fr, pq = dims
    own, width = fr * pq, HEADS * HEAD_DIM
    grad_out = dot(grad_hidden[...], weights[3]).astype(BF16)
    parts = [kept[:, i * width : (i + 1) * width] for i in range(3)] + [grad_out]
    pieces = []
    for group in frame_groups(nq, fr, pq):
        same = same_frame(nq, group[1], pq)
        pieces.append(attend_back(*[pick_group(p, group, nq, fr, pq) for p in parts], same))
    grads = [join_groups([p[i] for p in pieces], nq, fr, pq)[:own] for i in range(3)]
    grad_one = dot_t(grads[0], weights[0]) + dot_t(grads[1], weights[1]) + dot_t(grads[2], weights[2])
    unit_one, inv_one = normalize(flat_wide(xs))
    back = normalize_back(grad_one, unit_one, inv_one, row_of(gain1))
    in_grad[...] = spread(grad_hidden[...][:own].astype(F32) + back, in_grad)


def call(kernel, name, outs, args, vmem, micros, scratch=()):
    in_specs = []
    for arg in args:
        space = pltpu.SMEM if arg.dtype == jnp.int32 else pltpu.VMEM
        in_specs.append(pl.BlockSpec(memory_space=space))
    return list(
        pl.pallas_call(
            kernel,
            out_shape=outs,
            in_specs=in_specs,
            out_specs=[pl.BlockSpec(memory_space=pltpu.VMEM) for _ in outs],
            scratch_shapes=list(scratch),
            compiler_params=pltpu.CompilerParams(vmem_limit_bytes=vmem * 1024 * 1024),
            cost_estimate=pl.CostEstimate(
                flops=int(micros * 1e9),
                bytes_accessed=2**20 if micros > 0.1 else 2**12,
                transcendentals=0,
            ),
            name=name,
        )(*args)
    )


def after(value, *others):
    return lax.optimization_barrier((value,) + others)[0]


def sds(*shape, dtype=BF16):
    return jax.ShapeDtypeStruct(shape, dtype)


def positional(first, frames, channels):
    frame_pos = (first + lax.broadcasted_iota(jnp.int32, (frames, channels), 0)).astype(F32)
    lane = lax.broadcasted_iota(jnp.int32, (frames, channels), 1)
    freq_index = (lane >> 1).astype(F32)
    phases = frame_pos * jnp.exp(freq_index * (-2.0 * math.log(10000.0) / channels))
    return jnp.sin(phases + (lane & 1).astype(F32) * (0.5 * math.pi))


def local(nq, nf, activations, cotangent, spatial_weights, spatial_gain, motion_weights, motion_gain):
    fr, pq, channels = activations.shape
    dims = (nq, nf, fr, pq)
    width = spatial_weights.shape[-1]
    half = channels // nq
    rows = nq * fr * pq
    tokens = nf * fr
    small = 16 if rows <= 256 else 40
    big = 16 if rows <= 256 else 52
    quad = lax.axis_index("quad")
    frame = lax.axis_index("frame")


    def from_quad(x, s):
        return lax.ppermute(x, "quad", [((d + s) % nq, d) for d in range(nq)])

    def to_quad(x, s):
        return lax.ppermute(x, "quad", [(d, (d + s) % nq) for d in range(nq)])

    def swap(x):
        return lax.all_to_all(x, "frame", split_axis=0, concat_axis=0, tiled=True)

    def run(kernel, name, outs, args, micros, vmem=small, **options):
        kernel = functools.partial(kernel, dims)
        return call(kernel, name, outs, args, vmem, micros, **options)

    def move(x, pairs):
        return lax.ppermute(x, "frame", pairs)

    geo = jnp.stack([quad, frame % 4, frame // 4]).astype(jnp.int32)

    def flipped(bits):
        return [(g, g ^ bits) for g in range(nf)]

    ring = [(g, (g + 4) % nf) for g in range(nf)]

    gain1, gain2 = spatial_gain, motion_gain
    sent = sds(nf, nq * fr, half)
    acts = [activations] + [from_quad(activations, s) for s in range(1, nq)]
    both = sds(nf, 2 * nq * fr, half)
    (own_part,) = run(
        order_kernel, "order_cotangent", [sent], [geo, cotangent, spatial_weights], 0.5, big
    )
    cot_later = after(cotangent, acts[-1])
    cots = [cotangent] + [from_quad(cot_later, s) for s in range(1, nq)]
    pos = positional(frame * fr, fr, channels)
    kept, normed = run(
        spatial_kernel,
        "spatial_forward",
        [sds(rows, 3 * width + channels), sent],
        [geo] + acts + [gain1, gain2, pos, spatial_weights],
        3,
        big,
    )
    (send,) = run(join_kernel, "join_sent", [both], [geo, normed, own_part] + cots[1:], 0.5)
    received = swap(send)
    parts = run(
        motion_kernel,
        "motion_projection",
        [sds(tokens, 4 * width, dtype=F32)] + [sds(tokens, 4 * width)] * (nq - 1),
        [geo, received, motion_weights],
        1.5,
    )
    factors = run(
        cut_kernel,
        "cut_factors",
        [sds(2, rows, half // 4)] * 4,
        [geo, after(received, parts[0])],
        0.5,
    )
    factors = [factors[0]] + [move(factors[d], flipped(d)) for d in range(1, 4)]
    parts = [after(parts[0], factors[0])] + [to_quad(p, s + 1) for s, p in enumerate(parts[1:])]
    (terms,) = run(temporal_kernel, "temporal_attention", [sds(tokens, 4 * width)], parts, 2)
    terms = after(terms, *factors)
    (table,) = run(
        table_kernel,
        "positional_table",
        [sds(tokens, channels, dtype=F32)],
        [after(geo, terms)],
        1.5,
    )
    all_terms = [terms] + [after(from_quad(terms, s), table) for s in range(1, nq)]
    pair_terms = [move(t, flipped(2)) for t in all_terms]
    core_terms = [move(t, flipped(1)) for t in all_terms]
    back_send, quarter = run(
        back_kernel,
        "temporal_back_projection",
        [sds(nf, 2 * nq * fr, half), sds(3, half // 4, width)],
        [geo] + all_terms + [motion_weights],
        0.01,
    )
    pair_terms[0] = after(pair_terms[0], back_send)
    last_terms = [move(pair_terms[0], flipped(1))]

    stage, block = nf // 4, half // nf
    sums, gain_sum, late_left = run(
        first_weight_kernel,
        "weight_terms_first_tokens",
        [
            sds(4, stage, block, width, dtype=F32),
            sds(1, half // 4, dtype=F32),
            sds(2, 2 * (nq - 1) * tokens, half // 4),
        ],
        [geo] + factors + [quarter, table] + all_terms + core_terms
        + pair_terms[:1] + last_terms,
        0.01,
    )
    late_terms = [after(t, back_send, sums) for t in pair_terms[1:]]
    late_terms += [move(t, flipped(1)) for t in late_terms]
    parts_w = run(
        second_weight_kernel,
        "weight_terms_last_tokens",
        [sds(2 * block + 8, width)] * stage + [sds(2 * block, width)] * stage,
        [geo, sums, gain_sum, late_left, quarter, table, gain2] + late_terms,
        0.01,
        scratch=[pltpu.VMEM((4, stage, block, width), F32)],
    )

    def add(a, b):
        return (a.astype(F32) + b.astype(F32)).astype(BF16)

    back_recv = swap(back_send)
    backs = [back_recv] + [from_quad(back_recv, s) for s in range(1, nq)]
    block_output, grad_hidden = run(
        middle_kernel,
        "block_output_hidden_gradient",
        [sds(fr, pq, channels), sds(rows, channels)],
        [geo] + backs + cots + [kept, gain2],
        6,
        big,
    )
    totals = [parts_w[stage - 1], parts_w[2 * stage - 1]]
    for step in range(1, stage):
        for i in range(2):
            if step == stage - 2:
                totals[i] = after(totals[i], back_recv)
            moved = move(totals[i], ring)
            if step == stage - 1:
                moved = after(moved, grad_hidden)
            totals[i] = add(moved, parts_w[(i + 1) * stage - 1 - step])
    final = []
    for g in range(nf):
        for q in range(nq):
            j = quarter_of(g % 4) * stage + g // 4
            final.append((g * nq + q, nf * q + j))
    grad_hidden = after(grad_hidden, *totals)
    totals = [lax.ppermute(t, ("frame", "quad"), final) for t in totals]
    (input_grad,) = run(
        tail_kernel,
        "spatial_backward",
        [sds(fr, pq, channels)],
        [grad_hidden, activations, kept, gain1, spatial_weights],
        3.5,
        big,
    )
    everyone = nf * nq
    factor = 1.0 / math.sqrt(everyone * fr * pq)
    weight_grad = jnp.concatenate([totals[0][: 2 * block], totals[1]], axis=0)
    weight_grad = weight_grad.reshape(4, block, width).astype(F32) * factor
    place = ((frame * nq + quad) % stage) * block
    gain_grad = lax.dynamic_slice(totals[0][2 * block], (place,), (block,)).astype(F32) * factor
    return block_output, input_grad, weight_grad, gain_grad


def solution(mesh):
    in_specs = (
        P("frame", "quad", None),
        P("frame", "quad", None),
        P(),
        P(),
        P(None, "quad", None),
        P(),
    )
    out_specs = (
        P("frame", "quad", None),
        P("frame", "quad", None),
        P(None, ("frame", "quad"), None),
        P(("frame", "quad")),
    )
    body = functools.partial(local, mesh.shape["quad"], mesh.shape["frame"])
    return jax.shard_map(
        body, mesh=mesh, in_specs=in_specs, out_specs=out_specs, check_vma=False
    )
```

```python
import functools
import math

import jax
import jax.numpy as jnp
from jax import lax
from jax.experimental import pallas as pl
from jax.experimental.pallas import tpu as pltpu
from jax.sharding import PartitionSpec as P

HEADS = 4
HEAD_DIM = 160
EPSILON = 1e-05
SCALE = HEAD_DIM ** (-0.5)
F32 = jnp.float32
BF16 = jnp.bfloat16


def log2(n):
    return int(n).bit_length() - 1


def dot(a, b):
    return jnp.dot(a, b, preferred_element_type=F32)


def dot_t(a, b):
    return lax.dot_general(a, b, (((1,), (1,)), ((), ())), preferred_element_type=F32)


def t_dot(a, b):
    return lax.dot_general(a, b, (((0,), (0,)), ((), ())), preferred_element_type=F32)


def normalize(values):
    average = jnp.mean(values, axis=-1, keepdims=True)
    centred = values - average
    inv_scale = lax.rsqrt(jnp.mean(centred * centred, axis=-1, keepdims=True) + EPSILON)
    return centred * inv_scale, inv_scale


def normalize_back(grad_rows, unit_rows, inv_scale, gain):
    scaled = grad_rows * gain
    first_mean = jnp.mean(scaled, axis=-1, keepdims=True)
    second_mean = jnp.mean(scaled * unit_rows, axis=-1, keepdims=True)
    return inv_scale * (scaled - first_mean - unit_rows * second_mean)


def iota(shape, dim):
    return lax.broadcasted_iota(jnp.int32, shape, dim)


def head_mask(dtype):
    lane = iota((1, HEADS * HEAD_DIM), 1)
    return [
        jnp.where((lane >= h * HEAD_DIM) & (lane < (h + 1) * HEAD_DIM), 1.0, 0.0).astype(dtype)
        for h in range(HEADS)
    ]


def stack_heads(rows):
    return jnp.concatenate([rows * mask for mask in head_mask(rows.dtype)], axis=0)


def fold_heads(stacked):
    rows = stacked.shape[0] // HEADS
    total = None
    for h, mask in enumerate(head_mask(F32)):
        piece = stacked[h * rows : (h + 1) * rows] * mask
        total = piece if total is None else total + piece
    return total


def probabilities(query_stack, keys, same):
    scores = dot_t(query_stack, keys) * SCALE
    if same is not None:
        scores = jnp.where(same, scores, -1e30)
    highest = jnp.max(scores, axis=-1, keepdims=True)
    expo = jnp.exp(scores - highest)
    return expo / jnp.sum(expo, axis=-1, keepdims=True)


def attend(query, keys, values, same):
    probs = probabilities(stack_heads(query), keys, same)
    return fold_heads(dot(probs.astype(BF16), values)).astype(BF16)


def attend_back(query, keys, values, grad, same, probs=None):
    query_stack = stack_heads(query)
    grad_stack = stack_heads(grad)
    if probs is None:
        probs = probabilities(query_stack, keys, same)
    grad_probs = dot_t(grad_stack, values)
    inner = jnp.sum(probs * grad_probs, axis=-1, keepdims=True)
    grad_scores = (probs * (grad_probs - inner) * SCALE).astype(BF16)
    grad_query = fold_heads(dot(grad_scores, keys)).astype(BF16)
    grad_key = t_dot(grad_scores, query_stack).astype(BF16)
    grad_value = t_dot(probs.astype(BF16), grad_stack).astype(BF16)
    return grad_query, grad_key, grad_value


def rows_to_sent(quad, nq, fr, pq, transposed):
    rows = nq * fr * pq
    out_dim = 1 if transposed else 0
    out = iota((rows, rows), out_dim)
    src = iota((rows, rows), 1 - out_dim)
    cell = out >> log2(nq * fr)
    other = (out >> log2(fr)) & (nq - 1)
    frame = out & (fr - 1)
    want = (((other - quad) & (nq - 1)) << log2(fr * pq)) + (frame << log2(pq)) + cell
    return jnp.where(want == src, 1.0, 0.0).astype(BF16)


def received_to_rows(quad, nq, nf, fr, transposed):
    rows = nq * nf * fr
    out_dim = 1 if transposed else 0
    out = iota((rows, rows), out_dim)
    src = iota((rows, rows), 1 - out_dim)
    step = out >> log2(nf * fr)
    device = (out >> log2(fr)) & (nf - 1)
    frame = out & (fr - 1)
    want = (device << log2(nq * fr)) + (((step + quad) & (nq - 1)) << log2(fr)) + frame
    return jnp.where(want == src, 1.0, 0.0).astype(BF16)


def own_lanes(values, quad, nq):
    width = values.shape[1] // nq
    picked = values[:, :width]
    for t in range(1, nq):
        picked = jnp.where(quad == t, values[:, t * width : (t + 1) * width], picked)
    return picked


def place_lanes(parts, quad, nq):
    placed = []
    for t in range(nq):
        piece = parts[t]
        for q in range(1, nq):
            piece = jnp.where(quad == q, parts[(t - q) % nq], piece)
        placed.append(piece)
    return jnp.concatenate(placed, axis=1)


def frame_groups(nq, fr, pq):
    size = max(1, min(fr, 128 // (nq * pq)))
    return [(start, size) for start in range(0, fr, size)]


def pick_group(rows, group, nq, fr, pq):
    start, size = group
    if size == fr:
        return rows
    cut = rows.reshape(nq, fr, pq, rows.shape[-1])[:, start : start + size]
    return cut.reshape(nq * size * pq, rows.shape[-1])


def join_groups(pieces, nq, fr, pq):
    if len(pieces) == 1:
        return pieces[0]
    size = fr // len(pieces)
    width = pieces[0].shape[-1]
    joined = jnp.concatenate([p.reshape(nq, size, pq, width) for p in pieces], axis=1)
    return joined.reshape(nq * fr * pq, width)


def same_frame(nq, size, pq):
    if size == 1:
        return None
    rows = nq * size * pq
    shape = (HEADS * rows, rows)
    left = (iota(shape, 0) >> log2(pq)) & (size - 1)
    right = (iota(shape, 1) >> log2(pq)) & (size - 1)
    return left == right


def row_of(ref):
    return ref[...].reshape(1, -1)


def flat(ref):
    value = ref[...]
    return value.reshape(-1, value.shape[-1])


def flat_wide(ref):
    value = ref[...].astype(F32)
    return value.reshape(-1, value.shape[-1])


def spread(rows, like):
    return rows.reshape(like.shape).astype(like.dtype)


def spatial_kernel(dims, *refs):
    nq, nf, fr, pq = dims
    quad, xs, refs = refs[0][0], refs[1 : 1 + nq], refs[1 + nq :]
    gain1, gain2, pos, weights, kept_out, send_out = refs
    width = HEADS * HEAD_DIM
    wide = jnp.concatenate([flat_wide(x) for x in xs], axis=0)
    unit, _ = normalize(wide)
    normed = (unit * row_of(gain1)).astype(BF16)
    query = dot(normed, weights[0]).astype(BF16)
    keys = dot(normed, weights[1]).astype(BF16)
    values = dot(normed, weights[2]).astype(BF16)
    for i, part in enumerate((query, keys, values)):
        kept_out[:, i * width : (i + 1) * width] = part
    pieces = []
    for group in frame_groups(nq, fr, pq):
        same = same_frame(nq, group[1], pq)
        cut = [pick_group(part, group, nq, fr, pq) for part in (query, keys, values)]
        pieces.append(attend(*cut, same))
    out = join_groups(pieces, nq, fr, pq)
    hidden = (wide + dot_t(out, weights[3])).astype(BF16)
    kept_out[:, 3 * width :] = hidden
    unit_two, _ = normalize(hidden.astype(F32))
    table = jnp.broadcast_to(pos[...][:, None, :], (fr, pq, pos.shape[-1]))
    table = table.reshape(fr * pq, pos.shape[-1])
    table = jnp.concatenate([table] * nq, axis=0)
    normed_two = own_lanes(unit_two * row_of(gain2) + table, quad, nq).astype(BF16)
    send_out[...] = spread(dot(rows_to_sent(quad, nq, fr, pq, False), normed_two), send_out)


def order_kernel(dims, geo, cot, weights, send_out):
    nq, nf, fr, pq = dims
    order = rows_to_sent(geo[0], nq, fr, pq, False)[:, : fr * pq]
    send_out[...] = spread(dot(order, own_lanes(flat(cot), geo[0], nq)), send_out)


def join_kernel(dims, geo, normed, own_part, *refs):
    nq, nf, fr, pq = dims
    cots, send_out = refs[:-1], refs[-1]
    order = rows_to_sent(geo[0], nq, fr, pq, False)[:, fr * pq :]
    rows = own_lanes(jnp.concatenate([flat(c) for c in cots], axis=0), geo[0], nq)
    total = own_part[...].astype(F32) + dot(order, rows).reshape(own_part.shape)
    send_out[:, : nq * fr, :] = normed[...]
    send_out[:, nq * fr :, :] = total.astype(BF16)


def sent_part(received, i, rows):
    part = received[:, i * rows : (i + 1) * rows, :].astype(F32)
    return part.reshape(-1, part.shape[-1]).astype(BF16)


def motion_kernel(dims, geo, received, weights, own_out, *sends):
    nq, nf, fr, pq = dims
    order = received_to_rows(geo[0], nq, nf, fr, False)
    normed, cot = [dot(order, sent_part(received, i, nq * fr)).astype(BF16) for i in range(2)]
    tokens = nf * fr
    for k in range(4):
        width = weights.shape[-1]
        lanes = slice(k * width, (k + 1) * width)
        product = dot(normed if k < 3 else cot, weights[k])
        own_out[:, lanes] = product[:tokens]
        for s, send in enumerate(sends):
            send[:, lanes] = product[(s + 1) * tokens : (s + 2) * tokens].astype(BF16)


def quarter_of(four):
    return ((four & 1) << 1) | (four >> 1)


def quarter_lanes(values, quarter):
    width = values.shape[1] // 4
    picked = values[:, :width]
    for t in range(1, 4):
        picked = jnp.where(quarter == t, values[:, t * width : (t + 1) * width], picked)
    return picked


def cut_kernel(dims, geo, received, *outs):
    nq, nf, fr, pq = dims
    order = received_to_rows(geo[0], nq, nf, fr, False)
    for i in range(2):
        rows = dot(order, sent_part(received, i, nq * fr))
        for d in range(4):
            outs[d][i] = quarter_lanes(rows, quarter_of(geo[1] ^ d)).astype(BF16)


def table_kernel(dims, geo, *refs):
    nq, nf, fr, pq = dims
    factors, (out, early_out, late_out) = refs[:4], refs[4:]
    shape = out.shape
    lane = iota(shape, 1)
    freq = jnp.exp((lane >> 1).astype(F32) * (-2.0 * math.log(10000.0) / shape[1]))
    turn = (lane & 1).astype(F32) * (0.5 * math.pi)
    out[...] = jnp.sin(iota(shape, 0).astype(F32) * freq + turn)
    tokens = nf * fr
    for i in range(2):
        early = [factors[0][i], factors[1][i], factors[2][i, :tokens], factors[3][i, :tokens]]
        early_out[i] = jnp.concatenate(early, axis=0)
        late = [factors[2][i, tokens:], factors[3][i, tokens:]]
        late_out[i] = jnp.concatenate(late, axis=0)


def temporal_kernel(dims, *refs):
    nq, nf, fr, pq = dims
    parts, out = refs[:nq], refs[nq]
    width = HEADS * HEAD_DIM
    total = parts[0][...]
    for part in parts[1:]:
        total = total + part[...].astype(F32)
    query, keys, values, grad = [
        total[:, k * width : (k + 1) * width].astype(BF16) for k in range(4)
    ]
    probs = probabilities(stack_heads(query), keys, None)
    motion_out = fold_heads(dot(probs.astype(BF16), values)).astype(BF16)
    grads = attend_back(query, keys, values, grad, None, probs)
    for k, piece in enumerate(grads + (motion_out,)):
        out[:, k * width : (k + 1) * width] = piece


def part_of(terms, k):
    width = HEADS * HEAD_DIM
    return jnp.concatenate([t[:, k * width : (k + 1) * width] for t in terms], axis=0)


def back_kernel(dims, quad_ref, *refs):
    nq, nf, fr, pq = dims
    terms, (weights, out, quarter_out) = refs[:nq], refs[nq:]
    order = received_to_rows(quad_ref[0], nq, nf, fr, True)
    quarter, rows = quarter_of(quad_ref[1]), quarter_out.shape[1]
    for k in range(3):
        if rows % 16 == 0:
            own = weights[k, pl.ds(pl.multiple_of(quarter * rows, 16), rows), :]
        else:
            wide = weights[k].astype(F32)
            own = wide[:rows]
            for t in range(1, 4):
                own = jnp.where(quarter == t, wide[t * rows : (t + 1) * rows], own)
            own = own.astype(BF16)
        quarter_out[k] = own
    grad = None
    for k in range(3):
        product = dot_t(part_of(terms, k), weights[k])
        grad = product if grad is None else grad + product
    delta = dot_t(part_of(terms, 3), weights[3])
    for i, rows in enumerate((grad, delta)):
        rows = dot(order, rows.astype(BF16))
        out[:, i * nq * fr : (i + 1) * nq * fr, :] = rows.reshape(nf, nq * fr, -1).astype(BF16)


def weight_sums(geo, nq, normed, cot, weights, pos, terms):
    products, grad = [], None
    for k in range(4):
        right = part_of(terms, k)
        products.append(t_dot(normed if k < 3 else cot, right))
        if k < 3:
            back = dot_t(right, weights[k])
            grad = back if grad is None else grad + back
    table = quarter_lanes(own_lanes(pos[...], geo[0], nq), quarter_of(geo[1]))
    table = jnp.concatenate([table] * len(terms), axis=0)
    return products, jnp.sum(grad * (normed.astype(F32) - table), axis=0, keepdims=True)


def first_weight_kernel(dims, geo, left, weights, pos, *refs):
    nq, nf, fr, pq = dims
    terms, (blocks, gain_out) = refs[: 2 * nq + 2], refs[2 * nq + 2 :]
    _, stage, block, _ = blocks.shape
    products, gain_out[...] = weight_sums(geo, nq, left[0], left[1], weights, pos, terms)
    for k in range(4):
        for z in range(stage):
            blocks[k, z] = products[k][z * block : (z + 1) * block]


def second_weight_kernel(dims, geo, sums, gain_sum, left, weights, pos, gain2, *refs):
    nq, nf, fr, pq = dims
    terms, outs, blocks = refs[: 2 * nq - 2], refs[2 * nq - 2 : -1], refs[-1]
    _, stage, block, width = blocks.shape
    products, gain = weight_sums(geo, nq, left[0], left[1], weights, pos, terms)
    for k in range(4):
        for z in range(stage):
            blocks[k, z] = sums[k, z] + products[k][z * block : (z + 1) * block]
    gain = gain + gain_sum[...]
    rows = gain.shape[1]
    gain = gain / quarter_lanes(own_lanes(row_of(gain2), geo[0], nq), quarter_of(geo[1]))
    extra = jnp.concatenate([gain, jnp.zeros((1, width - rows), F32)], axis=1)
    extra = jnp.where(iota((8, width), 0) == 0, extra, 0.0)
    for r in range(stage):
        z = (geo[2] + r) & (stage - 1)
        rows_out = jnp.concatenate([blocks[0, z], blocks[1, z], extra], axis=0)
        outs[r][...] = rows_out.astype(BF16)
        rows_out = jnp.concatenate([blocks[2, z], blocks[3, z]], axis=0)
        outs[stage + r][...] = rows_out.astype(BF16)


def middle_kernel(dims, *refs):
    nq, nf, fr, pq = dims
    quad, received, cots = refs[0][0], refs[1 : 1 + nq], refs[1 + nq : 1 + 2 * nq]
    kept, gain2, block_out, grad_out = refs[1 + 2 * nq :]
    own = fr * pq
    order = rows_to_sent(quad, nq, fr, pq, True)

    def lanes(i):
        parts = []
        for r in received:
            parts.append(dot(order, sent_part(r, i, nq * fr)))
        return place_lanes(parts, quad, nq)

    hidden = kept[:, 3 * HEADS * HEAD_DIM :].astype(F32)
    grad_normed, delta = lanes(0), lanes(1)
    block_out[...] = spread(hidden[:own] + delta[:own], block_out)
    unit_two, inv_two = normalize(hidden)
    cot = jnp.concatenate([flat_wide(c) for c in cots], axis=0)
    back = normalize_back(grad_normed, unit_two, inv_two, row_of(gain2))
    grad_out[...] = (cot + back).astype(BF16)


def tail_kernel(dims, grad_hidden, xs, kept, gain1, weights, in_grad):
    nq, nf, fr, pq = dims
    own, width = fr * pq, HEADS * HEAD_DIM
    grad_out = dot(grad_hidden[...], weights[3]).astype(BF16)
    parts = [kept[:, i * width : (i + 1) * width] for i in range(3)] + [grad_out]
    pieces = []
    for group in frame_groups(nq, fr, pq):
        same = same_frame(nq, group[1], pq)
        pieces.append(attend_back(*[pick_group(p, group, nq, fr, pq) for p in parts], same))
    grads = [join_groups([p[i] for p in pieces], nq, fr, pq)[:own] for i in range(3)]
    grad_one = dot_t(grads[0], weights[0]) + dot_t(grads[1], weights[1]) + dot_t(grads[2], weights[2])
    unit_one, inv_one = normalize(flat_wide(xs))
    back = normalize_back(grad_one, unit_one, inv_one, row_of(gain1))
    in_grad[...] = spread(grad_hidden[...][:own].astype(F32) + back, in_grad)


def call(kernel, name, outs, args, vmem, micros, scratch=()):
    in_specs = []
    for arg in args:
        space = pltpu.SMEM if arg.dtype == jnp.int32 else pltpu.VMEM
        in_specs.append(pl.BlockSpec(memory_space=space))
    return list(
        pl.pallas_call(
            kernel,
            out_shape=outs,
            in_specs=in_specs,
            out_specs=[pl.BlockSpec(memory_space=pltpu.VMEM) for _ in outs],
            scratch_shapes=list(scratch),
            compiler_params=pltpu.CompilerParams(vmem_limit_bytes=vmem * 1024 * 1024),
            cost_estimate=pl.CostEstimate(
                flops=int(micros * 1e9),
                bytes_accessed=2**20 if micros > 0.1 else 2**12,
                transcendentals=0,
            ),
            name=name,
        )(*args)
    )


def after(value, *others):
    return lax.optimization_barrier((value,) + others)[0]


def sds(*shape, dtype=BF16):
    return jax.ShapeDtypeStruct(shape, dtype)


def positional(first, frames, channels):
    frame_pos = (first + lax.broadcasted_iota(jnp.int32, (frames, channels), 0)).astype(F32)
    lane = lax.broadcasted_iota(jnp.int32, (frames, channels), 1)
    freq_index = (lane >> 1).astype(F32)
    phases = frame_pos * jnp.exp(freq_index * (-2.0 * math.log(10000.0) / channels))
    return jnp.sin(phases + (lane & 1).astype(F32) * (0.5 * math.pi))


def local(nq, nf, activations, cotangent, spatial_weights, spatial_gain, motion_weights, motion_gain):
    fr, pq, channels = activations.shape
    dims = (nq, nf, fr, pq)
    width = spatial_weights.shape[-1]
    half = channels // nq
    rows = nq * fr * pq
    tokens = nf * fr
    small = 16 if rows <= 256 else 40
    big = 16 if rows <= 256 else 52
    quad = lax.axis_index("quad")
    frame = lax.axis_index("frame")


    def from_quad(x, s):
        return lax.ppermute(x, "quad", [((d + s) % nq, d) for d in range(nq)])

    def to_quad(x, s):
        return lax.ppermute(x, "quad", [(d, (d + s) % nq) for d in range(nq)])

    def swap(x):
        return lax.all_to_all(x, "frame", split_axis=0, concat_axis=0, tiled=True)

    def run(kernel, name, outs, args, micros, vmem=small, **options):
        kernel = functools.partial(kernel, dims)
        return call(kernel, name, outs, args, vmem, micros, **options)

    def move(x, pairs):
        return lax.ppermute(x, "frame", pairs)

    geo = jnp.stack([quad, frame % 4, frame // 4]).astype(jnp.int32)

    def flipped(bits):
        return [(g, g ^ bits) for g in range(nf)]

    ring = [(g, (g + 4) % nf) for g in range(nf)]

    gain1, gain2 = spatial_gain, motion_gain
    sent = sds(nf, nq * fr, half)
    acts = [activations] + [from_quad(activations, s) for s in range(1, nq)]
    both = sds(nf, 2 * nq * fr, half)
    (own_part,) = run(
        order_kernel, "order_cotangent", [sent], [geo, cotangent, spatial_weights], 0.5, big
    )
    cot_later = after(cotangent, acts[-1])
    cots = [cotangent] + [from_quad(cot_later, s) for s in range(1, nq)]
    pos = positional(frame * fr, fr, channels)
    kept, normed = run(
        spatial_kernel,
        "spatial_forward",
        [sds(rows, 3 * width + channels), sent],
        [geo] + acts + [gain1, gain2, pos, spatial_weights],
        3,
        big,
    )
    (send,) = run(join_kernel, "join_sent", [both], [geo, normed, own_part] + cots[1:], 0.5)
    received = swap(send)
    parts = run(
        motion_kernel,
        "motion_projection",
        [sds(tokens, 4 * width, dtype=F32)] + [sds(tokens, 4 * width)] * (nq - 1),
        [geo, received, motion_weights],
        1.5,
    )
    factors = run(
        cut_kernel,
        "cut_factors",
        [sds(2, rows, half // 4)] * 4,
        [geo, after(received, parts[0])],
        0.5,
    )
    factors = [factors[0]] + [move(factors[d], flipped(d)) for d in range(1, 4)]
    parts = [after(parts[0], factors[0])] + [to_quad(p, s + 1) for s, p in enumerate(parts[1:])]
    (terms,) = run(temporal_kernel, "temporal_attention", [sds(tokens, 4 * width)], parts, 2)
    table, early_left, late_left = run(
        table_kernel,
        "positional_table_factors",
        [
            sds(tokens, channels, dtype=F32),
            sds(2, (2 * nq + 2) * tokens, half // 4),
            sds(2, 2 * (nq - 1) * tokens, half // 4),
        ],
        [after(geo, terms)] + factors,
        1.5,
    )
    all_terms = [terms] + [after(from_quad(terms, s), table) for s in range(1, nq)]
    pair_terms = [move(t, flipped(2)) for t in all_terms]
    core_terms = [move(t, flipped(1)) for t in all_terms]
    back_send, quarter = run(
        back_kernel,
        "temporal_back_projection",
        [sds(nf, 2 * nq * fr, half), sds(3, half // 4, width)],
        [geo] + all_terms + [motion_weights],
        0.01,
    )
    pair_terms[0] = after(pair_terms[0], back_send)
    last_terms = [move(pair_terms[0], flipped(1))]

    stage, block = nf // 4, half // nf
    sums, gain_sum = run(
        first_weight_kernel,
        "weight_terms_first_tokens",
        [
            sds(4, stage, block, width, dtype=F32),
            sds(1, half // 4, dtype=F32),
        ],
        [geo, early_left, quarter, table] + all_terms + core_terms
        + pair_terms[:1] + last_terms,
        0.01,
    )
    late_terms = [after(t, back_send, sums) for t in pair_terms[1:]]
    late_terms += [move(t, flipped(1)) for t in late_terms]
    parts_w = run(
        second_weight_kernel,
        "weight_terms_last_tokens",
        [sds(2 * block + 8, width)] * stage + [sds(2 * block, width)] * stage,
        [geo, sums, gain_sum, late_left, quarter, table, gain2] + late_terms,
        0.01,
        scratch=[pltpu.VMEM((4, stage, block, width), F32)],
    )

    def add(a, b):
        return (a.astype(F32) + b.astype(F32)).astype(BF16)

    back_recv = swap(back_send)
    backs = [back_recv] + [from_quad(back_recv, s) for s in range(1, nq)]
    block_output, grad_hidden = run(
        middle_kernel,
        "block_output_hidden_gradient",
        [sds(fr, pq, channels), sds(rows, channels)],
        [geo] + backs + cots + [kept, gain2],
        6,
        big,
    )
    totals = [parts_w[stage - 1], parts_w[2 * stage - 1]]
    for step in range(1, stage):
        for i in range(2):
            if step == stage - 2:
                totals[i] = after(totals[i], back_recv)
            if i == 1:
                totals[i] = after(totals[i], totals[0])
            moved = move(totals[i], ring)
            totals[i] = add(moved, parts_w[(i + 1) * stage - 1 - step])
    final = []
    for g in range(nf):
        for q in range(nq):
            j = quarter_of(g % 4) * stage + g // 4
            final.append((g * nq + q, nf * q + j))
    grad_hidden = after(grad_hidden, *totals)
    totals = [lax.ppermute(t, ("frame", "quad"), final) for t in totals]
    (input_grad,) = run(
        tail_kernel,
        "spatial_backward",
        [sds(fr, pq, channels)],
        [grad_hidden, activations, kept, gain1, spatial_weights],
        3.5,
        big,
    )
    everyone = nf * nq
    factor = 1.0 / math.sqrt(everyone * fr * pq)
    weight_grad = jnp.concatenate([totals[0][: 2 * block], totals[1]], axis=0)
    weight_grad = weight_grad.reshape(4, block, width).astype(F32) * factor
    place = ((frame * nq + quad) % stage) * block
    gain_grad = lax.dynamic_slice(totals[0][2 * block], (place,), (block,)).astype(F32) * factor
    return block_output, input_grad, weight_grad, gain_grad


def solution(mesh):
    in_specs = (
        P("frame", "quad", None),
        P("frame", "quad", None),
        P(),
        P(),
        P(None, "quad", None),
        P(),
    )
    out_specs = (
        P("frame", "quad", None),
        P("frame", "quad", None),
        P(None, ("frame", "quad"), None),
        P(("frame", "quad")),
    )
    body = functools.partial(local, mesh.shape["quad"], mesh.shape["frame"])
    return jax.shard_map(
        body, mesh=mesh, in_specs=in_specs, out_specs=out_specs, check_vma=False
    )
```

```python
import functools
import math

import jax
import jax.numpy as jnp
from jax import lax
from jax.experimental import pallas as pl
from jax.experimental.pallas import tpu as pltpu
from jax.sharding import PartitionSpec as P

HEADS = 4
HEAD_DIM = 160
EPSILON = 1e-05
SCALE = HEAD_DIM ** (-0.5)
F32 = jnp.float32
BF16 = jnp.bfloat16


def log2(n):
    return int(n).bit_length() - 1


def dot(a, b):
    return jnp.dot(a, b, preferred_element_type=F32)


def dot_t(a, b):
    return lax.dot_general(a, b, (((1,), (1,)), ((), ())), preferred_element_type=F32)


def t_dot(a, b):
    return lax.dot_general(a, b, (((0,), (0,)), ((), ())), preferred_element_type=F32)


def normalize(values):
    average = jnp.mean(values, axis=-1, keepdims=True)
    centred = values - average
    inv_scale = lax.rsqrt(jnp.mean(centred * centred, axis=-1, keepdims=True) + EPSILON)
    return centred * inv_scale, inv_scale


def normalize_back(grad_rows, unit_rows, inv_scale, gain):
    scaled = grad_rows * gain
    first_mean = jnp.mean(scaled, axis=-1, keepdims=True)
    second_mean = jnp.mean(scaled * unit_rows, axis=-1, keepdims=True)
    return inv_scale * (scaled - first_mean - unit_rows * second_mean)


def iota(shape, dim):
    return lax.broadcasted_iota(jnp.int32, shape, dim)


def head_mask(dtype):
    lane = iota((1, HEADS * HEAD_DIM), 1)
    return [
        jnp.where((lane >= h * HEAD_DIM) & (lane < (h + 1) * HEAD_DIM), 1.0, 0.0).astype(dtype)
        for h in range(HEADS)
    ]


def stack_heads(rows):
    return jnp.concatenate([rows * mask for mask in head_mask(rows.dtype)], axis=0)


def fold_heads(stacked):
    rows = stacked.shape[0] // HEADS
    total = None
    for h, mask in enumerate(head_mask(F32)):
        piece = stacked[h * rows : (h + 1) * rows] * mask
        total = piece if total is None else total + piece
    return total


def probabilities(query_stack, keys, same):
    scores = dot_t(query_stack, keys) * SCALE
    if same is not None:
        scores = jnp.where(same, scores, -1e30)
    highest = jnp.max(scores, axis=-1, keepdims=True)
    expo = jnp.exp(scores - highest)
    return expo / jnp.sum(expo, axis=-1, keepdims=True)


def attend(query, keys, values, same):
    probs = probabilities(stack_heads(query), keys, same)
    return fold_heads(dot(probs.astype(BF16), values)).astype(BF16)


def attend_back(query, keys, values, grad, same, probs=None):
    query_stack = stack_heads(query)
    grad_stack = stack_heads(grad)
    if probs is None:
        probs = probabilities(query_stack, keys, same)
    grad_probs = dot_t(grad_stack, values)
    inner = jnp.sum(probs * grad_probs, axis=-1, keepdims=True)
    grad_scores = (probs * (grad_probs - inner) * SCALE).astype(BF16)
    grad_query = fold_heads(dot(grad_scores, keys)).astype(BF16)
    grad_key = t_dot(grad_scores, query_stack).astype(BF16)
    grad_value = t_dot(probs.astype(BF16), grad_stack).astype(BF16)
    return grad_query, grad_key, grad_value


def rows_to_sent(quad, nq, fr, pq, transposed):
    rows = nq * fr * pq
    out_dim = 1 if transposed else 0
    out = iota((rows, rows), out_dim)
    src = iota((rows, rows), 1 - out_dim)
    cell = out >> log2(nq * fr)
    other = (out >> log2(fr)) & (nq - 1)
    frame = out & (fr - 1)
    want = (((other - quad) & (nq - 1)) << log2(fr * pq)) + (frame << log2(pq)) + cell
    return jnp.where(want == src, 1.0, 0.0).astype(BF16)


def received_to_rows(quad, nq, nf, fr, transposed):
    rows = nq * nf * fr
    out_dim = 1 if transposed else 0
    out = iota((rows, rows), out_dim)
    src = iota((rows, rows), 1 - out_dim)
    step = out >> log2(nf * fr)
    device = (out >> log2(fr)) & (nf - 1)
    frame = out & (fr - 1)
    want = (device << log2(nq * fr)) + (((step + quad) & (nq - 1)) << log2(fr)) + frame
    return jnp.where(want == src, 1.0, 0.0).astype(BF16)


def own_lanes(values, quad, nq):
    width = values.shape[1] // nq
    picked = values[:, :width]
    for t in range(1, nq):
        picked = jnp.where(quad == t, values[:, t * width : (t + 1) * width], picked)
    return picked


def place_lanes(parts, quad, nq):
    placed = []
    for t in range(nq):
        piece = parts[t]
        for q in range(1, nq):
            piece = jnp.where(quad == q, parts[(t - q) % nq], piece)
        placed.append(piece)
    return jnp.concatenate(placed, axis=1)


def frame_groups(nq, fr, pq):
    size = max(1, min(fr, 128 // (nq * pq)))
    return [(start, size) for start in range(0, fr, size)]


def pick_group(rows, group, nq, fr, pq):
    start, size = group
    if size == fr:
        return rows
    cut = rows.reshape(nq, fr, pq, rows.shape[-1])[:, start : start + size]
    return cut.reshape(nq * size * pq, rows.shape[-1])


def join_groups(pieces, nq, fr, pq):
    if len(pieces) == 1:
        return pieces[0]
    size = fr // len(pieces)
    width = pieces[0].shape[-1]
    joined = jnp.concatenate([p.reshape(nq, size, pq, width) for p in pieces], axis=1)
    return joined.reshape(nq * fr * pq, width)


def same_frame(nq, size, pq):
    if size == 1:
        return None
    rows = nq * size * pq
    shape = (HEADS * rows, rows)
    left = (iota(shape, 0) >> log2(pq)) & (size - 1)
    right = (iota(shape, 1) >> log2(pq)) & (size - 1)
    return left == right


def row_of(ref):
    return ref[...].reshape(1, -1)


def flat(ref):
    value = ref[...]
    return value.reshape(-1, value.shape[-1])


def flat_wide(ref):
    value = ref[...].astype(F32)
    return value.reshape(-1, value.shape[-1])


def spread(rows, like):
    return rows.reshape(like.shape).astype(like.dtype)


def spatial_kernel(dims, *refs):
    nq, nf, fr, pq = dims
    quad, xs, refs = refs[0][0], refs[1 : 1 + nq], refs[1 + nq :]
    gain1, gain2, pos, weights, kept_out, send_out = refs
    width = HEADS * HEAD_DIM
    wide = jnp.concatenate([flat_wide(x) for x in xs], axis=0)
    unit, _ = normalize(wide)
    normed = (unit * row_of(gain1)).astype(BF16)
    query = dot(normed, weights[0]).astype(BF16)
    keys = dot(normed, weights[1]).astype(BF16)
    values = dot(normed, weights[2]).astype(BF16)
    for i, part in enumerate((query, keys, values)):
        kept_out[:, i * width : (i + 1) * width] = part
    pieces = []
    for group in frame_groups(nq, fr, pq):
        same = same_frame(nq, group[1], pq)
        cut = [pick_group(part, group, nq, fr, pq) for part in (query, keys, values)]
        pieces.append(attend(*cut, same))
    out = join_groups(pieces, nq, fr, pq)
    hidden = (wide + dot_t(out, weights[3])).astype(BF16)
    kept_out[:, 3 * width :] = hidden
    unit_two, _ = normalize(hidden.astype(F32))
    table = jnp.broadcast_to(pos[...][:, None, :], (fr, pq, pos.shape[-1]))
    table = table.reshape(fr * pq, pos.shape[-1])
    table = jnp.concatenate([table] * nq, axis=0)
    normed_two = own_lanes(unit_two * row_of(gain2) + table, quad, nq).astype(BF16)
    send_out[...] = spread(dot(rows_to_sent(quad, nq, fr, pq, False), normed_two), send_out)


def order_kernel(dims, geo, cot, weights, send_out):
    nq, nf, fr, pq = dims
    order = rows_to_sent(geo[0], nq, fr, pq, False)[:, : fr * pq]
    send_out[...] = spread(dot(order, own_lanes(flat(cot), geo[0], nq)), send_out)


def join_kernel(dims, geo, normed, own_part, *refs):
    nq, nf, fr, pq = dims
    cots, send_out = refs[:-1], refs[-1]
    order = rows_to_sent(geo[0], nq, fr, pq, False)[:, fr * pq :]
    rows = own_lanes(jnp.concatenate([flat(c) for c in cots], axis=0), geo[0], nq)
    total = own_part[...].astype(F32) + dot(order, rows).reshape(own_part.shape)
    send_out[:, : nq * fr, :] = normed[...]
    send_out[:, nq * fr :, :] = total.astype(BF16)


def sent_part(received, i, rows):
    part = received[:, i * rows : (i + 1) * rows, :].astype(F32)
    return part.reshape(-1, part.shape[-1]).astype(BF16)


def motion_kernel(dims, geo, received, weights, own_out, *sends):
    nq, nf, fr, pq = dims
    order = received_to_rows(geo[0], nq, nf, fr, False)
    normed, cot = [dot(order, sent_part(received, i, nq * fr)).astype(BF16) for i in range(2)]
    tokens = nf * fr
    for k in range(4):
        width = weights.shape[-1]
        lanes = slice(k * width, (k + 1) * width)
        product = dot(normed if k < 3 else cot, weights[k])
        own_out[:, lanes] = product[:tokens]
        for s, send in enumerate(sends):
            send[:, lanes] = product[(s + 1) * tokens : (s + 2) * tokens].astype(BF16)


def quarter_of(four):
    return ((four & 1) << 1) | (four >> 1)


def quarter_lanes(values, quarter):
    width = values.shape[1] // 4
    picked = values[:, :width]
    for t in range(1, 4):
        picked = jnp.where(quarter == t, values[:, t * width : (t + 1) * width], picked)
    return picked


def cut_kernel(dims, geo, received, *outs):
    nq, nf, fr, pq = dims
    order = received_to_rows(geo[0], nq, nf, fr, False)
    for i in range(2):
        rows = dot(order, sent_part(received, i, nq * fr))
        for d in range(4):
            outs[d][i] = quarter_lanes(rows, quarter_of(geo[1] ^ d)).astype(BF16)


def table_kernel(dims, geo, *refs):
    nq, nf, fr, pq = dims
    factors, (out, early_out, late_out) = refs[:4], refs[4:]
    shape = out.shape
    lane = iota(shape, 1)
    freq = jnp.exp((lane >> 1).astype(F32) * (-2.0 * math.log(10000.0) / shape[1]))
    turn = (lane & 1).astype(F32) * (0.5 * math.pi)
    out[...] = jnp.sin(iota(shape, 0).astype(F32) * freq + turn)
    tokens = nf * fr
    for i in range(2):
        early = [factors[0][i], factors[1][i], factors[2][i, :tokens], factors[3][i, :tokens]]
        early_out[i] = jnp.concatenate(early, axis=0)
        late = [factors[2][i, tokens:], factors[3][i, tokens:]]
        late_out[i] = jnp.concatenate(late, axis=0)


def temporal_kernel(dims, *refs):
    nq, nf, fr, pq = dims
    parts, out = refs[:nq], refs[nq]
    width = HEADS * HEAD_DIM
    total = parts[0][...]
    for part in parts[1:]:
        total = total + part[...].astype(F32)
    query, keys, values, grad = [
        total[:, k * width : (k + 1) * width].astype(BF16) for k in range(4)
    ]
    probs = probabilities(stack_heads(query), keys, None)
    motion_out = fold_heads(dot(probs.astype(BF16), values)).astype(BF16)
    grads = attend_back(query, keys, values, grad, None, probs)
    for k, piece in enumerate(grads + (motion_out,)):
        out[:, k * width : (k + 1) * width] = piece


def part_of(terms, k):
    width = HEADS * HEAD_DIM
    return jnp.concatenate([t[:, k * width : (k + 1) * width] for t in terms], axis=0)


def back_kernel(dims, quad_ref, *refs):
    nq, nf, fr, pq = dims
    terms, (weights, out, quarter_out) = refs[:nq], refs[nq:]
    order = received_to_rows(quad_ref[0], nq, nf, fr, True)
    quarter, rows = quarter_of(quad_ref[1]), quarter_out.shape[1]
    for k in range(3):
        if rows % 16 == 0:
            own = weights[k, pl.ds(pl.multiple_of(quarter * rows, 16), rows), :]
        else:
            wide = weights[k].astype(F32)
            own = wide[:rows]
            for t in range(1, 4):
                own = jnp.where(quarter == t, wide[t * rows : (t + 1) * rows], own)
            own = own.astype(BF16)
        quarter_out[k] = own
    grad = None
    for k in range(3):
        product = dot_t(part_of(terms, k), weights[k])
        grad = product if grad is None else grad + product
    delta = dot_t(part_of(terms, 3), weights[3])
    for i, rows in enumerate((grad, delta)):
        rows = dot(order, rows.astype(BF16))
        out[:, i * nq * fr : (i + 1) * nq * fr, :] = rows.reshape(nf, nq * fr, -1).astype(BF16)


def weight_sums(geo, nq, normed, cot, weights, pos, terms):
    products, grad = [], None
    for k in range(4):
        right = part_of(terms, k)
        products.append(t_dot(normed if k < 3 else cot, right))
        if k < 3:
            back = dot_t(right, weights[k])
            grad = back if grad is None else grad + back
    table = quarter_lanes(own_lanes(pos[...], geo[0], nq), quarter_of(geo[1]))
    table = jnp.concatenate([table] * len(terms), axis=0)
    return products, jnp.sum(grad * (normed.astype(F32) - table), axis=0, keepdims=True)


def first_weight_kernel(dims, geo, left, weights, pos, *refs):
    nq, nf, fr, pq = dims
    terms, (blocks, gain_out) = refs[: 2 * nq + 2], refs[2 * nq + 2 :]
    _, stage, block, _ = blocks.shape
    products, gain_out[...] = weight_sums(geo, nq, left[0], left[1], weights, pos, terms)
    for k in range(4):
        for z in range(stage):
            blocks[k, z] = products[k][z * block : (z + 1) * block]


def second_weight_kernel(dims, geo, sums, gain_sum, left, weights, pos, gain2, *refs):
    nq, nf, fr, pq = dims
    terms, outs, blocks = refs[: 2 * nq - 2], refs[2 * nq - 2 : -1], refs[-1]
    _, stage, block, width = blocks.shape
    products, gain = weight_sums(geo, nq, left[0], left[1], weights, pos, terms)
    for k in range(4):
        for z in range(stage):
            blocks[k, z] = sums[k, z] + products[k][z * block : (z + 1) * block]
    gain = gain + gain_sum[...]
    rows = gain.shape[1]
    gain = gain / quarter_lanes(own_lanes(row_of(gain2), geo[0], nq), quarter_of(geo[1]))
    extra = jnp.concatenate([gain, jnp.zeros((1, width - rows), F32)], axis=1)
    extra = jnp.where(iota((8, width), 0) == 0, extra, 0.0)
    for r in range(stage):
        z = (geo[2] + r) & (stage - 1)
        rows_out = jnp.concatenate([blocks[0, z], blocks[1, z], extra], axis=0)
        outs[r][...] = rows_out.astype(BF16)
        rows_out = jnp.concatenate([blocks[2, z], blocks[3, z]], axis=0)
        outs[stage + r][...] = rows_out.astype(BF16)


def middle_kernel(dims, *refs):
    nq, nf, fr, pq = dims
    quad, received, cots = refs[0][0], refs[1 : 1 + nq], refs[1 + nq : 1 + 2 * nq]
    kept, gain2, block_out, grad_out = refs[1 + 2 * nq :]
    own = fr * pq
    order = rows_to_sent(quad, nq, fr, pq, True)

    def lanes(i):
        parts = []
        for r in received:
            parts.append(dot(order, sent_part(r, i, nq * fr)))
        return place_lanes(parts, quad, nq)

    hidden = kept[:, 3 * HEADS * HEAD_DIM :].astype(F32)
    grad_normed, delta = lanes(0), lanes(1)
    block_out[...] = spread(hidden[:own] + delta[:own], block_out)
    unit_two, inv_two = normalize(hidden)
    cot = jnp.concatenate([flat_wide(c) for c in cots], axis=0)
    back = normalize_back(grad_normed, unit_two, inv_two, row_of(gain2))
    grad_out[...] = (cot + back).astype(BF16)


def tail_kernel(dims, grad_hidden, xs, kept, gain1, weights, in_grad):
    nq, nf, fr, pq = dims
    own, width = fr * pq, HEADS * HEAD_DIM
    grad_out = dot(grad_hidden[...], weights[3]).astype(BF16)
    parts = [kept[:, i * width : (i + 1) * width] for i in range(3)] + [grad_out]
    pieces = []
    for group in frame_groups(nq, fr, pq):
        same = same_frame(nq, group[1], pq)
        pieces.append(attend_back(*[pick_group(p, group, nq, fr, pq) for p in parts], same))
    grads = [join_groups([p[i] for p in pieces], nq, fr, pq)[:own] for i in range(3)]
    grad_one = dot_t(grads[0], weights[0]) + dot_t(grads[1], weights[1]) + dot_t(grads[2], weights[2])
    unit_one, inv_one = normalize(flat_wide(xs))
    back = normalize_back(grad_one, unit_one, inv_one, row_of(gain1))
    in_grad[...] = spread(grad_hidden[...][:own].astype(F32) + back, in_grad)


def call(kernel, name, outs, args, vmem, micros, scratch=()):
    in_specs = []
    for arg in args:
        space = pltpu.SMEM if arg.dtype == jnp.int32 else pltpu.VMEM
        in_specs.append(pl.BlockSpec(memory_space=space))
    return list(
        pl.pallas_call(
            kernel,
            out_shape=outs,
            in_specs=in_specs,
            out_specs=[pl.BlockSpec(memory_space=pltpu.VMEM) for _ in outs],
            scratch_shapes=list(scratch),
            compiler_params=pltpu.CompilerParams(vmem_limit_bytes=vmem * 1024 * 1024),
            cost_estimate=pl.CostEstimate(
                flops=int(micros * 1e9),
                bytes_accessed=2**20 if micros > 0.1 else 2**12,
                transcendentals=0,
            ),
            name=name,
        )(*args)
    )


def after(value, *others):
    return lax.optimization_barrier((value,) + others)[0]


def sds(*shape, dtype=BF16):
    return jax.ShapeDtypeStruct(shape, dtype)


def positional(first, frames, channels):
    frame_pos = (first + lax.broadcasted_iota(jnp.int32, (frames, channels), 0)).astype(F32)
    lane = lax.broadcasted_iota(jnp.int32, (frames, channels), 1)
    freq_index = (lane >> 1).astype(F32)
    phases = frame_pos * jnp.exp(freq_index * (-2.0 * math.log(10000.0) / channels))
    return jnp.sin(phases + (lane & 1).astype(F32) * (0.5 * math.pi))


def local(nq, nf, activations, cotangent, spatial_weights, spatial_gain, motion_weights, motion_gain):
    fr, pq, channels = activations.shape
    dims = (nq, nf, fr, pq)
    width = spatial_weights.shape[-1]
    half = channels // nq
    rows = nq * fr * pq
    tokens = nf * fr
    small = 16 if rows <= 256 else 40
    big = 16 if rows <= 256 else 52
    quad = lax.axis_index("quad")
    frame = lax.axis_index("frame")


    def from_quad(x, s):
        return lax.ppermute(x, "quad", [((d + s) % nq, d) for d in range(nq)])

    def to_quad(x, s):
        return lax.ppermute(x, "quad", [(d, (d + s) % nq) for d in range(nq)])

    def swap(x):
        return lax.all_to_all(x, "frame", split_axis=0, concat_axis=0, tiled=True)

    def run(kernel, name, outs, args, micros, vmem=small, **options):
        kernel = functools.partial(kernel, dims)
        return call(kernel, name, outs, args, vmem, micros, **options)

    def move(x, pairs):
        return lax.ppermute(x, "frame", pairs)

    geo = jnp.stack([quad, frame % 4, frame // 4]).astype(jnp.int32)

    def flipped(bits):
        return [(g, g ^ bits) for g in range(nf)]

    ring = [(g, (g + 4) % nf) for g in range(nf)]

    gain1, gain2 = spatial_gain, motion_gain
    sent = sds(nf, nq * fr, half)
    acts = [activations] + [from_quad(activations, s) for s in range(1, nq)]
    both = sds(nf, 2 * nq * fr, half)
    (own_part,) = run(
        order_kernel, "order_cotangent", [sent], [geo, cotangent, spatial_weights], 0.5, big
    )
    cot_later = after(cotangent, acts[-1])
    cots = [cotangent] + [from_quad(cot_later, s) for s in range(1, nq)]
    pos = positional(frame * fr, fr, channels)
    kept, normed = run(
        spatial_kernel,
        "spatial_forward",
        [sds(rows, 3 * width + channels), sent],
        [geo] + acts + [gain1, gain2, pos, spatial_weights],
        3,
        big,
    )
    (send,) = run(join_kernel, "join_sent", [both], [geo, normed, own_part] + cots[1:], 0.5)
    received = swap(send)
    parts = run(
        motion_kernel,
        "motion_projection",
        [sds(tokens, 4 * width, dtype=F32)] + [sds(tokens, 4 * width)] * (nq - 1),
        [geo, received, motion_weights],
        1.5,
    )
    factors = run(
        cut_kernel,
        "cut_factors",
        [sds(2, rows, half // 4)] * 4,
        [geo, after(received, parts[0])],
        0.5,
    )
    factors = [factors[0]] + [move(factors[d], flipped(d)) for d in range(1, 4)]
    parts = [after(parts[0], factors[0])] + [to_quad(p, s + 1) for s, p in enumerate(parts[1:])]
    (terms,) = run(temporal_kernel, "temporal_attention", [sds(tokens, 4 * width)], parts, 2)
    terms = after(terms, *factors)
    table, early_left, late_left = run(
        table_kernel,
        "positional_table_factors",
        [
            sds(tokens, channels, dtype=F32),
            sds(2, (2 * nq + 2) * tokens, half // 4),
            sds(2, 2 * (nq - 1) * tokens, half // 4),
        ],
        [after(geo, terms)] + factors,
        1.5,
    )
    all_terms = [terms] + [after(from_quad(terms, s), table) for s in range(1, nq)]
    pair_terms = [move(t, flipped(2)) for t in all_terms]
    core_terms = [move(t, flipped(1)) for t in all_terms]
    back_send, quarter = run(
        back_kernel,
        "temporal_back_projection",
        [sds(nf, 2 * nq * fr, half), sds(3, half // 4, width)],
        [geo] + all_terms + [motion_weights],
        0.01,
    )
    pair_terms[0] = after(pair_terms[0], back_send)
    last_terms = [move(pair_terms[0], flipped(1))]

    stage, block = nf // 4, half // nf
    sums, gain_sum = run(
        first_weight_kernel,
        "weight_terms_first_tokens",
        [
            sds(4, stage, block, width, dtype=F32),
            sds(1, half // 4, dtype=F32),
        ],
        [geo, early_left, quarter, table] + all_terms + core_terms
        + pair_terms[:1] + last_terms,
        0.01,
    )
    late_terms = [after(t, back_send, sums) for t in pair_terms[1:]]
    late_terms += [move(t, flipped(1)) for t in late_terms]
    parts_w = run(
        second_weight_kernel,
        "weight_terms_last_tokens",
        [sds(2 * block + 8, width)] * stage + [sds(2 * block, width)] * stage,
        [geo, sums, gain_sum, late_left, quarter, table, gain2] + late_terms,
        0.01,
        scratch=[pltpu.VMEM((4, stage, block, width), F32)],
    )

    def add(a, b):
        return (a.astype(F32) + b.astype(F32)).astype(BF16)

    back_recv = swap(back_send)
    backs = [back_recv] + [from_quad(back_recv, s) for s in range(1, nq)]
    totals = [parts_w[stage - 1], parts_w[2 * stage - 1]]
    for step in range(1, stage):
        for i in range(2):
            if step == stage - 2:
                totals[i] = after(totals[i], back_recv)
            moved = move(totals[i], ring)
            totals[i] = add(moved, parts_w[(i + 1) * stage - 1 - step])
    backs[0] = after(backs[0], *totals)
    block_output, grad_hidden = run(
        middle_kernel,
        "block_output_hidden_gradient",
        [sds(fr, pq, channels), sds(rows, channels)],
        [geo] + backs + cots + [kept, gain2],
        6,
        big,
    )
    final = []
    for g in range(nf):
        for q in range(nq):
            j = quarter_of(g % 4) * stage + g // 4
            final.append((g * nq + q, nf * q + j))
    totals = [lax.ppermute(t, ("frame", "quad"), final) for t in totals]
    (input_grad,) = run(
        tail_kernel,
        "spatial_backward",
        [sds(fr, pq, channels)],
        [grad_hidden, activations, kept, gain1, spatial_weights],
        3.5,
        big,
    )
    everyone = nf * nq
    factor = 1.0 / math.sqrt(everyone * fr * pq)
    weight_grad = jnp.concatenate([totals[0][: 2 * block], totals[1]], axis=0)
    weight_grad = weight_grad.reshape(4, block, width).astype(F32) * factor
    place = ((frame * nq + quad) % stage) * block
    gain_grad = lax.dynamic_slice(totals[0][2 * block], (place,), (block,)).astype(F32) * factor
    return block_output, input_grad, weight_grad, gain_grad


def solution(mesh):
    in_specs = (
        P("frame", "quad", None),
        P("frame", "quad", None),
        P(),
        P(),
        P(None, "quad", None),
        P(),
    )
    out_specs = (
        P("frame", "quad", None),
        P("frame", "quad", None),
        P(None, ("frame", "quad"), None),
        P(("frame", "quad")),
    )
    body = functools.partial(local, mesh.shape["quad"], mesh.shape["frame"])
    return jax.shard_map(
        body, mesh=mesh, in_specs=in_specs, out_specs=out_specs, check_vma=False
    )
```

```python
import functools
import math

import jax
import jax.numpy as jnp
from jax import lax
from jax.experimental import pallas as pl
from jax.experimental.pallas import tpu as pltpu
from jax.sharding import PartitionSpec as P

HEADS = 4
HEAD_DIM = 160
EPSILON = 1e-05
SCALE = HEAD_DIM ** (-0.5)
F32 = jnp.float32
BF16 = jnp.bfloat16


def log2(n):
    return int(n).bit_length() - 1


def dot(a, b):
    return jnp.dot(a, b, preferred_element_type=F32)


def dot_t(a, b):
    return lax.dot_general(a, b, (((1,), (1,)), ((), ())), preferred_element_type=F32)


def t_dot(a, b):
    return lax.dot_general(a, b, (((0,), (0,)), ((), ())), preferred_element_type=F32)


def normalize(values):
    average = jnp.mean(values, axis=-1, keepdims=True)
    centred = values - average
    inv_scale = lax.rsqrt(jnp.mean(centred * centred, axis=-1, keepdims=True) + EPSILON)
    return centred * inv_scale, inv_scale


def normalize_back(grad_rows, unit_rows, inv_scale, gain):
    scaled = grad_rows * gain
    first_mean = jnp.mean(scaled, axis=-1, keepdims=True)
    second_mean = jnp.mean(scaled * unit_rows, axis=-1, keepdims=True)
    return inv_scale * (scaled - first_mean - unit_rows * second_mean)


def iota(shape, dim):
    return lax.broadcasted_iota(jnp.int32, shape, dim)


def head_mask(dtype):
    lane = iota((1, HEADS * HEAD_DIM), 1)
    return [
        jnp.where((lane >= h * HEAD_DIM) & (lane < (h + 1) * HEAD_DIM), 1.0, 0.0).astype(dtype)
        for h in range(HEADS)
    ]


def stack_heads(rows):
    return jnp.concatenate([rows * mask for mask in head_mask(rows.dtype)], axis=0)


def fold_heads(stacked):
    rows = stacked.shape[0] // HEADS
    total = None
    for h, mask in enumerate(head_mask(F32)):
        piece = stacked[h * rows : (h + 1) * rows] * mask
        total = piece if total is None else total + piece
    return total


def probabilities(query_stack, keys, same):
    scores = dot_t(query_stack, keys) * SCALE
    if same is not None:
        scores = jnp.where(same, scores, -1e30)
    highest = jnp.max(scores, axis=-1, keepdims=True)
    expo = jnp.exp(scores - highest)
    return expo / jnp.sum(expo, axis=-1, keepdims=True)


def attend(query, keys, values, same):
    probs = probabilities(stack_heads(query), keys, same)
    return fold_heads(dot(probs.astype(BF16), values)).astype(BF16)


def attend_back(query, keys, values, grad, same, probs=None):
    query_stack = stack_heads(query)
    grad_stack = stack_heads(grad)
    if probs is None:
        probs = probabilities(query_stack, keys, same)
    grad_probs = dot_t(grad_stack, values)
    inner = jnp.sum(probs * grad_probs, axis=-1, keepdims=True)
    grad_scores = (probs * (grad_probs - inner) * SCALE).astype(BF16)
    grad_query = fold_heads(dot(grad_scores, keys)).astype(BF16)
    grad_key = t_dot(grad_scores, query_stack).astype(BF16)
    grad_value = t_dot(probs.astype(BF16), grad_stack).astype(BF16)
    return grad_query, grad_key, grad_value


def rows_to_sent(quad, nq, fr, pq, transposed):
    rows = nq * fr * pq
    out_dim = 1 if transposed else 0
    out = iota((rows, rows), out_dim)
    src = iota((rows, rows), 1 - out_dim)
    cell = out >> log2(nq * fr)
    other = (out >> log2(fr)) & (nq - 1)
    frame = out & (fr - 1)
    want = (((other - quad) & (nq - 1)) << log2(fr * pq)) + (frame << log2(pq)) + cell
    return jnp.where(want == src, 1.0, 0.0).astype(BF16)


def received_to_rows(quad, nq, nf, fr, transposed):
    rows = nq * nf * fr
    out_dim = 1 if transposed else 0
    out = iota((rows, rows), out_dim)
    src = iota((rows, rows), 1 - out_dim)
    step = out >> log2(nf * fr)
    device = (out >> log2(fr)) & (nf - 1)
    frame = out & (fr - 1)
    want = (device << log2(nq * fr)) + (((step + quad) & (nq - 1)) << log2(fr)) + frame
    return jnp.where(want == src, 1.0, 0.0).astype(BF16)


def own_lanes(values, quad, nq):
    width = values.shape[1] // nq
    picked = values[:, :width]
    for t in range(1, nq):
        picked = jnp.where(quad == t, values[:, t * width : (t + 1) * width], picked)
    return picked


def place_lanes(parts, quad, nq):
    placed = []
    for t in range(nq):
        piece = parts[t]
        for q in range(1, nq):
            piece = jnp.where(quad == q, parts[(t - q) % nq], piece)
        placed.append(piece)
    return jnp.concatenate(placed, axis=1)


def frame_groups(nq, fr, pq):
    size = max(1, min(fr, 128 // (nq * pq)))
    return [(start, size) for start in range(0, fr, size)]


def pick_group(rows, group, nq, fr, pq):
    start, size = group
    if size == fr:
        return rows
    cut = rows.reshape(nq, fr, pq, rows.shape[-1])[:, start : start + size]
    return cut.reshape(nq * size * pq, rows.shape[-1])


def join_groups(pieces, nq, fr, pq):
    if len(pieces) == 1:
        return pieces[0]
    size = fr // len(pieces)
    width = pieces[0].shape[-1]
    joined = jnp.concatenate([p.reshape(nq, size, pq, width) for p in pieces], axis=1)
    return joined.reshape(nq * fr * pq, width)


def same_frame(nq, size, pq):
    if size == 1:
        return None
    rows = nq * size * pq
    shape = (HEADS * rows, rows)
    left = (iota(shape, 0) >> log2(pq)) & (size - 1)
    right = (iota(shape, 1) >> log2(pq)) & (size - 1)
    return left == right


def row_of(ref):
    return ref[...].reshape(1, -1)


def flat(ref):
    value = ref[...]
    return value.reshape(-1, value.shape[-1])


def flat_wide(ref):
    value = ref[...].astype(F32)
    return value.reshape(-1, value.shape[-1])


def spread(rows, like):
    return rows.reshape(like.shape).astype(like.dtype)


def spatial_kernel(dims, *refs):
    nq, nf, fr, pq = dims
    quad, xs, refs = refs[0][0], refs[1 : 1 + nq], refs[1 + nq :]
    gain1, gain2, pos, weights, kept_out, send_out = refs
    width = HEADS * HEAD_DIM
    wide = jnp.concatenate([flat_wide(x) for x in xs], axis=0)
    unit, _ = normalize(wide)
    normed = (unit * row_of(gain1)).astype(BF16)
    query = dot(normed, weights[0]).astype(BF16)
    keys = dot(normed, weights[1]).astype(BF16)
    values = dot(normed, weights[2]).astype(BF16)
    for i, part in enumerate((query, keys, values)):
        kept_out[:, i * width : (i + 1) * width] = part
    pieces = []
    for group in frame_groups(nq, fr, pq):
        same = same_frame(nq, group[1], pq)
        cut = [pick_group(part, group, nq, fr, pq) for part in (query, keys, values)]
        pieces.append(attend(*cut, same))
    out = join_groups(pieces, nq, fr, pq)
    hidden = (wide + dot_t(out, weights[3])).astype(BF16)
    kept_out[:, 3 * width :] = hidden
    unit_two, _ = normalize(hidden.astype(F32))
    table = jnp.broadcast_to(pos[...][:, None, :], (fr, pq, pos.shape[-1]))
    table = table.reshape(fr * pq, pos.shape[-1])
    table = jnp.concatenate([table] * nq, axis=0)
    normed_two = own_lanes(unit_two * row_of(gain2) + table, quad, nq).astype(BF16)
    send_out[...] = spread(dot(rows_to_sent(quad, nq, fr, pq, False), normed_two), send_out)


def order_kernel(dims, geo, cot, weights, send_out):
    nq, nf, fr, pq = dims
    order = rows_to_sent(geo[0], nq, fr, pq, False)[:, : fr * pq]
    send_out[...] = spread(dot(order, own_lanes(flat(cot), geo[0], nq)), send_out)


def join_kernel(dims, geo, normed, own_part, *refs):
    nq, nf, fr, pq = dims
    cots, send_out = refs[:-1], refs[-1]
    order = rows_to_sent(geo[0], nq, fr, pq, False)[:, fr * pq :]
    rows = own_lanes(jnp.concatenate([flat(c) for c in cots], axis=0), geo[0], nq)
    total = own_part[...].astype(F32) + dot(order, rows).reshape(own_part.shape)
    send_out[:, : nq * fr, :] = normed[...]
    send_out[:, nq * fr :, :] = total.astype(BF16)


def sent_part(received, i, rows):
    part = received[:, i * rows : (i + 1) * rows, :].astype(F32)
    return part.reshape(-1, part.shape[-1]).astype(BF16)


def motion_kernel(dims, geo, received, weights, own_out, *sends):
    nq, nf, fr, pq = dims
    order = received_to_rows(geo[0], nq, nf, fr, False)
    normed, cot = [dot(order, sent_part(received, i, nq * fr)).astype(BF16) for i in range(2)]
    tokens = nf * fr
    for k in range(4):
        width = weights.shape[-1]
        lanes = slice(k * width, (k + 1) * width)
        product = dot(normed if k < 3 else cot, weights[k])
        own_out[:, lanes] = product[:tokens]
        for s, send in enumerate(sends):
            send[:, lanes] = product[(s + 1) * tokens : (s + 2) * tokens].astype(BF16)


def quarter_of(four):
    return ((four & 1) << 1) | (four >> 1)


def quarter_lanes(values, quarter):
    width = values.shape[1] // 4
    picked = values[:, :width]
    for t in range(1, 4):
        picked = jnp.where(quarter == t, values[:, t * width : (t + 1) * width], picked)
    return picked


def cut_kernel(dims, geo, received, *outs):
    nq, nf, fr, pq = dims
    order = received_to_rows(geo[0], nq, nf, fr, False)
    for i in range(2):
        rows = dot(order, sent_part(received, i, nq * fr))
        for d in range(4):
            outs[d][i] = quarter_lanes(rows, quarter_of(geo[1] ^ d)).astype(BF16)


def table_kernel(dims, geo, *refs):
    nq, nf, fr, pq = dims
    factors, (out, early_out, late_out) = refs[:4], refs[4:]
    shape = out.shape
    lane = iota(shape, 1)
    freq = jnp.exp((lane >> 1).astype(F32) * (-2.0 * math.log(10000.0) / shape[1]))
    turn = (lane & 1).astype(F32) * (0.5 * math.pi)
    out[...] = jnp.sin(iota(shape, 0).astype(F32) * freq + turn)
    tokens = nf * fr
    for i in range(2):
        early = [factors[0][i], factors[1][i], factors[2][i, :tokens], factors[3][i, :tokens]]
        early_out[i] = jnp.concatenate(early, axis=0)
        late = [factors[2][i, tokens:], factors[3][i, tokens:]]
        late_out[i] = jnp.concatenate(late, axis=0)


def temporal_kernel(dims, *refs):
    nq, nf, fr, pq = dims
    parts, out = refs[:nq], refs[nq]
    width = HEADS * HEAD_DIM
    total = parts[0][...]
    for part in parts[1:]:
        total = total + part[...].astype(F32)
    query, keys, values, grad = [
        total[:, k * width : (k + 1) * width].astype(BF16) for k in range(4)
    ]
    probs = probabilities(stack_heads(query), keys, None)
    motion_out = fold_heads(dot(probs.astype(BF16), values)).astype(BF16)
    grads = attend_back(query, keys, values, grad, None, probs)
    for k, piece in enumerate(grads + (motion_out,)):
        out[:, k * width : (k + 1) * width] = piece


def part_of(terms, k):
    width = HEADS * HEAD_DIM
    return jnp.concatenate([t[:, k * width : (k + 1) * width] for t in terms], axis=0)


def back_kernel(dims, quad_ref, *refs):
    nq, nf, fr, pq = dims
    terms, (weights, out, quarter_out) = refs[:nq], refs[nq:]
    order = received_to_rows(quad_ref[0], nq, nf, fr, True)
    quarter, rows = quarter_of(quad_ref[1]), quarter_out.shape[1]
    for k in range(3):
        if rows % 16 == 0:
            own = weights[k, pl.ds(pl.multiple_of(quarter * rows, 16), rows), :]
        else:
            wide = weights[k].astype(F32)
            own = wide[:rows]
            for t in range(1, 4):
                own = jnp.where(quarter == t, wide[t * rows : (t + 1) * rows], own)
            own = own.astype(BF16)
        quarter_out[k] = own
    grad = None
    for k in range(3):
        product = dot_t(part_of(terms, k), weights[k])
        grad = product if grad is None else grad + product
    delta = dot_t(part_of(terms, 3), weights[3])
    for i, rows in enumerate((grad, delta)):
        rows = dot(order, rows.astype(BF16))
        out[:, i * nq * fr : (i + 1) * nq * fr, :] = rows.reshape(nf, nq * fr, -1).astype(BF16)


def weight_sums(geo, nq, normed, cot, weights, pos, terms):
    products, grad = [], None
    for k in range(4):
        right = part_of(terms, k)
        products.append(t_dot(normed if k < 3 else cot, right))
        if k < 3:
            back = dot_t(right, weights[k])
            grad = back if grad is None else grad + back
    table = quarter_lanes(own_lanes(pos[...], geo[0], nq), quarter_of(geo[1]))
    table = jnp.concatenate([table] * len(terms), axis=0)
    return products, jnp.sum(grad * (normed.astype(F32) - table), axis=0, keepdims=True)


def first_weight_kernel(dims, geo, left, weights, pos, *refs):
    nq, nf, fr, pq = dims
    terms, (blocks, gain_out) = refs[: 2 * nq + 2], refs[2 * nq + 2 :]
    _, stage, block, _ = blocks.shape
    products, gain_out[...] = weight_sums(geo, nq, left[0], left[1], weights, pos, terms)
    for k in range(4):
        for z in range(stage):
            blocks[k, z] = products[k][z * block : (z + 1) * block]


def second_weight_kernel(dims, geo, sums, gain_sum, left, weights, pos, gain2, *refs):
    nq, nf, fr, pq = dims
    terms, outs, blocks = refs[: 2 * nq - 2], refs[2 * nq - 2 : -1], refs[-1]
    _, stage, block, width = blocks.shape
    products, gain = weight_sums(geo, nq, left[0], left[1], weights, pos, terms)
    for k in range(4):
        for z in range(stage):
            blocks[k, z] = sums[k, z] + products[k][z * block : (z + 1) * block]
    gain = gain + gain_sum[...]
    rows = gain.shape[1]
    gain = gain / quarter_lanes(own_lanes(row_of(gain2), geo[0], nq), quarter_of(geo[1]))
    extra = jnp.concatenate([gain, jnp.zeros((1, width - rows), F32)], axis=1)
    extra = jnp.where(iota((8, width), 0) == 0, extra, 0.0)
    for r in range(stage):
        z = (geo[2] + r) & (stage - 1)
        rows_out = jnp.concatenate([blocks[0, z], blocks[1, z], extra], axis=0)
        outs[r][...] = rows_out.astype(BF16)
        rows_out = jnp.concatenate([blocks[2, z], blocks[3, z]], axis=0)
        outs[stage + r][...] = rows_out.astype(BF16)


def middle_kernel(dims, *refs):
    nq, nf, fr, pq = dims
    quad, received, cots = refs[0][0], refs[1 : 1 + nq], refs[1 + nq : 1 + 2 * nq]
    kept, gain2, block_out, grad_out = refs[1 + 2 * nq :]
    own = fr * pq
    order = rows_to_sent(quad, nq, fr, pq, True)

    def lanes(i):
        parts = []
        for r in received:
            parts.append(dot(order, sent_part(r, i, nq * fr)))
        return place_lanes(parts, quad, nq)

    hidden = kept[:, 3 * HEADS * HEAD_DIM :].astype(F32)
    grad_normed, delta = lanes(0), lanes(1)
    block_out[...] = spread(hidden[:own] + delta[:own], block_out)
    unit_two, inv_two = normalize(hidden)
    cot = jnp.concatenate([flat_wide(c) for c in cots], axis=0)
    back = normalize_back(grad_normed, unit_two, inv_two, row_of(gain2))
    grad_out[...] = (cot + back).astype(BF16)


def tail_kernel(dims, grad_hidden, xs, kept, gain1, weights, in_grad):
    nq, nf, fr, pq = dims
    own, width = fr * pq, HEADS * HEAD_DIM
    grad_out = dot(grad_hidden[...], weights[3]).astype(BF16)
    parts = [kept[:, i * width : (i + 1) * width] for i in range(3)] + [grad_out]
    pieces = []
    for group in frame_groups(nq, fr, pq):
        same = same_frame(nq, group[1], pq)
        pieces.append(attend_back(*[pick_group(p, group, nq, fr, pq) for p in parts], same))
    grads = [join_groups([p[i] for p in pieces], nq, fr, pq)[:own] for i in range(3)]
    grad_one = dot_t(grads[0], weights[0]) + dot_t(grads[1], weights[1]) + dot_t(grads[2], weights[2])
    unit_one, inv_one = normalize(flat_wide(xs))
    back = normalize_back(grad_one, unit_one, inv_one, row_of(gain1))
    in_grad[...] = spread(grad_hidden[...][:own].astype(F32) + back, in_grad)


def call(kernel, name, outs, args, vmem, micros, scratch=()):
    in_specs = []
    for arg in args:
        space = pltpu.SMEM if arg.dtype == jnp.int32 else pltpu.VMEM
        in_specs.append(pl.BlockSpec(memory_space=space))
    return list(
        pl.pallas_call(
            kernel,
            out_shape=outs,
            in_specs=in_specs,
            out_specs=[pl.BlockSpec(memory_space=pltpu.VMEM) for _ in outs],
            scratch_shapes=list(scratch),
            compiler_params=pltpu.CompilerParams(vmem_limit_bytes=vmem * 1024 * 1024),
            cost_estimate=pl.CostEstimate(
                flops=int(micros * 1e9),
                bytes_accessed=2**20 if micros > 0.1 else 2**12,
                transcendentals=0,
            ),
            name=name,
        )(*args)
    )


def after(value, *others):
    return lax.optimization_barrier((value,) + others)[0]


def sds(*shape, dtype=BF16):
    return jax.ShapeDtypeStruct(shape, dtype)


def positional(first, frames, channels):
    frame_pos = (first + lax.broadcasted_iota(jnp.int32, (frames, channels), 0)).astype(F32)
    lane = lax.broadcasted_iota(jnp.int32, (frames, channels), 1)
    freq_index = (lane >> 1).astype(F32)
    phases = frame_pos * jnp.exp(freq_index * (-2.0 * math.log(10000.0) / channels))
    return jnp.sin(phases + (lane & 1).astype(F32) * (0.5 * math.pi))


def local(nq, nf, activations, cotangent, spatial_weights, spatial_gain, motion_weights, motion_gain):
    fr, pq, channels = activations.shape
    dims = (nq, nf, fr, pq)
    width = spatial_weights.shape[-1]
    half = channels // nq
    rows = nq * fr * pq
    tokens = nf * fr
    small = 16 if rows <= 256 else 40
    big = 16 if rows <= 256 else 52
    quad = lax.axis_index("quad")
    frame = lax.axis_index("frame")


    def from_quad(x, s):
        return lax.ppermute(x, "quad", [((d + s) % nq, d) for d in range(nq)])

    def to_quad(x, s):
        return lax.ppermute(x, "quad", [(d, (d + s) % nq) for d in range(nq)])

    def swap(x):
        return lax.all_to_all(x, "frame", split_axis=0, concat_axis=0, tiled=True)

    def run(kernel, name, outs, args, micros, vmem=small, **options):
        kernel = functools.partial(kernel, dims)
        return call(kernel, name, outs, args, vmem, micros, **options)

    def move(x, pairs):
        return lax.ppermute(x, "frame", pairs)

    geo = jnp.stack([quad, frame % 4, frame // 4]).astype(jnp.int32)

    def flipped(bits):
        return [(g, g ^ bits) for g in range(nf)]

    ring = [(g, (g + 4) % nf) for g in range(nf)]

    gain1, gain2 = spatial_gain, motion_gain
    sent = sds(nf, nq * fr, half)
    acts = [activations] + [from_quad(activations, s) for s in range(1, nq)]
    both = sds(nf, 2 * nq * fr, half)
    (own_part,) = run(
        order_kernel, "order_cotangent", [sent], [geo, cotangent, spatial_weights], 0.5, big
    )
    cot_later = after(cotangent, acts[-1])
    cots = [cotangent] + [from_quad(cot_later, s) for s in range(1, nq)]
    pos = positional(frame * fr, fr, channels)
    kept, normed = run(
        spatial_kernel,
        "spatial_forward",
        [sds(rows, 3 * width + channels), sent],
        [geo] + acts + [gain1, gain2, pos, spatial_weights],
        3,
        big,
    )
    (send,) = run(join_kernel, "join_sent", [both], [geo, normed, own_part] + cots[1:], 0.5)
    received = swap(send)
    parts = run(
        motion_kernel,
        "motion_projection",
        [sds(tokens, 4 * width, dtype=F32)] + [sds(tokens, 4 * width)] * (nq - 1),
        [geo, received, motion_weights],
        1.5,
    )
    factors = run(
        cut_kernel,
        "cut_factors",
        [sds(2, rows, half // 4)] * 4,
        [geo, after(received, parts[0])],
        0.5,
    )
    factors = [factors[0]] + [move(factors[d], flipped(d)) for d in range(1, 4)]
    parts = [after(parts[0], factors[0])] + [to_quad(p, s + 1) for s, p in enumerate(parts[1:])]
    (terms,) = run(temporal_kernel, "temporal_attention", [sds(tokens, 4 * width)], parts, 2)
    terms = after(terms, *factors)
    table, early_left, late_left = run(
        table_kernel,
        "positional_table_factors",
        [
            sds(tokens, channels, dtype=F32),
            sds(2, (2 * nq + 2) * tokens, half // 4),
            sds(2, 2 * (nq - 1) * tokens, half // 4),
        ],
        [after(geo, terms)] + factors,
        1.5,
    )
    all_terms = [terms] + [after(from_quad(terms, s), table) for s in range(1, nq)]
    pair_terms = [move(t, flipped(2)) for t in all_terms]
    core_terms = [move(t, flipped(1)) for t in all_terms]
    back_send, quarter = run(
        back_kernel,
        "temporal_back_projection",
        [sds(nf, 2 * nq * fr, half), sds(3, half // 4, width)],
        [geo] + all_terms + [motion_weights],
        0.01,
    )
    pair_terms[0] = after(pair_terms[0], back_send)
    last_terms = [move(pair_terms[0], flipped(1))]

    stage, block = nf // 4, half // nf
    sums, gain_sum = run(
        first_weight_kernel,
        "weight_terms_first_tokens",
        [
            sds(4, stage, block, width, dtype=F32),
            sds(1, half // 4, dtype=F32),
        ],
        [geo, early_left, quarter, table] + all_terms + core_terms
        + pair_terms[:1] + last_terms,
        0.01,
    )
    late_terms = [after(t, back_send, sums) for t in pair_terms[1:]]
    late_terms += [move(t, flipped(1)) for t in late_terms]
    parts_w = run(
        second_weight_kernel,
        "weight_terms_last_tokens",
        [sds(2 * block + 8, width)] * stage + [sds(2 * block, width)] * stage,
        [geo, sums, gain_sum, late_left, quarter, table, gain2] + late_terms,
        0.01,
        scratch=[pltpu.VMEM((4, stage, block, width), F32)],
    )

    def add(a, b):
        return (a.astype(F32) + b.astype(F32)).astype(BF16)

    back_recv = swap(back_send)
    backs = [back_recv] + [from_quad(back_recv, s) for s in range(1, nq)]
    block_output, grad_hidden = run(
        middle_kernel,
        "block_output_hidden_gradient",
        [sds(fr, pq, channels), sds(rows, channels)],
        [geo] + backs + cots + [kept, gain2],
        6,
        big,
    )
    totals = [parts_w[stage - 1], parts_w[2 * stage - 1]]
    for step in range(1, stage):
        for i in range(2):
            if step == stage - 2:
                totals[i] = after(totals[i], back_recv)
            moved = move(totals[i], ring)
            if step == stage - 1:
                moved = after(moved, grad_hidden)
            totals[i] = add(moved, parts_w[(i + 1) * stage - 1 - step])
    final = []
    for g in range(nf):
        for q in range(nq):
            j = quarter_of(g % 4) * stage + g // 4
            final.append((g * nq + q, nf * q + j))
    grad_hidden = after(grad_hidden, *totals)
    totals = [lax.ppermute(t, ("frame", "quad"), final) for t in totals]
    (input_grad,) = run(
        tail_kernel,
        "spatial_backward",
        [sds(fr, pq, channels)],
        [grad_hidden, activations, kept, gain1, spatial_weights],
        3.5,
        big,
    )
    everyone = nf * nq
    factor = 1.0 / math.sqrt(everyone * fr * pq)
    weight_grad = jnp.concatenate([totals[0][: 2 * block], totals[1]], axis=0)
    weight_grad = weight_grad.reshape(4, block, width).astype(F32) * factor
    place = ((frame * nq + quad) % stage) * block
    gain_grad = lax.dynamic_slice(totals[0][2 * block], (place,), (block,)).astype(F32) * factor
    return block_output, input_grad, weight_grad, gain_grad


def solution(mesh):
    in_specs = (
        P("frame", "quad", None),
        P("frame", "quad", None),
        P(),
        P(),
        P(None, "quad", None),
        P(),
    )
    out_specs = (
        P("frame", "quad", None),
        P("frame", "quad", None),
        P(None, ("frame", "quad"), None),
        P(("frame", "quad")),
    )
    body = functools.partial(local, mesh.shape["quad"], mesh.shape["frame"])
    return jax.shard_map(
        body, mesh=mesh, in_specs=in_specs, out_specs=out_specs, check_vma=False
    )
```

```python
import functools
import math

import jax
import jax.numpy as jnp
from jax import lax
from jax.experimental import pallas as pl
from jax.experimental.pallas import tpu as pltpu
from jax.sharding import PartitionSpec as P

HEADS = 4
HEAD_DIM = 160
EPSILON = 1e-05
SCALE = HEAD_DIM ** (-0.5)
F32 = jnp.float32
BF16 = jnp.bfloat16


def log2(n):
    return int(n).bit_length() - 1


def dot(a, b):
    return jnp.dot(a, b, preferred_element_type=F32)


def dot_t(a, b):
    return lax.dot_general(a, b, (((1,), (1,)), ((), ())), preferred_element_type=F32)


def t_dot(a, b):
    return lax.dot_general(a, b, (((0,), (0,)), ((), ())), preferred_element_type=F32)


def normalize(values):
    average = jnp.mean(values, axis=-1, keepdims=True)
    centred = values - average
    inv_scale = lax.rsqrt(jnp.mean(centred * centred, axis=-1, keepdims=True) + EPSILON)
    return centred * inv_scale, inv_scale


def normalize_back(grad_rows, unit_rows, inv_scale, gain):
    scaled = grad_rows * gain
    first_mean = jnp.mean(scaled, axis=-1, keepdims=True)
    second_mean = jnp.mean(scaled * unit_rows, axis=-1, keepdims=True)
    return inv_scale * (scaled - first_mean - unit_rows * second_mean)


def iota(shape, dim):
    return lax.broadcasted_iota(jnp.int32, shape, dim)


def head_mask(dtype):
    lane = iota((1, HEADS * HEAD_DIM), 1)
    return [
        jnp.where((lane >= h * HEAD_DIM) & (lane < (h + 1) * HEAD_DIM), 1.0, 0.0).astype(dtype)
        for h in range(HEADS)
    ]


def stack_heads(rows):
    return jnp.concatenate([rows * mask for mask in head_mask(rows.dtype)], axis=0)


def fold_heads(stacked):
    rows = stacked.shape[0] // HEADS
    total = None
    for h, mask in enumerate(head_mask(F32)):
        piece = stacked[h * rows : (h + 1) * rows] * mask
        total = piece if total is None else total + piece
    return total


def probabilities(query_stack, keys, same):
    scores = dot_t(query_stack, keys) * SCALE
    if same is not None:
        scores = jnp.where(same, scores, -1e30)
    highest = jnp.max(scores, axis=-1, keepdims=True)
    expo = jnp.exp(scores - highest)
    return expo / jnp.sum(expo, axis=-1, keepdims=True)


def attend(query, keys, values, same):
    probs = probabilities(stack_heads(query), keys, same)
    return fold_heads(dot(probs.astype(BF16), values)).astype(BF16)


def attend_back(query, keys, values, grad, same, probs=None):
    query_stack = stack_heads(query)
    grad_stack = stack_heads(grad)
    if probs is None:
        probs = probabilities(query_stack, keys, same)
    grad_probs = dot_t(grad_stack, values)
    inner = jnp.sum(probs * grad_probs, axis=-1, keepdims=True)
    grad_scores = (probs * (grad_probs - inner) * SCALE).astype(BF16)
    grad_query = fold_heads(dot(grad_scores, keys)).astype(BF16)
    grad_key = t_dot(grad_scores, query_stack).astype(BF16)
    grad_value = t_dot(probs.astype(BF16), grad_stack).astype(BF16)
    return grad_query, grad_key, grad_value


def rows_to_sent(quad, nq, fr, pq, transposed):
    rows = nq * fr * pq
    out_dim = 1 if transposed else 0
    out = iota((rows, rows), out_dim)
    src = iota((rows, rows), 1 - out_dim)
    cell = out >> log2(nq * fr)
    other = (out >> log2(fr)) & (nq - 1)
    frame = out & (fr - 1)
    want = (((other - quad) & (nq - 1)) << log2(fr * pq)) + (frame << log2(pq)) + cell
    return jnp.where(want == src, 1.0, 0.0).astype(BF16)


def received_to_rows(quad, nq, nf, fr, transposed):
    rows = nq * nf * fr
    out_dim = 1 if transposed else 0
    out = iota((rows, rows), out_dim)
    src = iota((rows, rows), 1 - out_dim)
    step = out >> log2(nf * fr)
    device = (out >> log2(fr)) & (nf - 1)
    frame = out & (fr - 1)
    want = (device << log2(nq * fr)) + (((step + quad) & (nq - 1)) << log2(fr)) + frame
    return jnp.where(want == src, 1.0, 0.0).astype(BF16)


def own_lanes(values, quad, nq):
    width = values.shape[1] // nq
    picked = values[:, :width]
    for t in range(1, nq):
        picked = jnp.where(quad == t, values[:, t * width : (t + 1) * width], picked)
    return picked


def place_lanes(parts, quad, nq):
    placed = []
    for t in range(nq):
        piece = parts[t]
        for q in range(1, nq):
            piece = jnp.where(quad == q, parts[(t - q) % nq], piece)
        placed.append(piece)
    return jnp.concatenate(placed, axis=1)


def frame_groups(nq, fr, pq):
    size = max(1, min(fr, 128 // (nq * pq)))
    return [(start, size) for start in range(0, fr, size)]


def pick_group(rows, group, nq, fr, pq):
    start, size = group
    if size == fr:
        return rows
    cut = rows.reshape(nq, fr, pq, rows.shape[-1])[:, start : start + size]
    return cut.reshape(nq * size * pq, rows.shape[-1])


def join_groups(pieces, nq, fr, pq):
    if len(pieces) == 1:
        return pieces[0]
    size = fr // len(pieces)
    width = pieces[0].shape[-1]
    joined = jnp.concatenate([p.reshape(nq, size, pq, width) for p in pieces], axis=1)
    return joined.reshape(nq * fr * pq, width)


def same_frame(nq, size, pq):
    if size == 1:
        return None
    rows = nq * size * pq
    shape = (HEADS * rows, rows)
    left = (iota(shape, 0) >> log2(pq)) & (size - 1)
    right = (iota(shape, 1) >> log2(pq)) & (size - 1)
    return left == right


def row_of(ref):
    return ref[...].reshape(1, -1)


def flat(ref):
    value = ref[...]
    return value.reshape(-1, value.shape[-1])


def flat_wide(ref):
    value = ref[...].astype(F32)
    return value.reshape(-1, value.shape[-1])


def spread(rows, like):
    return rows.reshape(like.shape).astype(like.dtype)


def spatial_kernel(dims, *refs):
    nq, nf, fr, pq = dims
    quad, xs, refs = refs[0][0], refs[1 : 1 + nq], refs[1 + nq :]
    gain1, gain2, pos, weights, kept_out, send_out = refs
    width = HEADS * HEAD_DIM
    wide = jnp.concatenate([flat_wide(x) for x in xs], axis=0)
    unit, _ = normalize(wide)
    normed = (unit * row_of(gain1)).astype(BF16)
    query = dot(normed, weights[0]).astype(BF16)
    keys = dot(normed, weights[1]).astype(BF16)
    values = dot(normed, weights[2]).astype(BF16)
    for i, part in enumerate((query, keys, values)):
        kept_out[:, i * width : (i + 1) * width] = part
    pieces = []
    for group in frame_groups(nq, fr, pq):
        same = same_frame(nq, group[1], pq)
        cut = [pick_group(part, group, nq, fr, pq) for part in (query, keys, values)]
        pieces.append(attend(*cut, same))
    out = join_groups(pieces, nq, fr, pq)
    hidden = (wide + dot_t(out, weights[3])).astype(BF16)
    kept_out[:, 3 * width :] = hidden
    unit_two, _ = normalize(hidden.astype(F32))
    table = jnp.broadcast_to(pos[...][:, None, :], (fr, pq, pos.shape[-1]))
    table = table.reshape(fr * pq, pos.shape[-1])
    table = jnp.concatenate([table] * nq, axis=0)
    normed_two = own_lanes(unit_two * row_of(gain2) + table, quad, nq).astype(BF16)
    send_out[...] = spread(dot(rows_to_sent(quad, nq, fr, pq, False), normed_two), send_out)


def order_kernel(dims, geo, cot, weights, send_out):
    nq, nf, fr, pq = dims
    order = rows_to_sent(geo[0], nq, fr, pq, False)[:, : fr * pq]
    send_out[...] = spread(dot(order, own_lanes(flat(cot), geo[0], nq)), send_out)


def join_kernel(dims, geo, normed, own_part, *refs):
    nq, nf, fr, pq = dims
    cots, send_out = refs[:-1], refs[-1]
    order = rows_to_sent(geo[0], nq, fr, pq, False)[:, fr * pq :]
    rows = own_lanes(jnp.concatenate([flat(c) for c in cots], axis=0), geo[0], nq)
    total = own_part[...].astype(F32) + dot(order, rows).reshape(own_part.shape)
    send_out[:, : nq * fr, :] = normed[...]
    send_out[:, nq * fr :, :] = total.astype(BF16)


def sent_part(received, i, rows):
    part = received[:, i * rows : (i + 1) * rows, :].astype(F32)
    return part.reshape(-1, part.shape[-1]).astype(BF16)


def motion_kernel(dims, geo, received, weights, own_out, *sends):
    nq, nf, fr, pq = dims
    order = received_to_rows(geo[0], nq, nf, fr, False)
    normed, cot = [dot(order, sent_part(received, i, nq * fr)).astype(BF16) for i in range(2)]
    tokens = nf * fr
    for k in range(4):
        width = weights.shape[-1]
        lanes = slice(k * width, (k + 1) * width)
        product = dot(normed if k < 3 else cot, weights[k])
        own_out[:, lanes] = product[:tokens]
        for s, send in enumerate(sends):
            send[:, lanes] = product[(s + 1) * tokens : (s + 2) * tokens].astype(BF16)


def gray(place):
    return place ^ (place >> 1)


def place_of(z, stage):
    place, shift = z, z >> 1
    for _ in range(log2(stage) - 1):
        place, shift = place ^ shift, shift >> 1
    return place


def quarter_of(four):
    return ((four & 1) << 1) | (four >> 1)


def quarter_lanes(values, quarter):
    width = values.shape[1] // 4
    picked = values[:, :width]
    for t in range(1, 4):
        picked = jnp.where(quarter == t, values[:, t * width : (t + 1) * width], picked)
    return picked


def cut_kernel(dims, geo, received, *outs):
    nq, nf, fr, pq = dims
    order = received_to_rows(geo[0], nq, nf, fr, False)
    for i in range(2):
        rows = dot(order, sent_part(received, i, nq * fr))
        for d in range(4):
            outs[d][i] = quarter_lanes(rows, quarter_of(geo[1] ^ d)).astype(BF16)


def table_kernel(dims, geo, *refs):
    nq, nf, fr, pq = dims
    factors, (out, early_out, late_out) = refs[:4], refs[4:]
    shape = out.shape
    lane = iota(shape, 1)
    freq = jnp.exp((lane >> 1).astype(F32) * (-2.0 * math.log(10000.0) / shape[1]))
    turn = (lane & 1).astype(F32) * (0.5 * math.pi)
    out[...] = jnp.sin(iota(shape, 0).astype(F32) * freq + turn)
    tokens = nf * fr
    for i in range(2):
        early = [factors[0][i], factors[1][i], factors[2][i, :tokens], factors[3][i, :tokens]]
        early_out[i] = jnp.concatenate(early, axis=0)
        late = [factors[2][i, tokens:], factors[3][i, tokens:]]
        late_out[i] = jnp.concatenate(late, axis=0)


def temporal_kernel(dims, *refs):
    nq, nf, fr, pq = dims
    parts, out = refs[:nq], refs[nq]
    width = HEADS * HEAD_DIM
    total = parts[0][...]
    for part in parts[1:]:
        total = total + part[...].astype(F32)
    query, keys, values, grad = [
        total[:, k * width : (k + 1) * width].astype(BF16) for k in range(4)
    ]
    probs = probabilities(stack_heads(query), keys, None)
    motion_out = fold_heads(dot(probs.astype(BF16), values)).astype(BF16)
    grads = attend_back(query, keys, values, grad, None, probs)
    for k, piece in enumerate(grads + (motion_out,)):
        out[:, k * width : (k + 1) * width] = piece


def part_of(terms, k):
    width = HEADS * HEAD_DIM
    return jnp.concatenate([t[:, k * width : (k + 1) * width] for t in terms], axis=0)


def back_kernel(dims, quad_ref, *refs):
    nq, nf, fr, pq = dims
    terms, (weights, out, quarter_out) = refs[:nq], refs[nq:]
    order = received_to_rows(quad_ref[0], nq, nf, fr, True)
    quarter, rows = quarter_of(quad_ref[1]), quarter_out.shape[1]
    for k in range(3):
        if rows % 16 == 0:
            own = weights[k, pl.ds(pl.multiple_of(quarter * rows, 16), rows), :]
        else:
            wide = weights[k].astype(F32)
            own = wide[:rows]
            for t in range(1, 4):
                own = jnp.where(quarter == t, wide[t * rows : (t + 1) * rows], own)
            own = own.astype(BF16)
        quarter_out[k] = own
    grad = None
    for k in range(3):
        product = dot_t(part_of(terms, k), weights[k])
        grad = product if grad is None else grad + product
    delta = dot_t(part_of(terms, 3), weights[3])
    for i, rows in enumerate((grad, delta)):
        rows = dot(order, rows.astype(BF16))
        out[:, i * nq * fr : (i + 1) * nq * fr, :] = rows.reshape(nf, nq * fr, -1).astype(BF16)


def weight_sums(geo, nq, normed, cot, weights, pos, terms):
    products, grad = [], None
    for k in range(4):
        right = part_of(terms, k)
        products.append(t_dot(normed if k < 3 else cot, right))
        if k < 3:
            back = dot_t(right, weights[k])
            grad = back if grad is None else grad + back
    table = quarter_lanes(own_lanes(pos[...], geo[0], nq), quarter_of(geo[1]))
    table = jnp.concatenate([table] * len(terms), axis=0)
    return products, jnp.sum(grad * (normed.astype(F32) - table), axis=0, keepdims=True)


def first_weight_kernel(dims, geo, left, weights, pos, *refs):
    nq, nf, fr, pq = dims
    terms, (blocks, gain_out) = refs[: 2 * nq + 2], refs[2 * nq + 2 :]
    _, stage, block, _ = blocks.shape
    products, gain_out[...] = weight_sums(geo, nq, left[0], left[1], weights, pos, terms)
    for k in range(4):
        for z in range(stage):
            blocks[k, z] = products[k][z * block : (z + 1) * block]


def second_weight_kernel(dims, geo, sums, gain_sum, left, weights, pos, gain2, *refs):
    nq, nf, fr, pq = dims
    terms, outs, blocks = refs[: 2 * nq - 2], refs[2 * nq - 2 : -1], refs[-1]
    _, stage, block, width = blocks.shape
    products, gain = weight_sums(geo, nq, left[0], left[1], weights, pos, terms)
    for k in range(4):
        for z in range(stage):
            blocks[k, z] = sums[k, z] + products[k][z * block : (z + 1) * block]
    gain = gain + gain_sum[...]
    rows = gain.shape[1]
    gain = gain / quarter_lanes(own_lanes(row_of(gain2), geo[0], nq), quarter_of(geo[1]))
    extra = jnp.concatenate([gain, jnp.zeros((1, width - rows), F32)], axis=1)
    extra = jnp.where(iota((8, width), 0) == 0, extra, 0.0)
    for r in range(stage):
        z = gray((place_of(geo[2], stage) + r) & (stage - 1))
        rows_out = jnp.concatenate([blocks[0, z], blocks[1, z], extra], axis=0)
        outs[r][...] = rows_out.astype(BF16)
        rows_out = jnp.concatenate([blocks[2, z], blocks[3, z]], axis=0)
        outs[stage + r][...] = rows_out.astype(BF16)


def middle_kernel(dims, *refs):
    nq, nf, fr, pq = dims
    quad, received, cots = refs[0][0], refs[1 : 1 + nq], refs[1 + nq : 1 + 2 * nq]
    kept, gain2, block_out, grad_out = refs[1 + 2 * nq :]
    own = fr * pq
    order = rows_to_sent(quad, nq, fr, pq, True)

    def lanes(i):
        parts = []
        for r in received:
            parts.append(dot(order, sent_part(r, i, nq * fr)))
        return place_lanes(parts, quad, nq)

    hidden = kept[:, 3 * HEADS * HEAD_DIM :].astype(F32)
    grad_normed, delta = lanes(0), lanes(1)
    block_out[...] = spread(hidden[:own] + delta[:own], block_out)
    unit_two, inv_two = normalize(hidden)
    cot = jnp.concatenate([flat_wide(c) for c in cots], axis=0)
    back = normalize_back(grad_normed, unit_two, inv_two, row_of(gain2))
    grad_out[...] = (cot + back).astype(BF16)


def tail_kernel(dims, grad_hidden, xs, kept, gain1, weights, in_grad):
    nq, nf, fr, pq = dims
    own, width = fr * pq, HEADS * HEAD_DIM
    grad_out = dot(grad_hidden[...], weights[3]).astype(BF16)
    parts = [kept[:, i * width : (i + 1) * width] for i in range(3)] + [grad_out]
    pieces = []
    for group in frame_groups(nq, fr, pq):
        same = same_frame(nq, group[1], pq)
        pieces.append(attend_back(*[pick_group(p, group, nq, fr, pq) for p in parts], same))
    grads = [join_groups([p[i] for p in pieces], nq, fr, pq)[:own] for i in range(3)]
    grad_one = dot_t(grads[0], weights[0]) + dot_t(grads[1], weights[1]) + dot_t(grads[2], weights[2])
    unit_one, inv_one = normalize(flat_wide(xs))
    back = normalize_back(grad_one, unit_one, inv_one, row_of(gain1))
    in_grad[...] = spread(grad_hidden[...][:own].astype(F32) + back, in_grad)


def call(kernel, name, outs, args, vmem, micros, scratch=()):
    in_specs = []
    for arg in args:
        space = pltpu.SMEM if arg.dtype == jnp.int32 else pltpu.VMEM
        in_specs.append(pl.BlockSpec(memory_space=space))
    return list(
        pl.pallas_call(
            kernel,
            out_shape=outs,
            in_specs=in_specs,
            out_specs=[pl.BlockSpec(memory_space=pltpu.VMEM) for _ in outs],
            scratch_shapes=list(scratch),
            compiler_params=pltpu.CompilerParams(vmem_limit_bytes=vmem * 1024 * 1024),
            cost_estimate=pl.CostEstimate(
                flops=int(micros * 1e9),
                bytes_accessed=2**20 if micros > 0.1 else 2**12,
                transcendentals=0,
            ),
            name=name,
        )(*args)
    )


def after(value, *others):
    return lax.optimization_barrier((value,) + others)[0]


def sds(*shape, dtype=BF16):
    return jax.ShapeDtypeStruct(shape, dtype)


def positional(first, frames, channels):
    frame_pos = (first + lax.broadcasted_iota(jnp.int32, (frames, channels), 0)).astype(F32)
    lane = lax.broadcasted_iota(jnp.int32, (frames, channels), 1)
    freq_index = (lane >> 1).astype(F32)
    phases = frame_pos * jnp.exp(freq_index * (-2.0 * math.log(10000.0) / channels))
    return jnp.sin(phases + (lane & 1).astype(F32) * (0.5 * math.pi))


def local(nq, nf, activations, cotangent, spatial_weights, spatial_gain, motion_weights, motion_gain):
    fr, pq, channels = activations.shape
    dims = (nq, nf, fr, pq)
    width = spatial_weights.shape[-1]
    half = channels // nq
    rows = nq * fr * pq
    tokens = nf * fr
    small = 16 if rows <= 256 else 40
    big = 16 if rows <= 256 else 52
    quad = lax.axis_index("quad")
    frame = lax.axis_index("frame")


    def from_quad(x, s):
        return lax.ppermute(x, "quad", [((d + s) % nq, d) for d in range(nq)])

    def to_quad(x, s):
        return lax.ppermute(x, "quad", [(d, (d + s) % nq) for d in range(nq)])

    def swap(x):
        return lax.all_to_all(x, "frame", split_axis=0, concat_axis=0, tiled=True)

    def run(kernel, name, outs, args, micros, vmem=small, **options):
        kernel = functools.partial(kernel, dims)
        return call(kernel, name, outs, args, vmem, micros, **options)

    def move(x, pairs):
        return lax.ppermute(x, "frame", pairs)

    geo = jnp.stack([quad, frame % 4, frame // 4]).astype(jnp.int32)

    def flipped(bits):
        return [(g, g ^ bits) for g in range(nf)]

    turns = [gray((place_of(z, nf // 4) + 1) % (nf // 4)) for z in range(nf // 4)]
    ring = [(g, turns[g // 4] * 4 + g % 4) for g in range(nf)]

    gain1, gain2 = spatial_gain, motion_gain
    sent = sds(nf, nq * fr, half)
    acts = [activations] + [from_quad(activations, s) for s in range(1, nq)]
    both = sds(nf, 2 * nq * fr, half)
    (own_part,) = run(
        order_kernel, "order_cotangent", [sent], [geo, cotangent, spatial_weights], 0.5, big
    )
    cot_later = after(cotangent, acts[-1])
    cots = [cotangent] + [from_quad(cot_later, s) for s in range(1, nq)]
    pos = positional(frame * fr, fr, channels)
    kept, normed = run(
        spatial_kernel,
        "spatial_forward",
        [sds(rows, 3 * width + channels), sent],
        [geo] + acts + [gain1, gain2, pos, spatial_weights],
        3,
        big,
    )
    (send,) = run(join_kernel, "join_sent", [both], [geo, normed, own_part] + cots[1:], 0.5)
    received = swap(send)
    parts = run(
        motion_kernel,
        "motion_projection",
        [sds(tokens, 4 * width, dtype=F32)] + [sds(tokens, 4 * width)] * (nq - 1),
        [geo, received, motion_weights],
        1.5,
    )
    factors = run(
        cut_kernel,
        "cut_factors",
        [sds(2, rows, half // 4)] * 4,
        [geo, after(received, parts[0])],
        0.5,
    )
    factors = [factors[0]] + [move(factors[d], flipped(d)) for d in range(1, 4)]
    parts = [after(parts[0], factors[0])] + [to_quad(p, s + 1) for s, p in enumerate(parts[1:])]
    (terms,) = run(temporal_kernel, "temporal_attention", [sds(tokens, 4 * width)], parts, 2)
    terms = after(terms, *factors)
    table, early_left, late_left = run(
        table_kernel,
        "positional_table_factors",
        [
            sds(tokens, channels, dtype=F32),
            sds(2, (2 * nq + 2) * tokens, half // 4),
            sds(2, 2 * (nq - 1) * tokens, half // 4),
        ],
        [after(geo, terms)] + factors,
        1.5,
    )
    all_terms = [terms] + [after(from_quad(terms, s), table) for s in range(1, nq)]
    pair_terms = [move(t, flipped(2)) for t in all_terms]
    core_terms = [move(t, flipped(1)) for t in all_terms]
    back_send, quarter = run(
        back_kernel,
        "temporal_back_projection",
        [sds(nf, 2 * nq * fr, half), sds(3, half // 4, width)],
        [geo, after(all_terms[0], core_terms[-1])] + all_terms[1:] + [motion_weights],
        0.01,
    )
    pair_terms[0] = after(pair_terms[0], back_send)
    last_terms = [move(pair_terms[0], flipped(1))]

    stage, block = nf // 4, half // nf
    sums, gain_sum = run(
        first_weight_kernel,
        "weight_terms_first_tokens",
        [
            sds(4, stage, block, width, dtype=F32),
            sds(1, half // 4, dtype=F32),
        ],
        [geo, early_left, quarter, table] + all_terms + core_terms
        + pair_terms[:1] + last_terms,
        0.01,
    )
    late_terms = [after(t, back_send, sums) for t in pair_terms[1:]]
    late_terms += [move(t, flipped(1)) for t in late_terms]
    parts_w = run(
        second_weight_kernel,
        "weight_terms_last_tokens",
        [sds(2 * block + 8, width)] * stage + [sds(2 * block, width)] * stage,
        [geo, sums, gain_sum, late_left, quarter, table, gain2] + late_terms,
        0.01,
        scratch=[pltpu.VMEM((4, stage, block, width), F32)],
    )

    def add(a, b):
        return (a.astype(F32) + b.astype(F32)).astype(BF16)

    back_recv = swap(back_send)
    backs = [back_recv] + [from_quad(back_recv, s) for s in range(1, nq)]
    block_output, grad_hidden = run(
        middle_kernel,
        "block_output_hidden_gradient",
        [sds(fr, pq, channels), sds(rows, channels)],
        [geo] + backs + cots + [kept, gain2],
        6,
        big,
    )
    totals = [parts_w[stage - 1], parts_w[2 * stage - 1]]
    for step in range(1, stage):
        for i in range(2):
            if step == stage - 2:
                totals[i] = after(totals[i], back_recv)
            moved = move(totals[i], ring)
            if step == stage - 1:
                moved = after(moved, grad_hidden)
            totals[i] = add(moved, parts_w[(i + 1) * stage - 1 - step])
    final = []
    for g in range(nf):
        for q in range(nq):
            j = quarter_of(g % 4) * stage + g // 4
            final.append((g * nq + q, nf * q + j))
    grad_hidden = after(grad_hidden, *totals)
    totals = [lax.ppermute(t, ("frame", "quad"), final) for t in totals]
    (input_grad,) = run(
        tail_kernel,
        "spatial_backward",
        [sds(fr, pq, channels)],
        [grad_hidden, activations, kept, gain1, spatial_weights],
        3.5,
        big,
    )
    everyone = nf * nq
    factor = 1.0 / math.sqrt(everyone * fr * pq)
    weight_grad = jnp.concatenate([totals[0][: 2 * block], totals[1]], axis=0)
    weight_grad = weight_grad.reshape(4, block, width).astype(F32) * factor
    place = ((frame * nq + quad) % stage) * block
    gain_grad = lax.dynamic_slice(totals[0][2 * block], (place,), (block,)).astype(F32) * factor
    return block_output, input_grad, weight_grad, gain_grad


def solution(mesh):
    in_specs = (
        P("frame", "quad", None),
        P("frame", "quad", None),
        P(),
        P(),
        P(None, "quad", None),
        P(),
    )
    out_specs = (
        P("frame", "quad", None),
        P("frame", "quad", None),
        P(None, ("frame", "quad"), None),
        P(("frame", "quad")),
    )
    body = functools.partial(local, mesh.shape["quad"], mesh.shape["frame"])
    return jax.shard_map(
        body, mesh=mesh, in_specs=in_specs, out_specs=out_specs, check_vma=False
    )
```

```python
import functools
import math

import jax
import jax.numpy as jnp
from jax import lax
from jax.experimental import pallas as pl
from jax.experimental.pallas import tpu as pltpu
from jax.sharding import PartitionSpec as P

HEADS = 4
HEAD_DIM = 160
EPSILON = 1e-05
SCALE = HEAD_DIM ** (-0.5)
F32 = jnp.float32
BF16 = jnp.bfloat16


def log2(n):
    return int(n).bit_length() - 1


def dot(a, b):
    return jnp.dot(a, b, preferred_element_type=F32)


def dot_t(a, b):
    return lax.dot_general(a, b, (((1,), (1,)), ((), ())), preferred_element_type=F32)


def t_dot(a, b):
    return lax.dot_general(a, b, (((0,), (0,)), ((), ())), preferred_element_type=F32)


def normalize(values):
    average = jnp.mean(values, axis=-1, keepdims=True)
    centred = values - average
    inv_scale = lax.rsqrt(jnp.mean(centred * centred, axis=-1, keepdims=True) + EPSILON)
    return centred * inv_scale, inv_scale


def normalize_back(grad_rows, unit_rows, inv_scale, gain):
    scaled = grad_rows * gain
    first_mean = jnp.mean(scaled, axis=-1, keepdims=True)
    second_mean = jnp.mean(scaled * unit_rows, axis=-1, keepdims=True)
    return inv_scale * (scaled - first_mean - unit_rows * second_mean)


def iota(shape, dim):
    return lax.broadcasted_iota(jnp.int32, shape, dim)


def head_mask(dtype):
    lane = iota((1, HEADS * HEAD_DIM), 1)
    return [
        jnp.where((lane >= h * HEAD_DIM) & (lane < (h + 1) * HEAD_DIM), 1.0, 0.0).astype(dtype)
        for h in range(HEADS)
    ]


def stack_heads(rows):
    return jnp.concatenate([rows * mask for mask in head_mask(rows.dtype)], axis=0)


def fold_heads(stacked):
    rows = stacked.shape[0] // HEADS
    total = None
    for h, mask in enumerate(head_mask(F32)):
        piece = stacked[h * rows : (h + 1) * rows] * mask
        total = piece if total is None else total + piece
    return total


def probabilities(query_stack, keys, same):
    scores = dot_t(query_stack, keys) * SCALE
    if same is not None:
        scores = jnp.where(same, scores, -1e30)
    highest = jnp.max(scores, axis=-1, keepdims=True)
    expo = jnp.exp(scores - highest)
    return expo / jnp.sum(expo, axis=-1, keepdims=True)


def attend(query, keys, values, same):
    probs = probabilities(stack_heads(query), keys, same)
    return fold_heads(dot(probs.astype(BF16), values)).astype(BF16)


def attend_back(query, keys, values, grad, same, probs=None):
    query_stack = stack_heads(query)
    grad_stack = stack_heads(grad)
    if probs is None:
        probs = probabilities(query_stack, keys, same)
    grad_probs = dot_t(grad_stack, values)
    inner = jnp.sum(probs * grad_probs, axis=-1, keepdims=True)
    grad_scores = (probs * (grad_probs - inner) * SCALE).astype(BF16)
    grad_query = fold_heads(dot(grad_scores, keys)).astype(BF16)
    grad_key = t_dot(grad_scores, query_stack).astype(BF16)
    grad_value = t_dot(probs.astype(BF16), grad_stack).astype(BF16)
    return grad_query, grad_key, grad_value


def rows_to_sent(quad, nq, fr, pq, transposed):
    rows = nq * fr * pq
    out_dim = 1 if transposed else 0
    out = iota((rows, rows), out_dim)
    src = iota((rows, rows), 1 - out_dim)
    cell = out >> log2(nq * fr)
    other = (out >> log2(fr)) & (nq - 1)
    frame = out & (fr - 1)
    want = (((other - quad) & (nq - 1)) << log2(fr * pq)) + (frame << log2(pq)) + cell
    return jnp.where(want == src, 1.0, 0.0).astype(BF16)


def received_to_rows(quad, nq, nf, fr, transposed):
    rows = nq * nf * fr
    out_dim = 1 if transposed else 0
    out = iota((rows, rows), out_dim)
    src = iota((rows, rows), 1 - out_dim)
    step = out >> log2(nf * fr)
    device = (out >> log2(fr)) & (nf - 1)
    frame = out & (fr - 1)
    want = (device << log2(nq * fr)) + (((step + quad) & (nq - 1)) << log2(fr)) + frame
    return jnp.where(want == src, 1.0, 0.0).astype(BF16)


def own_lanes(values, quad, nq):
    width = values.shape[1] // nq
    picked = values[:, :width]
    for t in range(1, nq):
        picked = jnp.where(quad == t, values[:, t * width : (t + 1) * width], picked)
    return picked


def place_lanes(parts, quad, nq):
    placed = []
    for t in range(nq):
        piece = parts[t]
        for q in range(1, nq):
            piece = jnp.where(quad == q, parts[(t - q) % nq], piece)
        placed.append(piece)
    return jnp.concatenate(placed, axis=1)


def frame_groups(nq, fr, pq):
    size = max(1, min(fr, 128 // (nq * pq)))
    return [(start, size) for start in range(0, fr, size)]


def pick_group(rows, group, nq, fr, pq):
    start, size = group
    if size == fr:
        return rows
    cut = rows.reshape(nq, fr, pq, rows.shape[-1])[:, start : start + size]
    return cut.reshape(nq * size * pq, rows.shape[-1])


def join_groups(pieces, nq, fr, pq):
    if len(pieces) == 1:
        return pieces[0]
    size = fr // len(pieces)
    width = pieces[0].shape[-1]
    joined = jnp.concatenate([p.reshape(nq, size, pq, width) for p in pieces], axis=1)
    return joined.reshape(nq * fr * pq, width)


def same_frame(nq, size, pq):
    if size == 1:
        return None
    rows = nq * size * pq
    shape = (HEADS * rows, rows)
    left = (iota(shape, 0) >> log2(pq)) & (size - 1)
    right = (iota(shape, 1) >> log2(pq)) & (size - 1)
    return left == right


def row_of(ref):
    return ref[...].reshape(1, -1)


def flat(ref):
    value = ref[...]
    return value.reshape(-1, value.shape[-1])


def flat_wide(ref):
    value = ref[...].astype(F32)
    return value.reshape(-1, value.shape[-1])


def spread(rows, like):
    return rows.reshape(like.shape).astype(like.dtype)


def spatial_kernel(dims, *refs):
    nq, nf, fr, pq = dims
    quad, xs, refs = refs[0][0], refs[1 : 1 + nq], refs[1 + nq :]
    gain1, gain2, pos, weights, kept_out, send_out = refs
    width = HEADS * HEAD_DIM
    wide = jnp.concatenate([flat_wide(x) for x in xs], axis=0)
    unit, _ = normalize(wide)
    normed = (unit * row_of(gain1)).astype(BF16)
    query = dot(normed, weights[0]).astype(BF16)
    keys = dot(normed, weights[1]).astype(BF16)
    values = dot(normed, weights[2]).astype(BF16)
    for i, part in enumerate((query, keys, values)):
        kept_out[:, i * width : (i + 1) * width] = part
    pieces = []
    for group in frame_groups(nq, fr, pq):
        same = same_frame(nq, group[1], pq)
        cut = [pick_group(part, group, nq, fr, pq) for part in (query, keys, values)]
        pieces.append(attend(*cut, same))
    out = join_groups(pieces, nq, fr, pq)
    hidden = (wide + dot_t(out, weights[3])).astype(BF16)
    kept_out[:, 3 * width :] = hidden
    unit_two, _ = normalize(hidden.astype(F32))
    table = jnp.broadcast_to(pos[...][:, None, :], (fr, pq, pos.shape[-1]))
    table = table.reshape(fr * pq, pos.shape[-1])
    table = jnp.concatenate([table] * nq, axis=0)
    normed_two = own_lanes(unit_two * row_of(gain2) + table, quad, nq).astype(BF16)
    send_out[...] = spread(dot(rows_to_sent(quad, nq, fr, pq, False), normed_two), send_out)


def order_kernel(dims, geo, cot, weights, send_out):
    nq, nf, fr, pq = dims
    order = rows_to_sent(geo[0], nq, fr, pq, False)[:, : fr * pq]
    send_out[...] = spread(dot(order, own_lanes(flat(cot), geo[0], nq)), send_out)


def join_kernel(dims, geo, normed, own_part, *refs):
    nq, nf, fr, pq = dims
    cots, send_out = refs[:-1], refs[-1]
    order = rows_to_sent(geo[0], nq, fr, pq, False)[:, fr * pq :]
    rows = own_lanes(jnp.concatenate([flat(c) for c in cots], axis=0), geo[0], nq)
    total = own_part[...].astype(F32) + dot(order, rows).reshape(own_part.shape)
    send_out[:, : nq * fr, :] = normed[...]
    send_out[:, nq * fr :, :] = total.astype(BF16)


def sent_part(received, i, rows):
    part = received[:, i * rows : (i + 1) * rows, :].astype(F32)
    return part.reshape(-1, part.shape[-1]).astype(BF16)


def motion_kernel(dims, geo, received, weights, own_out, *sends):
    nq, nf, fr, pq = dims
    order = received_to_rows(geo[0], nq, nf, fr, False)
    normed, cot = [dot(order, sent_part(received, i, nq * fr)).astype(BF16) for i in range(2)]
    tokens = nf * fr
    for k in range(4):
        width = weights.shape[-1]
        lanes = slice(k * width, (k + 1) * width)
        product = dot(normed if k < 3 else cot, weights[k])
        own_out[:, lanes] = product[:tokens]
        for s, send in enumerate(sends):
            send[:, lanes] = product[(s + 1) * tokens : (s + 2) * tokens].astype(BF16)


def gray(place):
    return place ^ (place >> 1)


def place_of(z, stage):
    place, shift = z, z >> 1
    for _ in range(log2(stage) - 1):
        place, shift = place ^ shift, shift >> 1
    return place


def quarter_of(four):
    return ((four & 1) << 1) | (four >> 1)


def quarter_lanes(values, quarter):
    width = values.shape[1] // 4
    picked = values[:, :width]
    for t in range(1, 4):
        picked = jnp.where(quarter == t, values[:, t * width : (t + 1) * width], picked)
    return picked


def cut_kernel(dims, geo, received, *outs):
    nq, nf, fr, pq = dims
    order = received_to_rows(geo[0], nq, nf, fr, False)
    for i in range(2):
        rows = dot(order, sent_part(received, i, nq * fr))
        for d in range(4):
            outs[d][i] = quarter_lanes(rows, quarter_of(geo[1] ^ d)).astype(BF16)


def table_kernel(dims, geo, *refs):
    nq, nf, fr, pq = dims
    factors, (out, early_out, late_out) = refs[:4], refs[4:]
    shape = out.shape
    lane = iota(shape, 1)
    freq = jnp.exp((lane >> 1).astype(F32) * (-2.0 * math.log(10000.0) / shape[1]))
    turn = (lane & 1).astype(F32) * (0.5 * math.pi)
    out[...] = jnp.sin(iota(shape, 0).astype(F32) * freq + turn)
    tokens = nf * fr
    for i in range(2):
        early = [factors[0][i], factors[1][i], factors[2][i, :tokens], factors[3][i, :tokens]]
        early_out[i] = jnp.concatenate(early, axis=0)
        late = [factors[2][i, tokens:], factors[3][i, tokens:]]
        late_out[i] = jnp.concatenate(late, axis=0)


def temporal_kernel(dims, *refs):
    nq, nf, fr, pq = dims
    parts, out = refs[:nq], refs[nq]
    width = HEADS * HEAD_DIM
    total = parts[0][...]
    for part in parts[1:]:
        total = total + part[...].astype(F32)
    query, keys, values, grad = [
        total[:, k * width : (k + 1) * width].astype(BF16) for k in range(4)
    ]
    probs = probabilities(stack_heads(query), keys, None)
    motion_out = fold_heads(dot(probs.astype(BF16), values)).astype(BF16)
    grads = attend_back(query, keys, values, grad, None, probs)
    for k, piece in enumerate(grads + (motion_out,)):
        out[:, k * width : (k + 1) * width] = piece


def part_of(terms, k):
    width = HEADS * HEAD_DIM
    return jnp.concatenate([t[:, k * width : (k + 1) * width] for t in terms], axis=0)


def back_kernel(dims, quad_ref, *refs):
    nq, nf, fr, pq = dims
    terms, (weights, out, quarter_out) = refs[:nq], refs[nq:]
    order = received_to_rows(quad_ref[0], nq, nf, fr, True)
    quarter, rows = quarter_of(quad_ref[1]), quarter_out.shape[1]
    for k in range(3):
        if rows % 16 == 0:
            own = weights[k, pl.ds(pl.multiple_of(quarter * rows, 16), rows), :]
        else:
            wide = weights[k].astype(F32)
            own = wide[:rows]
            for t in range(1, 4):
                own = jnp.where(quarter == t, wide[t * rows : (t + 1) * rows], own)
            own = own.astype(BF16)
        quarter_out[k] = own
    grad = None
    for k in range(3):
        product = dot_t(part_of(terms, k), weights[k])
        grad = product if grad is None else grad + product
    delta = dot_t(part_of(terms, 3), weights[3])
    for i, rows in enumerate((grad, delta)):
        rows = dot(order, rows.astype(BF16))
        out[:, i * nq * fr : (i + 1) * nq * fr, :] = rows.reshape(nf, nq * fr, -1).astype(BF16)


def weight_sums(geo, nq, normed, cot, weights, pos, terms):
    products, grad = [], None
    for k in range(4):
        right = part_of(terms, k)
        products.append(t_dot(normed if k < 3 else cot, right))
        if k < 3:
            back = dot_t(right, weights[k])
            grad = back if grad is None else grad + back
    table = quarter_lanes(own_lanes(pos[...], geo[0], nq), quarter_of(geo[1]))
    table = jnp.concatenate([table] * len(terms), axis=0)
    return products, jnp.sum(grad * (normed.astype(F32) - table), axis=0, keepdims=True)


def first_weight_kernel(dims, geo, left, weights, pos, *refs):
    nq, nf, fr, pq = dims
    terms, (blocks, gain_out) = refs[: 2 * nq + 2], refs[2 * nq + 2 :]
    _, stage, block, _ = blocks.shape
    products, gain_out[...] = weight_sums(geo, nq, left[0], left[1], weights, pos, terms)
    for k in range(4):
        for z in range(stage):
            blocks[k, z] = products[k][z * block : (z + 1) * block]


def second_weight_kernel(dims, geo, sums, gain_sum, left, weights, pos, gain2, *refs):
    nq, nf, fr, pq = dims
    terms, outs, blocks = refs[: 2 * nq - 2], refs[2 * nq - 2 : -1], refs[-1]
    _, stage, block, width = blocks.shape
    products, gain = weight_sums(geo, nq, left[0], left[1], weights, pos, terms)
    for k in range(4):
        for z in range(stage):
            blocks[k, z] = sums[k, z] + products[k][z * block : (z + 1) * block]
    gain = gain + gain_sum[...]
    rows = gain.shape[1]
    gain = gain / quarter_lanes(own_lanes(row_of(gain2), geo[0], nq), quarter_of(geo[1]))
    extra = jnp.concatenate([gain, jnp.zeros((1, width - rows), F32)], axis=1)
    extra = jnp.where(iota((8, width), 0) == 0, extra, 0.0)
    for r in range(stage):
        z = gray((place_of(geo[2], stage) + r) & (stage - 1))
        rows_out = jnp.concatenate([blocks[0, z], blocks[1, z], extra], axis=0)
        outs[r][...] = rows_out.astype(BF16)
        rows_out = jnp.concatenate([blocks[2, z], blocks[3, z]], axis=0)
        outs[stage + r][...] = rows_out.astype(BF16)


def middle_kernel(dims, *refs):
    nq, nf, fr, pq = dims
    quad, received, cots = refs[0][0], refs[1 : 1 + nq], refs[1 + nq : 1 + 2 * nq]
    kept, gain2, block_out, grad_out = refs[1 + 2 * nq :]
    own = fr * pq
    order = rows_to_sent(quad, nq, fr, pq, True)

    def lanes(i):
        parts = []
        for r in received:
            parts.append(dot(order, sent_part(r, i, nq * fr)))
        return place_lanes(parts, quad, nq)

    hidden = kept[:, 3 * HEADS * HEAD_DIM :].astype(F32)
    grad_normed, delta = lanes(0), lanes(1)
    block_out[...] = spread(hidden[:own] + delta[:own], block_out)
    unit_two, inv_two = normalize(hidden)
    cot = jnp.concatenate([flat_wide(c) for c in cots], axis=0)
    back = normalize_back(grad_normed, unit_two, inv_two, row_of(gain2))
    grad_out[...] = (cot + back).astype(BF16)


def tail_kernel(dims, grad_hidden, xs, kept, gain1, weights, in_grad):
    nq, nf, fr, pq = dims
    own, width = fr * pq, HEADS * HEAD_DIM
    grad_out = dot(grad_hidden[...], weights[3]).astype(BF16)
    parts = [kept[:, i * width : (i + 1) * width] for i in range(3)] + [grad_out]
    pieces = []
    for group in frame_groups(nq, fr, pq):
        same = same_frame(nq, group[1], pq)
        pieces.append(attend_back(*[pick_group(p, group, nq, fr, pq) for p in parts], same))
    grads = [join_groups([p[i] for p in pieces], nq, fr, pq)[:own] for i in range(3)]
    grad_one = dot_t(grads[0], weights[0]) + dot_t(grads[1], weights[1]) + dot_t(grads[2], weights[2])
    unit_one, inv_one = normalize(flat_wide(xs))
    back = normalize_back(grad_one, unit_one, inv_one, row_of(gain1))
    in_grad[...] = spread(grad_hidden[...][:own].astype(F32) + back, in_grad)


def call(kernel, name, outs, args, vmem, micros, scratch=()):
    in_specs = []
    for arg in args:
        space = pltpu.SMEM if arg.dtype == jnp.int32 else pltpu.VMEM
        in_specs.append(pl.BlockSpec(memory_space=space))
    return list(
        pl.pallas_call(
            kernel,
            out_shape=outs,
            in_specs=in_specs,
            out_specs=[pl.BlockSpec(memory_space=pltpu.VMEM) for _ in outs],
            scratch_shapes=list(scratch),
            compiler_params=pltpu.CompilerParams(vmem_limit_bytes=vmem * 1024 * 1024),
            cost_estimate=pl.CostEstimate(
                flops=int(micros * 1e9),
                bytes_accessed=2**20 if micros > 0.1 else 2**12,
                transcendentals=0,
            ),
            name=name,
        )(*args)
    )


def after(value, *others):
    return lax.optimization_barrier((value,) + others)[0]


def sds(*shape, dtype=BF16):
    return jax.ShapeDtypeStruct(shape, dtype)


def positional(first, frames, channels):
    frame_pos = (first + lax.broadcasted_iota(jnp.int32, (frames, channels), 0)).astype(F32)
    lane = lax.broadcasted_iota(jnp.int32, (frames, channels), 1)
    freq_index = (lane >> 1).astype(F32)
    phases = frame_pos * jnp.exp(freq_index * (-2.0 * math.log(10000.0) / channels))
    return jnp.sin(phases + (lane & 1).astype(F32) * (0.5 * math.pi))


def local(nq, nf, activations, cotangent, spatial_weights, spatial_gain, motion_weights, motion_gain):
    fr, pq, channels = activations.shape
    dims = (nq, nf, fr, pq)
    width = spatial_weights.shape[-1]
    half = channels // nq
    rows = nq * fr * pq
    tokens = nf * fr
    small = 16 if rows <= 256 else 40
    big = 16 if rows <= 256 else 52
    quad = lax.axis_index("quad")
    frame = lax.axis_index("frame")


    def from_quad(x, s):
        return lax.ppermute(x, "quad", [((d + s) % nq, d) for d in range(nq)])

    def to_quad(x, s):
        return lax.ppermute(x, "quad", [(d, (d + s) % nq) for d in range(nq)])

    def swap(x):
        return lax.all_to_all(x, "frame", split_axis=0, concat_axis=0, tiled=True)

    def run(kernel, name, outs, args, micros, vmem=small, **options):
        kernel = functools.partial(kernel, dims)
        return call(kernel, name, outs, args, vmem, micros, **options)

    def move(x, pairs):
        return lax.ppermute(x, "frame", pairs)

    geo = jnp.stack([quad, frame % 4, frame // 4]).astype(jnp.int32)

    def flipped(bits):
        return [(g, g ^ bits) for g in range(nf)]

    turns = [gray((place_of(z, nf // 4) + 1) % (nf // 4)) for z in range(nf // 4)]
    ring = [(g, turns[g // 4] * 4 + g % 4) for g in range(nf)]

    gain1, gain2 = spatial_gain, motion_gain
    sent = sds(nf, nq * fr, half)
    acts = [activations] + [from_quad(activations, s) for s in range(1, nq)]
    both = sds(nf, 2 * nq * fr, half)
    (own_part,) = run(
        order_kernel, "order_cotangent", [sent], [geo, cotangent, spatial_weights], 0.5, big
    )
    cot_later = after(cotangent, acts[-1])
    cots = [cotangent] + [from_quad(cot_later, s) for s in range(1, nq)]
    pos = positional(frame * fr, fr, channels)
    kept, normed = run(
        spatial_kernel,
        "spatial_forward",
        [sds(rows, 3 * width + channels), sent],
        [geo] + acts + [gain1, gain2, pos, spatial_weights],
        3,
        big,
    )
    (send,) = run(join_kernel, "join_sent", [both], [geo, normed, own_part] + cots[1:], 0.5)
    received = swap(send)
    parts = run(
        motion_kernel,
        "motion_projection",
        [sds(tokens, 4 * width, dtype=F32)] + [sds(tokens, 4 * width)] * (nq - 1),
        [geo, received, motion_weights],
        1.5,
    )
    factors = run(
        cut_kernel,
        "cut_factors",
        [sds(2, rows, half // 4)] * 4,
        [geo, after(received, parts[0])],
        0.5,
    )
    factors = [factors[0]] + [move(factors[d], flipped(d)) for d in range(1, 4)]
    parts = [after(parts[0], factors[0])] + [to_quad(p, s + 1) for s, p in enumerate(parts[1:])]
    (terms,) = run(temporal_kernel, "temporal_attention", [sds(tokens, 4 * width)], parts, 2)
    terms = after(terms, *factors)
    table, early_left, late_left = run(
        table_kernel,
        "positional_table_factors",
        [
            sds(tokens, channels, dtype=F32),
            sds(2, (2 * nq + 2) * tokens, half // 4),
            sds(2, 2 * (nq - 1) * tokens, half // 4),
        ],
        [after(geo, terms)] + factors,
        1.5,
    )
    all_terms = [terms] + [after(from_quad(terms, s), table) for s in range(1, nq)]
    pair_terms = [move(t, flipped(2)) for t in all_terms]
    core_terms = [move(t, flipped(1)) for t in all_terms]
    back_send, quarter = run(
        back_kernel,
        "temporal_back_projection",
        [sds(nf, 2 * nq * fr, half), sds(3, half // 4, width)],
        [geo] + all_terms + [motion_weights],
        0.01,
    )
    pair_terms[0] = after(pair_terms[0], back_send)
    last_terms = [move(pair_terms[0], flipped(1))]

    stage, block = nf // 4, half // nf
    sums, gain_sum = run(
        first_weight_kernel,
        "weight_terms_first_tokens",
        [
            sds(4, stage, block, width, dtype=F32),
            sds(1, half // 4, dtype=F32),
        ],
        [geo, early_left, quarter, table] + all_terms + core_terms
        + pair_terms[:1] + last_terms,
        0.01,
    )
    late_terms = [after(t, back_send, sums) for t in pair_terms[1:]]
    late_terms += [move(t, flipped(1)) for t in late_terms]
    parts_w = run(
        second_weight_kernel,
        "weight_terms_last_tokens",
        [sds(2 * block + 8, width)] * stage + [sds(2 * block, width)] * stage,
        [geo, sums, gain_sum, late_left, quarter, table, gain2] + late_terms,
        0.01,
        scratch=[pltpu.VMEM((4, stage, block, width), F32)],
    )

    def add(a, b):
        return (a.astype(F32) + b.astype(F32)).astype(BF16)

    back_recv = swap(back_send)
    backs = [back_recv] + [from_quad(back_recv, s) for s in range(1, nq)]
    block_output, grad_hidden = run(
        middle_kernel,
        "block_output_hidden_gradient",
        [sds(fr, pq, channels), sds(rows, channels)],
        [geo] + backs + cots + [kept, gain2],
        6,
        big,
    )
    totals = [parts_w[stage - 1], parts_w[2 * stage - 1]]
    for step in range(1, stage):
        for i in range(2):
            if step == stage - 2:
                totals[i] = after(totals[i], back_recv)
            moved = move(totals[i], ring)
            if step == stage - 1:
                moved = after(moved, grad_hidden)
            totals[i] = add(moved, parts_w[(i + 1) * stage - 1 - step])
    final = []
    for g in range(nf):
        for q in range(nq):
            j = quarter_of(g % 4) * stage + g // 4
            final.append((g * nq + q, nf * q + j))
    grad_hidden = after(grad_hidden, *totals)
    totals = [lax.ppermute(t, ("frame", "quad"), final) for t in totals]
    (input_grad,) = run(
        tail_kernel,
        "spatial_backward",
        [sds(fr, pq, channels)],
        [grad_hidden, activations, kept, gain1, spatial_weights],
        3.5,
        big,
    )
    everyone = nf * nq
    factor = 1.0 / math.sqrt(everyone * fr * pq)
    weight_grad = jnp.concatenate([totals[0][: 2 * block], totals[1]], axis=0)
    weight_grad = weight_grad.reshape(4, block, width).astype(F32) * factor
    place = ((frame * nq + quad) % stage) * block
    gain_grad = lax.dynamic_slice(totals[0][2 * block], (place,), (block,)).astype(F32) * factor
    return block_output, input_grad, weight_grad, gain_grad


def solution(mesh):
    in_specs = (
        P("frame", "quad", None),
        P("frame", "quad", None),
        P(),
        P(),
        P(None, "quad", None),
        P(),
    )
    out_specs = (
        P("frame", "quad", None),
        P("frame", "quad", None),
        P(None, ("frame", "quad"), None),
        P(("frame", "quad")),
    )
    body = functools.partial(local, mesh.shape["quad"], mesh.shape["frame"])
    return jax.shard_map(
        body, mesh=mesh, in_specs=in_specs, out_specs=out_specs, check_vma=False
    )
```

```python
import functools
import math

import jax
import jax.numpy as jnp
from jax import lax
from jax.experimental import pallas as pl
from jax.experimental.pallas import tpu as pltpu
from jax.sharding import PartitionSpec as P

HEADS = 4
HEAD_DIM = 160
EPSILON = 1e-05
SCALE = HEAD_DIM ** (-0.5)
F32 = jnp.float32
BF16 = jnp.bfloat16


def log2(n):
    return int(n).bit_length() - 1


def dot(a, b):
    return jnp.dot(a, b, preferred_element_type=F32)


def dot_t(a, b):
    return lax.dot_general(a, b, (((1,), (1,)), ((), ())), preferred_element_type=F32)


def t_dot(a, b):
    return lax.dot_general(a, b, (((0,), (0,)), ((), ())), preferred_element_type=F32)


def normalize(values):
    average = jnp.mean(values, axis=-1, keepdims=True)
    centred = values - average
    inv_scale = lax.rsqrt(jnp.mean(centred * centred, axis=-1, keepdims=True) + EPSILON)
    return centred * inv_scale, inv_scale


def normalize_back(grad_rows, unit_rows, inv_scale, gain):
    scaled = grad_rows * gain
    first_mean = jnp.mean(scaled, axis=-1, keepdims=True)
    second_mean = jnp.mean(scaled * unit_rows, axis=-1, keepdims=True)
    return inv_scale * (scaled - first_mean - unit_rows * second_mean)


def iota(shape, dim):
    return lax.broadcasted_iota(jnp.int32, shape, dim)


def head_mask(dtype):
    lane = iota((1, HEADS * HEAD_DIM), 1)
    return [
        jnp.where((lane >= h * HEAD_DIM) & (lane < (h + 1) * HEAD_DIM), 1.0, 0.0).astype(dtype)
        for h in range(HEADS)
    ]


def stack_heads(rows):
    return jnp.concatenate([rows * mask for mask in head_mask(rows.dtype)], axis=0)


def fold_heads(stacked):
    rows = stacked.shape[0] // HEADS
    total = None
    for h, mask in enumerate(head_mask(F32)):
        piece = stacked[h * rows : (h + 1) * rows] * mask
        total = piece if total is None else total + piece
    return total


def probabilities(query_stack, keys, same):
    scores = dot_t(query_stack, keys) * SCALE
    if same is not None:
        scores = jnp.where(same, scores, -1e30)
    highest = jnp.max(scores, axis=-1, keepdims=True)
    expo = jnp.exp(scores - highest)
    return expo / jnp.sum(expo, axis=-1, keepdims=True)


def attend(query, keys, values, same):
    probs = probabilities(stack_heads(query), keys, same)
    return fold_heads(dot(probs.astype(BF16), values)).astype(BF16)


def attend_back(query, keys, values, grad, same, probs=None):
    query_stack = stack_heads(query)
    grad_stack = stack_heads(grad)
    if probs is None:
        probs = probabilities(query_stack, keys, same)
    grad_probs = dot_t(grad_stack, values)
    inner = jnp.sum(probs * grad_probs, axis=-1, keepdims=True)
    grad_scores = (probs * (grad_probs - inner) * SCALE).astype(BF16)
    grad_query = fold_heads(dot(grad_scores, keys)).astype(BF16)
    grad_key = t_dot(grad_scores, query_stack).astype(BF16)
    grad_value = t_dot(probs.astype(BF16), grad_stack).astype(BF16)
    return grad_query, grad_key, grad_value


def rows_to_sent(quad, nq, fr, pq, transposed):
    rows = nq * fr * pq
    out_dim = 1 if transposed else 0
    out = iota((rows, rows), out_dim)
    src = iota((rows, rows), 1 - out_dim)
    cell = out >> log2(nq * fr)
    other = (out >> log2(fr)) & (nq - 1)
    frame = out & (fr - 1)
    want = (((other - quad) & (nq - 1)) << log2(fr * pq)) + (frame << log2(pq)) + cell
    return jnp.where(want == src, 1.0, 0.0).astype(BF16)


def received_to_rows(quad, nq, nf, fr, transposed):
    rows = nq * nf * fr
    out_dim = 1 if transposed else 0
    out = iota((rows, rows), out_dim)
    src = iota((rows, rows), 1 - out_dim)
    step = out >> log2(nf * fr)
    device = (out >> log2(fr)) & (nf - 1)
    frame = out & (fr - 1)
    want = (device << log2(nq * fr)) + (((step + quad) & (nq - 1)) << log2(fr)) + frame
    return jnp.where(want == src, 1.0, 0.0).astype(BF16)


def own_lanes(values, quad, nq):
    width = values.shape[1] // nq
    picked = values[:, :width]
    for t in range(1, nq):
        picked = jnp.where(quad == t, values[:, t * width : (t + 1) * width], picked)
    return picked


def place_lanes(parts, quad, nq):
    placed = []
    for t in range(nq):
        piece = parts[t]
        for q in range(1, nq):
            piece = jnp.where(quad == q, parts[(t - q) % nq], piece)
        placed.append(piece)
    return jnp.concatenate(placed, axis=1)


def frame_groups(nq, fr, pq):
    size = max(1, min(fr, 128 // (nq * pq)))
    return [(start, size) for start in range(0, fr, size)]


def pick_group(rows, group, nq, fr, pq):
    start, size = group
    if size == fr:
        return rows
    cut = rows.reshape(nq, fr, pq, rows.shape[-1])[:, start : start + size]
    return cut.reshape(nq * size * pq, rows.shape[-1])


def join_groups(pieces, nq, fr, pq):
    if len(pieces) == 1:
        return pieces[0]
    size = fr // len(pieces)
    width = pieces[0].shape[-1]
    joined = jnp.concatenate([p.reshape(nq, size, pq, width) for p in pieces], axis=1)
    return joined.reshape(nq * fr * pq, width)


def same_frame(nq, size, pq):
    if size == 1:
        return None
    rows = nq * size * pq
    shape = (HEADS * rows, rows)
    left = (iota(shape, 0) >> log2(pq)) & (size - 1)
    right = (iota(shape, 1) >> log2(pq)) & (size - 1)
    return left == right


def row_of(ref):
    return ref[...].reshape(1, -1)


def flat(ref):
    value = ref[...]
    return value.reshape(-1, value.shape[-1])


def flat_wide(ref):
    value = ref[...].astype(F32)
    return value.reshape(-1, value.shape[-1])


def spread(rows, like):
    return rows.reshape(like.shape).astype(like.dtype)


def spatial_kernel(dims, *refs):
    nq, nf, fr, pq = dims
    quad, xs, refs = refs[0][0], refs[1 : 1 + nq], refs[1 + nq :]
    gain1, gain2, pos, weights, kept_out, send_out = refs
    width = HEADS * HEAD_DIM
    wide = jnp.concatenate([flat_wide(x) for x in xs], axis=0)
    unit, _ = normalize(wide)
    normed = (unit * row_of(gain1)).astype(BF16)
    query = dot(normed, weights[0]).astype(BF16)
    keys = dot(normed, weights[1]).astype(BF16)
    values = dot(normed, weights[2]).astype(BF16)
    for i, part in enumerate((query, keys, values)):
        kept_out[:, i * width : (i + 1) * width] = part
    pieces = []
    for group in frame_groups(nq, fr, pq):
        same = same_frame(nq, group[1], pq)
        cut = [pick_group(part, group, nq, fr, pq) for part in (query, keys, values)]
        pieces.append(attend(*cut, same))
    out = join_groups(pieces, nq, fr, pq)
    hidden = (wide + dot_t(out, weights[3])).astype(BF16)
    kept_out[:, 3 * width :] = hidden
    unit_two, _ = normalize(hidden.astype(F32))
    table = jnp.broadcast_to(pos[...][:, None, :], (fr, pq, pos.shape[-1]))
    table = table.reshape(fr * pq, pos.shape[-1])
    table = jnp.concatenate([table] * nq, axis=0)
    normed_two = own_lanes(unit_two * row_of(gain2) + table, quad, nq).astype(BF16)
    send_out[...] = spread(dot(rows_to_sent(quad, nq, fr, pq, False), normed_two), send_out)


def order_kernel(dims, geo, cot, weights, send_out):
    nq, nf, fr, pq = dims
    order = rows_to_sent(geo[0], nq, fr, pq, False)[:, : fr * pq]
    send_out[...] = spread(dot(order, own_lanes(flat(cot), geo[0], nq)), send_out)


def join_kernel(dims, geo, normed, own_part, *refs):
    nq, nf, fr, pq = dims
    cots, send_out = refs[:-1], refs[-1]
    order = rows_to_sent(geo[0], nq, fr, pq, False)[:, fr * pq :]
    rows = own_lanes(jnp.concatenate([flat(c) for c in cots], axis=0), geo[0], nq)
    total = own_part[...].astype(F32) + dot(order, rows).reshape(own_part.shape)
    send_out[:, : nq * fr, :] = normed[...]
    send_out[:, nq * fr :, :] = total.astype(BF16)


def sent_part(received, i, rows):
    part = received[:, i * rows : (i + 1) * rows, :].astype(F32)
    return part.reshape(-1, part.shape[-1]).astype(BF16)


def motion_kernel(dims, geo, received, weights, own_out, *sends):
    nq, nf, fr, pq = dims
    order = received_to_rows(geo[0], nq, nf, fr, False)
    normed, cot = [dot(order, sent_part(received, i, nq * fr)).astype(BF16) for i in range(2)]
    tokens = nf * fr
    for k in range(4):
        width = weights.shape[-1]
        lanes = slice(k * width, (k + 1) * width)
        product = dot(normed if k < 3 else cot, weights[k])
        own_out[:, lanes] = product[:tokens]
        for s, send in enumerate(sends):
            send[:, lanes] = product[(s + 1) * tokens : (s + 2) * tokens].astype(BF16)


def gray(place):
    return place ^ (place >> 1)


def place_of(z, stage):
    place, shift = z, z >> 1
    for _ in range(log2(stage) - 1):
        place, shift = place ^ shift, shift >> 1
    return place


def quarter_of(four):
    return ((four & 1) << 1) | (four >> 1)


def quarter_lanes(values, quarter):
    width = values.shape[1] // 4
    picked = values[:, :width]
    for t in range(1, 4):
        picked = jnp.where(quarter == t, values[:, t * width : (t + 1) * width], picked)
    return picked


def cut_kernel(dims, geo, received, *outs):
    nq, nf, fr, pq = dims
    order = received_to_rows(geo[0], nq, nf, fr, False)
    for i in range(2):
        rows = dot(order, sent_part(received, i, nq * fr))
        for d in range(4):
            outs[d][i] = quarter_lanes(rows, quarter_of(geo[1] ^ d)).astype(BF16)


def table_kernel(dims, geo, *refs):
    nq, nf, fr, pq = dims
    factors, (out, early_out, late_out) = refs[:4], refs[4:]
    shape = out.shape
    lane = iota(shape, 1)
    freq = jnp.exp((lane >> 1).astype(F32) * (-2.0 * math.log(10000.0) / shape[1]))
    turn = (lane & 1).astype(F32) * (0.5 * math.pi)
    out[...] = jnp.sin(iota(shape, 0).astype(F32) * freq + turn)
    tokens = nf * fr
    for i in range(2):
        early = [factors[0][i], factors[1][i], factors[2][i, :tokens], factors[3][i, :tokens]]
        early_out[i] = jnp.concatenate(early, axis=0)
        late = [factors[2][i, tokens:], factors[3][i, tokens:]]
        late_out[i] = jnp.concatenate(late, axis=0)


def temporal_kernel(dims, *refs):
    nq, nf, fr, pq = dims
    parts, out = refs[:nq], refs[nq]
    width = HEADS * HEAD_DIM
    total = parts[0][...]
    for part in parts[1:]:
        total = total + part[...].astype(F32)
    query, keys, values, grad = [
        total[:, k * width : (k + 1) * width].astype(BF16) for k in range(4)
    ]
    probs = probabilities(stack_heads(query), keys, None)
    motion_out = fold_heads(dot(probs.astype(BF16), values)).astype(BF16)
    grads = attend_back(query, keys, values, grad, None, probs)
    for k, piece in enumerate(grads + (motion_out,)):
        out[:, k * width : (k + 1) * width] = piece


def part_of(terms, k):
    width = HEADS * HEAD_DIM
    return jnp.concatenate([t[:, k * width : (k + 1) * width] for t in terms], axis=0)


def back_kernel(dims, quad_ref, *refs):
    nq, nf, fr, pq = dims
    terms, (weights, out, quarter_out) = refs[:nq], refs[nq:]
    order = received_to_rows(quad_ref[0], nq, nf, fr, True)
    quarter, rows = quarter_of(quad_ref[1]), quarter_out.shape[1]
    for k in range(3):
        if rows % 16 == 0:
            own = weights[k, pl.ds(pl.multiple_of(quarter * rows, 16), rows), :]
        else:
            wide = weights[k].astype(F32)
            own = wide[:rows]
            for t in range(1, 4):
                own = jnp.where(quarter == t, wide[t * rows : (t + 1) * rows], own)
            own = own.astype(BF16)
        quarter_out[k] = own
    grad = None
    for k in range(3):
        product = dot_t(part_of(terms, k), weights[k])
        grad = product if grad is None else grad + product
    delta = dot_t(part_of(terms, 3), weights[3])
    for i, rows in enumerate((grad, delta)):
        rows = dot(order, rows.astype(BF16))
        out[:, i * nq * fr : (i + 1) * nq * fr, :] = rows.reshape(nf, nq * fr, -1).astype(BF16)


def weight_sums(geo, nq, normed, cot, weights, pos, terms):
    products, grad = [], None
    for k in range(4):
        right = part_of(terms, k)
        products.append(t_dot(normed if k < 3 else cot, right))
        if k < 3:
            back = dot_t(right, weights[k])
            grad = back if grad is None else grad + back
    table = quarter_lanes(own_lanes(pos[...], geo[0], nq), quarter_of(geo[1]))
    table = jnp.concatenate([table] * len(terms), axis=0)
    return products, jnp.sum(grad * (normed.astype(F32) - table), axis=0, keepdims=True)


def first_weight_kernel(dims, geo, left, weights, pos, *refs):
    nq, nf, fr, pq = dims
    terms, (blocks, gain_out) = refs[: 2 * nq + 2], refs[2 * nq + 2 :]
    _, stage, block, _ = blocks.shape
    products, gain_out[...] = weight_sums(geo, nq, left[0], left[1], weights, pos, terms)
    for k in range(4):
        for z in range(stage):
            blocks[k, z] = products[k][z * block : (z + 1) * block]


def second_weight_kernel(dims, geo, sums, gain_sum, left, weights, pos, gain2, *refs):
    nq, nf, fr, pq = dims
    terms, outs, blocks = refs[: 2 * nq - 2], refs[2 * nq - 2 : -1], refs[-1]
    _, stage, block, width = blocks.shape
    products, gain = weight_sums(geo, nq, left[0], left[1], weights, pos, terms)
    for k in range(4):
        for z in range(stage):
            blocks[k, z] = sums[k, z] + products[k][z * block : (z + 1) * block]
    gain = gain + gain_sum[...]
    rows = gain.shape[1]
    gain = gain / quarter_lanes(own_lanes(row_of(gain2), geo[0], nq), quarter_of(geo[1]))
    extra = jnp.concatenate([gain, jnp.zeros((1, width - rows), F32)], axis=1)
    extra = jnp.where(iota((8, width), 0) == 0, extra, 0.0)
    for r in range(stage):
        z = gray((place_of(geo[2], stage) + r) & (stage - 1))
        rows_out = jnp.concatenate([blocks[0, z], blocks[1, z]], axis=0)
        outs[r][...] = rows_out.astype(BF16)
        rows_out = jnp.concatenate([blocks[2, z], blocks[3, z], extra], axis=0)
        outs[stage + r][...] = rows_out.astype(BF16)


def middle_kernel(dims, *refs):
    nq, nf, fr, pq = dims
    quad, received, cots = refs[0][0], refs[1 : 1 + nq], refs[1 + nq : 1 + 2 * nq]
    kept, gain2, block_out, grad_out = refs[1 + 2 * nq :]
    own = fr * pq
    order = rows_to_sent(quad, nq, fr, pq, True)

    def lanes(i):
        parts = []
        for r in received:
            parts.append(dot(order, sent_part(r, i, nq * fr)))
        return place_lanes(parts, quad, nq)

    hidden = kept[:, 3 * HEADS * HEAD_DIM :].astype(F32)
    grad_normed, delta = lanes(0), lanes(1)
    block_out[...] = spread(hidden[:own] + delta[:own], block_out)
    unit_two, inv_two = normalize(hidden)
    cot = jnp.concatenate([flat_wide(c) for c in cots], axis=0)
    back = normalize_back(grad_normed, unit_two, inv_two, row_of(gain2))
    grad_out[...] = (cot + back).astype(BF16)


def tail_kernel(dims, grad_hidden, xs, kept, gain1, weights, in_grad):
    nq, nf, fr, pq = dims
    own, width = fr * pq, HEADS * HEAD_DIM
    grad_out = dot(grad_hidden[...], weights[3]).astype(BF16)
    parts = [kept[:, i * width : (i + 1) * width] for i in range(3)] + [grad_out]
    pieces = []
    for group in frame_groups(nq, fr, pq):
        same = same_frame(nq, group[1], pq)
        pieces.append(attend_back(*[pick_group(p, group, nq, fr, pq) for p in parts], same))
    grads = [join_groups([p[i] for p in pieces], nq, fr, pq)[:own] for i in range(3)]
    grad_one = dot_t(grads[0], weights[0]) + dot_t(grads[1], weights[1]) + dot_t(grads[2], weights[2])
    unit_one, inv_one = normalize(flat_wide(xs))
    back = normalize_back(grad_one, unit_one, inv_one, row_of(gain1))
    in_grad[...] = spread(grad_hidden[...][:own].astype(F32) + back, in_grad)


def call(kernel, name, outs, args, vmem, micros, scratch=()):
    in_specs = []
    for arg in args:
        space = pltpu.SMEM if arg.dtype == jnp.int32 else pltpu.VMEM
        in_specs.append(pl.BlockSpec(memory_space=space))
    return list(
        pl.pallas_call(
            kernel,
            out_shape=outs,
            in_specs=in_specs,
            out_specs=[pl.BlockSpec(memory_space=pltpu.VMEM) for _ in outs],
            scratch_shapes=list(scratch),
            compiler_params=pltpu.CompilerParams(vmem_limit_bytes=vmem * 1024 * 1024),
            cost_estimate=pl.CostEstimate(
                flops=int(micros * 1e9),
                bytes_accessed=2**20 if micros > 0.1 else 2**12,
                transcendentals=0,
            ),
            name=name,
        )(*args)
    )


def after(value, *others):
    return lax.optimization_barrier((value,) + others)[0]


def sds(*shape, dtype=BF16):
    return jax.ShapeDtypeStruct(shape, dtype)


def positional(first, frames, channels):
    frame_pos = (first + lax.broadcasted_iota(jnp.int32, (frames, channels), 0)).astype(F32)
    lane = lax.broadcasted_iota(jnp.int32, (frames, channels), 1)
    freq_index = (lane >> 1).astype(F32)
    phases = frame_pos * jnp.exp(freq_index * (-2.0 * math.log(10000.0) / channels))
    return jnp.sin(phases + (lane & 1).astype(F32) * (0.5 * math.pi))


def local(nq, nf, activations, cotangent, spatial_weights, spatial_gain, motion_weights, motion_gain):
    fr, pq, channels = activations.shape
    dims = (nq, nf, fr, pq)
    width = spatial_weights.shape[-1]
    half = channels // nq
    rows = nq * fr * pq
    tokens = nf * fr
    small = 16 if rows <= 256 else 40
    big = 16 if rows <= 256 else 52
    quad = lax.axis_index("quad")
    frame = lax.axis_index("frame")


    def from_quad(x, s):
        return lax.ppermute(x, "quad", [((d + s) % nq, d) for d in range(nq)])

    def to_quad(x, s):
        return lax.ppermute(x, "quad", [(d, (d + s) % nq) for d in range(nq)])

    def swap(x):
        return lax.all_to_all(x, "frame", split_axis=0, concat_axis=0, tiled=True)

    def run(kernel, name, outs, args, micros, vmem=small, **options):
        kernel = functools.partial(kernel, dims)
        return call(kernel, name, outs, args, vmem, micros, **options)

    def move(x, pairs):
        return lax.ppermute(x, "frame", pairs)

    geo = jnp.stack([quad, frame % 4, frame // 4]).astype(jnp.int32)

    def flipped(bits):
        return [(g, g ^ bits) for g in range(nf)]

    turns = [gray((place_of(z, nf // 4) + 1) % (nf // 4)) for z in range(nf // 4)]
    ring = [(g, turns[g // 4] * 4 + g % 4) for g in range(nf)]

    gain1, gain2 = spatial_gain, motion_gain
    sent = sds(nf, nq * fr, half)
    acts = [activations] + [from_quad(activations, s) for s in range(1, nq)]
    both = sds(nf, 2 * nq * fr, half)
    (own_part,) = run(
        order_kernel, "order_cotangent", [sent], [geo, cotangent, spatial_weights], 0.5, big
    )
    cot_later = after(cotangent, acts[-1])
    cots = [cotangent] + [from_quad(cot_later, s) for s in range(1, nq)]
    pos = positional(frame * fr, fr, channels)
    kept, normed = run(
        spatial_kernel,
        "spatial_forward",
        [sds(rows, 3 * width + channels), sent],
        [geo] + acts + [gain1, gain2, pos, spatial_weights],
        3,
        big,
    )
    (send,) = run(join_kernel, "join_sent", [both], [geo, normed, own_part] + cots[1:], 0.5)
    received = swap(send)
    parts = run(
        motion_kernel,
        "motion_projection",
        [sds(tokens, 4 * width, dtype=F32)] + [sds(tokens, 4 * width)] * (nq - 1),
        [geo, received, motion_weights],
        1.5,
    )
    factors = run(
        cut_kernel,
        "cut_factors",
        [sds(2, rows, half // 4)] * 4,
        [geo, after(received, parts[0])],
        0.5,
    )
    factors = [factors[0]] + [move(factors[d], flipped(d)) for d in range(1, 4)]
    parts = [after(parts[0], factors[0])] + [to_quad(p, s + 1) for s, p in enumerate(parts[1:])]
    (terms,) = run(temporal_kernel, "temporal_attention", [sds(tokens, 4 * width)], parts, 2)
    terms = after(terms, *factors)
    table, early_left, late_left = run(
        table_kernel,
        "positional_table_factors",
        [
            sds(tokens, channels, dtype=F32),
            sds(2, (2 * nq + 2) * tokens, half // 4),
            sds(2, 2 * (nq - 1) * tokens, half // 4),
        ],
        [after(geo, terms)] + factors,
        1.5,
    )
    all_terms = [terms] + [after(from_quad(terms, s), table) for s in range(1, nq)]
    pair_terms = [move(t, flipped(2)) for t in all_terms]
    core_terms = [move(t, flipped(1)) for t in all_terms]
    back_send, quarter = run(
        back_kernel,
        "temporal_back_projection",
        [sds(nf, 2 * nq * fr, half), sds(3, half // 4, width)],
        [geo, after(all_terms[0], pair_terms[0])] + all_terms[1:] + [motion_weights],
        0.01,
    )
    last_terms = [move(pair_terms[0], flipped(1))]

    stage, block = nf // 4, half // nf
    sums, gain_sum = run(
        first_weight_kernel,
        "weight_terms_first_tokens",
        [
            sds(4, stage, block, width, dtype=F32),
            sds(1, half // 4, dtype=F32),
        ],
        [geo, early_left, quarter, table] + all_terms + core_terms
        + pair_terms[:1] + last_terms,
        0.01,
    )
    late_terms = [after(t, back_send, sums) for t in pair_terms[1:]]
    late_terms += [move(t, flipped(1)) for t in late_terms]
    parts_w = run(
        second_weight_kernel,
        "weight_terms_last_tokens",
        [sds(2 * block, width)] * stage + [sds(2 * block + 8, width)] * stage,
        [geo, sums, gain_sum, late_left, quarter, table, gain2] + late_terms,
        0.01,
        scratch=[pltpu.VMEM((4, stage, block, width), F32)],
    )

    def add(a, b):
        return (a.astype(F32) + b.astype(F32)).astype(BF16)

    back_recv = swap(back_send)
    backs = [back_recv] + [from_quad(back_recv, s) for s in range(1, nq)]
    block_output, grad_hidden = run(
        middle_kernel,
        "block_output_hidden_gradient",
        [sds(fr, pq, channels), sds(rows, channels)],
        [geo] + backs + cots + [kept, gain2],
        6,
        big,
    )
    totals = [parts_w[stage - 1], parts_w[2 * stage - 1]]
    for step in range(1, stage):
        for i in range(2):
            if step == stage - 2:
                totals[i] = after(totals[i], back_recv)
            moved = move(totals[i], ring)
            if step == stage - 1:
                moved = after(moved, grad_hidden)
            totals[i] = add(moved, parts_w[(i + 1) * stage - 1 - step])
    final = []
    for g in range(nf):
        for q in range(nq):
            j = quarter_of(g % 4) * stage + g // 4
            final.append((g * nq + q, nf * q + j))
    grad_hidden = after(grad_hidden, *totals)
    totals = [lax.ppermute(t, ("frame", "quad"), final) for t in totals]
    (input_grad,) = run(
        tail_kernel,
        "spatial_backward",
        [sds(fr, pq, channels)],
        [grad_hidden, activations, kept, gain1, spatial_weights],
        3.5,
        big,
    )
    everyone = nf * nq
    factor = 1.0 / math.sqrt(everyone * fr * pq)
    weight_grad = jnp.concatenate([totals[0], totals[1][: 2 * block]], axis=0)
    weight_grad = weight_grad.reshape(4, block, width).astype(F32) * factor
    place = ((frame * nq + quad) % stage) * block
    gain_grad = lax.dynamic_slice(totals[1][2 * block], (place,), (block,)).astype(F32) * factor
    return block_output, input_grad, weight_grad, gain_grad


def solution(mesh):
    in_specs = (
        P("frame", "quad", None),
        P("frame", "quad", None),
        P(),
        P(),
        P(None, "quad", None),
        P(),
    )
    out_specs = (
        P("frame", "quad", None),
        P("frame", "quad", None),
        P(None, ("frame", "quad"), None),
        P(("frame", "quad")),
    )
    body = functools.partial(local, mesh.shape["quad"], mesh.shape["frame"])
    return jax.shard_map(
        body, mesh=mesh, in_specs=in_specs, out_specs=out_specs, check_vma=False
    )
```

```python
import functools
import math

import jax
import jax.numpy as jnp
from jax import lax
from jax.experimental import pallas as pl
from jax.experimental.pallas import tpu as pltpu
from jax.sharding import PartitionSpec as P

HEADS = 4
HEAD_DIM = 160
EPSILON = 1e-05
SCALE = HEAD_DIM ** (-0.5)
F32 = jnp.float32
BF16 = jnp.bfloat16


def log2(n):
    return int(n).bit_length() - 1


def dot(a, b):
    return jnp.dot(a, b, preferred_element_type=F32)


def dot_t(a, b):
    return lax.dot_general(a, b, (((1,), (1,)), ((), ())), preferred_element_type=F32)


def t_dot(a, b):
    return lax.dot_general(a, b, (((0,), (0,)), ((), ())), preferred_element_type=F32)


def normalize(values):
    average = jnp.mean(values, axis=-1, keepdims=True)
    centred = values - average
    inv_scale = lax.rsqrt(jnp.mean(centred * centred, axis=-1, keepdims=True) + EPSILON)
    return centred * inv_scale, inv_scale


def normalize_back(grad_rows, unit_rows, inv_scale, gain):
    scaled = grad_rows * gain
    first_mean = jnp.mean(scaled, axis=-1, keepdims=True)
    second_mean = jnp.mean(scaled * unit_rows, axis=-1, keepdims=True)
    return inv_scale * (scaled - first_mean - unit_rows * second_mean)


def iota(shape, dim):
    return lax.broadcasted_iota(jnp.int32, shape, dim)


def head_mask(dtype):
    lane = iota((1, HEADS * HEAD_DIM), 1)
    return [
        jnp.where((lane >= h * HEAD_DIM) & (lane < (h + 1) * HEAD_DIM), 1.0, 0.0).astype(dtype)
        for h in range(HEADS)
    ]


def stack_heads(rows):
    return jnp.concatenate([rows * mask for mask in head_mask(rows.dtype)], axis=0)


def fold_heads(stacked):
    rows = stacked.shape[0] // HEADS
    total = None
    for h, mask in enumerate(head_mask(F32)):
        piece = stacked[h * rows : (h + 1) * rows] * mask
        total = piece if total is None else total + piece
    return total


def probabilities(query_stack, keys, same):
    scores = dot_t(query_stack, keys) * SCALE
    if same is not None:
        scores = jnp.where(same, scores, -1e30)
    highest = jnp.max(scores, axis=-1, keepdims=True)
    expo = jnp.exp(scores - highest)
    return expo / jnp.sum(expo, axis=-1, keepdims=True)


def attend(query, keys, values, same):
    probs = probabilities(stack_heads(query), keys, same)
    return fold_heads(dot(probs.astype(BF16), values)).astype(BF16)


def attend_back(query, keys, values, grad, same, probs=None):
    query_stack = stack_heads(query)
    grad_stack = stack_heads(grad)
    if probs is None:
        probs = probabilities(query_stack, keys, same)
    grad_probs = dot_t(grad_stack, values)
    inner = jnp.sum(probs * grad_probs, axis=-1, keepdims=True)
    grad_scores = (probs * (grad_probs - inner) * SCALE).astype(BF16)
    grad_query = fold_heads(dot(grad_scores, keys)).astype(BF16)
    grad_key = t_dot(grad_scores, query_stack).astype(BF16)
    grad_value = t_dot(probs.astype(BF16), grad_stack).astype(BF16)
    return grad_query, grad_key, grad_value


def rows_to_sent(quad, nq, fr, pq, transposed):
    rows = nq * fr * pq
    out_dim = 1 if transposed else 0
    out = iota((rows, rows), out_dim)
    src = iota((rows, rows), 1 - out_dim)
    cell = out >> log2(nq * fr)
    other = (out >> log2(fr)) & (nq - 1)
    frame = out & (fr - 1)
    want = (((other - quad) & (nq - 1)) << log2(fr * pq)) + (frame << log2(pq)) + cell
    return jnp.where(want == src, 1.0, 0.0).astype(BF16)


def received_to_rows(quad, nq, nf, fr, transposed):
    rows = nq * nf * fr
    out_dim = 1 if transposed else 0
    out = iota((rows, rows), out_dim)
    src = iota((rows, rows), 1 - out_dim)
    step = out >> log2(nf * fr)
    device = (out >> log2(fr)) & (nf - 1)
    frame = out & (fr - 1)
    want = (device << log2(nq * fr)) + (((step + quad) & (nq - 1)) << log2(fr)) + frame
    return jnp.where(want == src, 1.0, 0.0).astype(BF16)


def own_lanes(values, quad, nq):
    width = values.shape[1] // nq
    picked = values[:, :width]
    for t in range(1, nq):
        picked = jnp.where(quad == t, values[:, t * width : (t + 1) * width], picked)
    return picked


def place_lanes(parts, quad, nq):
    placed = []
    for t in range(nq):
        piece = parts[t]
        for q in range(1, nq):
            piece = jnp.where(quad == q, parts[(t - q) % nq], piece)
        placed.append(piece)
    return jnp.concatenate(placed, axis=1)


def frame_groups(nq, fr, pq):
    size = max(1, min(fr, 128 // (nq * pq)))
    return [(start, size) for start in range(0, fr, size)]


def pick_group(rows, group, nq, fr, pq):
    start, size = group
    if size == fr:
        return rows
    cut = rows.reshape(nq, fr, pq, rows.shape[-1])[:, start : start + size]
    return cut.reshape(nq * size * pq, rows.shape[-1])


def join_groups(pieces, nq, fr, pq):
    if len(pieces) == 1:
        return pieces[0]
    size = fr // len(pieces)
    width = pieces[0].shape[-1]
    joined = jnp.concatenate([p.reshape(nq, size, pq, width) for p in pieces], axis=1)
    return joined.reshape(nq * fr * pq, width)


def same_frame(nq, size, pq):
    if size == 1:
        return None
    rows = nq * size * pq
    shape = (HEADS * rows, rows)
    left = (iota(shape, 0) >> log2(pq)) & (size - 1)
    right = (iota(shape, 1) >> log2(pq)) & (size - 1)
    return left == right


def row_of(ref):
    return ref[...].reshape(1, -1)


def flat(ref):
    value = ref[...]
    return value.reshape(-1, value.shape[-1])


def flat_wide(ref):
    value = ref[...].astype(F32)
    return value.reshape(-1, value.shape[-1])


def spread(rows, like):
    return rows.reshape(like.shape).astype(like.dtype)


def spatial_kernel(dims, *refs):
    nq, nf, fr, pq = dims
    quad, xs, refs = refs[0][0], refs[1 : 1 + nq], refs[1 + nq :]
    gain1, gain2, pos, weights, kept_out, send_out = refs
    width = HEADS * HEAD_DIM
    wide = jnp.concatenate([flat_wide(x) for x in xs], axis=0)
    unit, _ = normalize(wide)
    normed = (unit * row_of(gain1)).astype(BF16)
    query = dot(normed, weights[0]).astype(BF16)
    keys = dot(normed, weights[1]).astype(BF16)
    values = dot(normed, weights[2]).astype(BF16)
    for i, part in enumerate((query, keys, values)):
        kept_out[:, i * width : (i + 1) * width] = part
    pieces = []
    for group in frame_groups(nq, fr, pq):
        same = same_frame(nq, group[1], pq)
        cut = [pick_group(part, group, nq, fr, pq) for part in (query, keys, values)]
        pieces.append(attend(*cut, same))
    out = join_groups(pieces, nq, fr, pq)
    hidden = (wide + dot_t(out, weights[3])).astype(BF16)
    kept_out[:, 3 * width :] = hidden
    unit_two, _ = normalize(hidden.astype(F32))
    table = jnp.broadcast_to(pos[...][:, None, :], (fr, pq, pos.shape[-1]))
    table = table.reshape(fr * pq, pos.shape[-1])
    table = jnp.concatenate([table] * nq, axis=0)
    normed_two = own_lanes(unit_two * row_of(gain2) + table, quad, nq).astype(BF16)
    send_out[...] = spread(dot(rows_to_sent(quad, nq, fr, pq, False), normed_two), send_out)


def order_kernel(dims, geo, cot, weights, send_out):
    nq, nf, fr, pq = dims
    order = rows_to_sent(geo[0], nq, fr, pq, False)[:, : fr * pq]
    send_out[...] = spread(dot(order, own_lanes(flat(cot), geo[0], nq)), send_out)


def join_kernel(dims, geo, normed, own_part, *refs):
    nq, nf, fr, pq = dims
    cots, send_out = refs[:-1], refs[-1]
    order = rows_to_sent(geo[0], nq, fr, pq, False)[:, fr * pq :]
    rows = own_lanes(jnp.concatenate([flat(c) for c in cots], axis=0), geo[0], nq)
    total = own_part[...].astype(F32) + dot(order, rows).reshape(own_part.shape)
    send_out[:, : nq * fr, :] = normed[...]
    send_out[:, nq * fr :, :] = total.astype(BF16)


def sent_part(received, i, rows):
    part = received[:, i * rows : (i + 1) * rows, :].astype(F32)
    return part.reshape(-1, part.shape[-1]).astype(BF16)


def motion_kernel(dims, geo, received, weights, own_out, *sends):
    nq, nf, fr, pq = dims
    order = received_to_rows(geo[0], nq, nf, fr, False)
    normed, cot = [dot(order, sent_part(received, i, nq * fr)).astype(BF16) for i in range(2)]
    tokens = nf * fr
    for k in range(4):
        width = weights.shape[-1]
        lanes = slice(k * width, (k + 1) * width)
        product = dot(normed if k < 3 else cot, weights[k])
        own_out[:, lanes] = product[:tokens]
        for s, send in enumerate(sends):
            send[:, lanes] = product[(s + 1) * tokens : (s + 2) * tokens].astype(BF16)


def gray(place):
    return place ^ (place >> 1)


def place_of(z, stage):
    place, shift = z, z >> 1
    for _ in range(log2(stage) - 1):
        place, shift = place ^ shift, shift >> 1
    return place


def quarter_of(four):
    return ((four & 1) << 1) | (four >> 1)


def quarter_lanes(values, quarter):
    width = values.shape[1] // 4
    picked = values[:, :width]
    for t in range(1, 4):
        picked = jnp.where(quarter == t, values[:, t * width : (t + 1) * width], picked)
    return picked


def cut_kernel(dims, geo, received, *outs):
    nq, nf, fr, pq = dims
    order = received_to_rows(geo[0], nq, nf, fr, False)
    for i in range(2):
        rows = dot(order, sent_part(received, i, nq * fr))
        for d in range(4):
            outs[d][i] = quarter_lanes(rows, quarter_of(geo[1] ^ d)).astype(BF16)


def table_kernel(dims, geo, *refs):
    nq, nf, fr, pq = dims
    factors, (out, early_out, late_out) = refs[:4], refs[4:]
    shape = out.shape
    lane = iota(shape, 1)
    freq = jnp.exp((lane >> 1).astype(F32) * (-2.0 * math.log(10000.0) / shape[1]))
    turn = (lane & 1).astype(F32) * (0.5 * math.pi)
    out[...] = jnp.sin(iota(shape, 0).astype(F32) * freq + turn)
    tokens = nf * fr
    for i in range(2):
        early = [factors[0][i], factors[1][i], factors[2][i, :tokens], factors[3][i, :tokens]]
        early_out[i] = jnp.concatenate(early, axis=0)
        late = [factors[2][i, tokens:], factors[3][i, tokens:]]
        late_out[i] = jnp.concatenate(late, axis=0)


def temporal_kernel(dims, *refs):
    nq, nf, fr, pq = dims
    parts, out = refs[:nq], refs[nq]
    width = HEADS * HEAD_DIM
    total = parts[0][...]
    for part in parts[1:]:
        total = total + part[...].astype(F32)
    query, keys, values, grad = [
        total[:, k * width : (k + 1) * width].astype(BF16) for k in range(4)
    ]
    probs = probabilities(stack_heads(query), keys, None)
    motion_out = fold_heads(dot(probs.astype(BF16), values)).astype(BF16)
    grads = attend_back(query, keys, values, grad, None, probs)
    for k, piece in enumerate(grads + (motion_out,)):
        out[:, k * width : (k + 1) * width] = piece


def part_of(terms, k):
    width = HEADS * HEAD_DIM
    return jnp.concatenate([t[:, k * width : (k + 1) * width] for t in terms], axis=0)


def back_kernel(dims, quad_ref, *refs):
    nq, nf, fr, pq = dims
    terms, (weights, out, quarter_out) = refs[:nq], refs[nq:]
    order = received_to_rows(quad_ref[0], nq, nf, fr, True)
    quarter, rows = quarter_of(quad_ref[1]), quarter_out.shape[1]
    for k in range(3):
        if rows % 16 == 0:
            own = weights[k, pl.ds(pl.multiple_of(quarter * rows, 16), rows), :]
        else:
            wide = weights[k].astype(F32)
            own = wide[:rows]
            for t in range(1, 4):
                own = jnp.where(quarter == t, wide[t * rows : (t + 1) * rows], own)
            own = own.astype(BF16)
        quarter_out[k] = own
    grad = None
    for k in range(3):
        product = dot_t(part_of(terms, k), weights[k])
        grad = product if grad is None else grad + product
    delta = dot_t(part_of(terms, 3), weights[3])
    for i, rows in enumerate((grad, delta)):
        rows = dot(order, rows.astype(BF16))
        out[:, i * nq * fr : (i + 1) * nq * fr, :] = rows.reshape(nf, nq * fr, -1).astype(BF16)


def weight_sums(geo, nq, normed, cot, weights, pos, terms):
    products, grad = [], None
    for k in range(4):
        right = part_of(terms, k)
        products.append(t_dot(normed if k < 3 else cot, right))
        if k < 3:
            back = dot_t(right, weights[k])
            grad = back if grad is None else grad + back
    table = quarter_lanes(own_lanes(pos[...], geo[0], nq), quarter_of(geo[1]))
    table = jnp.concatenate([table] * len(terms), axis=0)
    return products, jnp.sum(grad * (normed.astype(F32) - table), axis=0, keepdims=True)


def first_weight_kernel(dims, geo, left, weights, pos, *refs):
    nq, nf, fr, pq = dims
    terms, (blocks, gain_out) = refs[: 2 * nq + 2], refs[2 * nq + 2 :]
    _, stage, block, _ = blocks.shape
    products, gain_out[...] = weight_sums(geo, nq, left[0], left[1], weights, pos, terms)
    for k in range(4):
        for z in range(stage):
            blocks[k, z] = products[k][z * block : (z + 1) * block]


def second_weight_kernel(dims, geo, sums, gain_sum, left, weights, pos, gain2, *refs):
    nq, nf, fr, pq = dims
    terms, outs, blocks = refs[: 2 * nq - 2], refs[2 * nq - 2 : -1], refs[-1]
    _, stage, block, width = blocks.shape
    products, gain = weight_sums(geo, nq, left[0], left[1], weights, pos, terms)
    for k in range(4):
        for z in range(stage):
            blocks[k, z] = sums[k, z] + products[k][z * block : (z + 1) * block]
    gain = gain + gain_sum[...]
    rows = gain.shape[1]
    gain = gain / quarter_lanes(own_lanes(row_of(gain2), geo[0], nq), quarter_of(geo[1]))
    extra = jnp.concatenate([gain, jnp.zeros((1, width - rows), F32)], axis=1)
    extra = jnp.where(iota((8, width), 0) == 0, extra, 0.0)
    for r in range(stage):
        z = gray((place_of(geo[2], stage) + r) & (stage - 1))
        rows_out = jnp.concatenate([blocks[0, z], blocks[1, z], extra], axis=0)
        outs[r][...] = rows_out.astype(BF16)
        rows_out = jnp.concatenate([blocks[2, z], blocks[3, z]], axis=0)
        outs[stage + r][...] = rows_out.astype(BF16)


def middle_kernel(dims, *refs):
    nq, nf, fr, pq = dims
    quad, received, cots = refs[0][0], refs[1 : 1 + nq], refs[1 + nq : 1 + 2 * nq]
    kept, gain2, block_out, grad_out = refs[1 + 2 * nq :]
    own = fr * pq
    order = rows_to_sent(quad, nq, fr, pq, True)

    def lanes(i):
        parts = []
        for r in received:
            parts.append(dot(order, sent_part(r, i, nq * fr)))
        return place_lanes(parts, quad, nq)

    hidden = kept[:, 3 * HEADS * HEAD_DIM :].astype(F32)
    grad_normed, delta = lanes(0), lanes(1)
    block_out[...] = spread(hidden[:own] + delta[:own], block_out)
    unit_two, inv_two = normalize(hidden)
    cot = jnp.concatenate([flat_wide(c) for c in cots], axis=0)
    back = normalize_back(grad_normed, unit_two, inv_two, row_of(gain2))
    grad_out[...] = (cot + back).astype(BF16)


def tail_kernel(dims, grad_hidden, xs, kept, gain1, weights, in_grad):
    nq, nf, fr, pq = dims
    own, width = fr * pq, HEADS * HEAD_DIM
    grad_out = dot(grad_hidden[...], weights[3]).astype(BF16)
    parts = [kept[:, i * width : (i + 1) * width] for i in range(3)] + [grad_out]
    pieces = []
    for group in frame_groups(nq, fr, pq):
        same = same_frame(nq, group[1], pq)
        pieces.append(attend_back(*[pick_group(p, group, nq, fr, pq) for p in parts], same))
    grads = [join_groups([p[i] for p in pieces], nq, fr, pq)[:own] for i in range(3)]
    grad_one = dot_t(grads[0], weights[0]) + dot_t(grads[1], weights[1]) + dot_t(grads[2], weights[2])
    unit_one, inv_one = normalize(flat_wide(xs))
    back = normalize_back(grad_one, unit_one, inv_one, row_of(gain1))
    in_grad[...] = spread(grad_hidden[...][:own].astype(F32) + back, in_grad)


def call(kernel, name, outs, args, vmem, micros, scratch=()):
    in_specs = []
    for arg in args:
        space = pltpu.SMEM if arg.dtype == jnp.int32 else pltpu.VMEM
        in_specs.append(pl.BlockSpec(memory_space=space))
    return list(
        pl.pallas_call(
            kernel,
            out_shape=outs,
            in_specs=in_specs,
            out_specs=[pl.BlockSpec(memory_space=pltpu.VMEM) for _ in outs],
            scratch_shapes=list(scratch),
            compiler_params=pltpu.CompilerParams(vmem_limit_bytes=vmem * 1024 * 1024),
            cost_estimate=pl.CostEstimate(
                flops=int(micros * 1e9),
                bytes_accessed=2**20 if micros > 0.1 else 2**12,
                transcendentals=0,
            ),
            name=name,
        )(*args)
    )


def after(value, *others):
    return lax.optimization_barrier((value,) + others)[0]


def sds(*shape, dtype=BF16):
    return jax.ShapeDtypeStruct(shape, dtype)


def positional(first, frames, channels):
    frame_pos = (first + lax.broadcasted_iota(jnp.int32, (frames, channels), 0)).astype(F32)
    lane = lax.broadcasted_iota(jnp.int32, (frames, channels), 1)
    freq_index = (lane >> 1).astype(F32)
    phases = frame_pos * jnp.exp(freq_index * (-2.0 * math.log(10000.0) / channels))
    return jnp.sin(phases + (lane & 1).astype(F32) * (0.5 * math.pi))


def local(nq, nf, activations, cotangent, spatial_weights, spatial_gain, motion_weights, motion_gain):
    fr, pq, channels = activations.shape
    dims = (nq, nf, fr, pq)
    width = spatial_weights.shape[-1]
    half = channels // nq
    rows = nq * fr * pq
    tokens = nf * fr
    small = 16 if rows <= 256 else 40
    big = 16 if rows <= 256 else 52
    quad = lax.axis_index("quad")
    frame = lax.axis_index("frame")


    def from_quad(x, s):
        return lax.ppermute(x, "quad", [((d + s) % nq, d) for d in range(nq)])

    def to_quad(x, s):
        return lax.ppermute(x, "quad", [(d, (d + s) % nq) for d in range(nq)])

    def swap(x):
        return lax.all_to_all(x, "frame", split_axis=0, concat_axis=0, tiled=True)

    def run(kernel, name, outs, args, micros, vmem=small, **options):
        kernel = functools.partial(kernel, dims)
        return call(kernel, name, outs, args, vmem, micros, **options)

    def move(x, pairs):
        return lax.ppermute(x, "frame", pairs)

    geo = jnp.stack([quad, frame % 4, frame // 4]).astype(jnp.int32)

    def flipped(bits):
        return [(g, g ^ bits) for g in range(nf)]

    turns = [gray((place_of(z, nf // 4) + 1) % (nf // 4)) for z in range(nf // 4)]
    ring = [(g, turns[g // 4] * 4 + g % 4) for g in range(nf)]

    gain1, gain2 = spatial_gain, motion_gain
    sent = sds(nf, nq * fr, half)
    acts = [activations] + [from_quad(activations, s) for s in range(1, nq)]
    both = sds(nf, 2 * nq * fr, half)
    (own_part,) = run(
        order_kernel, "order_cotangent", [sent], [geo, cotangent, spatial_weights], 0.5, big
    )
    cot_later = after(cotangent, acts[-1])
    cots = [cotangent] + [from_quad(cot_later, s) for s in range(1, nq)]
    pos = positional(frame * fr, fr, channels)
    kept, normed = run(
        spatial_kernel,
        "spatial_forward",
        [sds(rows, 3 * width + channels), sent],
        [geo] + acts + [gain1, gain2, pos, spatial_weights],
        3,
        big,
    )
    (send,) = run(join_kernel, "join_sent", [both], [geo, normed, own_part] + cots[1:], 0.5)
    received = swap(send)
    parts = run(
        motion_kernel,
        "motion_projection",
        [sds(tokens, 4 * width, dtype=F32)] + [sds(tokens, 4 * width)] * (nq - 1),
        [geo, received, motion_weights],
        1.5,
    )
    factors = run(
        cut_kernel,
        "cut_factors",
        [sds(2, rows, half // 4)] * 4,
        [geo, after(received, parts[0])],
        0.5,
    )
    factors = [factors[0]] + [move(factors[d], flipped(d)) for d in range(1, 4)]
    parts = [after(parts[0], factors[0])] + [to_quad(p, s + 1) for s, p in enumerate(parts[1:])]
    (terms,) = run(temporal_kernel, "temporal_attention", [sds(tokens, 4 * width)], parts, 2)
    terms = after(terms, *factors)
    table, early_left, late_left = run(
        table_kernel,
        "positional_table_factors",
        [
            sds(tokens, channels, dtype=F32),
            sds(2, (2 * nq + 2) * tokens, half // 4),
            sds(2, 2 * (nq - 1) * tokens, half // 4),
        ],
        [after(geo, terms)] + factors,
        1.5,
    )
    all_terms = [terms] + [after(from_quad(terms, s), table) for s in range(1, nq)]
    pair_terms = [move(t, flipped(2)) for t in all_terms]
    core_terms = [move(t, flipped(1)) for t in all_terms]
    back_send, quarter = run(
        back_kernel,
        "temporal_back_projection",
        [sds(nf, 2 * nq * fr, half), sds(3, half // 4, width)],
        [geo, after(all_terms[0], pair_terms[0])] + all_terms[1:] + [motion_weights],
        0.01,
    )
    last_terms = [move(pair_terms[0], flipped(1))]

    stage, block = nf // 4, half // nf
    sums, gain_sum = run(
        first_weight_kernel,
        "weight_terms_first_tokens",
        [
            sds(4, stage, block, width, dtype=F32),
            sds(1, half // 4, dtype=F32),
        ],
        [geo, early_left, quarter, table] + all_terms + core_terms
        + pair_terms[:1] + last_terms,
        0.01,
    )
    late_terms = [after(t, back_send, sums) for t in pair_terms[1:]]
    late_terms += [move(t, flipped(1)) for t in late_terms]
    parts_w = run(
        second_weight_kernel,
        "weight_terms_last_tokens",
        [sds(2 * block + 8, width)] * stage + [sds(2 * block, width)] * stage,
        [geo, sums, gain_sum, late_left, quarter, table, gain2] + late_terms,
        0.01,
        scratch=[pltpu.VMEM((4, stage, block, width), F32)],
    )

    def add(a, b):
        return (a.astype(F32) + b.astype(F32)).astype(BF16)

    back_recv = swap(back_send)
    backs = [back_recv] + [from_quad(back_recv, s) for s in range(1, nq)]
    block_output, grad_hidden = run(
        middle_kernel,
        "block_output_hidden_gradient",
        [sds(fr, pq, channels), sds(rows, channels)],
        [geo] + backs + cots + [kept, gain2],
        6,
        big,
    )
    totals = [parts_w[stage - 1], parts_w[2 * stage - 1]]
    for step in range(1, stage):
        for i in range(2):
            if step == stage - 2:
                totals[i] = after(totals[i], back_recv)
            moved = move(totals[i], ring)
            if step == stage - 1:
                moved = after(moved, grad_hidden)
            totals[i] = add(moved, parts_w[(i + 1) * stage - 1 - step])
    final = []
    for g in range(nf):
        for q in range(nq):
            j = quarter_of(g % 4) * stage + g // 4
            final.append((g * nq + q, nf * q + j))
    grad_hidden = after(grad_hidden, *totals)
    totals = [lax.ppermute(t, ("frame", "quad"), final) for t in totals]
    (input_grad,) = run(
        tail_kernel,
        "spatial_backward",
        [sds(fr, pq, channels)],
        [grad_hidden, activations, kept, gain1, spatial_weights],
        3.5,
        big,
    )
    everyone = nf * nq
    factor = 1.0 / math.sqrt(everyone * fr * pq)
    weight_grad = jnp.concatenate([totals[0][: 2 * block], totals[1]], axis=0)
    weight_grad = weight_grad.reshape(4, block, width).astype(F32) * factor
    place = ((frame * nq + quad) % stage) * block
    gain_grad = lax.dynamic_slice(totals[0][2 * block], (place,), (block,)).astype(F32) * factor
    return block_output, input_grad, weight_grad, gain_grad


def solution(mesh):
    in_specs = (
        P("frame", "quad", None),
        P("frame", "quad", None),
        P(),
        P(),
        P(None, "quad", None),
        P(),
    )
    out_specs = (
        P("frame", "quad", None),
        P("frame", "quad", None),
        P(None, ("frame", "quad"), None),
        P(("frame", "quad")),
    )
    body = functools.partial(local, mesh.shape["quad"], mesh.shape["frame"])
    return jax.shard_map(
        body, mesh=mesh, in_specs=in_specs, out_specs=out_specs, check_vma=False
    )
```
